32 devices in a mesh: batch: 8 (over z, y), freq: 4 (over x, core).
Axes of the slice: x: 2, y: 2, z: 4, core: 2. Of those that a mesh axis runs over, the one named last changes fastest.
Arguments:
- tokens: bfloat16 [1024, 8, 768], P('freq', 'batch'), may hold values from -6 to 6
- seg_ids: int32 [8, 1024], P('batch'), may hold values from 0 to 2, never falling along the last dimension, each value on 1 to 770 neighbouring positions
- cotangent: bfloat16 [1024, 8, 768], P('freq', 'batch'), may hold values from -6 to 6
- ln1_gain: float32 [768], replicated, may hold values from 0.25 to 1.75
- ln1_shift: float32 [768], replicated, may hold values from -3 to 3
- w_in: bfloat16 [768, 1536], replicated, may hold values from -0.21875 to 0.21875
- conv_taps: float32 [3, 1536], replicated, may hold values from -3 to 3
- freq_w1: float32 [64, 64], replicated, may hold values from -1 to 1
- freq_b1: float32 [64], replicated, may hold values from -3 to 3
- freq_w2: float32 [64, 1536], replicated, may hold values from -1 to 1
- cond_w: float32 [768, 64], replicated, may hold values from -0.625 to 0.625
- w_out: bfloat16 [768, 768], replicated, may hold values from -0.3125 to 0.3125
- ln2_gain: float32 [768], replicated, may hold values from 0.25 to 1.75
- ln2_shift: float32 [768], replicated, may hold values from -3 to 3
- w_gate: bfloat16 [768, 3072], replicated, may hold values from -0.21875 to 0.21875
- w_up: bfloat16 [768, 3072], replicated, may hold values from -0.21875 to 0.21875
- w_down: bfloat16 [3072, 768], replicated, may hold values from -0.15625 to 0.15625
Outputs:
- mixed_out: bfloat16 [1024, 8, 768], P('freq', 'batch')
- grad_tokens: float32 [1024, 8, 768], P('freq', 'batch')
- grad_ln1_gain: float32 [768], replicated
- grad_ln1_shift: float32 [768], replicated
- grad_w_in: float32 [768, 1536], P(None, ('batch', 'freq'))
- grad_conv_taps: float32 [3, 1536], replicated
- grad_freq_w1: float32 [64, 64], replicated
- grad_freq_b1: float32 [64], replicated
- grad_freq_w2: float32 [64, 1536], replicated
- grad_cond_w: float32 [768, 64], replicated
- grad_w_out: float32 [768, 768], P(None, ('batch', 'freq'))
- grad_ln2_gain: float32 [768], replicated
- grad_ln2_shift: float32 [768], replicated
- grad_w_gate: float32 [768, 3072], P(None, ('batch', 'freq'))
- grad_w_up: float32 [768, 3072], P(None, ('batch', 'freq'))
- grad_w_down: float32 [3072, 768], P(('batch', 'freq'))
The draws below stay inside these ranges and needn't reach their ends.
Inputs may be any that keep to these rules, and one draw needn't show every extreme that they name: `seg_ids`: in each row the document numbers run 0, 1, .. 2 without falling, each present; one document of each row has exactly 770 tokens.
All inputs are finite; a program needn't handle non-finite values.
Results may differ from the reference program's by a relative error of at most 0.013.
Values may be sent and summed in bfloat16 or wider, within the bound.
No kernel may reach another device: no remote copies, remote signals or barrier semaphores. Data moves between devices by JAX's collectives and lax.ppermute only.
A program may use at most 128 MiB of HBM per device.

```python
import math
import jax
import jax.numpy as jnp
import numpy as np
from jax import lax

D = 768
FF = 3072
L = 1024
KE = 64
KH = 64
SEGS = 3
ROWS = 8
SEG_MOST = 770


def raised(values, key, source, target, shards_of, factor):
    owner, partner = [(jnp.arange(values.shape[position]) // (values.shape[position] // shards_of)).reshape([-1 if axis == position else 1 for axis in range(values.ndim)]) for position in (source, target)]
    chosen = jax.random.permutation(key, shards_of)[partner]
    strong = (owner == chosen) | (owner == (partner + shards_of // 2) % shards_of)
    return jnp.where(strong, factor * values, values)


def steps_of(rng, dims, cuts, low, top_value):
    loudness = 1.0
    for dim, parts in cuts:
        draws = jax.random.uniform(jax.random.fold_in(jax.random.fold_in(rng, 6), dim), (parts,), jnp.float32, low / len(cuts), top_value / len(cuts))
        loudness = loudness * jnp.repeat(jnp.exp(draws), dims[dim] // parts).reshape((-1,) + (1,) * (len(dims) - 1 - dim))
    return loudness


def profile(amount, total, most, lean):
    loads = [(1 << 20) // math.isqrt(rank ** lean) + 1 for rank in range(2, amount + 1)]
    surplus, given = total - most - (amount - 1), [1] * (amount - 1)
    while surplus > 0:
        free = [i for i in range(amount - 1) if given[i] < most]
        pool, left = sum([loads[i] for i in free]), surplus
        for i in free:
            more = min(most - given[i], max(1, left * loads[i] // pool), surplus)
            given[i] = given[i] + more
            surplus = surplus - more
    return np.array([most] + given)


def ragged_sizes(own_key, amount, total, reach, lean):
    if amount == 2:
        one = jax.random.randint(own_key, (), max(1, total - reach), min(reach, total - 1) + 1)
        return jnp.stack([one, total - one])
    sizes = jnp.asarray(profile(amount, total, reach, lean), jnp.int32)
    couples = (amount - 1) // 2
    giver, taker = sizes[1:1 + 2 * couples:2], sizes[2:2 + 2 * couples:2]
    room = jnp.minimum(giver - 1, reach - taker)
    shifted = jax.random.randint(jax.random.fold_in(own_key, 1), (couples,), 0, 1 << 20) % (room + 1)
    sizes = sizes.at[1:1 + 2 * couples:2].set(giver - shifted).at[2:2 + 2 * couples:2].set(taker + shifted)
    return sizes[jax.random.permutation(jax.random.fold_in(own_key, 2), amount)]


def gaussian(stream_key, dims, deviation, most, cuts=(), kind=jnp.bfloat16):
    values = deviation * jax.random.normal(stream_key, dims, jnp.float32)
    if cuts:
        values = values * steps_of(stream_key, dims, cuts, -0.22, 0.18)
    return jnp.clip(values, -most, most).astype(kind)


def bell_draw_with(own_key, shape, scale, reach, pieces, heavy, kind=jnp.bfloat16):
    values = scale * jax.random.normal(own_key, shape, jnp.float32)
    if pieces:
        values = values * steps_of(own_key, shape, pieces, -0.22, 0.18)
    return jnp.clip(raised(values, jax.random.fold_in(own_key, 3), *heavy), -reach, reach).astype(kind)


def setup_inputs(seed: int = 0) -> dict:
    seeds = jax.random.split(jax.random.key(seed), 18)
    return {
        "tokens": gaussian(seeds[0], (L, ROWS, D), 1.0, 6.0, ((0, 4), (1, 8))),
        "seg_ids": jax.vmap(lambda own: jnp.searchsorted(jnp.cumsum(ragged_sizes(own, SEGS, L, SEG_MOST, 0)), jnp.arange(L), side="right"))(jax.random.split(seeds[1], ROWS)).reshape((ROWS, L)).astype(jnp.int32),
        "cotangent": bell_draw_with(seeds[2], (L, ROWS, D), 1.0, 6.0, ((0, 4), (1, 8)), (1, 2, 8, 2.0)),
        "ln1_gain": jnp.clip(1.0 + 0.15 * jax.random.normal(seeds[3], (D,), jnp.float32), 0.25, 1.75),
        "ln1_shift": gaussian(seeds[4], (D,), 0.4, 3.0, (), jnp.float32),
        "w_in": gaussian(seeds[5], (D, 2 * D), D ** -0.5, 0.21875),
        "conv_taps": gaussian(seeds[6], (3, 2 * D), 0.6, 3.0, (), jnp.float32),
        "freq_w1": gaussian(seeds[7], (KE, KH), (KE // 2) ** -0.5, 1.0, (), jnp.float32),
        "freq_b1": gaussian(seeds[8], (KH,), 0.5, 3.0, (), jnp.float32),
        "freq_w2": gaussian(seeds[9], (KH, 2 * D), (KH // 2) ** -0.5, 1.0, (), jnp.float32),
        "cond_w": gaussian(seeds[10], (D, KH), (D // 8) ** -0.5, 0.625, (), jnp.float32),
        "w_out": gaussian(seeds[11], (D, D), (D // 2) ** -0.5, 0.3125),
        "ln2_gain": jnp.clip(1.0 + 0.15 * jax.random.normal(seeds[12], (D,), jnp.float32), 0.25, 1.75),
        "ln2_shift": gaussian(seeds[13], (D,), 0.4, 3.0, (), jnp.float32),
        "w_gate": gaussian(seeds[14], (D, FF), D ** -0.5, 0.21875),
        "w_up": gaussian(seeds[15], (D, FF), D ** -0.5, 0.21875),
        "w_down": gaussian(seeds[16], (FF, D), (FF // 2) ** -0.5, 0.15625),
    }


full_precision = lax.Precision.HIGHEST
epsilon = 1e-05

@jax.custom_vjp
def low(v):
    return lax.optimization_barrier(v.astype(jnp.bfloat16)).astype(jnp.float32)

@jax.custom_vjp
def low_back(v):
    return v

def low_keep(v):
    return (low(v), None)

def low_pass(kept, grad):
    return (grad,)

def back_keep(v):
    return (v, None)

def back_low(kept, grad):
    return (low(grad),)
low.defvjp(low_keep, low_pass)
low_back.defvjp(back_keep, back_low)

def layer_norm(values, gain, shift):
    centered = values - lax.optimization_barrier(jnp.mean(values, axis=-1, keepdims=True))
    variance = lax.optimization_barrier(jnp.mean(centered * centered, axis=-1, keepdims=True))
    return centered * lax.rsqrt(variance + epsilon) * gain + shift

def kernel_mlp(first_w, first_b, second_w, cond_bias, freq_ids, length):
    half_count = first_w.shape[0] // 2
    lag_list = (jnp.arange(half_count, dtype=jnp.int32) + 1) ** 2
    phase_index = freq_ids[:, None] * lag_list[None, :] % (2 * length)
    angles = phase_index.astype(jnp.float32) * (jnp.pi / length)
    features = jnp.concatenate([jnp.cos(angles), jnp.sin(angles)], axis=1)
    base = jnp.dot(features, first_w, precision=full_precision) + first_b
    hidden = jax.nn.silu(base[None, None] + cond_bias[:, :, None, :])
    spectral_kernel = jnp.einsum('srfk,kc->srfc', hidden, second_w, precision=full_precision)
    channels = second_w.shape[1] // 2
    return (spectral_kernel[..., :channels], spectral_kernel[..., channels:])

def block_forward(params, kernel_params, block_tokens, block_ids):
    gain_one, shift_one, weight_in, taps, weight_out, gain_two, shift_two, weight_gate, weight_up, weight_down = params
    first_w, first_b, second_w, cond_weight = kernel_params
    normed_one = low(layer_norm(block_tokens, gain_one, shift_one))
    numbers = jnp.arange(SEGS, dtype=jnp.int32)
    all_masks = (block_ids[None] == numbers[:, None, None]).astype(jnp.float32)
    counts = lax.optimization_barrier(jnp.sum(all_masks, axis=2))
    seg_sums = jnp.einsum('srt,rtd->srd', all_masks, normed_one, precision=full_precision)
    cond_bias = jnp.einsum('srd,dk->srk', seg_sums / counts[..., None], cond_weight, precision=full_precision)
    freq_ids = jnp.arange(L, dtype=jnp.int32)
    kernel_real, kernel_imag = kernel_mlp(first_w, first_b, second_w, cond_bias, freq_ids, L)
    projected = low_back(jnp.einsum('rtd,de->rte', normed_one, weight_in, precision=full_precision))
    matches = (block_ids[:, 1:] == block_ids[:, :-1]).astype(jnp.float32)
    zero_column = jnp.zeros((block_ids.shape[0], 1), jnp.float32)
    same_prev = jnp.concatenate([zero_column, matches], axis=1)[..., None]
    same_next = jnp.concatenate([matches, zero_column], axis=1)[..., None]
    before = jnp.pad(projected, ((0, 0), (1, 0), (0, 0)))[:, :-1]
    after = jnp.pad(projected, ((0, 0), (0, 1), (0, 0)))[:, 1:]
    mixed = taps[0] * before * same_prev + taps[1] * projected + taps[2] * after * same_next
    gate_part = mixed[..., :D]
    value_part = mixed[..., D:]
    convolved = jnp.zeros_like(value_part)
    for segment in range(SEGS):
        member = all_masks[segment][..., None]
        kernel = lax.complex(kernel_real[segment], kernel_imag[segment])
        spectrum = jnp.fft.rfft(value_part * member, n=2 * L, axis=1)[:, :L]
        product = spectrum * kernel
        extended = jnp.concatenate([product, jnp.zeros_like(product[:, :1])], axis=1)
        convolved = convolved + jnp.fft.irfft(extended, n=2 * L, axis=1)[:, :L] * member
    gated = low(gate_part * convolved)
    branch_out = low_back(jnp.einsum('rtd,de->rte', gated, weight_out, precision=full_precision))
    middle = block_tokens + branch_out
    normed_two = low(layer_norm(middle, gain_two, shift_two))
    gate_value = low_back(jnp.einsum('rtd,dh->rth', normed_two, weight_gate, precision=full_precision))
    up_value = low_back(jnp.einsum('rtd,dh->rth', normed_two, weight_up, precision=full_precision))
    hidden = low(jax.nn.silu(gate_value) * up_value)
    feed_out = low_back(jnp.einsum('rth,hd->rtd', hidden, weight_down, precision=full_precision))
    return middle + feed_out

def reference(tokens, seg_ids, cotangent, ln1_gain, ln1_shift, w_in, conv_taps, freq_w1, freq_b1, freq_w2, cond_w, w_out, ln2_gain, ln2_shift, w_gate, w_up, w_down):
    floats = (tokens.astype(jnp.float32), ln1_gain.astype(jnp.float32), ln1_shift.astype(jnp.float32), w_in.astype(jnp.float32), conv_taps.astype(jnp.float32), freq_w1.astype(jnp.float32), freq_b1.astype(jnp.float32), freq_w2.astype(jnp.float32), cond_w.astype(jnp.float32), w_out.astype(jnp.float32), ln2_gain.astype(jnp.float32), ln2_shift.astype(jnp.float32), w_gate.astype(jnp.float32), w_up.astype(jnp.float32), w_down.astype(jnp.float32))

    def forward(token_values, gain_one, shift_one, weight_in, taps, first_w, first_b, second_w, cond_weight, weight_out, gain_two, shift_two, weight_gate, weight_up, weight_down):
        params = (gain_one, shift_one, weight_in, taps, weight_out, gain_two, shift_two, weight_gate, weight_up, weight_down)
        kernel_params = (first_w, first_b, second_w, cond_weight)
        group_count = ROWS // 4
        grouped = jnp.transpose(token_values, (1, 0, 2)).reshape(group_count, 4, L, D)
        ids_grouped = seg_ids.reshape(group_count, 4, L)

        def one_group(inputs_pair):
            return block_forward(params, kernel_params, inputs_pair[0], inputs_pair[1])
        result = lax.map(jax.checkpoint(one_group), (grouped, ids_grouped))
        return jnp.transpose(result.reshape(ROWS, L, D), (1, 0, 2))
    mixed_out, pullback = jax.vjp(forward, *floats)
    gradients = pullback(cotangent.astype(jnp.float32))
    return (mixed_out.astype(jnp.bfloat16), gradients[0], gradients[1], gradients[2], gradients[3], gradients[4], gradients[5], gradients[6], gradients[7], gradients[8], gradients[9], gradients[10], gradients[11], gradients[12], gradients[13], gradients[14])
```

```python
import jax
import jax.numpy as jnp
import ml_dtypes
import numpy as np
from jax import lax
from jax.sharding import PartitionSpec as P

SEGS = 3
EPS = 1e-05
HIGH = lax.Precision.HIGHEST
F32 = jnp.float32
BF16 = jnp.bfloat16


def mm(a, b):
    return jnp.dot(a, b, preferred_element_type=F32)


def mm_nt(a, b):
    return lax.dot_general(a, b, (((1,), (1,)), ((), ())), preferred_element_type=F32)


def mm_tn(a, b):
    return lax.dot_general(a, b, (((0,), (0,)), ((), ())), preferred_element_type=F32)


def swap(value, axis, mask):
    count = lax.axis_size(axis)
    return lax.ppermute(value, axis, [(i, i ^ mask) for i in range(count)])


def pick(parts, index):
    return lax.dynamic_index_in_dim(parts, index, 0, keepdims=False)


def in_order(received, me):
    a, b, c, d = received
    low = (me & 1) == 1
    a, b = jnp.where(low, b, a), jnp.where(low, a, b)
    c, d = jnp.where(low, d, c), jnp.where(low, c, d)
    high = (me & 2) == 2
    a, c = jnp.where(high, c, a), jnp.where(high, a, c)
    b, d = jnp.where(high, d, b), jnp.where(high, b, d)
    return (a, b, c, d)


def trade(blocks, me):
    return [pick(blocks, me)] + [swap(pick(blocks, me ^ k), "freq", k) for k in (2, 3, 1)]


def trade_sorted(blocks, me):
    own, two, three, one = trade(blocks, me)
    return in_order((own, one, two, three), me)


def gather_freq(value, me):
    two = swap(value, "freq", 2)
    one = swap(value, "freq", 1)
    three = swap(two, "freq", 1)
    return (value, one, two, three)


def scatter_sum(value, order):
    bits = lax.axis_size("batch").bit_length() - 1
    me = lax.axis_index("batch")
    rest = value.shape[1:]
    value = value.reshape((2,) * bits + rest)
    left = list(range(bits - 1, -1, -1))
    for bit in order:
        dim = left.index(bit)
        mine = (me >> bit) & 1
        keep = lax.dynamic_index_in_dim(value, mine, dim, keepdims=False)
        give = lax.dynamic_index_in_dim(value, 1 - mine, dim, keepdims=False)
        got = swap(give, "batch", 1 << bit)
        total = keep.astype(F32) + got.astype(F32)
        left.remove(bit)
        value = total.astype(value.dtype) if left else total
    return value


def tables(length):
    index = np.arange(length, dtype=np.int64)
    angle = (index[:, None] * index[None, :] % (2 * length)) * (np.pi / length)
    return (
        np.cos(angle).astype(ml_dtypes.bfloat16),
        np.sin(angle).astype(ml_dtypes.bfloat16),
    )


def features(length, half):
    index = np.arange(length, dtype=np.int64)
    lags = (np.arange(half, dtype=np.int64) + 1) ** 2
    angle = (lags[:, None] * index[None, :] % (2 * length)) * (np.pi / length)
    return np.concatenate([np.cos(angle), np.sin(angle)], axis=0).astype(np.float32)


def normed(values):
    centered = values - jnp.mean(values, axis=-1, keepdims=True)
    scale = lax.rsqrt(jnp.mean(centered * centered, axis=-1, keepdims=True) + EPS)
    return centered * scale, scale


def norm_back(unit, scale, grad):
    return scale * (
        grad
        - jnp.mean(grad, axis=-1, keepdims=True)
        - unit * jnp.mean(grad * unit, axis=-1, keepdims=True)
    )


def shift_right(values):
    return jnp.pad(values, ((0, 0), (1, 0)))[:, :-1]


def shift_left(values):
    return jnp.pad(values, ((0, 0), (0, 1)))[:, 1:]


def per_device(
    tokens,
    seg_ids,
    cotangent,
    ln1_gain,
    ln1_shift,
    w_in,
    conv_taps,
    freq_w1,
    freq_b1,
    freq_w2,
    cond_w,
    w_out,
    ln2_gain,
    ln2_shift,
    w_gate,
    w_up,
    w_down,
):
    quarter, _, channels = tokens.shape
    length = seg_ids.shape[1]
    ff = w_gate.shape[1]
    fs = lax.axis_size("freq")
    bs = lax.axis_size("batch")
    me = lax.axis_index("freq")
    width = channels // fs
    half = bs // 2
    step = channels // (half * fs)
    cos_table, sin_table = tables(length)
    feats = features(length, freq_w1.shape[0] // 2)

    x_own = tokens[:, 0]
    ct_own = cotangent[:, 0]
    ids = seg_ids
    x_parts = gather_freq(x_own, me)
    ct_parts = gather_freq(ct_own, me)

    w_in_t = (
        w_in.T.reshape(2, half, fs, step, channels)
        .transpose(2, 0, 1, 3, 4)
        .reshape(fs, 2 * width, channels)
    )
    w_in_mine = pick(w_in_t, me)
    w_out_p = (
        w_out.reshape(half, fs, step, channels).transpose(1, 0, 2, 3).reshape(channels, channels)
    )
    taps_mine = pick(
        conv_taps.reshape(3, 2, half, fs, step).transpose(3, 0, 1, 2, 4).reshape(fs, 3, 2 * width), me
    )[:, :, None]
    w2_mine = pick(
        freq_w2.reshape(-1, 2, half, fs, step).transpose(3, 0, 1, 2, 4).reshape(fs, -1, 2 * width), me
    )
    fw = ff // (bs * fs)
    wide = ff // fs

    def mine_rows(weight):
        return pick(
            weight.reshape(bs, fs, fw, channels).transpose(1, 0, 2, 3).reshape(fs, wide, channels), me
        )

    wg_mine, wu_mine, wd_mine = (mine_rows(w_gate.T), mine_rows(w_up.T), mine_rows(w_down))

    base = jnp.dot(freq_w1.T, feats, precision=HIGH) + freq_b1[:, None]

    x_row = jnp.concatenate(in_order(x_parts, me), axis=0).astype(F32)
    unit1, _ = normed(x_row)
    u1 = (unit1 * ln1_gain + ln1_shift).astype(BF16)
    n1 = unit1.astype(BF16)
    masks = (ids == jnp.arange(SEGS, dtype=jnp.int32)[:, None]).astype(F32)
    counts = jnp.sum(masks, axis=1, keepdims=True)
    mu = mm(masks.astype(BF16), u1) / counts
    mn = mm(masks.astype(BF16), n1) / counts
    cb = jnp.dot(mu, cond_w, precision=HIGH)
    p = mm_nt(w_in_mine, u1)
    same = (ids[:, 1:] == ids[:, :-1]).astype(F32)
    zero = jnp.zeros((1, 1), F32)
    prev = jnp.concatenate([zero, same], axis=1)
    nxt = jnp.concatenate([same, zero], axis=1)
    p_prev = shift_right(p) * prev
    p_next = shift_left(p) * nxt
    s = taps_mine[0] * p_prev + taps_mine[1] * p + taps_mine[2] * p_next
    q, v = s[:width], s[width:]

    pre = base[None] + cb[:, :, None]
    gate_pre = jax.nn.sigmoid(pre)
    hk = pre * gate_pre
    kk = jnp.einsum("kc,jkf->jcf", w2_mine, hk, precision=HIGH)
    kr, ki = kk[:, :width], kk[:, width:]
    vm = (v[None] * masks[:, None, :]).astype(BF16).reshape(SEGS * width, length)
    vr = mm(vm, cos_table).reshape(SEGS, width, length)
    vi = -mm(vm, sin_table).reshape(SEGS, width, length)
    weights = np.full((length,), 2.0 / (2 * length), np.float32)
    weights[0] = 1.0 / (2 * length)
    yr = ((kr * vr - ki * vi) * weights).astype(BF16).reshape(SEGS * width, length)
    yi = ((kr * vi + ki * vr) * weights).astype(BF16).reshape(SEGS * width, length)
    conv = (mm(yr, cos_table) - mm(yi, sin_table)).reshape(SEGS, width, length)
    c = jnp.sum(conv * masks[:, None, :], axis=0)
    z_mine = (q * c).astype(BF16)

    z_blocks = z_mine.reshape(width, fs, quarter).transpose(1, 0, 2)
    z_t = jnp.concatenate(trade_sorted(z_blocks, me), axis=0)

    x32 = x_own.astype(F32)
    ct32 = ct_own.astype(F32)
    h = x32 + mm_tn(z_t, w_out_p)
    unit2, scale2 = normed(h)
    u2 = (unit2 * ln2_gain + ln2_shift).astype(BF16)
    u2_parts = gather_freq(u2, me)
    g = mm(u2, w_gate)
    a = mm(u2, w_up)
    gh = mm_nt(ct_own, w_down)
    sg = jax.nn.sigmoid(g)
    silu = g * sg
    hid = (silu * a).astype(BF16)
    mixed_out = (h + mm(hid, w_down)).astype(BF16)
    gg = (gh * a * sg * (1.0 + g * (1.0 - sg))).astype(BF16)
    ga = (gh * silu).astype(BF16)
    gu2 = mm_nt(gg, w_gate) + mm_nt(ga, w_up)
    grad_ln2_gain = jnp.sum(gu2 * unit2, axis=0)
    grad_ln2_shift = jnp.sum(gu2, axis=0)
    big_g = ct32 + norm_back(unit2, scale2, gu2 * ln2_gain)
    gb = big_g.astype(BF16)
    gz_blocks = mm_nt(w_out_p, gb).astype(BF16).reshape(fs, width, quarter)
    gz = jnp.concatenate(trade_sorted(gz_blocks, me), axis=1).astype(F32)
    gb_parts = gather_freq(gb, me)

    u2_row = jnp.concatenate(u2_parts, axis=0)
    ct_row = jnp.concatenate(ct_parts, axis=0)
    g_t = mm_nt(wg_mine, u2_row)
    a_t = mm_nt(wu_mine, u2_row)
    gh_t = mm_nt(wd_mine, ct_row)
    sg_t = jax.nn.sigmoid(g_t)
    silu_t = g_t * sg_t
    hid_t = (silu_t * a_t).astype(BF16)
    gg_t = (gh_t * a_t * sg_t * (1.0 + g_t * (1.0 - sg_t))).astype(BF16)
    ga_t = (gh_t * silu_t).astype(BF16)
    d_gate = mm(gg_t, u2_row).astype(BF16)
    d_up = mm(ga_t, u2_row).astype(BF16)
    d_down = mm(hid_t, ct_row).astype(BF16)
    d_ff = jnp.stack([d_gate, d_up, d_down], axis=0).reshape(3, bs, fw, channels).transpose(1, 0, 2, 3)
    bits = bs.bit_length() - 1
    order_a = list(range(bits))
    order_b = [1, 0] + list(range(2, bits))
    cut = channels // 2
    ff_a = scatter_sum(d_ff[..., :cut], order_a)
    ff_b = scatter_sum(d_ff[..., cut:], order_b)
    d_ff = jnp.concatenate([ff_a, ff_b], axis=-1)

    gq = gz * c
    gc = gz * q
    gcm = (gc[None] * masks[:, None, :]).astype(BF16).reshape(SEGS * width, length)
    gyr = mm(gcm, cos_table).reshape(SEGS, width, length) * weights
    gyi = -mm(gcm, sin_table).reshape(SEGS, width, length) * weights
    gkr = gyr * vr + gyi * vi
    gki = gyi * vr - gyr * vi
    gvr = (kr * gyr + ki * gyi).astype(BF16).reshape(SEGS * width, length)
    gvi = (kr * gyi - ki * gyr).astype(BF16).reshape(SEGS * width, length)
    gv_all = (mm(gvr, cos_table) - mm(gvi, sin_table)).reshape(SEGS, width, length)
    gv = jnp.sum(gv_all * masks[:, None, :], axis=0)
    gs = jnp.concatenate([gq, gv], axis=0)
    d_taps = jnp.stack(
        [jnp.sum(gs * p_prev, axis=1), jnp.sum(gs * p, axis=1), jnp.sum(gs * p_next, axis=1)]
    )
    gp = (
        taps_mine[1] * gs
        + taps_mine[0] * shift_left(gs * prev)
        + taps_mine[2] * shift_right(gs * nxt)
    ).astype(BF16)

    gkk = jnp.concatenate([gkr, gki], axis=1)
    gkk_low = gkk.astype(BF16)
    hk_low = hk.astype(BF16)
    d_w2 = jnp.einsum("jkf,jcf->kc", hk_low, gkk_low, preferred_element_type=F32)
    gpre = jnp.einsum("kc,jcf->jkf", w2_mine.astype(BF16), gkk_low, preferred_element_type=F32)
    gpre = gpre * gate_pre * (1.0 + pre * (1.0 - gate_pre))
    d_w1 = jnp.einsum("ef,jkf->ek", feats, gpre, precision=HIGH)
    gcb = jnp.sum(gpre, axis=2)
    gcb_row = lax.psum(gcb, "freq")

    gp_blocks = gp.reshape(2 * width, fs, quarter).transpose(1, 0, 2)
    gp_t = jnp.concatenate(trade_sorted(gp_blocks, me), axis=0)

    u1_row = u1
    d_in = mm(gp, u1_row).astype(BF16).reshape(bs, 2 * width // bs, channels)
    d_in = scatter_sum(d_in, order_a)
    gb_row = jnp.concatenate(in_order(gb_parts, me), axis=0)
    d_out = mm(z_mine, gb_row)
    narrow = channels // bs
    d_out = scatter_sum(d_out.T.astype(BF16).reshape(bs, narrow, width), order_a)
    d_out = d_out.reshape(fs, narrow // fs, width)
    d_out = jnp.stack(trade_sorted(d_out, me), axis=0)
    d_out = (
        d_out.reshape(fs, narrow // fs, half, step).transpose(2, 0, 3, 1).reshape(channels, -1)
    )

    gmu_part = jnp.dot(gcb, cond_w.T, precision=HIGH)
    sum_gp = jnp.sum(gp.astype(F32), axis=1)
    w_mine32 = w_in_mine.astype(F32)
    d_shift1 = jnp.dot(sum_gp[None], w_mine32, precision=HIGH)[0] + jnp.sum(gmu_part, axis=0)
    d_gain1 = jnp.sum(mm(gp, n1) * w_mine32, axis=0) + jnp.sum(gmu_part * mn, axis=0)

    gmu = jnp.dot(gcb_row, cond_w.T, precision=HIGH) / counts
    own_masks = lax.dynamic_slice_in_dim(masks, me * quarter, quarter, 1)
    gu1 = mm_tn(gp_t, w_in_t.reshape(2 * channels, channels)) + lax.dot_general(
        own_masks, gmu, (((0,), (0,)), ((), ())), precision=HIGH
    )
    unit_own, scale_own = normed(x32)
    grad_tokens = big_g + norm_back(unit_own, scale_own, gu1 * ln1_gain)

    shared = [
        d_gain1,
        d_shift1,
        d_w1.reshape(-1),
        jnp.sum(gcb, axis=0),
        jnp.dot(mu.T, gcb, precision=HIGH).reshape(-1),
        grad_ln2_gain,
        grad_ln2_shift,
    ]
    owned = jnp.concatenate([d_taps, d_w2], axis=0)
    packed = jnp.concatenate(shared + [owned.reshape(-1)])
    for bit in range(bits):
        packed = packed + swap(packed, "batch", 1 << bit)
    split = packed.shape[0] - owned.size
    common, owned = packed[:split], packed[split:]
    common = common + swap(common, "freq", 1)
    common = common + swap(common, "freq", 2)
    owned = jnp.stack(in_order(gather_freq(owned, me), me), axis=0)
    owned = (
        owned.reshape(fs, -1, 2, half, step).transpose(1, 2, 3, 0, 4).reshape(-1, 2 * channels)
    )
    sizes = np.cumsum([part.size for part in shared])
    got = jnp.split(common, sizes[:-1])
    return (
        mixed_out[:, None],
        grad_tokens[:, None],
        got[0],
        got[1],
        d_in.T,
        owned[:3],
        got[2].reshape(freq_w1.shape),
        got[3],
        owned[3:],
        got[4].reshape(cond_w.shape),
        d_out,
        got[5],
        got[6],
        d_ff[0].T,
        d_ff[1].T,
        d_ff[2],
    )


def solution(mesh):
    rows = P("freq", "batch", None)
    split = P(None, ("batch", "freq"))
    in_specs = (rows, P("batch", None), rows) + (P(),) * 14
    out_specs = (
        rows,
        rows,
        P(),
        P(),
        split,
        P(),
        P(),
        P(),
        P(),
        P(),
        split,
        P(),
        P(),
        split,
        split,
        P(("batch", "freq"), None),
    )
    return jax.shard_map(
        per_device, mesh=mesh, in_specs=in_specs, out_specs=out_specs, check_vma=False
    )
```

```python
import functools

import jax
import jax.numpy as jnp
import ml_dtypes
import numpy as np
from jax import lax
from jax.experimental import pallas as pl
from jax.experimental.pallas import tpu as pltpu
from jax.sharding import PartitionSpec as P

SEGS = 3
EPS = 1e-05
HIGH = lax.Precision.HIGHEST
F32 = jnp.float32
BF16 = jnp.bfloat16


def mm(a, b):
    return jnp.dot(a, b, preferred_element_type=F32)


def mm_nt(a, b):
    return lax.dot_general(a, b, (((1,), (1,)), ((), ())), preferred_element_type=F32)


def mm_tn(a, b):
    return lax.dot_general(a, b, (((0,), (0,)), ((), ())), preferred_element_type=F32)


def swap(value, axis, mask):
    count = lax.axis_size(axis)
    return lax.ppermute(value, axis, [(i, i ^ mask) for i in range(count)])


def pick(parts, index):
    return lax.dynamic_index_in_dim(parts, index, 0, keepdims=False)


def in_order(received, me):
    a, b, c, d = received
    low = (me & 1) == 1
    a, b = jnp.where(low, b, a), jnp.where(low, a, b)
    c, d = jnp.where(low, d, c), jnp.where(low, c, d)
    high = (me & 2) == 2
    a, c = jnp.where(high, c, a), jnp.where(high, a, c)
    b, d = jnp.where(high, d, b), jnp.where(high, b, d)
    return (a, b, c, d)


def trade(blocks, me):
    return [pick(blocks, me)] + [swap(pick(blocks, me ^ k), "freq", k) for k in (2, 3, 1)]


def trade_sorted(blocks, me):
    own, two, three, one = trade(blocks, me)
    return in_order((own, one, two, three), me)


def gather_freq(value, me):
    two = swap(value, "freq", 2)
    one = swap(value, "freq", 1)
    three = swap(two, "freq", 1)
    return (value, one, two, three)


def scatter_sum(value, order):
    bits = lax.axis_size("batch").bit_length() - 1
    me = lax.axis_index("batch")
    rest = value.shape[1:]
    value = value.reshape((2,) * bits + rest)
    left = list(range(bits - 1, -1, -1))
    for bit in order:
        dim = left.index(bit)
        mine = (me >> bit) & 1
        keep = lax.dynamic_index_in_dim(value, mine, dim, keepdims=False)
        give = lax.dynamic_index_in_dim(value, 1 - mine, dim, keepdims=False)
        got = swap(give, "batch", 1 << bit)
        total = keep.astype(F32) + got.astype(F32)
        left.remove(bit)
        value = total.astype(value.dtype) if left else total
    return value


def tables(length):
    index = np.arange(length, dtype=np.int64)
    angle = (index[:, None] * index[None, :] % (2 * length)) * (np.pi / length)
    return (
        np.cos(angle).astype(ml_dtypes.bfloat16),
        np.sin(angle).astype(ml_dtypes.bfloat16),
    )


def features(length, half):
    index = np.arange(length, dtype=np.int64)
    lags = (np.arange(half, dtype=np.int64) + 1) ** 2
    angle = (lags[:, None] * index[None, :] % (2 * length)) * (np.pi / length)
    return np.concatenate([np.cos(angle), np.sin(angle)], axis=0).astype(np.float32)


def normed(values):
    centered = values - jnp.mean(values, axis=-1, keepdims=True)
    scale = lax.rsqrt(jnp.mean(centered * centered, axis=-1, keepdims=True) + EPS)
    return centered * scale, scale


def norm_back(unit, scale, grad):
    return scale * (
        grad
        - jnp.mean(grad, axis=-1, keepdims=True)
        - unit * jnp.mean(grad * unit, axis=-1, keepdims=True)
    )


def shift_right(values):
    return jnp.pad(values, ((0, 0), (1, 0)))[:, :-1]


def shift_left(values):
    return jnp.pad(values, ((0, 0), (0, 1)))[:, 1:]


def plain_device(
    tokens,
    seg_ids,
    cotangent,
    ln1_gain,
    ln1_shift,
    w_in,
    conv_taps,
    freq_w1,
    freq_b1,
    freq_w2,
    cond_w,
    w_out,
    ln2_gain,
    ln2_shift,
    w_gate,
    w_up,
    w_down,
):
    quarter, _, channels = tokens.shape
    length = seg_ids.shape[1]
    ff = w_gate.shape[1]
    fs = lax.axis_size("freq")
    bs = lax.axis_size("batch")
    me = lax.axis_index("freq")
    width = channels // fs
    half = bs // 2
    step = channels // (half * fs)
    cos_table, sin_table = tables(length)
    feats = features(length, freq_w1.shape[0] // 2)

    x_own = tokens[:, 0]
    ct_own = cotangent[:, 0]
    ids = seg_ids
    x_parts = gather_freq(x_own, me)
    ct_parts = gather_freq(ct_own, me)

    w_in_t = (
        w_in.T.reshape(2, half, fs, step, channels)
        .transpose(2, 0, 1, 3, 4)
        .reshape(fs, 2 * width, channels)
    )
    w_in_mine = pick(w_in_t, me)
    w_out_p = (
        w_out.reshape(half, fs, step, channels).transpose(1, 0, 2, 3).reshape(channels, channels)
    )
    taps_mine = pick(
        conv_taps.reshape(3, 2, half, fs, step).transpose(3, 0, 1, 2, 4).reshape(fs, 3, 2 * width), me
    )[:, :, None]
    w2_mine = pick(
        freq_w2.reshape(-1, 2, half, fs, step).transpose(3, 0, 1, 2, 4).reshape(fs, -1, 2 * width), me
    )
    fw = ff // (bs * fs)
    wide = ff // fs

    def mine_rows(weight):
        return pick(
            weight.reshape(bs, fs, fw, channels).transpose(1, 0, 2, 3).reshape(fs, wide, channels), me
        )

    wg_mine, wu_mine, wd_mine = (mine_rows(w_gate.T), mine_rows(w_up.T), mine_rows(w_down))

    base = jnp.dot(freq_w1.T, feats, precision=HIGH) + freq_b1[:, None]

    x_row = jnp.concatenate(in_order(x_parts, me), axis=0).astype(F32)
    unit1, _ = normed(x_row)
    u1 = (unit1 * ln1_gain + ln1_shift).astype(BF16)
    n1 = unit1.astype(BF16)
    masks = (ids == jnp.arange(SEGS, dtype=jnp.int32)[:, None]).astype(F32)
    counts = jnp.sum(masks, axis=1, keepdims=True)
    mu = mm(masks.astype(BF16), u1) / counts
    mn = mm(masks.astype(BF16), n1) / counts
    cb = jnp.dot(mu, cond_w, precision=HIGH)
    p = mm_nt(w_in_mine, u1)
    same = (ids[:, 1:] == ids[:, :-1]).astype(F32)
    zero = jnp.zeros((1, 1), F32)
    prev = jnp.concatenate([zero, same], axis=1)
    nxt = jnp.concatenate([same, zero], axis=1)
    p_prev = shift_right(p) * prev
    p_next = shift_left(p) * nxt
    s = taps_mine[0] * p_prev + taps_mine[1] * p + taps_mine[2] * p_next
    q, v = s[:width], s[width:]

    pre = base[None] + cb[:, :, None]
    gate_pre = jax.nn.sigmoid(pre)
    hk = pre * gate_pre
    kk = jnp.einsum("kc,jkf->jcf", w2_mine, hk, precision=HIGH)
    kr, ki = kk[:, :width], kk[:, width:]
    vm = (v[None] * masks[:, None, :]).astype(BF16).reshape(SEGS * width, length)
    vr = mm(vm, cos_table).reshape(SEGS, width, length)
    vi = -mm(vm, sin_table).reshape(SEGS, width, length)
    weights = np.full((length,), 2.0 / (2 * length), np.float32)
    weights[0] = 1.0 / (2 * length)
    yr = ((kr * vr - ki * vi) * weights).astype(BF16).reshape(SEGS * width, length)
    yi = ((kr * vi + ki * vr) * weights).astype(BF16).reshape(SEGS * width, length)
    conv = (mm(yr, cos_table) - mm(yi, sin_table)).reshape(SEGS, width, length)
    c = jnp.sum(conv * masks[:, None, :], axis=0)
    z_mine = (q * c).astype(BF16)

    z_blocks = z_mine.reshape(width, fs, quarter).transpose(1, 0, 2)
    z_t = jnp.concatenate(trade_sorted(z_blocks, me), axis=0)

    x32 = x_own.astype(F32)
    ct32 = ct_own.astype(F32)
    h = x32 + mm_tn(z_t, w_out_p)
    unit2, scale2 = normed(h)
    u2 = (unit2 * ln2_gain + ln2_shift).astype(BF16)
    u2_parts = gather_freq(u2, me)
    g = mm(u2, w_gate)
    a = mm(u2, w_up)
    gh = mm_nt(ct_own, w_down)
    sg = jax.nn.sigmoid(g)
    silu = g * sg
    hid = (silu * a).astype(BF16)
    mixed_out = (h + mm(hid, w_down)).astype(BF16)
    gg = (gh * a * sg * (1.0 + g * (1.0 - sg))).astype(BF16)
    ga = (gh * silu).astype(BF16)
    gu2 = mm_nt(gg, w_gate) + mm_nt(ga, w_up)
    grad_ln2_gain = jnp.sum(gu2 * unit2, axis=0)
    grad_ln2_shift = jnp.sum(gu2, axis=0)
    big_g = ct32 + norm_back(unit2, scale2, gu2 * ln2_gain)
    gb = big_g.astype(BF16)
    gz_blocks = mm_nt(w_out_p, gb).astype(BF16).reshape(fs, width, quarter)
    gz = jnp.concatenate(trade_sorted(gz_blocks, me), axis=1).astype(F32)
    gb_parts = gather_freq(gb, me)

    u2_row = jnp.concatenate(u2_parts, axis=0)
    ct_row = jnp.concatenate(ct_parts, axis=0)
    g_t = mm_nt(wg_mine, u2_row)
    a_t = mm_nt(wu_mine, u2_row)
    gh_t = mm_nt(wd_mine, ct_row)
    sg_t = jax.nn.sigmoid(g_t)
    silu_t = g_t * sg_t
    hid_t = (silu_t * a_t).astype(BF16)
    gg_t = (gh_t * a_t * sg_t * (1.0 + g_t * (1.0 - sg_t))).astype(BF16)
    ga_t = (gh_t * silu_t).astype(BF16)
    d_gate = mm(gg_t, u2_row).astype(BF16)
    d_up = mm(ga_t, u2_row).astype(BF16)
    d_down = mm(hid_t, ct_row).astype(BF16)
    d_ff = jnp.stack([d_gate, d_up, d_down], axis=0).reshape(3, bs, fw, channels).transpose(1, 0, 2, 3)
    bits = bs.bit_length() - 1
    order_a = list(range(bits))
    order_b = [1, 0] + list(range(2, bits))
    cut = channels // 2
    ff_a = scatter_sum(d_ff[..., :cut], order_a)
    ff_b = scatter_sum(d_ff[..., cut:], order_b)
    d_ff = jnp.concatenate([ff_a, ff_b], axis=-1)

    gq = gz * c
    gc = gz * q
    gcm = (gc[None] * masks[:, None, :]).astype(BF16).reshape(SEGS * width, length)
    gyr = mm(gcm, cos_table).reshape(SEGS, width, length) * weights
    gyi = -mm(gcm, sin_table).reshape(SEGS, width, length) * weights
    gkr = gyr * vr + gyi * vi
    gki = gyi * vr - gyr * vi
    gvr = (kr * gyr + ki * gyi).astype(BF16).reshape(SEGS * width, length)
    gvi = (kr * gyi - ki * gyr).astype(BF16).reshape(SEGS * width, length)
    gv_all = (mm(gvr, cos_table) - mm(gvi, sin_table)).reshape(SEGS, width, length)
    gv = jnp.sum(gv_all * masks[:, None, :], axis=0)
    gs = jnp.concatenate([gq, gv], axis=0)
    d_taps = jnp.stack(
        [jnp.sum(gs * p_prev, axis=1), jnp.sum(gs * p, axis=1), jnp.sum(gs * p_next, axis=1)]
    )
    gp = (
        taps_mine[1] * gs
        + taps_mine[0] * shift_left(gs * prev)
        + taps_mine[2] * shift_right(gs * nxt)
    ).astype(BF16)

    gkk = jnp.concatenate([gkr, gki], axis=1)
    gkk_low = gkk.astype(BF16)
    hk_low = hk.astype(BF16)
    d_w2 = jnp.einsum("jkf,jcf->kc", hk_low, gkk_low, preferred_element_type=F32)
    gpre = jnp.einsum("kc,jcf->jkf", w2_mine.astype(BF16), gkk_low, preferred_element_type=F32)
    gpre = gpre * gate_pre * (1.0 + pre * (1.0 - gate_pre))
    d_w1 = jnp.einsum("ef,jkf->ek", feats, gpre, precision=HIGH)
    gcb = jnp.sum(gpre, axis=2)
    gcb_row = lax.psum(gcb, "freq")

    gp_blocks = gp.reshape(2 * width, fs, quarter).transpose(1, 0, 2)
    gp_t = jnp.concatenate(trade_sorted(gp_blocks, me), axis=0)

    u1_row = u1
    d_in = mm(gp, u1_row).astype(BF16).reshape(bs, 2 * width // bs, channels)
    d_in = scatter_sum(d_in, order_a)
    gb_row = jnp.concatenate(in_order(gb_parts, me), axis=0)
    d_out = mm(z_mine, gb_row)
    narrow = channels // bs
    d_out = scatter_sum(d_out.T.astype(BF16).reshape(bs, narrow, width), order_a)
    d_out = d_out.reshape(fs, narrow // fs, width)
    d_out = jnp.stack(trade_sorted(d_out, me), axis=0)
    d_out = (
        d_out.reshape(fs, narrow // fs, half, step).transpose(2, 0, 3, 1).reshape(channels, -1)
    )

    gmu_part = jnp.dot(gcb, cond_w.T, precision=HIGH)
    sum_gp = jnp.sum(gp.astype(F32), axis=1)
    w_mine32 = w_in_mine.astype(F32)
    d_shift1 = jnp.dot(sum_gp[None], w_mine32, precision=HIGH)[0] + jnp.sum(gmu_part, axis=0)
    d_gain1 = jnp.sum(mm(gp, n1) * w_mine32, axis=0) + jnp.sum(gmu_part * mn, axis=0)

    gmu = jnp.dot(gcb_row, cond_w.T, precision=HIGH) / counts
    own_masks = lax.dynamic_slice_in_dim(masks, me * quarter, quarter, 1)
    gu1 = mm_tn(gp_t, w_in_t.reshape(2 * channels, channels)) + lax.dot_general(
        own_masks, gmu, (((0,), (0,)), ((), ())), precision=HIGH
    )
    unit_own, scale_own = normed(x32)
    grad_tokens = big_g + norm_back(unit_own, scale_own, gu1 * ln1_gain)

    shared = [
        d_gain1,
        d_shift1,
        d_w1.reshape(-1),
        jnp.sum(gcb, axis=0),
        jnp.dot(mu.T, gcb, precision=HIGH).reshape(-1),
        grad_ln2_gain,
        grad_ln2_shift,
    ]
    owned = jnp.concatenate([d_taps, d_w2], axis=0)
    packed = jnp.concatenate(shared + [owned.reshape(-1)])
    for bit in range(bits):
        packed = packed + swap(packed, "batch", 1 << bit)
    split = packed.shape[0] - owned.size
    common, owned = packed[:split], packed[split:]
    common = common + swap(common, "freq", 1)
    common = common + swap(common, "freq", 2)
    owned = jnp.stack(in_order(gather_freq(owned, me), me), axis=0)
    owned = (
        owned.reshape(fs, -1, 2, half, step).transpose(1, 2, 3, 0, 4).reshape(-1, 2 * channels)
    )
    sizes = np.cumsum([part.size for part in shared])
    got = jnp.split(common, sizes[:-1])
    return (
        mixed_out[:, None],
        grad_tokens[:, None],
        got[0],
        got[1],
        d_in.T,
        owned[:3],
        got[2].reshape(freq_w1.shape),
        got[3],
        owned[3:],
        got[4].reshape(cond_w.shape),
        d_out,
        got[5],
        got[6],
        d_ff[0].T,
        d_ff[1].T,
        d_ff[2],
    )


VM = pl.BlockSpec(memory_space=pltpu.VMEM)
SM = pl.BlockSpec(memory_space=pltpu.SMEM)
HBM = pl.BlockSpec(memory_space=pl.ANY)
MIB = 1 << 20


def params():
    return pltpu.CompilerParams(vmem_limit_bytes=60 * MIB)


def cost(micros):
    return pl.CostEstimate(
        flops=int(micros * 1e9), bytes_accessed=int(micros * 3.5e6), transcendentals=0
    )


def shape(dims, dtype):
    return jax.ShapeDtypeStruct(dims, dtype)


def sigmoid(value):
    return 1.0 / (1.0 + jnp.exp(-value))


def dma_all(pairs, sems, first=0):
    copies = [
        pltpu.make_async_copy(source, target, sems.at[first + i])
        for i, (source, target) in enumerate(pairs)
    ]
    for copy in copies:
        copy.start()
    return copies


def one_hot_rows(me, rows, lanes, piece, fs):
    row = lax.broadcasted_iota(jnp.int32, (rows, lanes), 0)
    lane = lax.broadcasted_iota(jnp.int32, (rows, lanes), 1)
    block = jnp.zeros_like(row)
    for m in range(1, rows // piece):
        block = block + jnp.where(row >= m * piece, 1, 0)
    return jnp.where(lane == block * ((fs - 1) * piece) + me * piece + row, 1.0, 0.0)


def prepare_kernel(
    me_ref, w_in, freq_w2, conv_taps, freq_w1, freq_b1, feats,
    w_mine, w2x, w2t, taps, base, w1_aug, *, step, fs,
):
    lanes = w_in.shape[1] // 4
    rows = lanes // fs
    sel = one_hot_rows(me_ref[0], rows, lanes, step, fs)
    low = sel.astype(BF16)
    hidden = freq_w2.shape[0]
    for i in range(4):
        out = slice(i * rows, (i + 1) * rows)
        group = slice(i * lanes, (i + 1) * lanes)
        w_mine[out, :] = mm_nt(low, w_in[:, group]).astype(BF16)
        both = jnp.concatenate([freq_w2[:, group], conv_taps[:, group]], axis=0)
        mine = lax.dot_general(
            sel, both, (((1,), (1,)), ((), ())), precision=HIGH, preferred_element_type=F32
        )
        taps[out, :3] = mine[:, hidden:]
        mine = mine[:, :hidden]
        high = mine.astype(BF16)
        rest = (mine - high.astype(F32)).astype(BF16)
        w2x[out, :] = jnp.concatenate([high, high, rest], axis=1)
    w2t[...] = jnp.transpose(w2x[...][:, :hidden].astype(F32)).astype(BF16)
    w1_aug[...] = jnp.zeros_like(w1_aug)
    count = freq_w1.shape[0]
    w1_aug[:count, :] = freq_w1[...]
    w1_aug[count : count + 1, :] = freq_b1[...]
    base[...] = lax.dot_general(
        w1_aug[...], feats[...], (((0,), (0,)), ((), ())), precision=HIGH, preferred_element_type=F32
    )


def prepare(me, w_in, freq_w2, conv_taps, freq_w1, freq_b1, feats, step, fs):
    channels, both = w_in.shape
    hidden = freq_w2.shape[0]
    length = feats.shape[1]
    return pl.pallas_call(
        functools.partial(prepare_kernel, step=step, fs=fs),
        in_specs=[SM] + [VM] * 6,
        out_specs=[VM] * 5,
        out_shape=[
            shape((both // fs, channels), BF16),
            shape((both // fs, 3 * hidden), BF16),
            shape((hidden, both // fs), BF16),
            shape((both // fs, 8), F32),
            shape((hidden, length), F32),
        ],
        scratch_shapes=[pltpu.VMEM((feats.shape[0], hidden), F32)],
        compiler_params=params(),
        cost_estimate=cost(3),
        name="prepare",
    )(me, w_in, freq_w2, conv_taps, freq_w1, freq_b1[None], feats)


def select_kernel(me_ref, after, gate, up, gate_out, up_out, *, piece, fs):
    rows = gate_out.shape[0] // 2
    lanes = rows * fs
    sel = one_hot_rows(me_ref[0], rows, lanes, piece, fs).astype(BF16)
    for weight, out in ((gate, gate_out), (up, up_out)):
        for part in range(2):
            block = mm_nt(sel, weight[:, part * lanes : (part + 1) * lanes])
            out[part * rows : (part + 1) * rows, :] = block.astype(BF16)


def select_columns(me, after, w_gate, w_up, piece, fs):
    channels, ff = w_gate.shape
    big = ff // 4
    wide = pl.BlockSpec((channels, big), lambda i: (0, i))
    rows = pl.BlockSpec((big // fs, channels), lambda i: (i, 0))
    return pl.pallas_call(
        functools.partial(select_kernel, piece=piece, fs=fs),
        grid=(4,),
        in_specs=[SM, HBM, wide, wide],
        out_specs=[rows, rows],
        out_shape=[shape((ff // fs, channels), BF16)] * 2,
        compiler_params=params(),
        cost_estimate=cost(6),
        name="select_columns",
    )(me, after, w_gate, w_up)


def row_masks(ids):
    lane = lax.broadcasted_iota(jnp.int32, ids.shape, 1)
    length = ids.shape[1]
    prev = jnp.where((ids == pltpu.roll(ids, 1, 1)) & (lane > 0), 1.0, 0.0)
    nxt = jnp.where((ids == pltpu.roll(ids, length - 1, 1)) & (lane < length - 1), 1.0, 0.0)
    return prev, nxt


def bin_weights(start, width, length):
    lane = lax.broadcasted_iota(jnp.int32, (1, width), 1) + start
    return jnp.where(lane == 0, 0.5 / length, 1.0 / length)


def tile(index, size):
    return pl.ds(pl.multiple_of(index * size, size), size)


def hidden_tile(base, cb, j, lanes):
    pre = base[:, lanes] + cb[:, j : j + 1]
    return pre, sigmoid(pre)


def kernel_tile(w2x, hk):
    high = hk.astype(BF16)
    rest = (hk - high.astype(F32)).astype(BF16)
    return mm(w2x[...], jnp.concatenate([high, rest, high], axis=0))


def forward_kernel(
    me_ref, ids_at, x0, x1, x2, x3, ids_ref, norms, w, taps, base, w2x, condt, cos_hbm, sin_hbm,
    z0, z1, z2, z3, zrow_hbm, u1_hbm, n1_hbm, p_hbm, q_hbm, c_hbm, vr_hbm, vs_hbm, mu_out, mn_out, cb_out,
    cos, sin, z_row, u1, n1, p_out, q_out, c_out, vr_out, vs_out, p, q, vm, ycat, acc, sems,
):
    quarter = x0.shape[0]
    width, length = z_row.shape
    tiles = length // quarter
    me = me_ref[0]
    loads = dma_all([(cos_hbm, cos), (sin_hbm, sin)], sems)
    for k, x in enumerate((x0, x1, x2, x3)):
        values = x[...].astype(F32)
        unit, _ = normed(values)
        rows = tile(me ^ k, quarter)
        n1[rows, :] = unit.astype(BF16)
        u1[rows, :] = (unit * norms[0:1, :] + norms[1:2, :]).astype(BF16)
    stores = dma_all([(u1, u1_hbm), (n1, n1_hbm)], sems, 2)
    ids = ids_ref[...]
    number = lax.broadcasted_iota(jnp.int32, (8, length), 0)
    member = jnp.where(ids == number, 1.0, 0.0)
    counts = jnp.maximum(jnp.sum(member, axis=1, keepdims=True), 1.0)
    member_low = member.astype(BF16)
    mu = mm(member_low, u1[...]) / counts
    mu_out[...] = mu
    mn_out[...] = mm(member_low, n1[...]) / counts
    cb_out[...] = lax.dot_general(
        condt[...], mu, (((1,), (1,)), ((), ())), precision=HIGH, preferred_element_type=F32
    )
    prev, nxt = row_masks(ids)
    for t in range(tiles):
        at = slice(t * quarter, (t + 1) * quarter)
        p[:, at] = mm_nt(w[...], u1[at, :])
    chunk = width // 2
    for r in range(4):
        at = slice(r * chunk, (r + 1) * chunk)
        here = p[at, :]
        p_out[at, :] = here.astype(BF16)
        mixed = (
            taps[at, 0:1] * (pltpu.roll(here, 1, 1) * prev)
            + taps[at, 1:2] * here
            + taps[at, 2:3] * (pltpu.roll(here, length - 1, 1) * nxt)
        )
        if r < 2:
            q[at, :] = mixed
            q_out[at, :] = mixed.astype(BF16)
        else:
            for j in range(SEGS):
                lo = j * width + (r - 2) * chunk
                vm[lo : lo + chunk, :] = (mixed * member[j : j + 1, :]).astype(BF16)
    stores += dma_all([(p_out, p_hbm), (q_out, q_hbm)], sems, 4)
    for load in loads:
        load.wait()

    @pl.loop(0, tiles)
    def _(f):
        lanes = tile(f, quarter)
        upper = pl.ds(pl.multiple_of(f * quarter + length, quarter), quarter)
        weight = bin_weights(f * quarter, quarter, length)
        vr_all = mm(vm[...], cos[:, lanes])
        vs_all = mm(vm[...], sin[:, lanes])
        vr_out[:, lanes] = vr_all.astype(BF16)
        vs_out[:, lanes] = vs_all.astype(BF16)
        for j in range(SEGS):
            pre, gate = hidden_tile(base, cb_out, j, lanes)
            kk = kernel_tile(w2x, pre * gate)
            kr, ki = kk[:width] * weight, kk[width:] * weight
            at = slice(j * width, (j + 1) * width)
            vr, vs = vr_all[at], vs_all[at]
            ycat[at, lanes] = (kr * vr + ki * vs).astype(BF16)
            ycat[at, upper] = (kr * vs - ki * vr).astype(BF16)

    stores += dma_all([(vr_out, vr_hbm), (vs_out, vs_hbm)], sems, 6)
    for k, z_out in enumerate((z0, z1, z2, z3)):
        t = me ^ k
        lanes = tile(t, quarter)
        acc[...] = jnp.zeros_like(acc)
        ids_here = ids_ref[:, lanes]
        for j in range(SEGS):

            @pl.when((ids_at[0, t * quarter] <= j) & (ids_at[0, (t + 1) * quarter - 1] >= j))
            def _():
                at = slice(j * width, (j + 1) * width)
                part = mm(ycat[at, :length], cos[:, lanes]) + mm(ycat[at, length:], sin[:, lanes])
                acc[...] += jnp.where(ids_here == j, part, 0.0)

        c = acc[...]
        c_out[:, lanes] = c.astype(BF16)
        z = (q[:, lanes] * c).astype(BF16)
        z_out[...] = z
        z_row[:, lanes] = z
    stores += dma_all([(c_out, c_hbm), (z_row, zrow_hbm)], sems, 8)
    for store in stores:
        store.wait()


def forward_spectral(me, x_parts, ids, norms, w, taps, base, w2x, condt, cos, sin):
    quarter, channels = x_parts[0].shape
    length = ids.shape[1]
    width = w.shape[0] // 2
    saved = [
        (width, length),
        (length, channels),
        (length, channels),
        (2 * width, length),
        (width, length),
        (width, length),
        (SEGS * width, length),
        (SEGS * width, length),
    ]
    small = [
        shape((8, channels), F32),
        shape((8, channels), F32),
        shape((condt.shape[0], 8), F32),
    ]
    return pl.pallas_call(
        forward_kernel,
        in_specs=[SM, SM] + [VM] * 11 + [HBM, HBM],
        out_specs=[VM] * 4 + [HBM] * len(saved) + [VM] * 3,
        out_shape=[shape((width, quarter), BF16)] * 4 + [shape(dims, BF16) for dims in saved] + small,
        scratch_shapes=[pltpu.VMEM((length, length), BF16)] * 2
        + [pltpu.VMEM(dims, BF16) for dims in saved]
        + [
            pltpu.VMEM((2 * width, length), F32),
            pltpu.VMEM((width, length), F32),
            pltpu.VMEM((SEGS * width, length), BF16),
            pltpu.VMEM((SEGS * width, 2 * length), BF16),
            pltpu.VMEM((width, quarter), F32),
            pltpu.SemaphoreType.DMA((10,)),
        ],
        compiler_params=params(),
        cost_estimate=cost(15),
        name="forward_spectral",
    )(me, ids, *x_parts, ids, norms, w, taps, base, w2x, condt, cos, sin)


def backward_kernel(
    me_ref, ids_at, g0, g1, g2, g3, ids_ref, cb, taps, base, w2x, w2, feats,
    p_hbm, q_hbm, c_hbm, vr_hbm, vs_hbm, cos_hbm, sin_hbm, after,
    o0, o1, o2, o3, gp_hbm, d_taps, d_w2, d_w1, gcb,
    cos, sin, p, q, c, vr_in, vs_in, gp_row, gcm, gvcat, gs, acc, sems,
):
    width, quarter = g0.shape
    length = gp_row.shape[1]
    tiles = length // quarter
    hidden = base.shape[0]
    me = me_ref[0]
    loads = dma_all(
        [
            (c_hbm, c), (q_hbm, q), (cos_hbm, cos), (sin_hbm, sin),
            (vr_hbm, vr_in), (vs_hbm, vs_in), (p_hbm, p),
        ],
        sems,
    )
    loads[0].wait()
    loads[1].wait()
    for k, g in enumerate((g0, g1, g2, g3)):
        lanes = tile(me ^ k, quarter)
        gz = g[...].astype(F32)
        gs[:width, lanes] = gz * c[:, lanes].astype(F32)
        gc = gz * q[:, lanes].astype(F32)
        ids_here = ids_ref[:, lanes]
        for j in range(SEGS):
            gcm[j * width : (j + 1) * width, lanes] = jnp.where(ids_here == j, gc, 0.0).astype(BF16)
    d_w2[...] = jnp.zeros_like(d_w2)
    d_w1[...] = jnp.zeros_like(d_w1)
    gcb[...] = jnp.zeros_like(gcb)
    for load in loads[2:]:
        load.wait()

    @pl.loop(0, tiles)
    def _(f):
        lanes = tile(f, quarter)
        upper = pl.ds(pl.multiple_of(f * quarter + length, quarter), quarter)
        weight = bin_weights(f * quarter, quarter, length)
        gyr_all = mm(gcm[...], cos[:, lanes]) * weight
        gys_all = mm(gcm[...], sin[:, lanes]) * weight
        for j in range(SEGS):
            pre, gate = hidden_tile(base, cb, j, lanes)
            hk = pre * gate
            kk = kernel_tile(w2x, hk)
            kr, ki = kk[:width], kk[width:]
            at = slice(j * width, (j + 1) * width)
            gyr, gys = gyr_all[at], gys_all[at]
            vr, vs = vr_in[at, lanes].astype(F32), vs_in[at, lanes].astype(F32)
            gvcat[at, lanes] = (kr * gyr - ki * gys).astype(BF16)
            gvcat[at, upper] = (kr * gys + ki * gyr).astype(BF16)
            gkk = jnp.concatenate(
                [(gyr * vr + gys * vs).astype(BF16), (gyr * vs - gys * vr).astype(BF16)], axis=0
            )
            d_w2[...] += mm_nt(gkk, hk.astype(BF16))
            gpre = mm(w2[...], gkk) * (gate * (1.0 + pre * (1.0 - gate)))
            gcb[:, j : j + 1] += jnp.sum(gpre, axis=1, keepdims=True)
            d_w1[...] += mm_nt(feats[:, lanes], gpre.astype(BF16))

    for k in range(4):
        t = me ^ k
        lanes = tile(t, quarter)
        acc[...] = jnp.zeros_like(acc)
        ids_here = ids_ref[:, lanes]
        for j in range(SEGS):

            @pl.when((ids_at[0, t * quarter] <= j) & (ids_at[0, (t + 1) * quarter - 1] >= j))
            def _():
                at = slice(j * width, (j + 1) * width)
                part = mm(gvcat[at, :length], cos[:, lanes]) + mm(gvcat[at, length:], sin[:, lanes])
                acc[...] += jnp.where(ids_here == j, part, 0.0)

        gs[width:, lanes] = acc[...]
    prev, nxt = row_masks(ids_ref[...])
    chunk = width // 2
    for r in range(4):
        at = slice(r * chunk, (r + 1) * chunk)
        here = p[at, :].astype(F32)
        grad = gs[at, :]
        d_taps[at, 0:1] = jnp.sum(grad * (pltpu.roll(here, 1, 1) * prev), axis=1, keepdims=True)
        d_taps[at, 1:2] = jnp.sum(grad * here, axis=1, keepdims=True)
        d_taps[at, 2:3] = jnp.sum(
            grad * (pltpu.roll(here, length - 1, 1) * nxt), axis=1, keepdims=True
        )
        gp_row[at, :] = (
            taps[at, 1:2] * grad
            + taps[at, 0:1] * pltpu.roll(grad * prev, length - 1, 1)
            + taps[at, 2:3] * pltpu.roll(grad * nxt, 1, 1)
        ).astype(BF16)
    store = dma_all([(gp_row, gp_hbm)], sems, 7)[0]
    share = jnp.transpose(gcb[...])[:8, :]
    high = share.astype(BF16)
    rest = (share - high.astype(F32)).astype(BF16)
    extra = jnp.concatenate([high, rest], axis=0)
    extra = jnp.concatenate([extra, jnp.zeros((16, quarter - hidden), BF16)], axis=1)
    for k, out in enumerate((o0, o1, o2, o3)):
        out[: 2 * width, :] = gp_row[:, tile(me ^ k, quarter)]
        out[2 * width :, :] = extra
    store.wait()


def backward_spectral(
    me, gz_parts, ids, cb, taps, base, w2x, w2, feats, p, q, c, vr, vs, cos, sin, after
):
    width, quarter = gz_parts[0].shape
    length = ids.shape[1]
    hidden = base.shape[0]
    outs = [shape((2 * width + 16, quarter), BF16)] * 4 + [
        shape((2 * width, length), BF16),
        shape((2 * width, 128), F32),
        shape((2 * width, hidden), F32),
        shape((feats.shape[0], hidden), F32),
        shape((hidden, 128), F32),
    ]
    return pl.pallas_call(
        backward_kernel,
        in_specs=[SM, SM] + [VM] * 11 + [HBM] * 8,
        out_specs=[VM] * 4 + [HBM] + [VM] * 4,
        out_shape=outs,
        scratch_shapes=[
            pltpu.VMEM((length, length), BF16),
            pltpu.VMEM((length, length), BF16),
            pltpu.VMEM((2 * width, length), BF16),
            pltpu.VMEM((width, length), BF16),
            pltpu.VMEM((width, length), BF16),
            pltpu.VMEM((SEGS * width, length), BF16),
            pltpu.VMEM((SEGS * width, length), BF16),
            pltpu.VMEM((2 * width, length), BF16),
            pltpu.VMEM((SEGS * width, length), BF16),
            pltpu.VMEM((SEGS * width, 2 * length), BF16),
            pltpu.VMEM((2 * width, length), F32),
            pltpu.VMEM((width, quarter), F32),
            pltpu.SemaphoreType.DMA((8,)),
        ],
        compiler_params=params(),
        cost_estimate=cost(17),
        name="backward_spectral",
    )(
        me, ids, *gz_parts, ids, cb, taps, base, w2x, w2, feats, p, q, c, vr, vs, cos, sin, after
    )


def middle_kernel(me_ref, z0, z1, z2, z3, x, w_out, norms, after, h_out, u2_out, z_t, *, piece):
    me = me_ref[0]
    width = z0.shape[0]
    for k, z in enumerate((z0, z1, z2, z3)):
        for i in range(width // piece):
            at = pl.ds(pl.multiple_of((i * 4 + (me ^ k)) * piece, piece), piece)
            z_t[at, :] = z[i * piece : (i + 1) * piece, :]
    h = x[...].astype(F32) + mm(jnp.transpose(z_t[...]), w_out[...])
    h_out[...] = h
    unit, _ = normed(h)
    u2_out[...] = (unit * norms[2:3, :] + norms[3:4, :]).astype(BF16)


def middle(me, z_parts, x, w_out, norms, after, piece):
    quarter, channels = x.shape
    return pl.pallas_call(
        functools.partial(middle_kernel, piece=piece),
        in_specs=[SM] + [VM] * 7 + [HBM],
        out_specs=[VM] * 3,
        out_shape=[
            shape((quarter, channels), F32),
            shape((quarter, channels), BF16),
            shape((channels, quarter), BF16),
        ],
        compiler_params=params(),
        cost_estimate=cost(2),
        name="middle",
    )(me, *z_parts, x, w_out, norms, after)


def feed_kernel(
    me_ref, u2, h, ct, norms, w_out, gate, up, down,
    mixed, big_g, gb_out, g0, g1, g2, g3, sums, acc_out, acc_grad, gz_t, *, piece,
):
    i = pl.program_id(0)

    @pl.when(i == 0)
    def _():
        acc_out[...] = jnp.zeros_like(acc_out)
        acc_grad[...] = jnp.zeros_like(acc_grad)

    g = mm(u2[...], gate[...])
    a = mm(u2[...], up[...])
    gh = mm_nt(ct[...], down[...])
    sg = sigmoid(g)
    silu = g * sg
    hid = (silu * a).astype(BF16)
    gg = (gh * a * (sg * (1.0 + g * (1.0 - sg)))).astype(BF16)
    ga = (gh * silu).astype(BF16)
    acc_out[...] += mm(hid, down[...])
    acc_grad[...] += mm_nt(gg, gate[...]) + mm_nt(ga, up[...])

    @pl.when(i == pl.num_programs(0) - 1)
    def _():
        me = me_ref[0]
        width = g0.shape[0]
        here = h[...]
        mixed[...] = (here + acc_out[...]).astype(BF16)
        gu2 = acc_grad[...]
        unit, scale = normed(here)
        sums[0:1, :] = jnp.sum(gu2 * unit, axis=0, keepdims=True)
        sums[1:2, :] = jnp.sum(gu2, axis=0, keepdims=True)
        total = ct[...].astype(F32) + norm_back(unit, scale, gu2 * norms[2:3, :])
        big_g[...] = total
        low = total.astype(BF16)
        gb_out[...] = low
        gz_t[...] = mm_nt(w_out[...], low).astype(BF16)
        for k, out in enumerate((g0, g1, g2, g3)):
            for r in range(width // piece):
                at = pl.ds(pl.multiple_of((r * 4 + (me ^ k)) * piece, piece), piece)
                out[r * piece : (r + 1) * piece, :] = gz_t[at, :]


def feed_forward(me, u2, h, ct, norms, w_out, w_gate, w_up, w_down, piece):
    quarter, channels = u2.shape
    ff = w_gate.shape[1]
    block = 512

    def whole(*dims):
        return pl.BlockSpec(dims, lambda i: (0,) * len(dims))

    width = channels // 4
    outs = [
        ((quarter, channels), BF16),
        ((quarter, channels), F32),
        ((quarter, channels), BF16),
    ] + [((width, quarter), BF16)] * 4 + [((8, channels), F32)]
    return pl.pallas_call(
        functools.partial(feed_kernel, piece=piece),
        grid=(ff // block,),
        in_specs=[
            SM,
            whole(quarter, channels),
            whole(quarter, channels),
            whole(quarter, channels),
            whole(4, channels),
            whole(channels, channels),
            pl.BlockSpec((channels, block), lambda i: (0, i)),
            pl.BlockSpec((channels, block), lambda i: (0, i)),
            pl.BlockSpec((block, channels), lambda i: (i, 0)),
        ],
        out_specs=[whole(*dims) for dims, _ in outs],
        out_shape=[shape(*out) for out in outs],
        scratch_shapes=[
            pltpu.VMEM((quarter, channels), F32),
            pltpu.VMEM((quarter, channels), F32),
            pltpu.VMEM((channels, quarter), BF16),
        ],
        compiler_params=params(),
        cost_estimate=cost(13),
        name="feed_forward",
    )(me, u2, h, ct, norms, w_out, w_gate, w_up, w_down)


def hidden_grads_kernel(
    at_ref, u0, u1, u2, u3, c0, c1, c2, c3, gate, up, down, gb, z_in,
    keep_a, give_a, keep_b, give_b, t0, t1, t2, t3, z_out, u_row, c_row, d_all, gb_t, *, piece,
):
    quarter, channels = u0.shape
    i = pl.program_id(0)
    y, z = at_ref[1], at_ref[2]

    @pl.when(i == 0)
    def _():
        for k, (u, c) in enumerate(((u0, c0), (u1, c1), (u2, c2), (u3, c3))):
            u_row[k * quarter : (k + 1) * quarter, :] = u[...]
            c_row[k * quarter : (k + 1) * quarter, :] = c[...]

    @pl.when(i == pl.num_programs(0) - 1)
    def _():
        z_out[...] = z_in[...]
        gb_t[...] = jnp.transpose(gb[...].astype(F32))
        for k, out in enumerate((t0, t1, t2, t3)):
            parts = []
            for r in range(out.shape[0] // piece):
                lo = pl.multiple_of((r * 4 + (at_ref[0] ^ k)) * piece, piece)
                parts.append(gb_t[pl.ds(lo, piece), :])
            out[...] = jnp.concatenate(parts, axis=0).astype(BF16)

    rows = gate.shape[0]
    g = mm_nt(gate[...], u_row[...])
    a = mm_nt(up[...], u_row[...])
    gh = mm_nt(down[...].reshape(rows, channels), c_row[...])
    sg = sigmoid(g)
    silu = g * sg
    hid = (silu * a).astype(BF16)
    gg = (gh * a * (sg * (1.0 + g * (1.0 - sg)))).astype(BF16)
    ga = (gh * silu).astype(BF16)
    half = rows // 2
    for m, grad in enumerate((mm(gg, u_row[...]), mm(ga, u_row[...]), mm(hid, c_row[...]))):
        d_all[0, m] = grad[:half].astype(BF16)
        d_all[1, m] = grad[half:].astype(BF16)
    cut = channels // 2
    keep_a[0] = d_all[y, :, :, :cut]
    give_a[0] = d_all[1 - y, :, :, :cut]

    @pl.when((i & 1) == z)
    def _():
        keep_b[0] = d_all[:, :, :, cut:]

    @pl.when((i & 1) != z)
    def _():
        give_b[0] = d_all[:, :, :, cut:]


def hidden_grads(at, u2_parts, ct_parts, gate, up, down, gb, z_t):
    quarter, channels = u2_parts[0].shape
    wide = gate.shape[0]
    bs, fs, fw, _ = down.shape
    block = 2 * fw
    cut = channels // 2
    whole = pl.BlockSpec((quarter, channels), lambda i, at: (0, 0))
    tall = pl.BlockSpec((channels, quarter), lambda i, at: (0, 0))
    part = pl.BlockSpec((channels // fs, quarter), lambda i, at: (0, 0))
    rows = pl.BlockSpec((block, channels), lambda i, at: (i, 0))
    down_spec = pl.BlockSpec((2, 1, fw, channels), lambda i, at: (i, at[0], 0, 0))
    a_spec = pl.BlockSpec((1, 3, fw, cut), lambda i, at: (i, 0, 0, 0))
    b_spec = pl.BlockSpec((1, 2, 3, fw, cut), lambda i, at: (i // 2, 0, 0, 0, 0))
    return pl.pallas_call(
        functools.partial(hidden_grads_kernel, piece=channels // (bs * fs)),
        grid_spec=pltpu.PrefetchScalarGridSpec(
            num_scalar_prefetch=1,
            grid=(bs // 2,),
            in_specs=[whole] * 8 + [rows, rows, down_spec, whole, tall],
            out_specs=[a_spec, a_spec, b_spec, b_spec] + [part] * 4 + [tall],
            scratch_shapes=[
                pltpu.VMEM((4 * quarter, channels), BF16),
                pltpu.VMEM((4 * quarter, channels), BF16),
                pltpu.VMEM((2, 3, fw, channels), BF16),
                pltpu.VMEM((channels, quarter), F32),
            ],
        ),
        out_shape=[shape((bs // 2, 3, fw, cut), BF16)] * 2
        + [shape((bs // 4, 2, 3, fw, cut), BF16)] * 2
        + [shape((channels // fs, quarter), BF16)] * 4
        + [shape((channels, quarter), BF16)],
        compiler_params=params(),
        cost_estimate=cost(14),
        name="hidden_grads",
    )(at, *u2_parts, *ct_parts, gate, up, down, gb, z_t)


def halve_kernel(bit_ref, after, *refs, pairs):
    ins, outs = refs[: 2 * pairs], refs[2 * pairs :]
    for n in range(pairs):
        mine = bit_ref[n]
        keep, got = ins[2 * n], ins[2 * n + 1]
        next_keep, next_give = outs[2 * n], outs[2 * n + 1]
        for i in range(keep.shape[0]):
            for side, out in ((mine, next_keep), (1 - mine, next_give)):
                out[i] = (keep[i, side].astype(F32) + got[i, side].astype(F32)).astype(BF16)


def halve(bits, after, *sums):
    pairs = len(sums) // 2
    outs = []
    for n in range(pairs):
        dims = sums[2 * n].shape
        outs += [shape((dims[0],) + dims[2:], BF16)] * 2
    return pl.pallas_call(
        functools.partial(halve_kernel, pairs=pairs),
        in_specs=[SM, HBM] + [VM] * len(sums),
        out_specs=[VM] * len(outs),
        out_shape=outs,
        compiler_params=params(),
        cost_estimate=cost(2),
        name="halve",
    )(bits, after, *sums)


def join_kernel(bit_ref, after, keep_a, got_a, keep_b, got_b, keep, give):
    cut = keep_a.shape[-1]
    for side, out in ((bit_ref[0], keep), (1 - bit_ref[0], give)):
        for m in range(keep_a.shape[1]):
            for ours, theirs, lanes in ((keep_a, got_a, slice(0, cut)), (keep_b, got_b, slice(cut, 2 * cut))):
                total = ours[side, m].astype(F32) + theirs[side, m].astype(F32)
                out[m, :, lanes] = total.astype(BF16)


def join(bit, after, keep_a, got_a, keep_b, got_b):
    _, count, rows, cut = keep_a.shape
    return pl.pallas_call(
        join_kernel,
        in_specs=[SM, HBM] + [VM] * 4,
        out_specs=[VM] * 2,
        out_shape=[shape((count, rows, 2 * cut), BF16)] * 2,
        compiler_params=params(),
        cost_estimate=cost(2),
        name="join",
    )(bit, after, keep_a, got_a, keep_b, got_b)


def projection_kernel(
    at_ref, gp, u1, n1, w_mine, b0, b1, b2, b3, z0, z1, z2, z3, d_w2, d_w1, d_taps, gcb, condt, mu, mn,
    sums2, after, keep, give, packed, gb_row, z_row, d_in, d_out, *, layout,
):
    me, y = at_ref[0], at_ref[1]
    quarter = b0.shape[1]
    channels = u1.shape[1]
    width = b0.shape[0]
    for k, (b, z) in enumerate(((b0, z0), (b1, z1), (b2, z2), (b3, z3))):
        gb_row[:, k * quarter : (k + 1) * quarter] = b[...]
        z_row[:, k * quarter : (k + 1) * quarter] = z[...]
    d_in[...] = mm(gp[...], u1[...])
    d_out[...] = mm_nt(gb_row[...], z_row[...])
    blocks = 2 * keep.shape[0]
    first = 2 * width // blocks
    second = width // blocks
    for b in range(blocks // 2):
        for side, out in ((y, keep), (1 - y, give)):
            lo = pl.multiple_of((2 * b + side) * first, first)
            out[b, :first, :] = d_in[pl.ds(lo, first), :].astype(BF16)
            lo = pl.multiple_of((2 * b + side) * second, second)
            out[b, first:, :] = d_out[pl.ds(lo, second), :].astype(BF16)
    packed[...] = jnp.zeros_like(packed)
    packed[:width, :] = jnp.concatenate([d_w2[:width, :], d_w2[width:, :]], axis=1)
    taps_t = jnp.transpose(d_taps[...])
    gcb_t = jnp.transpose(gcb[...])[:8, :]
    gmu = lax.dot_general(
        gcb_t, condt[...], (((1,), (0,)), ((), ())), precision=HIGH, preferred_element_type=F32
    )
    gp_n = mm(gp[...], n1[...])
    w32 = w_mine[...].astype(F32)
    gain = jnp.sum(gp_n * w32, axis=0, keepdims=True) + jnp.sum(gmu * mn[...], axis=0, keepdims=True)
    total = jnp.sum(gp[...].astype(F32), axis=1, keepdims=True)
    shift = jnp.sum(total * w32, axis=0, keepdims=True) + jnp.sum(gmu, axis=0, keepdims=True)
    for i in range(3):
        for m in range(2 * width // 128):
            at = layout["taps"] + i * (2 * width // 128) + m
            packed[at : at + 1, :] = taps_t[i : i + 1, m * 128 : (m + 1) * 128]
    for i, row in enumerate((gain, shift, sums2[0:1, :], sums2[1:2, :])):
        for m in range(channels // 128):
            at = layout["ln"] + i * (channels // 128) + m
            packed[at : at + 1, :] = row[:, m * 128 : (m + 1) * 128]
    half = d_w1.shape[0] // 2
    packed[layout["w1"] : layout["w1"] + half, :] = jnp.concatenate(
        [d_w1[:half, :], d_w1[half:, :]], axis=1
    )
    zeros = jnp.zeros_like(gcb_t)
    row = at_ref[4]
    odd = (row & 1) == 1
    both = jnp.concatenate([jnp.where(odd, zeros, gcb_t), jnp.where(odd, gcb_t, zeros)], axis=1)
    packed[pl.ds(pl.multiple_of(layout["cb"] + 8 * (row >> 1), 8), 8), :] = both
    share = jnp.zeros((8, width), F32)
    for f in range(channels // width):
        share = share + jnp.where(me == f, mu[:, f * width : (f + 1) * width], 0.0)
    rest = jnp.concatenate([share[:SEGS, 128:], jnp.zeros((SEGS, 256 - width), F32)], axis=1)
    block = jnp.concatenate([share[:SEGS, :128], rest, jnp.zeros((8 - 2 * SEGS, 128), F32)], axis=0)
    packed[pl.ds(pl.multiple_of(layout["mu"] + 8 * row, 8), 8), :] = block


def packed_layout(width, channels, bs):
    taps = width
    ln = taps + 3 * (2 * width // 128)
    w1 = -(-(ln + 4 * (channels // 128)) // 8) * 8
    cb = w1 + 32
    mu = cb + 4 * bs
    return {"taps": taps, "ln": ln, "w1": w1, "cb": cb, "mu": mu, "rows": mu + 8 * bs}


def projection_grads(
    at, gp, u1, n1, w_mine, gb_parts, z_parts, d_w2, d_w1, d_taps, gcb, condt, mu, mn, sums2, after, bs
):
    length, channels = u1.shape
    width = gb_parts[0].shape[0]
    layout = packed_layout(width, channels, bs)
    return pl.pallas_call(
        functools.partial(projection_kernel, layout=layout),
        in_specs=[SM] + [VM] * 20 + [HBM],
        out_specs=[VM] * 3,
        out_shape=[shape((bs // 2, 3 * width // bs, channels), BF16)] * 2
        + [shape((layout["rows"], 128), F32)],
        scratch_shapes=[
            pltpu.VMEM((width, length), BF16),
            pltpu.VMEM((channels, length), BF16),
            pltpu.VMEM((2 * width, channels), F32),
            pltpu.VMEM((width, channels), F32),
        ],
        compiler_params=params(),
        cost_estimate=cost(4),
        name="projection_grads",
    )(
        at, gp, u1, n1, w_mine, *gb_parts, *z_parts, d_w2, d_w1, d_taps, gcb, condt, mu, mn, sums2, after
    )


def final_kernel(
    me_ref, p0, p1, p2, p3, x, big_g, norms, ids_row, condt, w_in, after, out, gp_t, *, piece
):
    me = me_ref[0]
    rows = gp_t.shape[0] // 4
    hidden = condt.shape[0]
    share = jnp.zeros((8, hidden), F32)
    for k, part in enumerate((p0, p1, p2, p3)):
        for i in range(rows // piece):
            at = pl.ds(pl.multiple_of((i * 4 + (me ^ k)) * piece, piece), piece)
            gp_t[at, :] = part[i * piece : (i + 1) * piece, :]
        extra = part[rows:, :hidden].astype(F32)
        share = share + extra[:8] + extra[8:]
    ids = ids_row[...]
    number = lax.broadcasted_iota(jnp.int32, (8, ids.shape[1]), 0)
    counts = jnp.sum(jnp.where(ids == number, 1.0, 0.0), axis=1, keepdims=True)
    gmu = lax.dot_general(
        share, condt[...], (((1,), (0,)), ((), ())), precision=HIGH, preferred_element_type=F32
    ) / jnp.maximum(counts, 1.0)
    gu1 = mm_nt(jnp.transpose(gp_t[...]), w_in[...])
    quarter = x.shape[0]
    own = jnp.broadcast_to(ids_row[:, tile(me, quarter)].astype(F32), (8, quarter))
    ids_own = jnp.transpose(own)[:, 0:1]
    for j in range(SEGS):
        gu1 = gu1 + jnp.where(ids_own == j, gmu[j : j + 1, :], 0.0)
    unit, scale = normed(x[...].astype(F32))
    out[...] = big_g[...] + norm_back(unit, scale, gu1 * norms[0:1, :])


def final(me, gp_parts, x, big_g, norms, ids, condt, w_in, after, piece):
    quarter, channels = x.shape
    return pl.pallas_call(
        functools.partial(final_kernel, piece=piece),
        in_specs=[SM] + [VM] * 10 + [HBM],
        out_specs=VM,
        out_shape=shape((quarter, channels), F32),
        scratch_shapes=[pltpu.VMEM((2 * channels, quarter), BF16)],
        compiler_params=params(),
        cost_estimate=cost(2),
        name="final",
    )(me, *gp_parts, x, big_g, norms, ids, condt, w_in, after)


def small_kernel(
    me_ref, j0, j1, j2, j3, w2, taps, ln, w1, b1, cond, wide, tap_t, cond_t, *, layout, step, width
):
    me = me_ref[0]
    parts = (j0, j1, j2, j3)
    hidden = w1.shape[0]
    half = width // step
    count = 2 * width // 128
    for k, part in enumerate(parts):
        who = me ^ k
        rows = jnp.concatenate(
            [
                jnp.concatenate([part[layout["taps"] + i * count + m : layout["taps"] + i * count + m + 1, :]
                                 for m in range(count)], axis=1)
                for i in range(3)
            ]
            + [jnp.zeros((125, 2 * width), F32)],
            axis=0,
        )
        tap_t[...] = jnp.transpose(rows)
        for side in range(2):
            for i in range(half):
                at = pl.ds(pl.multiple_of((side * half * 4 + i * 4 + who) * step, step), step)
                lo = i * step
                wide[at, :hidden] = part[lo : lo + step, side * hidden : (side + 1) * hidden]
                at2 = side * width + lo
                wide[at, hidden:] = tap_t[at2 : at2 + step, :hidden]
    whole = jnp.transpose(wide[...])
    w2[...] = whole[:hidden, :]
    taps[...] = whole[hidden : hidden + 3, :]

    def common(first, last):
        return (j0[first:last, :] + j1[first:last, :]) + (j2[first:last, :] + j3[first:last, :])

    lanes = ln.shape[1] // 128
    sums = common(layout["ln"], layout["ln"] + 4 * lanes)
    for i in range(4):
        for m in range(lanes):
            ln[i : i + 1, m * 128 : (m + 1) * 128] = sums[i * lanes + m : i * lanes + m + 1, :]
    both = common(layout["w1"], layout["w1"] + hidden // 2)
    w1[: hidden // 2, :] = both[:, :hidden]
    w1[hidden // 2 :, :] = both[:, hidden:]
    cb = common(layout["cb"], layout["mu"])
    shares = []
    for b in range(cb.shape[0] // 4):
        lo = 8 * (b // 2)
        shares.append(cb[lo : lo + 8, (b % 2) * hidden : (b % 2 + 1) * hidden])
    shares = jnp.concatenate(shares, axis=0)
    b1[...] = jnp.sum(shares, axis=0, keepdims=True)
    for k, part in enumerate(parts):
        rows = []
        for b in range(cb.shape[0] // 4):
            lo = layout["mu"] + 8 * b
            block = part[lo : lo + 8, :]
            rows.append(
                jnp.concatenate(
                    [
                        jnp.concatenate([block[:SEGS, :], jnp.zeros((8 - SEGS, 128), F32)], axis=0),
                        jnp.concatenate(
                            [block[SEGS : 2 * SEGS, : width - 128], jnp.zeros((8 - SEGS, width - 128), F32)],
                            axis=0,
                        ),
                    ],
                    axis=1,
                )
            )
        mu = jnp.concatenate(rows, axis=0)
        cond_t[tile(me ^ k, width), :] = lax.dot_general(
            jnp.transpose(mu), shares, (((1,), (0,)), ((), ())), precision=HIGH, preferred_element_type=F32
        )
    cond[...] = jnp.transpose(cond_t[...])


def small_grads(me, parts, hidden, channels, step, bs):
    width = channels // 4
    layout = packed_layout(width, channels, bs)
    return pl.pallas_call(
        functools.partial(small_kernel, layout=layout, step=step, width=width),
        in_specs=[SM] + [VM] * 4,
        out_specs=[VM] * 6,
        out_shape=[
            shape((hidden, 2 * channels), F32),
            shape((3, 2 * channels), F32),
            shape((4, channels), F32),
            shape((hidden, hidden), F32),
            shape((1, hidden), F32),
            shape((hidden, channels), F32),
        ],
        scratch_shapes=[
            pltpu.VMEM((2 * channels, 2 * hidden), F32),
            pltpu.VMEM((2 * width, 128), F32),
            pltpu.VMEM((channels, hidden), F32),
        ],
        compiler_params=params(),
        cost_estimate=cost(3),
        name="small_grads",
    )(me, *parts)


def trade_parts(parts):
    two, three, one = [swap(parts[k], "freq", k) for k in (2, 3, 1)]
    return (parts[0], one, two, three)


def tiled_device(
    tokens,
    seg_ids,
    cotangent,
    ln1_gain,
    ln1_shift,
    w_in,
    conv_taps,
    freq_w1,
    freq_b1,
    freq_w2,
    cond_w,
    w_out,
    ln2_gain,
    ln2_shift,
    w_gate,
    w_up,
    w_down,
):
    quarter, _, channels = tokens.shape
    length = seg_ids.shape[1]
    ff = w_gate.shape[1]
    fs = lax.axis_size("freq")
    bs = lax.axis_size("batch")
    me = lax.axis_index("freq")
    row = lax.axis_index("batch")
    width = channels // fs
    half = bs // 2
    step = channels // (half * fs)
    fw = ff // (bs * fs)
    cos_table, sin_table = tables(length)
    feats = features(length, freq_w1.shape[0] // 2)
    feats_aug = np.concatenate(
        [feats, np.ones((1, length), np.float32), np.zeros((7, length), np.float32)], axis=0
    )

    x_own = tokens[:, 0]
    ct_own = cotangent[:, 0]
    ids = seg_ids
    me1 = me.reshape(1)
    x_parts = gather_freq(x_own, me)
    ct_parts = gather_freq(ct_own, me)
    at = jnp.stack([me, row & 1, (row >> 1) & 1, (row >> 2) & 1, row]).astype(jnp.int32)
    norms = jnp.stack([ln1_gain, ln1_shift, ln2_gain, ln2_shift])
    condt = cond_w.T
    cos_c, sin_c = jnp.asarray(cos_table), jnp.asarray(sin_table)

    w_mine, w2x, w2t, taps, base = prepare(
        me1, w_in, freq_w2, conv_taps, freq_w1, freq_b1, jnp.asarray(feats_aug), step, fs
    )
    forward = forward_spectral(me1, x_parts, ids, norms, w_mine, taps, base, w2x, condt, cos_c, sin_c)
    z_parts, (z_row, u1, n1, p, q, c, vr, vs, mu, mn, cb) = forward[:4], forward[4:]
    z_got = trade_parts(z_parts)
    wg_mine, wu_mine = select_columns(me1, cb, w_gate, w_up, fw, fs)
    h, u2, z_t = middle(me1, z_got, x_own, w_out, norms, wg_mine, step)
    u2_parts = gather_freq(u2, me)
    fed = feed_forward(me1, u2, h, ct_own, norms, w_out, w_gate, w_up, w_down, step)
    mixed_out, big_g, gb, gz_parts, sums2 = fed[0], fed[1], fed[2], fed[3:7], fed[7]
    gz_got = trade_parts(gz_parts)

    hidden = hidden_grads(
        at, u2_parts, ct_parts, wg_mine, wu_mine, w_down.reshape(bs, fs, fw, channels), gb, z_t
    )
    keep_a, give_a, keep_b, give_b = hidden[:4]
    got_a = swap(give_a, "batch", 1)
    got_b = swap(give_b, "batch", 2)
    gb_got = trade_parts(hidden[4:8])
    z_all = gather_freq(hidden[8], me)

    back = backward_spectral(
        me1, gz_got, ids, cb, taps, base, w2x, w2t, jnp.asarray(feats).astype(BF16),
        p, q, c, vr, vs, cos_c, sin_c, give_a,
    )
    gp_parts, (gp, d_taps, d_w2, d_w1, gcb) = back[:4], back[4:]
    gp_got = trade_parts(gp_parts)

    def pairs(value):
        return value.reshape((value.shape[0] // 2, 2) + value.shape[1:])

    keep_a, give_a, keep_b, give_b = halve(
        jnp.stack([at[2], at[1]]), gp, pairs(keep_a), pairs(got_a), keep_b, got_b
    )
    got_a = swap(give_a, "batch", 2)
    got_b = swap(give_b, "batch", 1)

    keep, give, packed = projection_grads(
        at, gp, u1, n1, w_mine, gb_got, z_all, d_w2, d_w1, d_taps, gcb, condt, mu, mn, sums2, give_a, bs
    )
    got = swap(give, "batch", 1)
    grad_tokens = final(me1, gp_got, x_own, big_g, norms, ids, condt, w_in, packed, step)

    keep_ff, give_ff = join(at[3:4], grad_tokens, keep_a, got_a, keep_b, got_b)
    got_ff = swap(give_ff, "batch", 4)

    keep, give = halve(at[2:3], give_ff, pairs(keep), pairs(got))
    got = swap(give, "batch", 2)
    keep, give = halve(at[3:4], give_ff, pairs(keep), pairs(got))
    got = swap(give, "batch", 4)
    mine = keep[0].astype(F32) + got[0].astype(F32)
    first = 2 * width // bs

    for bit in range(bs.bit_length() - 1):
        packed = packed + swap(packed, "batch", 1 << bit)
    d_w2, d_taps, ln, d_w1, d_b1, d_cond = small_grads(
        me1, gather_freq(packed, me), freq_w1.shape[1], channels, step, bs
    )
    d_ff = keep_ff.astype(F32) + got_ff.astype(F32)
    return (
        mixed_out[:, None],
        grad_tokens[:, None],
        ln[0],
        ln[1],
        mine[:first].T,
        d_taps,
        d_w1,
        d_b1[0],
        d_w2,
        d_cond.T,
        mine[first:].T,
        ln[2],
        ln[3],
        d_ff[0].T,
        d_ff[1].T,
        d_ff[2],
    )


def per_device(*args):
    channels = args[0].shape[2]
    step = 2 * channels // (lax.axis_size("batch") * lax.axis_size("freq"))
    fits = lax.axis_size("batch") == 8 and lax.axis_size("freq") == 4 and step % 16 == 0
    return tiled_device(*args) if fits else plain_device(*args)


def solution(mesh):
    rows = P("freq", "batch", None)
    split = P(None, ("batch", "freq"))
    in_specs = (rows, P("batch", None), rows) + (P(),) * 14
    out_specs = (
        rows,
        rows,
        P(),
        P(),
        split,
        P(),
        P(),
        P(),
        P(),
        P(),
        split,
        P(),
        P(),
        split,
        split,
        P(("batch", "freq"), None),
    )
    return jax.shard_map(
        per_device, mesh=mesh, in_specs=in_specs, out_specs=out_specs, check_vma=False
    )
```

```python
import functools

import jax
import jax.numpy as jnp
import ml_dtypes
import numpy as np
from jax import lax
from jax.experimental import pallas as pl
from jax.experimental.pallas import tpu as pltpu
from jax.sharding import PartitionSpec as P

SEGS = 3
EPS = 1e-05
HIGH = lax.Precision.HIGHEST
F32 = jnp.float32
BF16 = jnp.bfloat16


def mm(a, b):
    return jnp.dot(a, b, preferred_element_type=F32)


def mm_nt(a, b):
    return lax.dot_general(a, b, (((1,), (1,)), ((), ())), preferred_element_type=F32)


def mm_tn(a, b):
    return lax.dot_general(a, b, (((0,), (0,)), ((), ())), preferred_element_type=F32)


def swap(value, axis, mask):
    count = lax.axis_size(axis)
    return lax.ppermute(value, axis, [(i, i ^ mask) for i in range(count)])


def pick(parts, index):
    return lax.dynamic_index_in_dim(parts, index, 0, keepdims=False)


def in_order(received, me):
    a, b, c, d = received
    low = (me & 1) == 1
    a, b = jnp.where(low, b, a), jnp.where(low, a, b)
    c, d = jnp.where(low, d, c), jnp.where(low, c, d)
    high = (me & 2) == 2
    a, c = jnp.where(high, c, a), jnp.where(high, a, c)
    b, d = jnp.where(high, d, b), jnp.where(high, b, d)
    return (a, b, c, d)


def trade(blocks, me):
    return [pick(blocks, me)] + [swap(pick(blocks, me ^ k), "freq", k) for k in (2, 3, 1)]


def trade_sorted(blocks, me):
    own, two, three, one = trade(blocks, me)
    return in_order((own, one, two, three), me)


def gather_freq(value, me):
    two = swap(value, "freq", 2)
    one = swap(value, "freq", 1)
    three = swap(two, "freq", 1)
    return (value, one, two, three)


def scatter_sum(value, order):
    bits = lax.axis_size("batch").bit_length() - 1
    me = lax.axis_index("batch")
    rest = value.shape[1:]
    value = value.reshape((2,) * bits + rest)
    left = list(range(bits - 1, -1, -1))
    for bit in order:
        dim = left.index(bit)
        mine = (me >> bit) & 1
        keep = lax.dynamic_index_in_dim(value, mine, dim, keepdims=False)
        give = lax.dynamic_index_in_dim(value, 1 - mine, dim, keepdims=False)
        got = swap(give, "batch", 1 << bit)
        total = keep.astype(F32) + got.astype(F32)
        left.remove(bit)
        value = total.astype(value.dtype) if left else total
    return value


def tables(length):
    index = np.arange(length, dtype=np.int64)
    angle = (index[:, None] * index[None, :] % (2 * length)) * (np.pi / length)
    return (
        np.cos(angle).astype(ml_dtypes.bfloat16),
        np.sin(angle).astype(ml_dtypes.bfloat16),
    )


def features(length, half):
    index = np.arange(length, dtype=np.int64)
    lags = (np.arange(half, dtype=np.int64) + 1) ** 2
    angle = (lags[:, None] * index[None, :] % (2 * length)) * (np.pi / length)
    return np.concatenate([np.cos(angle), np.sin(angle)], axis=0).astype(np.float32)


def normed(values):
    centered = values - jnp.mean(values, axis=-1, keepdims=True)
    scale = lax.rsqrt(jnp.mean(centered * centered, axis=-1, keepdims=True) + EPS)
    return centered * scale, scale


def norm_back(unit, scale, grad):
    return scale * (
        grad
        - jnp.mean(grad, axis=-1, keepdims=True)
        - unit * jnp.mean(grad * unit, axis=-1, keepdims=True)
    )


def shift_right(values):
    return jnp.pad(values, ((0, 0), (1, 0)))[:, :-1]


def shift_left(values):
    return jnp.pad(values, ((0, 0), (0, 1)))[:, 1:]


def plain_device(
    tokens,
    seg_ids,
    cotangent,
    ln1_gain,
    ln1_shift,
    w_in,
    conv_taps,
    freq_w1,
    freq_b1,
    freq_w2,
    cond_w,
    w_out,
    ln2_gain,
    ln2_shift,
    w_gate,
    w_up,
    w_down,
):
    quarter, _, channels = tokens.shape
    length = seg_ids.shape[1]
    ff = w_gate.shape[1]
    fs = lax.axis_size("freq")
    bs = lax.axis_size("batch")
    me = lax.axis_index("freq")
    width = channels // fs
    half = bs // 2
    step = channels // (half * fs)
    cos_table, sin_table = tables(length)
    feats = features(length, freq_w1.shape[0] // 2)

    x_own = tokens[:, 0]
    ct_own = cotangent[:, 0]
    ids = seg_ids
    x_parts = gather_freq(x_own, me)
    ct_parts = gather_freq(ct_own, me)

    w_in_t = (
        w_in.T.reshape(2, half, fs, step, channels)
        .transpose(2, 0, 1, 3, 4)
        .reshape(fs, 2 * width, channels)
    )
    w_in_mine = pick(w_in_t, me)
    w_out_p = (
        w_out.reshape(half, fs, step, channels).transpose(1, 0, 2, 3).reshape(channels, channels)
    )
    taps_mine = pick(
        conv_taps.reshape(3, 2, half, fs, step).transpose(3, 0, 1, 2, 4).reshape(fs, 3, 2 * width), me
    )[:, :, None]
    w2_mine = pick(
        freq_w2.reshape(-1, 2, half, fs, step).transpose(3, 0, 1, 2, 4).reshape(fs, -1, 2 * width), me
    )
    fw = ff // (bs * fs)
    wide = ff // fs

    def mine_rows(weight):
        return pick(
            weight.reshape(bs, fs, fw, channels).transpose(1, 0, 2, 3).reshape(fs, wide, channels), me
        )

    wg_mine, wu_mine, wd_mine = (mine_rows(w_gate.T), mine_rows(w_up.T), mine_rows(w_down))

    base = jnp.dot(freq_w1.T, feats, precision=HIGH) + freq_b1[:, None]

    x_row = jnp.concatenate(in_order(x_parts, me), axis=0).astype(F32)
    unit1, _ = normed(x_row)
    u1 = (unit1 * ln1_gain + ln1_shift).astype(BF16)
    n1 = unit1.astype(BF16)
    masks = (ids == jnp.arange(SEGS, dtype=jnp.int32)[:, None]).astype(F32)
    counts = jnp.sum(masks, axis=1, keepdims=True)
    mu = mm(masks.astype(BF16), u1) / counts
    mn = mm(masks.astype(BF16), n1) / counts
    cb = jnp.dot(mu, cond_w, precision=HIGH)
    p = mm_nt(w_in_mine, u1)
    same = (ids[:, 1:] == ids[:, :-1]).astype(F32)
    zero = jnp.zeros((1, 1), F32)
    prev = jnp.concatenate([zero, same], axis=1)
    nxt = jnp.concatenate([same, zero], axis=1)
    p_prev = shift_right(p) * prev
    p_next = shift_left(p) * nxt
    s = taps_mine[0] * p_prev + taps_mine[1] * p + taps_mine[2] * p_next
    q, v = s[:width], s[width:]

    pre = base[None] + cb[:, :, None]
    gate_pre = jax.nn.sigmoid(pre)
    hk = pre * gate_pre
    kk = jnp.einsum("kc,jkf->jcf", w2_mine, hk, precision=HIGH)
    kr, ki = kk[:, :width], kk[:, width:]
    vm = (v[None] * masks[:, None, :]).astype(BF16).reshape(SEGS * width, length)
    vr = mm(vm, cos_table).reshape(SEGS, width, length)
    vi = -mm(vm, sin_table).reshape(SEGS, width, length)
    weights = np.full((length,), 2.0 / (2 * length), np.float32)
    weights[0] = 1.0 / (2 * length)
    yr = ((kr * vr - ki * vi) * weights).astype(BF16).reshape(SEGS * width, length)
    yi = ((kr * vi + ki * vr) * weights).astype(BF16).reshape(SEGS * width, length)
    conv = (mm(yr, cos_table) - mm(yi, sin_table)).reshape(SEGS, width, length)
    c = jnp.sum(conv * masks[:, None, :], axis=0)
    z_mine = (q * c).astype(BF16)

    z_blocks = z_mine.reshape(width, fs, quarter).transpose(1, 0, 2)
    z_t = jnp.concatenate(trade_sorted(z_blocks, me), axis=0)

    x32 = x_own.astype(F32)
    ct32 = ct_own.astype(F32)
    h = x32 + mm_tn(z_t, w_out_p)
    unit2, scale2 = normed(h)
    u2 = (unit2 * ln2_gain + ln2_shift).astype(BF16)
    u2_parts = gather_freq(u2, me)
    g = mm(u2, w_gate)
    a = mm(u2, w_up)
    gh = mm_nt(ct_own, w_down)
    sg = jax.nn.sigmoid(g)
    silu = g * sg
    hid = (silu * a).astype(BF16)
    mixed_out = (h + mm(hid, w_down)).astype(BF16)
    gg = (gh * a * sg * (1.0 + g * (1.0 - sg))).astype(BF16)
    ga = (gh * silu).astype(BF16)
    gu2 = mm_nt(gg, w_gate) + mm_nt(ga, w_up)
    grad_ln2_gain = jnp.sum(gu2 * unit2, axis=0)
    grad_ln2_shift = jnp.sum(gu2, axis=0)
    big_g = ct32 + norm_back(unit2, scale2, gu2 * ln2_gain)
    gb = big_g.astype(BF16)
    gz_blocks = mm_nt(w_out_p, gb).astype(BF16).reshape(fs, width, quarter)
    gz = jnp.concatenate(trade_sorted(gz_blocks, me), axis=1).astype(F32)
    gb_parts = gather_freq(gb, me)

    u2_row = jnp.concatenate(u2_parts, axis=0)
    ct_row = jnp.concatenate(ct_parts, axis=0)
    g_t = mm_nt(wg_mine, u2_row)
    a_t = mm_nt(wu_mine, u2_row)
    gh_t = mm_nt(wd_mine, ct_row)
    sg_t = jax.nn.sigmoid(g_t)
    silu_t = g_t * sg_t
    hid_t = (silu_t * a_t).astype(BF16)
    gg_t = (gh_t * a_t * sg_t * (1.0 + g_t * (1.0 - sg_t))).astype(BF16)
    ga_t = (gh_t * silu_t).astype(BF16)
    d_gate = mm(gg_t, u2_row).astype(BF16)
    d_up = mm(ga_t, u2_row).astype(BF16)
    d_down = mm(hid_t, ct_row).astype(BF16)
    d_ff = jnp.stack([d_gate, d_up, d_down], axis=0).reshape(3, bs, fw, channels).transpose(1, 0, 2, 3)
    bits = bs.bit_length() - 1
    order_a = list(range(bits))
    order_b = [1, 0] + list(range(2, bits))
    cut = channels // 2
    ff_a = scatter_sum(d_ff[..., :cut], order_a)
    ff_b = scatter_sum(d_ff[..., cut:], order_b)
    d_ff = jnp.concatenate([ff_a, ff_b], axis=-1)

    gq = gz * c
    gc = gz * q
    gcm = (gc[None] * masks[:, None, :]).astype(BF16).reshape(SEGS * width, length)
    gyr = mm(gcm, cos_table).reshape(SEGS, width, length) * weights
    gyi = -mm(gcm, sin_table).reshape(SEGS, width, length) * weights
    gkr = gyr * vr + gyi * vi
    gki = gyi * vr - gyr * vi
    gvr = (kr * gyr + ki * gyi).astype(BF16).reshape(SEGS * width, length)
    gvi = (kr * gyi - ki * gyr).astype(BF16).reshape(SEGS * width, length)
    gv_all = (mm(gvr, cos_table) - mm(gvi, sin_table)).reshape(SEGS, width, length)
    gv = jnp.sum(gv_all * masks[:, None, :], axis=0)
    gs = jnp.concatenate([gq, gv], axis=0)
    d_taps = jnp.stack(
        [jnp.sum(gs * p_prev, axis=1), jnp.sum(gs * p, axis=1), jnp.sum(gs * p_next, axis=1)]
    )
    gp = (
        taps_mine[1] * gs
        + taps_mine[0] * shift_left(gs * prev)
        + taps_mine[2] * shift_right(gs * nxt)
    ).astype(BF16)

    gkk = jnp.concatenate([gkr, gki], axis=1)
    gkk_low = gkk.astype(BF16)
    hk_low = hk.astype(BF16)
    d_w2 = jnp.einsum("jkf,jcf->kc", hk_low, gkk_low, preferred_element_type=F32)
    gpre = jnp.einsum("kc,jcf->jkf", w2_mine.astype(BF16), gkk_low, preferred_element_type=F32)
    gpre = gpre * gate_pre * (1.0 + pre * (1.0 - gate_pre))
    d_w1 = jnp.einsum("ef,jkf->ek", feats, gpre, precision=HIGH)
    gcb = jnp.sum(gpre, axis=2)
    gcb_row = lax.psum(gcb, "freq")

    gp_blocks = gp.reshape(2 * width, fs, quarter).transpose(1, 0, 2)
    gp_t = jnp.concatenate(trade_sorted(gp_blocks, me), axis=0)

    u1_row = u1
    d_in = mm(gp, u1_row).astype(BF16).reshape(bs, 2 * width // bs, channels)
    d_in = scatter_sum(d_in, order_a)
    gb_row = jnp.concatenate(in_order(gb_parts, me), axis=0)
    d_out = mm(z_mine, gb_row)
    narrow = channels // bs
    d_out = scatter_sum(d_out.T.astype(BF16).reshape(bs, narrow, width), order_a)
    d_out = d_out.reshape(fs, narrow // fs, width)
    d_out = jnp.stack(trade_sorted(d_out, me), axis=0)
    d_out = (
        d_out.reshape(fs, narrow // fs, half, step).transpose(2, 0, 3, 1).reshape(channels, -1)
    )

    gmu_part = jnp.dot(gcb, cond_w.T, precision=HIGH)
    sum_gp = jnp.sum(gp.astype(F32), axis=1)
    w_mine32 = w_in_mine.astype(F32)
    d_shift1 = jnp.dot(sum_gp[None], w_mine32, precision=HIGH)[0] + jnp.sum(gmu_part, axis=0)
    d_gain1 = jnp.sum(mm(gp, n1) * w_mine32, axis=0) + jnp.sum(gmu_part * mn, axis=0)

    gmu = jnp.dot(gcb_row, cond_w.T, precision=HIGH) / counts
    own_masks = lax.dynamic_slice_in_dim(masks, me * quarter, quarter, 1)
    gu1 = mm_tn(gp_t, w_in_t.reshape(2 * channels, channels)) + lax.dot_general(
        own_masks, gmu, (((0,), (0,)), ((), ())), precision=HIGH
    )
    unit_own, scale_own = normed(x32)
    grad_tokens = big_g + norm_back(unit_own, scale_own, gu1 * ln1_gain)

    shared = [
        d_gain1,
        d_shift1,
        d_w1.reshape(-1),
        jnp.sum(gcb, axis=0),
        jnp.dot(mu.T, gcb, precision=HIGH).reshape(-1),
        grad_ln2_gain,
        grad_ln2_shift,
    ]
    owned = jnp.concatenate([d_taps, d_w2], axis=0)
    packed = jnp.concatenate(shared + [owned.reshape(-1)])
    for bit in range(bits):
        packed = packed + swap(packed, "batch", 1 << bit)
    split = packed.shape[0] - owned.size
    common, owned = packed[:split], packed[split:]
    common = common + swap(common, "freq", 1)
    common = common + swap(common, "freq", 2)
    owned = jnp.stack(in_order(gather_freq(owned, me), me), axis=0)
    owned = (
        owned.reshape(fs, -1, 2, half, step).transpose(1, 2, 3, 0, 4).reshape(-1, 2 * channels)
    )
    sizes = np.cumsum([part.size for part in shared])
    got = jnp.split(common, sizes[:-1])
    return (
        mixed_out[:, None],
        grad_tokens[:, None],
        got[0],
        got[1],
        d_in.T,
        owned[:3],
        got[2].reshape(freq_w1.shape),
        got[3],
        owned[3:],
        got[4].reshape(cond_w.shape),
        d_out,
        got[5],
        got[6],
        d_ff[0].T,
        d_ff[1].T,
        d_ff[2],
    )


VM = pl.BlockSpec(memory_space=pltpu.VMEM)
SM = pl.BlockSpec(memory_space=pltpu.SMEM)
HBM = pl.BlockSpec(memory_space=pl.ANY)
MIB = 1 << 20


def params():
    return pltpu.CompilerParams(vmem_limit_bytes=60 * MIB)


def cost(micros):
    return pl.CostEstimate(
        flops=int(micros * 1000000000.0), bytes_accessed=int(micros * 3500000.0), transcendentals=0
    )


def shape(dims, dtype):
    return jax.ShapeDtypeStruct(dims, dtype)


def sigmoid(value):
    return 1.0 / (1.0 + jnp.exp(-value))


def dma_all(pairs, sems, first=0):
    copies = [
        pltpu.make_async_copy(source, target, sems.at[first + i])
        for i, (source, target) in enumerate(pairs)
    ]
    for copy in copies:
        copy.start()
    return copies


def tie_kernel(value, after, out):
    pass


def tie(value, after):
    return pl.pallas_call(
        tie_kernel,
        in_specs=[HBM, HBM],
        out_specs=HBM,
        out_shape=shape(value.shape, value.dtype),
        input_output_aliases={0: 0},
        name="tie",
    )(value, after)


def one_hot_rows(me, rows, lanes, piece, fs):
    row = lax.broadcasted_iota(jnp.int32, (rows, lanes), 0)
    lane = lax.broadcasted_iota(jnp.int32, (rows, lanes), 1)
    block = jnp.zeros_like(row)
    for m in range(1, rows // piece):
        block = block + jnp.where(row >= m * piece, 1, 0)
    return jnp.where(lane == block * ((fs - 1) * piece) + me * piece + row, 1.0, 0.0)


def prepare_kernel(
    me_ref, w_in, freq_w2, conv_taps, freq_w1, freq_b1, feats,
    w_mine, w2x, w2t, taps, base, w1_aug, *, step, fs,
):
    lanes = w_in.shape[1] // 4
    rows = lanes // fs
    sel = one_hot_rows(me_ref[0], rows, lanes, step, fs)
    low = sel.astype(BF16)
    hidden = freq_w2.shape[0]
    for i in range(4):
        out = slice(i * rows, (i + 1) * rows)
        group = slice(i * lanes, (i + 1) * lanes)
        w_mine[out, :] = mm_nt(low, w_in[:, group]).astype(BF16)
        both = jnp.concatenate([freq_w2[:, group], conv_taps[:, group]], axis=0)
        mine = lax.dot_general(
            sel, both, (((1,), (1,)), ((), ())), precision=HIGH, preferred_element_type=F32
        )
        taps[out, :3] = mine[:, hidden:]
        mine = mine[:, :hidden]
        high = mine.astype(BF16)
        rest = (mine - high.astype(F32)).astype(BF16)
        w2x[out, :] = jnp.concatenate([high, high, rest], axis=1)
    w2t[...] = jnp.transpose(w2x[...][:, :hidden].astype(F32)).astype(BF16)
    w1_aug[...] = jnp.zeros_like(w1_aug)
    count = freq_w1.shape[0]
    w1_aug[:count, :] = freq_w1[...]
    w1_aug[count : count + 1, :] = freq_b1[...]
    base[...] = lax.dot_general(
        w1_aug[...], feats[...], (((0,), (0,)), ((), ())), precision=HIGH, preferred_element_type=F32
    )


def prepare(me, w_in, freq_w2, conv_taps, freq_w1, freq_b1, feats, step, fs):
    channels, both = w_in.shape
    hidden = freq_w2.shape[0]
    length = feats.shape[1]
    return pl.pallas_call(
        functools.partial(prepare_kernel, step=step, fs=fs),
        in_specs=[SM] + [VM] * 6,
        out_specs=[VM] * 5,
        out_shape=[
            shape((both // fs, channels), BF16),
            shape((both // fs, 3 * hidden), BF16),
            shape((hidden, both // fs), BF16),
            shape((both // fs, 8), F32),
            shape((hidden, length), F32),
        ],
        scratch_shapes=[pltpu.VMEM((feats.shape[0], hidden), F32)],
        compiler_params=params(),
        cost_estimate=cost(3),
        name="prepare",
    )(me, w_in, freq_w2, conv_taps, freq_w1, freq_b1[None], feats)


def select_kernel(me_ref, after, gate, up, gate_out, up_out, *, piece, fs):
    rows = gate_out.shape[0] // 2
    lanes = rows * fs
    sel = one_hot_rows(me_ref[0], rows, lanes, piece, fs).astype(BF16)
    for weight, out in ((gate, gate_out), (up, up_out)):
        for part in range(2):
            block = mm_nt(sel, weight[:, part * lanes : (part + 1) * lanes])
            out[part * rows : (part + 1) * rows, :] = block.astype(BF16)


def select_columns(me, after, w_gate, w_up, piece, fs):
    channels, ff = w_gate.shape
    big = ff // 4
    wide = pl.BlockSpec((channels, big), lambda i: (0, i))
    rows = pl.BlockSpec((big // fs, channels), lambda i: (i, 0))
    return pl.pallas_call(
        functools.partial(select_kernel, piece=piece, fs=fs),
        grid=(4,),
        in_specs=[SM, HBM, wide, wide],
        out_specs=[rows, rows],
        out_shape=[shape((ff // fs, channels), BF16)] * 2,
        compiler_params=params(),
        cost_estimate=cost(6),
        name="select_columns",
    )(me, after, w_gate, w_up)


def row_masks(ids):
    lane = lax.broadcasted_iota(jnp.int32, ids.shape, 1)
    length = ids.shape[1]
    prev = jnp.where((ids == pltpu.roll(ids, 1, 1)) & (lane > 0), 1.0, 0.0)
    nxt = jnp.where((ids == pltpu.roll(ids, length - 1, 1)) & (lane < length - 1), 1.0, 0.0)
    return prev, nxt


def bin_weights(start, width, length):
    lane = lax.broadcasted_iota(jnp.int32, (1, width), 1) + start
    return jnp.where(lane == 0, 0.5 / length, 1.0 / length)


def tile(index, size):
    return pl.ds(pl.multiple_of(index * size, size), size)


def hidden_tile(base, cb, j, lanes):
    pre = base[:, lanes] + cb[:, j : j + 1]
    return pre, sigmoid(pre)


def kernel_tile(w2x, hk):
    high = hk.astype(BF16)
    rest = (hk - high.astype(F32)).astype(BF16)
    return mm(w2x[...], jnp.concatenate([high, rest, high], axis=0))


def forward_kernel(
    me_ref, ids_at, x0, x1, x2, x3, ids_ref, norms, w, taps, base, w2x, condt, cos_hbm, sin_hbm,
    z0, z1, z2, z3, zrow_hbm, u1_hbm, n1_hbm, p_hbm, q_hbm, c_hbm, vr_hbm, vs_hbm, mu_out, mn_out, cb_out,
    cos, sin, z_row, u1, n1, p_out, q_out, c_out, vr_out, vs_out, p, q, vm, ycat, acc, sems,
):
    quarter = x0.shape[0]
    width, length = z_row.shape
    tiles = length // quarter
    me = me_ref[0]
    loads = dma_all([(cos_hbm, cos), (sin_hbm, sin)], sems)
    for k, x in enumerate((x0, x1, x2, x3)):
        values = x[...].astype(F32)
        unit, _ = normed(values)
        rows = tile(me ^ k, quarter)
        n1[rows, :] = unit.astype(BF16)
        u1[rows, :] = (unit * norms[0:1, :] + norms[1:2, :]).astype(BF16)
    stores = dma_all([(u1, u1_hbm), (n1, n1_hbm)], sems, 2)
    ids = ids_ref[...]
    number = lax.broadcasted_iota(jnp.int32, (8, length), 0)
    member = jnp.where(ids == number, 1.0, 0.0)
    counts = jnp.maximum(jnp.sum(member, axis=1, keepdims=True), 1.0)
    member_low = member.astype(BF16)
    mu = mm(member_low, u1[...]) / counts
    mu_out[...] = mu
    mn_out[...] = mm(member_low, n1[...]) / counts
    cb_out[...] = lax.dot_general(
        condt[...], mu, (((1,), (1,)), ((), ())), precision=HIGH, preferred_element_type=F32
    )
    prev, nxt = row_masks(ids)
    for t in range(tiles):
        at = slice(t * quarter, (t + 1) * quarter)
        p[:, at] = mm_nt(w[...], u1[at, :])
    chunk = width // 2
    for r in range(4):
        at = slice(r * chunk, (r + 1) * chunk)
        here = p[at, :]
        p_out[at, :] = here.astype(BF16)
        mixed = (
            taps[at, 0:1] * (pltpu.roll(here, 1, 1) * prev)
            + taps[at, 1:2] * here
            + taps[at, 2:3] * (pltpu.roll(here, length - 1, 1) * nxt)
        )
        if r < 2:
            q[at, :] = mixed
            q_out[at, :] = mixed.astype(BF16)
        else:
            for j in range(SEGS):
                lo = j * width + (r - 2) * chunk
                vm[lo : lo + chunk, :] = (mixed * member[j : j + 1, :]).astype(BF16)
    stores += dma_all([(p_out, p_hbm), (q_out, q_hbm)], sems, 4)
    for load in loads:
        load.wait()

    @pl.loop(0, tiles)
    def _(f):
        lanes = tile(f, quarter)
        upper = pl.ds(pl.multiple_of(f * quarter + length, quarter), quarter)
        weight = bin_weights(f * quarter, quarter, length)
        vr_all = mm(vm[...], cos[:, lanes])
        vs_all = mm(vm[...], sin[:, lanes])
        vr_out[:, lanes] = vr_all.astype(BF16)
        vs_out[:, lanes] = vs_all.astype(BF16)
        for j in range(SEGS):
            pre, gate = hidden_tile(base, cb_out, j, lanes)
            kk = kernel_tile(w2x, pre * gate)
            kr, ki = kk[:width] * weight, kk[width:] * weight
            at = slice(j * width, (j + 1) * width)
            vr, vs = vr_all[at], vs_all[at]
            ycat[at, lanes] = (kr * vr + ki * vs).astype(BF16)
            ycat[at, upper] = (kr * vs - ki * vr).astype(BF16)

    stores += dma_all([(vr_out, vr_hbm), (vs_out, vs_hbm)], sems, 6)
    for k, z_out in enumerate((z0, z1, z2, z3)):
        t = me ^ k
        lanes = tile(t, quarter)
        acc[...] = jnp.zeros_like(acc)
        ids_here = ids_ref[:, lanes]
        for j in range(SEGS):

            @pl.when((ids_at[0, t * quarter] <= j) & (ids_at[0, (t + 1) * quarter - 1] >= j))
            def _():
                at = slice(j * width, (j + 1) * width)
                part = mm(ycat[at, :length], cos[:, lanes]) + mm(ycat[at, length:], sin[:, lanes])
                acc[...] += jnp.where(ids_here == j, part, 0.0)

        c = acc[...]
        c_out[:, lanes] = c.astype(BF16)
        z = (q[:, lanes] * c).astype(BF16)
        z_out[...] = z
        z_row[:, lanes] = z
    stores += dma_all([(c_out, c_hbm), (z_row, zrow_hbm)], sems, 8)
    for store in stores:
        store.wait()


def forward_spectral(me, x_parts, ids, norms, w, taps, base, w2x, condt, cos, sin):
    quarter, channels = x_parts[0].shape
    length = ids.shape[1]
    width = w.shape[0] // 2
    saved = [
        (width, length),
        (length, channels),
        (length, channels),
        (2 * width, length),
        (width, length),
        (width, length),
        (SEGS * width, length),
        (SEGS * width, length),
    ]
    small = [
        shape((8, channels), F32),
        shape((8, channels), F32),
        shape((condt.shape[0], 8), F32),
    ]
    return pl.pallas_call(
        forward_kernel,
        in_specs=[SM, SM] + [VM] * 11 + [HBM, HBM],
        out_specs=[VM] * 4 + [HBM] * len(saved) + [VM] * 3,
        out_shape=[shape((width, quarter), BF16)] * 4 + [shape(dims, BF16) for dims in saved] + small,
        scratch_shapes=[pltpu.VMEM((length, length), BF16)] * 2
        + [pltpu.VMEM(dims, BF16) for dims in saved]
        + [
            pltpu.VMEM((2 * width, length), F32),
            pltpu.VMEM((width, length), F32),
            pltpu.VMEM((SEGS * width, length), BF16),
            pltpu.VMEM((SEGS * width, 2 * length), BF16),
            pltpu.VMEM((width, quarter), F32),
            pltpu.SemaphoreType.DMA((10,)),
        ],
        compiler_params=params(),
        cost_estimate=cost(15),
        name="forward_spectral",
    )(me, ids, *x_parts, ids, norms, w, taps, base, w2x, condt, cos, sin)


def backward_kernel(
    me_ref, ids_at, g0, g1, g2, g3, ids_ref, cb, taps, base, w2x, w2, feats,
    p_hbm, q_hbm, c_hbm, vr_hbm, vs_hbm, cos_hbm, sin_hbm, after,
    o0, o1, o2, o3, gp_hbm, d_taps, d_w2, d_w1, gcb,
    cos, sin, p, q, c, vr_in, vs_in, gp_row, gcm, gvcat, gs, acc, sems,
):
    width, quarter = g0.shape
    length = gp_row.shape[1]
    tiles = length // quarter
    hidden = base.shape[0]
    me = me_ref[0]
    loads = dma_all(
        [
            (c_hbm, c), (q_hbm, q), (cos_hbm, cos), (sin_hbm, sin),
            (vr_hbm, vr_in), (vs_hbm, vs_in), (p_hbm, p),
        ],
        sems,
    )
    loads[0].wait()
    loads[1].wait()
    for k, g in enumerate((g0, g1, g2, g3)):
        lanes = tile(me ^ k, quarter)
        gz = g[...].astype(F32)
        gs[:width, lanes] = gz * c[:, lanes].astype(F32)
        gc = gz * q[:, lanes].astype(F32)
        ids_here = ids_ref[:, lanes]
        for j in range(SEGS):
            gcm[j * width : (j + 1) * width, lanes] = jnp.where(ids_here == j, gc, 0.0).astype(BF16)
    d_w2[...] = jnp.zeros_like(d_w2)
    d_w1[...] = jnp.zeros_like(d_w1)
    gcb[...] = jnp.zeros_like(gcb)
    for load in loads[2:]:
        load.wait()

    @pl.loop(0, tiles)
    def _(f):
        lanes = tile(f, quarter)
        upper = pl.ds(pl.multiple_of(f * quarter + length, quarter), quarter)
        weight = bin_weights(f * quarter, quarter, length)
        gyr_all = mm(gcm[...], cos[:, lanes]) * weight
        gys_all = mm(gcm[...], sin[:, lanes]) * weight
        for j in range(SEGS):
            pre, gate = hidden_tile(base, cb, j, lanes)
            hk = pre * gate
            kk = kernel_tile(w2x, hk)
            kr, ki = kk[:width], kk[width:]
            at = slice(j * width, (j + 1) * width)
            gyr, gys = gyr_all[at], gys_all[at]
            vr, vs = vr_in[at, lanes].astype(F32), vs_in[at, lanes].astype(F32)
            gvcat[at, lanes] = (kr * gyr - ki * gys).astype(BF16)
            gvcat[at, upper] = (kr * gys + ki * gyr).astype(BF16)
            gkk = jnp.concatenate(
                [(gyr * vr + gys * vs).astype(BF16), (gyr * vs - gys * vr).astype(BF16)], axis=0
            )
            d_w2[...] += mm_nt(gkk, hk.astype(BF16))
            gpre = mm(w2[...], gkk) * (gate * (1.0 + pre * (1.0 - gate)))
            gcb[:, j : j + 1] += jnp.sum(gpre, axis=1, keepdims=True)
            d_w1[...] += mm_nt(feats[:, lanes], gpre.astype(BF16))

    for k in range(4):
        t = me ^ k
        lanes = tile(t, quarter)
        acc[...] = jnp.zeros_like(acc)
        ids_here = ids_ref[:, lanes]
        for j in range(SEGS):

            @pl.when((ids_at[0, t * quarter] <= j) & (ids_at[0, (t + 1) * quarter - 1] >= j))
            def _():
                at = slice(j * width, (j + 1) * width)
                part = mm(gvcat[at, :length], cos[:, lanes]) + mm(gvcat[at, length:], sin[:, lanes])
                acc[...] += jnp.where(ids_here == j, part, 0.0)

        gs[width:, lanes] = acc[...]
    prev, nxt = row_masks(ids_ref[...])
    chunk = width // 2
    for r in range(4):
        at = slice(r * chunk, (r + 1) * chunk)
        here = p[at, :].astype(F32)
        grad = gs[at, :]
        d_taps[at, 0:1] = jnp.sum(grad * (pltpu.roll(here, 1, 1) * prev), axis=1, keepdims=True)
        d_taps[at, 1:2] = jnp.sum(grad * here, axis=1, keepdims=True)
        d_taps[at, 2:3] = jnp.sum(
            grad * (pltpu.roll(here, length - 1, 1) * nxt), axis=1, keepdims=True
        )
        gp_row[at, :] = (
            taps[at, 1:2] * grad
            + taps[at, 0:1] * pltpu.roll(grad * prev, length - 1, 1)
            + taps[at, 2:3] * pltpu.roll(grad * nxt, 1, 1)
        ).astype(BF16)
    store = dma_all([(gp_row, gp_hbm)], sems, 7)[0]
    share = jnp.transpose(gcb[...])[:8, :]
    high = share.astype(BF16)
    rest = (share - high.astype(F32)).astype(BF16)
    extra = jnp.concatenate([high, rest], axis=0)
    extra = jnp.concatenate([extra, jnp.zeros((16, quarter - hidden), BF16)], axis=1)
    for k, out in enumerate((o0, o1, o2, o3)):
        out[: 2 * width, :] = gp_row[:, tile(me ^ k, quarter)]
        out[2 * width :, :] = extra
    store.wait()


def backward_spectral(
    me, gz_parts, ids, cb, taps, base, w2x, w2, feats, p, q, c, vr, vs, cos, sin, after
):
    width, quarter = gz_parts[0].shape
    length = ids.shape[1]
    hidden = base.shape[0]
    outs = [shape((2 * width + 16, quarter), BF16)] * 4 + [
        shape((2 * width, length), BF16),
        shape((2 * width, 128), F32),
        shape((2 * width, hidden), F32),
        shape((feats.shape[0], hidden), F32),
        shape((hidden, 128), F32),
    ]
    return pl.pallas_call(
        backward_kernel,
        in_specs=[SM, SM] + [VM] * 11 + [HBM] * 8,
        out_specs=[VM] * 4 + [HBM] + [VM] * 4,
        out_shape=outs,
        scratch_shapes=[
            pltpu.VMEM((length, length), BF16),
            pltpu.VMEM((length, length), BF16),
            pltpu.VMEM((2 * width, length), BF16),
            pltpu.VMEM((width, length), BF16),
            pltpu.VMEM((width, length), BF16),
            pltpu.VMEM((SEGS * width, length), BF16),
            pltpu.VMEM((SEGS * width, length), BF16),
            pltpu.VMEM((2 * width, length), BF16),
            pltpu.VMEM((SEGS * width, length), BF16),
            pltpu.VMEM((SEGS * width, 2 * length), BF16),
            pltpu.VMEM((2 * width, length), F32),
            pltpu.VMEM((width, quarter), F32),
            pltpu.SemaphoreType.DMA((8,)),
        ],
        compiler_params=params(),
        cost_estimate=cost(17),
        name="backward_spectral",
    )(
        me, ids, *gz_parts, ids, cb, taps, base, w2x, w2, feats, p, q, c, vr, vs, cos, sin, after
    )


def middle_kernel(me_ref, z0, z1, z2, z3, x, w_out, norms, after, h_out, u2_out, z_t, *, piece):
    me = me_ref[0]
    width = z0.shape[0]
    for k, z in enumerate((z0, z1, z2, z3)):
        for i in range(width // piece):
            at = pl.ds(pl.multiple_of((i * 4 + (me ^ k)) * piece, piece), piece)
            z_t[at, :] = z[i * piece : (i + 1) * piece, :]
    h = x[...].astype(F32) + mm(jnp.transpose(z_t[...]), w_out[...])
    h_out[...] = h
    unit, _ = normed(h)
    u2_out[...] = (unit * norms[2:3, :] + norms[3:4, :]).astype(BF16)


def middle(me, z_parts, x, w_out, norms, after, piece):
    quarter, channels = x.shape
    return pl.pallas_call(
        functools.partial(middle_kernel, piece=piece),
        in_specs=[SM] + [VM] * 7 + [HBM],
        out_specs=[VM] * 3,
        out_shape=[
            shape((quarter, channels), F32),
            shape((quarter, channels), BF16),
            shape((channels, quarter), BF16),
        ],
        compiler_params=params(),
        cost_estimate=cost(2),
        name="middle",
    )(me, *z_parts, x, w_out, norms, after)


def feed_kernel(
    me_ref, u2, h, ct, norms, w_out, gate, up, down,
    mixed, big_g, g0, g1, g2, g3, t0, t1, t2, t3, sums, acc_out, acc_grad, gz_t, gb_t, *, piece, thin,
):
    i = pl.program_id(0)

    @pl.when(i == 0)
    def _():
        acc_out[...] = jnp.zeros_like(acc_out)
        acc_grad[...] = jnp.zeros_like(acc_grad)

    g = mm(u2[...], gate[...])
    a = mm(u2[...], up[...])
    gh = mm_nt(ct[...], down[...])
    sg = sigmoid(g)
    silu = g * sg
    hid = (silu * a).astype(BF16)
    gg = (gh * a * (sg * (1.0 + g * (1.0 - sg)))).astype(BF16)
    ga = (gh * silu).astype(BF16)
    acc_out[...] += mm(hid, down[...])
    acc_grad[...] += mm_nt(gg, gate[...]) + mm_nt(ga, up[...])

    @pl.when(i == pl.num_programs(0) - 1)
    def _():
        me = me_ref[0]
        width = g0.shape[0]
        here = h[...]
        mixed[...] = (here + acc_out[...]).astype(BF16)
        gu2 = acc_grad[...]
        unit, scale = normed(here)
        sums[0:1, :] = jnp.sum(gu2 * unit, axis=0, keepdims=True)
        sums[1:2, :] = jnp.sum(gu2, axis=0, keepdims=True)
        total = ct[...].astype(F32) + norm_back(unit, scale, gu2 * norms[2:3, :])
        big_g[...] = total
        low = total.astype(BF16)
        gz_t[...] = mm_nt(w_out[...], low).astype(BF16)
        for k, out in enumerate((g0, g1, g2, g3)):
            for r in range(width // piece):
                at = pl.ds(pl.multiple_of((r * 4 + (me ^ k)) * piece, piece), piece)
                out[r * piece : (r + 1) * piece, :] = gz_t[at, :]
        gb_t[...] = jnp.transpose(total)
        for k, out in enumerate((t0, t1, t2, t3)):
            parts = []
            for r in range(width // thin):
                lo = pl.multiple_of((r * 4 + (me ^ k)) * thin, thin)
                parts.append(gb_t[pl.ds(lo, thin), :])
            out[...] = jnp.concatenate(parts, axis=0).astype(BF16)


def feed_forward(me, u2, h, ct, norms, w_out, w_gate, w_up, w_down, piece, thin):
    quarter, channels = u2.shape
    ff = w_gate.shape[1]
    block = 512

    def whole(*dims):
        return pl.BlockSpec(dims, lambda i: (0,) * len(dims))

    width = channels // 4
    outs = [
        ((quarter, channels), BF16),
        ((quarter, channels), F32),
    ] + [((width, quarter), BF16)] * 8 + [((8, channels), F32)]
    return pl.pallas_call(
        functools.partial(feed_kernel, piece=piece, thin=thin),
        grid=(ff // block,),
        in_specs=[
            SM,
            whole(quarter, channels),
            whole(quarter, channels),
            whole(quarter, channels),
            whole(4, channels),
            whole(channels, channels),
            pl.BlockSpec((channels, block), lambda i: (0, i)),
            pl.BlockSpec((channels, block), lambda i: (0, i)),
            pl.BlockSpec((block, channels), lambda i: (i, 0)),
        ],
        out_specs=[whole(*dims) for dims, _ in outs],
        out_shape=[shape(*out) for out in outs],
        scratch_shapes=[
            pltpu.VMEM((quarter, channels), F32),
            pltpu.VMEM((quarter, channels), F32),
            pltpu.VMEM((channels, quarter), BF16),
            pltpu.VMEM((channels, quarter), F32),
        ],
        compiler_params=params(),
        cost_estimate=cost(13),
        name="feed_forward",
    )(me, u2, h, ct, norms, w_out, w_gate, w_up, w_down)


def hidden_grads_kernel(
    at_ref, u0, u1, u2, u3, c0, c1, c2, c3, gate, up, down, after,
    keep_a, give_a, keep_b, give_b, u_row, c_row, d_all,
):
    quarter, channels = u0.shape
    i = pl.program_id(0)
    y, z = at_ref[1], at_ref[2]

    @pl.when(i == 0)
    def _():
        for k, (u, c) in enumerate(((u0, c0), (u1, c1), (u2, c2), (u3, c3))):
            u_row[k * quarter : (k + 1) * quarter, :] = u[...]
            c_row[k * quarter : (k + 1) * quarter, :] = c[...]

    rows = gate.shape[0]
    g = mm_nt(gate[...], u_row[...])
    a = mm_nt(up[...], u_row[...])
    gh = mm_nt(down[...].reshape(rows, channels), c_row[...])
    sg = sigmoid(g)
    silu = g * sg
    hid = (silu * a).astype(BF16)
    gg = (gh * a * (sg * (1.0 + g * (1.0 - sg)))).astype(BF16)
    ga = (gh * silu).astype(BF16)
    half = rows // 2
    for m, grad in enumerate((mm(gg, u_row[...]), mm(ga, u_row[...]), mm(hid, c_row[...]))):
        d_all[0, m] = grad[:half].astype(BF16)
        d_all[1, m] = grad[half:].astype(BF16)
    cut = channels // 2
    keep_a[0] = d_all[y, :, :, :cut]
    give_a[0] = d_all[1 - y, :, :, :cut]

    @pl.when((i & 1) == z)
    def _():
        keep_b[0] = d_all[:, :, :, cut:]

    @pl.when((i & 1) != z)
    def _():
        give_b[0] = d_all[:, :, :, cut:]


def hidden_grads(at, u2_parts, ct_parts, gate, up, down, after):
    quarter, channels = u2_parts[0].shape
    wide = gate.shape[0]
    bs, fs, fw, _ = down.shape
    block = 2 * fw
    cut = channels // 2
    whole = pl.BlockSpec((quarter, channels), lambda i, at: (0, 0))
    rows = pl.BlockSpec((block, channels), lambda i, at: (i, 0))
    down_spec = pl.BlockSpec((2, 1, fw, channels), lambda i, at: (i, at[0], 0, 0))
    a_spec = pl.BlockSpec((1, 3, fw, cut), lambda i, at: (i, 0, 0, 0))
    b_spec = pl.BlockSpec((1, 2, 3, fw, cut), lambda i, at: (i // 2, 0, 0, 0, 0))
    return pl.pallas_call(
        hidden_grads_kernel,
        grid_spec=pltpu.PrefetchScalarGridSpec(
            num_scalar_prefetch=1,
            grid=(bs // 2,),
            in_specs=[whole] * 8 + [rows, rows, down_spec, HBM],
            out_specs=[a_spec, a_spec, b_spec, b_spec],
            scratch_shapes=[
                pltpu.VMEM((4 * quarter, channels), BF16),
                pltpu.VMEM((4 * quarter, channels), BF16),
                pltpu.VMEM((2, 3, fw, channels), BF16),
            ],
        ),
        out_shape=[shape((bs // 2, 3, fw, cut), BF16)] * 2
        + [shape((bs // 4, 2, 3, fw, cut), BF16)] * 2,
        compiler_params=params(),
        cost_estimate=cost(14),
        name="hidden_grads",
    )(at, *u2_parts, *ct_parts, gate, up, down, after)


def halve_kernel(at_ref, after, *refs, bits):
    pairs = len(bits)
    ins, outs = refs[: 2 * pairs], refs[2 * pairs :]
    for n in range(pairs):
        mine = at_ref[bits[n] + 1]
        keep, got = ins[2 * n], ins[2 * n + 1]
        next_keep, next_give = outs[2 * n], outs[2 * n + 1]
        for i in range(keep.shape[0]):
            for side, out in ((mine, next_keep), (1 - mine, next_give)):
                out[i] = (keep[i, side].astype(F32) + got[i, side].astype(F32)).astype(BF16)


def halve(at, bits, after, *sums):
    outs = []
    for n in range(len(bits)):
        dims = sums[2 * n].shape
        outs += [shape((dims[0],) + dims[2:], BF16)] * 2
    return pl.pallas_call(
        functools.partial(halve_kernel, bits=bits),
        in_specs=[SM, HBM] + [VM] * len(sums),
        out_specs=[VM] * len(outs),
        out_shape=outs,
        compiler_params=params(),
        cost_estimate=cost(2),
        name="halve",
    )(at, after, *sums)


def join_kernel(at_ref, after, keep_a, got_a, keep_b, got_b, keep, give):
    cut = keep_a.shape[-1]
    for side, out in ((at_ref[3], keep), (1 - at_ref[3], give)):
        for m in range(keep_a.shape[1]):
            for ours, theirs, lanes in ((keep_a, got_a, slice(0, cut)), (keep_b, got_b, slice(cut, 2 * cut))):
                total = ours[side, m].astype(F32) + theirs[side, m].astype(F32)
                out[m, :, lanes] = total.astype(BF16)


def join(at, after, keep_a, got_a, keep_b, got_b):
    _, count, rows, cut = keep_a.shape
    return pl.pallas_call(
        join_kernel,
        in_specs=[SM, HBM] + [VM] * 4,
        out_specs=[VM] * 2,
        out_shape=[shape((count, rows, 2 * cut), BF16)] * 2,
        compiler_params=params(),
        cost_estimate=cost(2),
        name="join",
    )(at, after, keep_a, got_a, keep_b, got_b)


def projection_kernel(
    at_ref, gp, u1, n1, w_mine, b0, b1, b2, b3, z0, z1, z2, z3, d_w2, d_w1, d_taps, gcb, condt, mu, mn,
    sums2, after, keep, give, packed_out, gb_row, z_row, d_in, d_out, packed, *, layout,
):
    me, y = at_ref[0], at_ref[1]
    quarter = b0.shape[1]
    channels = u1.shape[1]
    width = b0.shape[0]
    for k, (b, z) in enumerate(((b0, z0), (b1, z1), (b2, z2), (b3, z3))):
        gb_row[:, k * quarter : (k + 1) * quarter] = b[...]
        z_row[:, k * quarter : (k + 1) * quarter] = z[...]
    d_in[...] = mm(gp[...], u1[...])
    d_out[...] = mm_nt(gb_row[...], z_row[...])
    blocks = 2 * keep.shape[0]
    first = 2 * width // blocks
    second = width // blocks
    for b in range(blocks // 2):
        for side, out in ((y, keep), (1 - y, give)):
            lo = pl.multiple_of((2 * b + side) * first, first)
            out[b, :first, :] = d_in[pl.ds(lo, first), :].astype(BF16)
            lo = pl.multiple_of((2 * b + side) * second, second)
            out[b, first:, :] = d_out[pl.ds(lo, second), :].astype(BF16)
    packed[...] = jnp.zeros_like(packed)
    packed[:width, :] = jnp.concatenate([d_w2[:width, :], d_w2[width:, :]], axis=1)
    taps_t = jnp.transpose(d_taps[...])
    gcb_t = jnp.transpose(gcb[...])[:8, :]
    gmu = lax.dot_general(
        gcb_t, condt[...], (((1,), (0,)), ((), ())), precision=HIGH, preferred_element_type=F32
    )
    gp_n = mm(gp[...], n1[...])
    w32 = w_mine[...].astype(F32)
    gain = jnp.sum(gp_n * w32, axis=0, keepdims=True) + jnp.sum(gmu * mn[...], axis=0, keepdims=True)
    total = jnp.sum(gp[...].astype(F32), axis=1, keepdims=True)
    shift = jnp.sum(total * w32, axis=0, keepdims=True) + jnp.sum(gmu, axis=0, keepdims=True)
    for i in range(3):
        for m in range(2 * width // 128):
            at = layout["taps"] + i * (2 * width // 128) + m
            packed[at : at + 1, :] = taps_t[i : i + 1, m * 128 : (m + 1) * 128]
    for i, row in enumerate((gain, shift, sums2[0:1, :], sums2[1:2, :])):
        for m in range(channels // 128):
            at = layout["ln"] + i * (channels // 128) + m
            packed[at : at + 1, :] = row[:, m * 128 : (m + 1) * 128]
    half = d_w1.shape[0] // 2
    packed[layout["w1"] : layout["w1"] + half, :] = jnp.concatenate(
        [d_w1[:half, :], d_w1[half:, :]], axis=1
    )
    zeros = jnp.zeros_like(gcb_t)
    row = at_ref[4]
    odd = (row & 1) == 1
    both = jnp.concatenate([jnp.where(odd, zeros, gcb_t), jnp.where(odd, gcb_t, zeros)], axis=1)
    packed[pl.ds(pl.multiple_of(layout["cb"] + 8 * (row >> 1), 8), 8), :] = both
    share = jnp.zeros((8, width), F32)
    for f in range(channels // width):
        share = share + jnp.where(me == f, mu[:, f * width : (f + 1) * width], 0.0)
    rest = jnp.concatenate([share[:SEGS, 128:], jnp.zeros((SEGS, 256 - width), F32)], axis=1)
    block = jnp.concatenate([share[:SEGS, :128], rest, jnp.zeros((8 - 2 * SEGS, 128), F32)], axis=0)
    packed[pl.ds(pl.multiple_of(layout["mu"] + 8 * row, 8), 8), :] = block
    packed_out[...] = packed[...].astype(BF16)


def packed_layout(width, channels, bs):
    taps = width
    ln = taps + 3 * (2 * width // 128)
    w1 = -(-(ln + 4 * (channels // 128)) // 8) * 8
    cb = w1 + 32
    mu = cb + 4 * bs
    return {"taps": taps, "ln": ln, "w1": w1, "cb": cb, "mu": mu, "rows": -(-(mu + 8 * bs) // 16) * 16}


def projection_grads(
    at, gp, u1, n1, w_mine, gb_parts, z_parts, d_w2, d_w1, d_taps, gcb, condt, mu, mn, sums2, after, bs
):
    length, channels = u1.shape
    width = gb_parts[0].shape[0]
    layout = packed_layout(width, channels, bs)
    return pl.pallas_call(
        functools.partial(projection_kernel, layout=layout),
        in_specs=[SM] + [VM] * 20 + [HBM],
        out_specs=[VM] * 3,
        out_shape=[shape((bs // 2, 3 * width // bs, channels), BF16)] * 2
        + [shape((layout["rows"], 128), BF16)],
        scratch_shapes=[
            pltpu.VMEM((width, length), BF16),
            pltpu.VMEM((channels, length), BF16),
            pltpu.VMEM((2 * width, channels), F32),
            pltpu.VMEM((width, channels), F32),
            pltpu.VMEM((layout["rows"], 128), F32),
        ],
        compiler_params=params(),
        cost_estimate=cost(6),
        name="projection_grads",
    )(
        at, gp, u1, n1, w_mine, *gb_parts, *z_parts, d_w2, d_w1, d_taps, gcb, condt, mu, mn, sums2, after
    )


def final_kernel(
    me_ref, p0, p1, p2, p3, x, big_g, norms, ids_row, condt, w_in, after, out, gp_t, *, piece
):
    me = me_ref[0]
    rows = gp_t.shape[0] // 4
    hidden = condt.shape[0]
    share = jnp.zeros((8, hidden), F32)
    for k, part in enumerate((p0, p1, p2, p3)):
        for i in range(rows // piece):
            at = pl.ds(pl.multiple_of((i * 4 + (me ^ k)) * piece, piece), piece)
            gp_t[at, :] = part[i * piece : (i + 1) * piece, :]
        extra = part[rows:, :hidden].astype(F32)
        share = share + extra[:8] + extra[8:]
    ids = ids_row[...]
    number = lax.broadcasted_iota(jnp.int32, (8, ids.shape[1]), 0)
    counts = jnp.sum(jnp.where(ids == number, 1.0, 0.0), axis=1, keepdims=True)
    gmu = lax.dot_general(
        share, condt[...], (((1,), (0,)), ((), ())), precision=HIGH, preferred_element_type=F32
    ) / jnp.maximum(counts, 1.0)
    gu1 = mm_nt(jnp.transpose(gp_t[...]), w_in[...])
    quarter = x.shape[0]
    own = jnp.broadcast_to(ids_row[:, tile(me, quarter)].astype(F32), (8, quarter))
    ids_own = jnp.transpose(own)[:, 0:1]
    for j in range(SEGS):
        gu1 = gu1 + jnp.where(ids_own == j, gmu[j : j + 1, :], 0.0)
    unit, scale = normed(x[...].astype(F32))
    out[...] = big_g[...] + norm_back(unit, scale, gu1 * norms[0:1, :])


def final(me, gp_parts, x, big_g, norms, ids, condt, w_in, after, piece):
    quarter, channels = x.shape
    return pl.pallas_call(
        functools.partial(final_kernel, piece=piece),
        in_specs=[SM] + [VM] * 10 + [HBM],
        out_specs=VM,
        out_shape=shape((quarter, channels), F32),
        scratch_shapes=[pltpu.VMEM((2 * channels, quarter), BF16)],
        compiler_params=params(),
        cost_estimate=cost(5),
        name="final",
    )(me, *gp_parts, x, big_g, norms, ids, condt, w_in, after)


def small_kernel(
    me_ref, j0, j1, j2, j3, w2, taps, ln, w1, b1, cond, wide, tap_t, cond_t, *, layout, step, width
):
    me = me_ref[0]
    parts = [part[...].astype(F32) for part in (j0, j1, j2, j3)]
    hidden = w1.shape[0]
    half = width // step
    count = 2 * width // 128
    for k, part in enumerate(parts):
        who = me ^ k
        rows = jnp.concatenate(
            [
                jnp.concatenate([part[layout["taps"] + i * count + m : layout["taps"] + i * count + m + 1, :]
                                 for m in range(count)], axis=1)
                for i in range(3)
            ]
            + [jnp.zeros((125, 2 * width), F32)],
            axis=0,
        )
        tap_t[...] = jnp.transpose(rows)
        for side in range(2):
            for i in range(half):
                at = pl.ds(pl.multiple_of((side * half * 4 + i * 4 + who) * step, step), step)
                lo = i * step
                wide[at, :hidden] = part[lo : lo + step, side * hidden : (side + 1) * hidden]
                at2 = side * width + lo
                wide[at, hidden:] = tap_t[at2 : at2 + step, :hidden]
    whole = jnp.transpose(wide[...])
    w2[...] = whole[:hidden, :]
    taps[...] = whole[hidden : hidden + 3, :]

    def common(first, last):
        a, b, c, d = [part[first:last, :] for part in parts]
        return (a + b) + (c + d)

    lanes = ln.shape[1] // 128
    sums = common(layout["ln"], layout["ln"] + 4 * lanes)
    for i in range(4):
        for m in range(lanes):
            ln[i : i + 1, m * 128 : (m + 1) * 128] = sums[i * lanes + m : i * lanes + m + 1, :]
    both = common(layout["w1"], layout["w1"] + hidden // 2)
    w1[: hidden // 2, :] = both[:, :hidden]
    w1[hidden // 2 :, :] = both[:, hidden:]
    cb = common(layout["cb"], layout["mu"])
    shares = []
    for b in range(cb.shape[0] // 4):
        lo = 8 * (b // 2)
        shares.append(cb[lo : lo + 8, (b % 2) * hidden : (b % 2 + 1) * hidden])
    shares = jnp.concatenate(shares, axis=0)
    b1[...] = jnp.sum(shares, axis=0, keepdims=True)
    for k, part in enumerate(parts):
        rows = []
        for b in range(cb.shape[0] // 4):
            lo = layout["mu"] + 8 * b
            block = part[lo : lo + 8, :]
            rows.append(
                jnp.concatenate(
                    [
                        jnp.concatenate([block[:SEGS, :], jnp.zeros((8 - SEGS, 128), F32)], axis=0),
                        jnp.concatenate(
                            [block[SEGS : 2 * SEGS, : width - 128], jnp.zeros((8 - SEGS, width - 128), F32)],
                            axis=0,
                        ),
                    ],
                    axis=1,
                )
            )
        mu = jnp.concatenate(rows, axis=0)
        cond_t[tile(me ^ k, width), :] = lax.dot_general(
            jnp.transpose(mu), shares, (((1,), (0,)), ((), ())), precision=HIGH, preferred_element_type=F32
        )
    cond[...] = jnp.transpose(cond_t[...])


def small_grads(me, parts, hidden, channels, step, bs):
    width = channels // 4
    layout = packed_layout(width, channels, bs)
    return pl.pallas_call(
        functools.partial(small_kernel, layout=layout, step=step, width=width),
        in_specs=[SM] + [VM] * 4,
        out_specs=[VM] * 6,
        out_shape=[
            shape((hidden, 2 * channels), F32),
            shape((3, 2 * channels), F32),
            shape((4, channels), F32),
            shape((hidden, hidden), F32),
            shape((1, hidden), F32),
            shape((hidden, channels), F32),
        ],
        scratch_shapes=[
            pltpu.VMEM((2 * channels, 2 * hidden), F32),
            pltpu.VMEM((2 * width, 128), F32),
            pltpu.VMEM((channels, hidden), F32),
        ],
        compiler_params=params(),
        cost_estimate=cost(3),
        name="small_grads",
    )(me, *parts)


def trade_parts(parts):
    two, three, one = [swap(parts[k], "freq", k) for k in (2, 3, 1)]
    return (parts[0], one, two, three)


def tiled_device(
    tokens,
    seg_ids,
    cotangent,
    ln1_gain,
    ln1_shift,
    w_in,
    conv_taps,
    freq_w1,
    freq_b1,
    freq_w2,
    cond_w,
    w_out,
    ln2_gain,
    ln2_shift,
    w_gate,
    w_up,
    w_down,
):
    quarter, _, channels = tokens.shape
    length = seg_ids.shape[1]
    ff = w_gate.shape[1]
    fs = lax.axis_size("freq")
    bs = lax.axis_size("batch")
    me = lax.axis_index("freq")
    row = lax.axis_index("batch")
    width = channels // fs
    half = bs // 2
    step = channels // (half * fs)
    fw = ff // (bs * fs)
    cos_table, sin_table = tables(length)
    feats = features(length, freq_w1.shape[0] // 2)
    feats_aug = np.concatenate(
        [feats, np.ones((1, length), np.float32), np.zeros((7, length), np.float32)], axis=0
    )

    x_own = tokens[:, 0]
    ct_own = cotangent[:, 0]
    ids = seg_ids
    at = jnp.stack([me, row & 1, (row >> 1) & 1, (row >> 2) & 1, row]).astype(jnp.int32)
    norms = jnp.stack([ln1_gain, ln1_shift, ln2_gain, ln2_shift])
    condt = cond_w.T
    cos_c, sin_c = jnp.asarray(cos_table), jnp.asarray(sin_table)

    def gather_after(value, after):
        two = swap(value, "freq", 2)
        one = swap(value, "freq", 1)
        two = tie(two, after)
        return (value, one, two, swap(two, "freq", 1))

    def pairs(value):
        return value.reshape((value.shape[0] // 2, 2) + value.shape[1:])

    w_mine, w2x, w2t, taps, base = prepare(
        at, w_in, freq_w2, conv_taps, freq_w1, freq_b1, jnp.asarray(feats_aug), step, fs
    )
    x_parts = gather_after(x_own, base)
    forward = forward_spectral(at, x_parts, ids, norms, w_mine, taps, base, w2x, condt, cos_c, sin_c)
    z_parts, (z_row, u1, n1, p, q, c, vr, vs, mu, mn, cb) = forward[:4], forward[4:]
    ct_parts = gather_after(ct_own, cb)
    z_got = trade_parts(z_parts)
    wg_mine, wu_mine = select_columns(at, cb, w_gate, w_up, fw, fs)
    h, u2, z_t = middle(at, z_got, x_own, w_out, norms, wg_mine, step)
    fed = feed_forward(
        at, u2, h, ct_own, norms, w_out, w_gate, w_up, w_down, step, channels // (bs * fs)
    )
    mixed_out, big_g, gz_parts, gb_parts, sums2 = fed[0], fed[1], fed[2:6], fed[6:10], fed[10]
    u2_parts = gather_after(u2, sums2)
    gz_got = trade_parts(gz_parts)

    keep_a, give_a, keep_b, give_b = hidden_grads(
        at, u2_parts, ct_parts, wg_mine, wu_mine, w_down.reshape(bs, fs, fw, channels), sums2
    )
    got_a = swap(give_a, "batch", 1)
    got_b = swap(give_b, "batch", 2)
    gb_got = trade_parts(gb_parts)

    back = backward_spectral(
        at, gz_got, ids, cb, taps, base, w2x, w2t, jnp.asarray(feats).astype(BF16),
        p, q, c, vr, vs, cos_c, sin_c, give_a,
    )
    gp_parts, (gp, d_taps, d_w2, d_w1, gcb) = back[:4], back[4:]
    gp_got = trade_parts(gp_parts)
    z_all = gather_after(z_t, gcb)

    keep_a, give_a, keep_b, give_b = halve(
        at, (1, 0), gp, pairs(keep_a), pairs(got_a), keep_b, got_b
    )
    got_a = swap(give_a, "batch", 2)
    got_b = swap(give_b, "batch", 1)

    keep, give, packed = projection_grads(
        at, gp, u1, n1, w_mine, gb_got, z_all, d_w2, d_w1, d_taps, gcb, condt, mu, mn, sums2, give_a, bs
    )
    got = swap(give, "batch", 1)
    keep_ff, give_ff = join(at, packed, keep_a, got_a, keep_b, got_b)
    got_ff = swap(give_ff, "batch", 4)
    grad_tokens = final(at, gp_got, x_own, big_g, norms, ids, condt, w_in, give_ff, step)

    keep, give = halve(at, (1,), grad_tokens, pairs(keep), pairs(got))
    got = swap(give, "batch", 2)
    keep, give = halve(at, (2,), grad_tokens, pairs(keep), pairs(got))
    got = swap(give, "batch", 4)
    mine = keep[0].astype(F32) + got[0].astype(F32)
    first = 2 * width // bs

    sent = packed
    for bit in range(bs.bit_length() - 1):
        got_small = swap(sent, "batch", 1 << bit).astype(F32)
        if bit == 0:
            sent = tie(sent, grad_tokens)
        sent = (sent.astype(F32) + got_small).astype(BF16)
    d_w2, d_taps, ln, d_w1, d_b1, d_cond = small_grads(
        at, gather_freq(sent, me), freq_w1.shape[1], channels, step, bs
    )
    d_ff = keep_ff.astype(F32) + got_ff.astype(F32)
    return (
        mixed_out[:, None],
        grad_tokens[:, None],
        ln[0],
        ln[1],
        mine[:first].T,
        d_taps,
        d_w1,
        d_b1[0],
        d_w2,
        d_cond.T,
        mine[first:].T,
        ln[2],
        ln[3],
        d_ff[0].T,
        d_ff[1].T,
        d_ff[2],
    )


def per_device(*args):
    channels = args[0].shape[2]
    step = 2 * channels // (lax.axis_size("batch") * lax.axis_size("freq"))
    fits = lax.axis_size("batch") == 8 and lax.axis_size("freq") == 4 and step % 16 == 0
    return tiled_device(*args) if fits else plain_device(*args)


def solution(mesh):
    rows = P("freq", "batch", None)
    split = P(None, ("batch", "freq"))
    in_specs = (rows, P("batch", None), rows) + (P(),) * 14
    out_specs = (
        rows,
        rows,
        P(),
        P(),
        split,
        P(),
        P(),
        P(),
        P(),
        P(),
        split,
        P(),
        P(),
        split,
        split,
        P(("batch", "freq"), None),
    )
    return jax.shard_map(
        per_device, mesh=mesh, in_specs=in_specs, out_specs=out_specs, check_vma=False
    )
```

```python
import functools

import jax
import jax.numpy as jnp
import ml_dtypes
import numpy as np
from jax import lax
from jax.experimental import pallas as pl
from jax.experimental.pallas import tpu as pltpu
from jax.sharding import PartitionSpec as P

SEGS = 3
EPS = 1e-05
HIGH = lax.Precision.HIGHEST
F32 = jnp.float32
BF16 = jnp.bfloat16


def mm(a, b):
    return jnp.dot(a, b, preferred_element_type=F32)


def mm_nt(a, b):
    return lax.dot_general(a, b, (((1,), (1,)), ((), ())), preferred_element_type=F32)


def mm_tn(a, b):
    return lax.dot_general(a, b, (((0,), (0,)), ((), ())), preferred_element_type=F32)


def swap(value, axis, mask):
    count = lax.axis_size(axis)
    return lax.ppermute(value, axis, [(i, i ^ mask) for i in range(count)])


def pick(parts, index):
    return lax.dynamic_index_in_dim(parts, index, 0, keepdims=False)


def in_order(received, me):
    a, b, c, d = received
    low = (me & 1) == 1
    a, b = jnp.where(low, b, a), jnp.where(low, a, b)
    c, d = jnp.where(low, d, c), jnp.where(low, c, d)
    high = (me & 2) == 2
    a, c = jnp.where(high, c, a), jnp.where(high, a, c)
    b, d = jnp.where(high, d, b), jnp.where(high, b, d)
    return (a, b, c, d)


def trade(blocks, me):
    return [pick(blocks, me)] + [swap(pick(blocks, me ^ k), "freq", k) for k in (2, 3, 1)]


def trade_sorted(blocks, me):
    own, two, three, one = trade(blocks, me)
    return in_order((own, one, two, three), me)


def gather_freq(value, me):
    two = swap(value, "freq", 2)
    one = swap(value, "freq", 1)
    three = swap(two, "freq", 1)
    return (value, one, two, three)


def scatter_sum(value, order):
    bits = lax.axis_size("batch").bit_length() - 1
    me = lax.axis_index("batch")
    rest = value.shape[1:]
    value = value.reshape((2,) * bits + rest)
    left = list(range(bits - 1, -1, -1))
    for bit in order:
        dim = left.index(bit)
        mine = (me >> bit) & 1
        keep = lax.dynamic_index_in_dim(value, mine, dim, keepdims=False)
        give = lax.dynamic_index_in_dim(value, 1 - mine, dim, keepdims=False)
        got = swap(give, "batch", 1 << bit)
        total = keep.astype(F32) + got.astype(F32)
        left.remove(bit)
        value = total.astype(value.dtype) if left else total
    return value


def tables(length):
    index = np.arange(length, dtype=np.int64)
    angle = (index[:, None] * index[None, :] % (2 * length)) * (np.pi / length)
    return (
        np.cos(angle).astype(ml_dtypes.bfloat16),
        np.sin(angle).astype(ml_dtypes.bfloat16),
    )


def features(length, half):
    index = np.arange(length, dtype=np.int64)
    lags = (np.arange(half, dtype=np.int64) + 1) ** 2
    angle = (lags[:, None] * index[None, :] % (2 * length)) * (np.pi / length)
    return np.concatenate([np.cos(angle), np.sin(angle)], axis=0).astype(np.float32)


def normed(values):
    centered = values - jnp.mean(values, axis=-1, keepdims=True)
    scale = lax.rsqrt(jnp.mean(centered * centered, axis=-1, keepdims=True) + EPS)
    return centered * scale, scale


def norm_back(unit, scale, grad):
    return scale * (
        grad
        - jnp.mean(grad, axis=-1, keepdims=True)
        - unit * jnp.mean(grad * unit, axis=-1, keepdims=True)
    )


def shift_right(values):
    return jnp.pad(values, ((0, 0), (1, 0)))[:, :-1]


def shift_left(values):
    return jnp.pad(values, ((0, 0), (0, 1)))[:, 1:]


def plain_device(
    tokens,
    seg_ids,
    cotangent,
    ln1_gain,
    ln1_shift,
    w_in,
    conv_taps,
    freq_w1,
    freq_b1,
    freq_w2,
    cond_w,
    w_out,
    ln2_gain,
    ln2_shift,
    w_gate,
    w_up,
    w_down,
):
    quarter, _, channels = tokens.shape
    length = seg_ids.shape[1]
    ff = w_gate.shape[1]
    fs = lax.axis_size("freq")
    bs = lax.axis_size("batch")
    me = lax.axis_index("freq")
    width = channels // fs
    half = bs // 2
    step = channels // (half * fs)
    cos_table, sin_table = tables(length)
    feats = features(length, freq_w1.shape[0] // 2)

    x_own = tokens[:, 0]
    ct_own = cotangent[:, 0]
    ids = seg_ids
    x_parts = gather_freq(x_own, me)
    ct_parts = gather_freq(ct_own, me)

    w_in_t = (
        w_in.T.reshape(2, half, fs, step, channels)
        .transpose(2, 0, 1, 3, 4)
        .reshape(fs, 2 * width, channels)
    )
    w_in_mine = pick(w_in_t, me)
    w_out_p = (
        w_out.reshape(half, fs, step, channels).transpose(1, 0, 2, 3).reshape(channels, channels)
    )
    taps_mine = pick(
        conv_taps.reshape(3, 2, half, fs, step).transpose(3, 0, 1, 2, 4).reshape(fs, 3, 2 * width), me
    )[:, :, None]
    w2_mine = pick(
        freq_w2.reshape(-1, 2, half, fs, step).transpose(3, 0, 1, 2, 4).reshape(fs, -1, 2 * width), me
    )
    fw = ff // (bs * fs)
    wide = ff // fs

    def mine_rows(weight):
        return pick(
            weight.reshape(bs, fs, fw, channels).transpose(1, 0, 2, 3).reshape(fs, wide, channels), me
        )

    wg_mine, wu_mine, wd_mine = (mine_rows(w_gate.T), mine_rows(w_up.T), mine_rows(w_down))

    base = jnp.dot(freq_w1.T, feats, precision=HIGH) + freq_b1[:, None]

    x_row = jnp.concatenate(in_order(x_parts, me), axis=0).astype(F32)
    unit1, _ = normed(x_row)
    u1 = (unit1 * ln1_gain + ln1_shift).astype(BF16)
    n1 = unit1.astype(BF16)
    masks = (ids == jnp.arange(SEGS, dtype=jnp.int32)[:, None]).astype(F32)
    counts = jnp.sum(masks, axis=1, keepdims=True)
    mu = mm(masks.astype(BF16), u1) / counts
    mn = mm(masks.astype(BF16), n1) / counts
    cb = jnp.dot(mu, cond_w, precision=HIGH)
    p = mm_nt(w_in_mine, u1)
    same = (ids[:, 1:] == ids[:, :-1]).astype(F32)
    zero = jnp.zeros((1, 1), F32)
    prev = jnp.concatenate([zero, same], axis=1)
    nxt = jnp.concatenate([same, zero], axis=1)
    p_prev = shift_right(p) * prev
    p_next = shift_left(p) * nxt
    s = taps_mine[0] * p_prev + taps_mine[1] * p + taps_mine[2] * p_next
    q, v = s[:width], s[width:]

    pre = base[None] + cb[:, :, None]
    gate_pre = jax.nn.sigmoid(pre)
    hk = pre * gate_pre
    kk = jnp.einsum("kc,jkf->jcf", w2_mine, hk, precision=HIGH)
    kr, ki = kk[:, :width], kk[:, width:]
    vm = (v[None] * masks[:, None, :]).astype(BF16).reshape(SEGS * width, length)
    vr = mm(vm, cos_table).reshape(SEGS, width, length)
    vi = -mm(vm, sin_table).reshape(SEGS, width, length)
    weights = np.full((length,), 2.0 / (2 * length), np.float32)
    weights[0] = 1.0 / (2 * length)
    yr = ((kr * vr - ki * vi) * weights).astype(BF16).reshape(SEGS * width, length)
    yi = ((kr * vi + ki * vr) * weights).astype(BF16).reshape(SEGS * width, length)
    conv = (mm(yr, cos_table) - mm(yi, sin_table)).reshape(SEGS, width, length)
    c = jnp.sum(conv * masks[:, None, :], axis=0)
    z_mine = (q * c).astype(BF16)

    z_blocks = z_mine.reshape(width, fs, quarter).transpose(1, 0, 2)
    z_t = jnp.concatenate(trade_sorted(z_blocks, me), axis=0)

    x32 = x_own.astype(F32)
    ct32 = ct_own.astype(F32)
    h = x32 + mm_tn(z_t, w_out_p)
    unit2, scale2 = normed(h)
    u2 = (unit2 * ln2_gain + ln2_shift).astype(BF16)
    u2_parts = gather_freq(u2, me)
    g = mm(u2, w_gate)
    a = mm(u2, w_up)
    gh = mm_nt(ct_own, w_down)
    sg = jax.nn.sigmoid(g)
    silu = g * sg
    hid = (silu * a).astype(BF16)
    mixed_out = (h + mm(hid, w_down)).astype(BF16)
    gg = (gh * a * sg * (1.0 + g * (1.0 - sg))).astype(BF16)
    ga = (gh * silu).astype(BF16)
    gu2 = mm_nt(gg, w_gate) + mm_nt(ga, w_up)
    grad_ln2_gain = jnp.sum(gu2 * unit2, axis=0)
    grad_ln2_shift = jnp.sum(gu2, axis=0)
    big_g = ct32 + norm_back(unit2, scale2, gu2 * ln2_gain)
    gb = big_g.astype(BF16)
    gz_blocks = mm_nt(w_out_p, gb).astype(BF16).reshape(fs, width, quarter)
    gz = jnp.concatenate(trade_sorted(gz_blocks, me), axis=1).astype(F32)
    gb_parts = gather_freq(gb, me)

    u2_row = jnp.concatenate(u2_parts, axis=0)
    ct_row = jnp.concatenate(ct_parts, axis=0)
    g_t = mm_nt(wg_mine, u2_row)
    a_t = mm_nt(wu_mine, u2_row)
    gh_t = mm_nt(wd_mine, ct_row)
    sg_t = jax.nn.sigmoid(g_t)
    silu_t = g_t * sg_t
    hid_t = (silu_t * a_t).astype(BF16)
    gg_t = (gh_t * a_t * sg_t * (1.0 + g_t * (1.0 - sg_t))).astype(BF16)
    ga_t = (gh_t * silu_t).astype(BF16)
    d_gate = mm(gg_t, u2_row).astype(BF16)
    d_up = mm(ga_t, u2_row).astype(BF16)
    d_down = mm(hid_t, ct_row).astype(BF16)
    d_ff = jnp.stack([d_gate, d_up, d_down], axis=0).reshape(3, bs, fw, channels).transpose(1, 0, 2, 3)
    bits = bs.bit_length() - 1
    order_a = list(range(bits))
    order_b = [1, 0] + list(range(2, bits))
    cut = channels // 2
    ff_a = scatter_sum(d_ff[..., :cut], order_a)
    ff_b = scatter_sum(d_ff[..., cut:], order_b)
    d_ff = jnp.concatenate([ff_a, ff_b], axis=-1)

    gq = gz * c
    gc = gz * q
    gcm = (gc[None] * masks[:, None, :]).astype(BF16).reshape(SEGS * width, length)
    gyr = mm(gcm, cos_table).reshape(SEGS, width, length) * weights
    gyi = -mm(gcm, sin_table).reshape(SEGS, width, length) * weights
    gkr = gyr * vr + gyi * vi
    gki = gyi * vr - gyr * vi
    gvr = (kr * gyr + ki * gyi).astype(BF16).reshape(SEGS * width, length)
    gvi = (kr * gyi - ki * gyr).astype(BF16).reshape(SEGS * width, length)
    gv_all = (mm(gvr, cos_table) - mm(gvi, sin_table)).reshape(SEGS, width, length)
    gv = jnp.sum(gv_all * masks[:, None, :], axis=0)
    gs = jnp.concatenate([gq, gv], axis=0)
    d_taps = jnp.stack(
        [jnp.sum(gs * p_prev, axis=1), jnp.sum(gs * p, axis=1), jnp.sum(gs * p_next, axis=1)]
    )
    gp = (
        taps_mine[1] * gs
        + taps_mine[0] * shift_left(gs * prev)
        + taps_mine[2] * shift_right(gs * nxt)
    ).astype(BF16)

    gkk = jnp.concatenate([gkr, gki], axis=1)
    gkk_low = gkk.astype(BF16)
    hk_low = hk.astype(BF16)
    d_w2 = jnp.einsum("jkf,jcf->kc", hk_low, gkk_low, preferred_element_type=F32)
    gpre = jnp.einsum("kc,jcf->jkf", w2_mine.astype(BF16), gkk_low, preferred_element_type=F32)
    gpre = gpre * gate_pre * (1.0 + pre * (1.0 - gate_pre))
    d_w1 = jnp.einsum("ef,jkf->ek", feats, gpre, precision=HIGH)
    gcb = jnp.sum(gpre, axis=2)
    gcb_row = lax.psum(gcb, "freq")

    gp_blocks = gp.reshape(2 * width, fs, quarter).transpose(1, 0, 2)
    gp_t = jnp.concatenate(trade_sorted(gp_blocks, me), axis=0)

    u1_row = u1
    d_in = mm(gp, u1_row).astype(BF16).reshape(bs, 2 * width // bs, channels)
    d_in = scatter_sum(d_in, order_a)
    gb_row = jnp.concatenate(in_order(gb_parts, me), axis=0)
    d_out = mm(z_mine, gb_row)
    narrow = channels // bs
    d_out = scatter_sum(d_out.T.astype(BF16).reshape(bs, narrow, width), order_a)
    d_out = d_out.reshape(fs, narrow // fs, width)
    d_out = jnp.stack(trade_sorted(d_out, me), axis=0)
    d_out = (
        d_out.reshape(fs, narrow // fs, half, step).transpose(2, 0, 3, 1).reshape(channels, -1)
    )

    gmu_part = jnp.dot(gcb, cond_w.T, precision=HIGH)
    sum_gp = jnp.sum(gp.astype(F32), axis=1)
    w_mine32 = w_in_mine.astype(F32)
    d_shift1 = jnp.dot(sum_gp[None], w_mine32, precision=HIGH)[0] + jnp.sum(gmu_part, axis=0)
    d_gain1 = jnp.sum(mm(gp, n1) * w_mine32, axis=0) + jnp.sum(gmu_part * mn, axis=0)

    gmu = jnp.dot(gcb_row, cond_w.T, precision=HIGH) / counts
    own_masks = lax.dynamic_slice_in_dim(masks, me * quarter, quarter, 1)
    gu1 = mm_tn(gp_t, w_in_t.reshape(2 * channels, channels)) + lax.dot_general(
        own_masks, gmu, (((0,), (0,)), ((), ())), precision=HIGH
    )
    unit_own, scale_own = normed(x32)
    grad_tokens = big_g + norm_back(unit_own, scale_own, gu1 * ln1_gain)

    shared = [
        d_gain1,
        d_shift1,
        d_w1.reshape(-1),
        jnp.sum(gcb, axis=0),
        jnp.dot(mu.T, gcb, precision=HIGH).reshape(-1),
        grad_ln2_gain,
        grad_ln2_shift,
    ]
    owned = jnp.concatenate([d_taps, d_w2], axis=0)
    packed = jnp.concatenate(shared + [owned.reshape(-1)])
    for bit in range(bits):
        packed = packed + swap(packed, "batch", 1 << bit)
    split = packed.shape[0] - owned.size
    common, owned = packed[:split], packed[split:]
    common = common + swap(common, "freq", 1)
    common = common + swap(common, "freq", 2)
    owned = jnp.stack(in_order(gather_freq(owned, me), me), axis=0)
    owned = (
        owned.reshape(fs, -1, 2, half, step).transpose(1, 2, 3, 0, 4).reshape(-1, 2 * channels)
    )
    sizes = np.cumsum([part.size for part in shared])
    got = jnp.split(common, sizes[:-1])
    return (
        mixed_out[:, None],
        grad_tokens[:, None],
        got[0],
        got[1],
        d_in.T,
        owned[:3],
        got[2].reshape(freq_w1.shape),
        got[3],
        owned[3:],
        got[4].reshape(cond_w.shape),
        d_out,
        got[5],
        got[6],
        d_ff[0].T,
        d_ff[1].T,
        d_ff[2],
    )


VM = pl.BlockSpec(memory_space=pltpu.VMEM)
SM = pl.BlockSpec(memory_space=pltpu.SMEM)
HBM = pl.BlockSpec(memory_space=pl.ANY)
MIB = 1 << 20


def params(mib):
    return pltpu.CompilerParams(vmem_limit_bytes=mib * MIB)


def cost(micros):
    return pl.CostEstimate(
        flops=int(micros * 1000000000.0), bytes_accessed=int(micros * 3500000.0), transcendentals=0
    )


def shape(dims, dtype):
    return pltpu.VMEM(dims, dtype)


def far(dims, dtype):
    return pltpu.HBM(dims, dtype)


def in_hbm(*values):
    kept = tuple(pltpu.with_memory_space_constraint(value, pltpu.HBM) for value in values)
    return kept if len(kept) > 1 else kept[0]


def in_vmem(value):
    return pltpu.with_memory_space_constraint(value, pltpu.VMEM)


def sigmoid(value):
    return 1.0 / (1.0 + jnp.exp(-value))


def dma_all(pairs, sems, first=0):
    copies = [
        pltpu.make_async_copy(source, target, sems.at[first + i])
        for i, (source, target) in enumerate(pairs)
    ]
    for copy in copies:
        copy.start()
    return copies


def tie_kernel(value, after, out):
    pass


def tie(value, after):
    return pl.pallas_call(
        tie_kernel,
        in_specs=[HBM, HBM],
        out_specs=HBM,
        out_shape=jax.ShapeDtypeStruct(value.shape, value.dtype),
        input_output_aliases={0: 0},
        compiler_params=params(1),
        name="tie",
    )(value, after)


def one_hot_rows(me, rows, lanes, piece, fs):
    row = lax.broadcasted_iota(jnp.int32, (rows, lanes), 0)
    lane = lax.broadcasted_iota(jnp.int32, (rows, lanes), 1)
    block = jnp.zeros_like(row)
    for m in range(1, rows // piece):
        block = block + jnp.where(row >= m * piece, 1, 0)
    return jnp.where(lane == block * ((fs - 1) * piece) + me * piece + row, 1.0, 0.0)


def prepare_kernel(
    me_ref, w_in, freq_w2, conv_taps, freq_w1, freq_b1, feats, cos_far, sin_far, norms,
    w_mine, w2x, w2t, taps, base, cos, sin, w1_aug, sems, *, step, fs,
):
    loads = dma_all([(cos_far, cos), (sin_far, sin)], sems)
    lanes = w_in.shape[1] // 4
    rows = lanes // fs
    sel = one_hot_rows(me_ref[0], rows, lanes, step, fs)
    low = sel.astype(BF16)
    hidden = freq_w2.shape[0]
    for i in range(4):
        out = slice(i * rows, (i + 1) * rows)
        group = slice(i * lanes, (i + 1) * lanes)
        w_mine[out, :] = mm_nt(low, w_in[:, group]).astype(BF16)
        both = jnp.concatenate([freq_w2[:, group], conv_taps[:, group]], axis=0)
        mine = lax.dot_general(
            sel, both, (((1,), (1,)), ((), ())), precision=HIGH, preferred_element_type=F32
        )
        taps[out, :3] = mine[:, hidden:]
        mine = mine[:, :hidden]
        high = mine.astype(BF16)
        rest = (mine - high.astype(F32)).astype(BF16)
        w2x[out, :] = jnp.concatenate([high, high, rest], axis=1)
    w2t[...] = jnp.transpose(w2x[...][:, :hidden].astype(F32)).astype(BF16)
    w1_aug[...] = jnp.zeros_like(w1_aug)
    count = freq_w1.shape[0]
    w1_aug[:count, :] = freq_w1[...]
    w1_aug[count : count + 1, :] = freq_b1[...]
    base[...] = lax.dot_general(
        w1_aug[...], feats[...], (((0,), (0,)), ((), ())), precision=HIGH, preferred_element_type=F32
    )
    for load in loads:
        load.wait()


def prepare(me, w_in, freq_w2, conv_taps, freq_w1, freq_b1, feats, cos, sin, norms, step, fs):
    channels, both = w_in.shape
    hidden = freq_w2.shape[0]
    length = feats.shape[1]
    return pl.pallas_call(
        functools.partial(prepare_kernel, step=step, fs=fs),
        in_specs=[SM] + [VM] * 6 + [HBM] * 3,
        out_specs=[VM] * 7,
        out_shape=[
            shape((both // fs, channels), BF16),
            shape((both // fs, 3 * hidden), BF16),
            shape((hidden, both // fs), BF16),
            shape((both // fs, 8), F32),
            shape((hidden, length), F32),
            shape((length, length), BF16),
            shape((length, length), BF16),
        ],
        scratch_shapes=[
            pltpu.VMEM((feats.shape[0], hidden), F32),
            pltpu.SemaphoreType.DMA((2,)),
        ],
        compiler_params=params(24),
        cost_estimate=cost(3),
        name="prepare",
    )(me, in_hbm(w_in), freq_w2, conv_taps, freq_w1, freq_b1[None], in_hbm(feats), in_hbm(cos), in_hbm(sin), norms)


def select_kernel(me_ref, after, gate, up, gate_out, up_out, *, piece, fs):
    rows = gate_out.shape[0] // 2
    lanes = rows * fs
    sel = one_hot_rows(me_ref[0], rows, lanes, piece, fs).astype(BF16)
    for weight, out in ((gate, gate_out), (up, up_out)):
        for part in range(2):
            block = mm_nt(sel, weight[:, part * lanes : (part + 1) * lanes])
            out[part * rows : (part + 1) * rows, :] = block.astype(BF16)


def select_columns(me, after, w_gate, w_up, piece, fs):
    channels, ff = w_gate.shape
    big = ff // 4
    wide = pl.BlockSpec((channels, big), lambda i: (0, i))
    rows = pl.BlockSpec((big // fs, channels), lambda i: (i, 0))
    return pl.pallas_call(
        functools.partial(select_kernel, piece=piece, fs=fs),
        grid=(4,),
        in_specs=[SM, HBM, wide, wide],
        out_specs=[rows, rows],
        out_shape=[far((ff // fs, channels), BF16)] * 2,
        compiler_params=params(24),
        cost_estimate=cost(6),
        name="select_columns",
    )(me, after, in_hbm(w_gate), in_hbm(w_up))


def row_masks(ids):
    lane = lax.broadcasted_iota(jnp.int32, ids.shape, 1)
    length = ids.shape[1]
    prev = jnp.where((ids == pltpu.roll(ids, 1, 1)) & (lane > 0), 1.0, 0.0)
    nxt = jnp.where((ids == pltpu.roll(ids, length - 1, 1)) & (lane < length - 1), 1.0, 0.0)
    return prev, nxt


def bin_weights(start, width, length):
    lane = lax.broadcasted_iota(jnp.int32, (1, width), 1) + start
    return jnp.where(lane == 0, 0.5 / length, 1.0 / length)


def tile(index, size):
    return pl.ds(pl.multiple_of(index * size, size), size)


def hidden_tile(base, cb, j, lanes):
    pre = base[:, lanes] + cb[:, j : j + 1]
    return pre, sigmoid(pre)


def kernel_tile(w2x, hk):
    high = hk.astype(BF16)
    rest = (hk - high.astype(F32)).astype(BF16)
    return mm(w2x[...], jnp.concatenate([high, rest, high], axis=0))


def forward_kernel(
    me_ref, ids_at, x0, x1, x2, x3, ids_ref, norms, w, taps, base, w2x, condt, cos, sin,
    z0, z1, z2, z3, u1, n1, p_out, q_out, c_out, vr_out, vs_out, mu_out, mn_out, cb_out,
    p, q, vm, ycat, acc,
):
    quarter = x0.shape[0]
    width, length = q_out.shape
    tiles = length // quarter
    me = me_ref[0]
    for k, x in enumerate((x0, x1, x2, x3)):
        values = x[...].astype(F32)
        unit, _ = normed(values)
        rows = tile(me ^ k, quarter)
        n1[rows, :] = unit.astype(BF16)
        u1[rows, :] = (unit * norms[0:1, :] + norms[1:2, :]).astype(BF16)
    ids = ids_ref[...]
    number = lax.broadcasted_iota(jnp.int32, (8, length), 0)
    member = jnp.where(ids == number, 1.0, 0.0)
    counts = jnp.maximum(jnp.sum(member, axis=1, keepdims=True), 1.0)
    member_low = member.astype(BF16)
    mu = mm(member_low, u1[...]) / counts
    mu_out[...] = mu
    mn_out[...] = mm(member_low, n1[...]) / counts
    cb_out[...] = lax.dot_general(
        condt[...], mu, (((1,), (1,)), ((), ())), precision=HIGH, preferred_element_type=F32
    )
    prev, nxt = row_masks(ids)
    for t in range(tiles):
        at = slice(t * quarter, (t + 1) * quarter)
        p[:, at] = mm_nt(w[...], u1[at, :])
    chunk = width // 2
    for r in range(4):
        at = slice(r * chunk, (r + 1) * chunk)
        here = p[at, :]
        p_out[at, :] = here.astype(BF16)
        mixed = (
            taps[at, 0:1] * (pltpu.roll(here, 1, 1) * prev)
            + taps[at, 1:2] * here
            + taps[at, 2:3] * (pltpu.roll(here, length - 1, 1) * nxt)
        )
        if r < 2:
            q[at, :] = mixed
            q_out[at, :] = mixed.astype(BF16)
        else:
            for j in range(SEGS):
                lo = j * width + (r - 2) * chunk
                vm[lo : lo + chunk, :] = (mixed * member[j : j + 1, :]).astype(BF16)

    @pl.loop(0, tiles)
    def _(f):
        lanes = tile(f, quarter)
        upper = pl.ds(pl.multiple_of(f * quarter + length, quarter), quarter)
        weight = bin_weights(f * quarter, quarter, length)
        vr_all = mm(vm[...], cos[:, lanes])
        vs_all = mm(vm[...], sin[:, lanes])
        vr_out[:, lanes] = vr_all.astype(BF16)
        vs_out[:, lanes] = vs_all.astype(BF16)
        for j in range(SEGS):
            pre, gate = hidden_tile(base, cb_out, j, lanes)
            kk = kernel_tile(w2x, pre * gate)
            kr, ki = kk[:width] * weight, kk[width:] * weight
            at = slice(j * width, (j + 1) * width)
            vr, vs = vr_all[at], vs_all[at]
            ycat[at, lanes] = (kr * vr + ki * vs).astype(BF16)
            ycat[at, upper] = (kr * vs - ki * vr).astype(BF16)

    for k, z_out in enumerate((z0, z1, z2, z3)):
        t = me ^ k
        lanes = tile(t, quarter)
        acc[...] = jnp.zeros_like(acc)
        ids_here = ids_ref[:, lanes]
        for j in range(SEGS):

            @pl.when((ids_at[0, t * quarter] <= j) & (ids_at[0, (t + 1) * quarter - 1] >= j))
            def _():
                at = slice(j * width, (j + 1) * width)
                part = mm(ycat[at, :length], cos[:, lanes]) + mm(ycat[at, length:], sin[:, lanes])
                acc[...] += jnp.where(ids_here == j, part, 0.0)

        c = acc[...]
        c_out[:, lanes] = c.astype(BF16)
        z = (q[:, lanes] * c).astype(BF16)
        z_out[...] = z


def forward_spectral(me, x_parts, ids, norms, w, taps, base, w2x, condt, cos, sin):
    quarter, channels = x_parts[0].shape
    length = ids.shape[1]
    width = w.shape[0] // 2
    saved = [
        (length, channels),
        (length, channels),
        (2 * width, length),
        (width, length),
        (width, length),
        (SEGS * width, length),
        (SEGS * width, length),
    ]
    small = [
        shape((8, channels), F32),
        shape((8, channels), F32),
        shape((condt.shape[0], 8), F32),
    ]
    return pl.pallas_call(
        forward_kernel,
        in_specs=[SM, SM] + [VM] * 13,
        out_specs=[VM] * (7 + len(saved)),
        out_shape=[shape((width, quarter), BF16)] * 4 + [shape(dims, BF16) for dims in saved] + small,
        scratch_shapes=[
            pltpu.VMEM((2 * width, length), F32),
            pltpu.VMEM((width, length), F32),
            pltpu.VMEM((SEGS * width, length), BF16),
            pltpu.VMEM((SEGS * width, 2 * length), BF16),
            pltpu.VMEM((width, quarter), F32),
        ],
        compiler_params=params(26),
        cost_estimate=cost(15),
        name="forward_spectral",
    )(me, ids, *x_parts, ids, norms, w, taps, base, w2x, condt, cos, sin)


def backward_kernel(
    me_ref, ids_at, g0, g1, g2, g3, ids_ref, cb, taps, base, w2x, w2, feats,
    p, q, c, vr_in, vs_in, cos, sin, after,
    o0, o1, o2, o3, gp_row, d_taps, d_w2, d_w1, gcb,
    gcm, gvcat, gs, acc,
):
    width, quarter = g0.shape
    length = gp_row.shape[1]
    tiles = length // quarter
    hidden = base.shape[0]
    me = me_ref[0]
    for k, g in enumerate((g0, g1, g2, g3)):
        lanes = tile(me ^ k, quarter)
        gz = g[...].astype(F32)
        gs[:width, lanes] = gz * c[:, lanes].astype(F32)
        gc = gz * q[:, lanes].astype(F32)
        ids_here = ids_ref[:, lanes]
        for j in range(SEGS):
            gcm[j * width : (j + 1) * width, lanes] = jnp.where(ids_here == j, gc, 0.0).astype(BF16)
    d_w2[...] = jnp.zeros_like(d_w2)
    d_w1[...] = jnp.zeros_like(d_w1)
    gcb[...] = jnp.zeros_like(gcb)

    @pl.loop(0, tiles)
    def _(f):
        lanes = tile(f, quarter)
        upper = pl.ds(pl.multiple_of(f * quarter + length, quarter), quarter)
        weight = bin_weights(f * quarter, quarter, length)
        gyr_all = mm(gcm[...], cos[:, lanes]) * weight
        gys_all = mm(gcm[...], sin[:, lanes]) * weight
        for j in range(SEGS):
            pre, gate = hidden_tile(base, cb, j, lanes)
            hk = pre * gate
            kk = kernel_tile(w2x, hk)
            kr, ki = kk[:width], kk[width:]
            at = slice(j * width, (j + 1) * width)
            gyr, gys = gyr_all[at], gys_all[at]
            vr, vs = vr_in[at, lanes].astype(F32), vs_in[at, lanes].astype(F32)
            gvcat[at, lanes] = (kr * gyr - ki * gys).astype(BF16)
            gvcat[at, upper] = (kr * gys + ki * gyr).astype(BF16)
            gkk = jnp.concatenate(
                [(gyr * vr + gys * vs).astype(BF16), (gyr * vs - gys * vr).astype(BF16)], axis=0
            )
            d_w2[...] += mm_nt(gkk, hk.astype(BF16))
            gpre = mm(w2[...], gkk) * (gate * (1.0 + pre * (1.0 - gate)))
            gcb[:, j : j + 1] += jnp.sum(gpre, axis=1, keepdims=True)
            d_w1[...] += mm_nt(feats[:, lanes], gpre.astype(BF16))

    for k in range(4):
        t = me ^ k
        lanes = tile(t, quarter)
        acc[...] = jnp.zeros_like(acc)
        ids_here = ids_ref[:, lanes]
        for j in range(SEGS):

            @pl.when((ids_at[0, t * quarter] <= j) & (ids_at[0, (t + 1) * quarter - 1] >= j))
            def _():
                at = slice(j * width, (j + 1) * width)
                part = mm(gvcat[at, :length], cos[:, lanes]) + mm(gvcat[at, length:], sin[:, lanes])
                acc[...] += jnp.where(ids_here == j, part, 0.0)

        gs[width:, lanes] = acc[...]
    prev, nxt = row_masks(ids_ref[...])
    chunk = width // 2
    for r in range(4):
        at = slice(r * chunk, (r + 1) * chunk)
        here = p[at, :].astype(F32)
        grad = gs[at, :]
        d_taps[at, 0:1] = jnp.sum(grad * (pltpu.roll(here, 1, 1) * prev), axis=1, keepdims=True)
        d_taps[at, 1:2] = jnp.sum(grad * here, axis=1, keepdims=True)
        d_taps[at, 2:3] = jnp.sum(
            grad * (pltpu.roll(here, length - 1, 1) * nxt), axis=1, keepdims=True
        )
        gp_row[at, :] = (
            taps[at, 1:2] * grad
            + taps[at, 0:1] * pltpu.roll(grad * prev, length - 1, 1)
            + taps[at, 2:3] * pltpu.roll(grad * nxt, 1, 1)
        ).astype(BF16)
    share = jnp.transpose(gcb[...])[:8, :]
    high = share.astype(BF16)
    rest = (share - high.astype(F32)).astype(BF16)
    extra = jnp.concatenate([high, rest], axis=0)
    extra = jnp.concatenate([extra, jnp.zeros((16, quarter - hidden), BF16)], axis=1)
    for k, out in enumerate((o0, o1, o2, o3)):
        out[: 2 * width, :] = gp_row[:, tile(me ^ k, quarter)]
        out[2 * width :, :] = extra


def backward_spectral(
    me, gz_parts, ids, cb, taps, base, w2x, w2, feats, p, q, c, vr, vs, cos, sin, after
):
    width, quarter = gz_parts[0].shape
    length = ids.shape[1]
    hidden = base.shape[0]
    outs = [shape((2 * width + 16, quarter), BF16)] * 4 + [
        shape((2 * width, length), BF16),
        shape((2 * width, 128), F32),
        shape((2 * width, hidden), F32),
        shape((feats.shape[0], hidden), F32),
        shape((hidden, 128), F32),
    ]
    return pl.pallas_call(
        backward_kernel,
        in_specs=[SM, SM] + [VM] * 18 + [HBM],
        out_specs=[VM] * 9,
        out_shape=outs,
        scratch_shapes=[
            pltpu.VMEM((SEGS * width, length), BF16),
            pltpu.VMEM((SEGS * width, 2 * length), BF16),
            pltpu.VMEM((2 * width, length), F32),
            pltpu.VMEM((width, quarter), F32),
        ],
        compiler_params=params(26),
        cost_estimate=cost(17),
        name="backward_spectral",
    )(
        me, ids, *gz_parts, ids, cb, taps, base, w2x, w2, feats, p, q, c, vr, vs, cos, sin, after
    )


def middle_kernel(me_ref, z0, z1, z2, z3, x, w_out, norms, after, h_out, u2_out, z_t, *, piece):
    me = me_ref[0]
    width = z0.shape[0]
    for k, z in enumerate((z0, z1, z2, z3)):
        for i in range(width // piece):
            at = pl.ds(pl.multiple_of((i * 4 + (me ^ k)) * piece, piece), piece)
            z_t[at, :] = z[i * piece : (i + 1) * piece, :]
    h = x[...].astype(F32) + mm(jnp.transpose(z_t[...]), w_out[...])
    h_out[...] = h
    unit, _ = normed(h)
    u2_out[...] = (unit * norms[2:3, :] + norms[3:4, :]).astype(BF16)


def middle(me, z_parts, x, w_out, norms, after, piece):
    quarter, channels = x.shape
    return pl.pallas_call(
        functools.partial(middle_kernel, piece=piece),
        in_specs=[SM] + [VM] * 7 + [HBM],
        out_specs=[VM] * 3,
        out_shape=[
            shape((quarter, channels), F32),
            shape((quarter, channels), BF16),
            shape((channels, quarter), BF16),
        ],
        compiler_params=params(24),
        cost_estimate=cost(2),
        name="middle",
    )(me, *z_parts, x, in_hbm(w_out), norms, after)


def feed_kernel(
    me_ref, u2, h, ct, norms, w_out, gate, up, down,
    mixed, big_g, g0, g1, g2, g3, t0, t1, t2, t3, sums, acc_out, acc_grad, gz_t, gb_t, *, piece, thin,
):
    i = pl.program_id(0)

    @pl.when(i == 0)
    def _():
        acc_out[...] = jnp.zeros_like(acc_out)
        acc_grad[...] = jnp.zeros_like(acc_grad)

    g = mm(u2[...], gate[...])
    a = mm(u2[...], up[...])
    gh = mm_nt(ct[...], down[...])
    sg = sigmoid(g)
    silu = g * sg
    hid = (silu * a).astype(BF16)
    gg = (gh * a * (sg * (1.0 + g * (1.0 - sg)))).astype(BF16)
    ga = (gh * silu).astype(BF16)
    acc_out[...] += mm(hid, down[...])
    acc_grad[...] += mm_nt(gg, gate[...]) + mm_nt(ga, up[...])

    @pl.when(i == pl.num_programs(0) - 1)
    def _():
        me = me_ref[0]
        width = g0.shape[0]
        here = h[...]
        mixed[...] = (here + acc_out[...]).astype(BF16)
        gu2 = acc_grad[...]
        unit, scale = normed(here)
        sums[0:1, :] = jnp.sum(gu2 * unit, axis=0, keepdims=True)
        sums[1:2, :] = jnp.sum(gu2, axis=0, keepdims=True)
        total = ct[...].astype(F32) + norm_back(unit, scale, gu2 * norms[2:3, :])
        big_g[...] = total
        low = total.astype(BF16)
        gz_t[...] = mm_nt(w_out[...], low).astype(BF16)
        for k, out in enumerate((g0, g1, g2, g3)):
            for r in range(width // piece):
                at = pl.ds(pl.multiple_of((r * 4 + (me ^ k)) * piece, piece), piece)
                out[r * piece : (r + 1) * piece, :] = gz_t[at, :]
        gb_t[...] = jnp.transpose(total)
        for k, out in enumerate((t0, t1, t2, t3)):
            parts = []
            for r in range(width // thin):
                lo = pl.multiple_of((r * 4 + (me ^ k)) * thin, thin)
                parts.append(gb_t[pl.ds(lo, thin), :])
            out[...] = jnp.concatenate(parts, axis=0).astype(BF16)


def feed_forward(me, u2, h, ct, norms, w_out, w_gate, w_up, w_down, piece, thin):
    quarter, channels = u2.shape
    ff = w_gate.shape[1]
    block = 512

    width = channels // 4
    outs = [
        ((quarter, channels), BF16),
        ((quarter, channels), F32),
    ] + [((width, quarter), BF16)] * 8 + [((8, channels), F32)]
    return pl.pallas_call(
        functools.partial(feed_kernel, piece=piece, thin=thin),
        grid=(ff // block,),
        in_specs=[
            SM,
            VM,
            VM,
            VM,
            VM,
            VM,
            pl.BlockSpec((channels, block), lambda i: (0, i)),
            pl.BlockSpec((channels, block), lambda i: (0, i)),
            pl.BlockSpec((block, channels), lambda i: (i, 0)),
        ],
        out_specs=[VM] * len(outs),
        out_shape=[far(*outs[0])] + [shape(*out) for out in outs[1:]],
        scratch_shapes=[
            pltpu.VMEM((quarter, channels), F32),
            pltpu.VMEM((quarter, channels), F32),
            pltpu.VMEM((channels, quarter), BF16),
            pltpu.VMEM((channels, quarter), F32),
        ],
        compiler_params=params(28),
        cost_estimate=cost(13),
        name="feed_forward",
    )(me, u2, h, ct, norms, in_hbm(w_out), in_hbm(w_gate), in_hbm(w_up), in_hbm(w_down))


def hidden_grads_kernel(
    at_ref, u0, u1, u2, u3, c0, c1, c2, c3, gate, up, down, after,
    keep_a, give_a, keep_b, give_b, u_row, c_row, d_all,
):
    quarter, channels = u0.shape
    i = pl.program_id(0)
    y, z = at_ref[1], at_ref[2]

    @pl.when(i == 0)
    def _():
        for k, (u, c) in enumerate(((u0, c0), (u1, c1), (u2, c2), (u3, c3))):
            u_row[k * quarter : (k + 1) * quarter, :] = u[...]
            c_row[k * quarter : (k + 1) * quarter, :] = c[...]

    rows = gate.shape[0]
    g = mm_nt(gate[...], u_row[...])
    a = mm_nt(up[...], u_row[...])
    gh = mm_nt(down[...].reshape(rows, channels), c_row[...])
    sg = sigmoid(g)
    silu = g * sg
    hid = (silu * a).astype(BF16)
    gg = (gh * a * (sg * (1.0 + g * (1.0 - sg)))).astype(BF16)
    ga = (gh * silu).astype(BF16)
    half = rows // 2
    for m, grad in enumerate((mm(gg, u_row[...]), mm(ga, u_row[...]), mm(hid, c_row[...]))):
        d_all[0, m] = grad[:half].astype(BF16)
        d_all[1, m] = grad[half:].astype(BF16)
    cut = channels // 2
    keep_a[0] = d_all[y, :, :, :cut]
    give_a[0] = d_all[1 - y, :, :, :cut]

    @pl.when((i & 1) == z)
    def _():
        keep_b[0] = d_all[:, :, :, cut:]

    @pl.when((i & 1) != z)
    def _():
        give_b[0] = d_all[:, :, :, cut:]


def hidden_grads(at, u2_parts, ct_parts, gate, up, down, after):
    quarter, channels = u2_parts[0].shape
    wide = gate.shape[0]
    bs, fs, fw, _ = down.shape
    block = 2 * fw
    cut = channels // 2
    rows = pl.BlockSpec((block, channels), lambda i, at: (i, 0))
    down_spec = pl.BlockSpec((2, 1, fw, channels), lambda i, at: (i, at[0], 0, 0))
    a_spec = pl.BlockSpec((1, 3, fw, cut), lambda i, at: (i, 0, 0, 0))
    b_spec = pl.BlockSpec((1, 2, 3, fw, cut), lambda i, at: (i // 2, 0, 0, 0, 0))
    return pl.pallas_call(
        hidden_grads_kernel,
        grid_spec=pltpu.PrefetchScalarGridSpec(
            num_scalar_prefetch=1,
            grid=(bs // 2,),
            in_specs=[VM] * 8 + [rows, rows, down_spec, HBM],
            out_specs=[a_spec, a_spec, b_spec, b_spec],
            scratch_shapes=[
                pltpu.VMEM((4 * quarter, channels), BF16),
                pltpu.VMEM((4 * quarter, channels), BF16),
                pltpu.VMEM((2, 3, fw, channels), BF16),
            ],
        ),
        out_shape=[shape((bs // 2, 3, fw, cut), BF16)] * 2
        + [shape((bs // 4, 2, 3, fw, cut), BF16)] * 2,
        compiler_params=params(30),
        cost_estimate=cost(14),
        name="hidden_grads",
    )(at, *u2_parts, *ct_parts, in_hbm(gate), in_hbm(up), in_hbm(down), after)


def halve_kernel(at_ref, after, *refs, bits):
    pairs = len(bits)
    ins, outs = refs[: 2 * pairs], refs[2 * pairs :]
    for n in range(pairs):
        mine = at_ref[bits[n] + 1]
        keep, got = ins[2 * n], ins[2 * n + 1]
        next_keep, next_give = outs[2 * n], outs[2 * n + 1]
        for i in range(keep.shape[0]):
            for side, out in ((mine, next_keep), (1 - mine, next_give)):
                out[i] = (keep[i, side].astype(F32) + got[i, side].astype(F32)).astype(BF16)


def halve(at, bits, after, *sums):
    outs = []
    for n in range(len(bits)):
        dims = sums[2 * n].shape
        outs += [shape((dims[0],) + dims[2:], BF16)] * 2
    return pl.pallas_call(
        functools.partial(halve_kernel, bits=bits),
        in_specs=[SM, HBM] + [VM] * len(sums),
        out_specs=[VM] * len(outs),
        out_shape=outs,
        compiler_params=params(24),
        cost_estimate=cost(2),
        name="halve",
    )(at, after, *sums)


def join_kernel(at_ref, after, keep_a, got_a, keep_b, got_b, keep, give):
    cut = keep_a.shape[-1]
    for side, out in ((at_ref[3], keep), (1 - at_ref[3], give)):
        for m in range(keep_a.shape[1]):
            for ours, theirs, lanes in ((keep_a, got_a, slice(0, cut)), (keep_b, got_b, slice(cut, 2 * cut))):
                total = ours[side, m].astype(F32) + theirs[side, m].astype(F32)
                out[m, :, lanes] = total.astype(BF16)


def join(at, after, keep_a, got_a, keep_b, got_b):
    _, count, rows, cut = keep_a.shape
    return pl.pallas_call(
        join_kernel,
        in_specs=[SM, HBM] + [VM] * 4,
        out_specs=[VM] * 2,
        out_shape=[shape((count, rows, 2 * cut), BF16)] * 2,
        compiler_params=params(24),
        cost_estimate=cost(2),
        name="join",
    )(at, after, keep_a, got_a, keep_b, got_b)


def add_kernel(ours, theirs, after, out):
    out[...] = (ours[...].astype(F32) + theirs[...].astype(F32)).astype(out.dtype)


def add(ours, theirs, after, dtype):
    return pl.pallas_call(
        add_kernel,
        in_specs=[VM, VM, HBM],
        out_specs=VM,
        out_shape=shape(ours.shape, dtype),
        compiler_params=params(8),
        cost_estimate=cost(1),
        name="add",
    )(ours, theirs, after)


def projection_kernel(
    at_ref, gp, u1, n1, w_mine, b0, b1, b2, b3, z0, z1, z2, z3, d_w2, d_w1, d_taps, gcb, condt, mu, mn,
    sums2, after, keep, give, packed_out, gb_row, z_row, d_in, d_out, packed, *, layout,
):
    me, y = at_ref[0], at_ref[1]
    quarter = b0.shape[1]
    channels = u1.shape[1]
    width = b0.shape[0]
    for k, (b, z) in enumerate(((b0, z0), (b1, z1), (b2, z2), (b3, z3))):
        gb_row[:, k * quarter : (k + 1) * quarter] = b[...]
        z_row[:, k * quarter : (k + 1) * quarter] = z[...]
    d_in[...] = mm(gp[...], u1[...])
    d_out[...] = mm_nt(gb_row[...], z_row[...])
    blocks = 2 * keep.shape[0]
    first = 2 * width // blocks
    second = width // blocks
    for b in range(blocks // 2):
        for side, out in ((y, keep), (1 - y, give)):
            lo = pl.multiple_of((2 * b + side) * first, first)
            out[b, :first, :] = d_in[pl.ds(lo, first), :].astype(BF16)
            lo = pl.multiple_of((2 * b + side) * second, second)
            out[b, first:, :] = d_out[pl.ds(lo, second), :].astype(BF16)
    packed[...] = jnp.zeros_like(packed)
    packed[:width, :] = jnp.concatenate([d_w2[:width, :], d_w2[width:, :]], axis=1)
    taps_t = jnp.transpose(d_taps[...])
    gcb_t = jnp.transpose(gcb[...])[:8, :]
    gmu = lax.dot_general(
        gcb_t, condt[...], (((1,), (0,)), ((), ())), precision=HIGH, preferred_element_type=F32
    )
    gp_n = mm(gp[...], n1[...])
    w32 = w_mine[...].astype(F32)
    gain = jnp.sum(gp_n * w32, axis=0, keepdims=True) + jnp.sum(gmu * mn[...], axis=0, keepdims=True)
    total = jnp.sum(gp[...].astype(F32), axis=1, keepdims=True)
    shift = jnp.sum(total * w32, axis=0, keepdims=True) + jnp.sum(gmu, axis=0, keepdims=True)
    for i in range(3):
        for m in range(2 * width // 128):
            at = layout["taps"] + i * (2 * width // 128) + m
            packed[at : at + 1, :] = taps_t[i : i + 1, m * 128 : (m + 1) * 128]
    for i, row in enumerate((gain, shift, sums2[0:1, :], sums2[1:2, :])):
        for m in range(channels // 128):
            at = layout["ln"] + i * (channels // 128) + m
            packed[at : at + 1, :] = row[:, m * 128 : (m + 1) * 128]
    half = d_w1.shape[0] // 2
    packed[layout["w1"] : layout["w1"] + half, :] = jnp.concatenate(
        [d_w1[:half, :], d_w1[half:, :]], axis=1
    )
    zeros = jnp.zeros_like(gcb_t)
    row = at_ref[4]
    odd = (row & 1) == 1
    both = jnp.concatenate([jnp.where(odd, zeros, gcb_t), jnp.where(odd, gcb_t, zeros)], axis=1)
    packed[pl.ds(pl.multiple_of(layout["cb"] + 8 * (row >> 1), 8), 8), :] = both
    share = jnp.zeros((8, width), F32)
    for f in range(channels // width):
        share = share + jnp.where(me == f, mu[:, f * width : (f + 1) * width], 0.0)
    rest = jnp.concatenate([share[:SEGS, 128:], jnp.zeros((SEGS, 256 - width), F32)], axis=1)
    block = jnp.concatenate([share[:SEGS, :128], rest, jnp.zeros((8 - 2 * SEGS, 128), F32)], axis=0)
    packed[pl.ds(pl.multiple_of(layout["mu"] + 8 * row, 8), 8), :] = block
    packed_out[...] = packed[...].astype(BF16)


def packed_layout(width, channels, bs):
    taps = width
    ln = taps + 3 * (2 * width // 128)
    w1 = -(-(ln + 4 * (channels // 128)) // 8) * 8
    cb = w1 + 32
    mu = cb + 4 * bs
    return {"taps": taps, "ln": ln, "w1": w1, "cb": cb, "mu": mu, "rows": -(-(mu + 8 * bs) // 16) * 16}


def projection_grads(
    at, gp, u1, n1, w_mine, gb_parts, z_parts, d_w2, d_w1, d_taps, gcb, condt, mu, mn, sums2, after, bs
):
    length, channels = u1.shape
    width = gb_parts[0].shape[0]
    layout = packed_layout(width, channels, bs)
    return pl.pallas_call(
        functools.partial(projection_kernel, layout=layout),
        in_specs=[SM] + [VM] * 20 + [HBM],
        out_specs=[VM] * 3,
        out_shape=[shape((bs // 2, 3 * width // bs, channels), BF16)] * 2
        + [shape((layout["rows"], 128), BF16)],
        scratch_shapes=[
            pltpu.VMEM((width, length), BF16),
            pltpu.VMEM((channels, length), BF16),
            pltpu.VMEM((2 * width, channels), F32),
            pltpu.VMEM((width, channels), F32),
            pltpu.VMEM((layout["rows"], 128), F32),
        ],
        compiler_params=params(24),
        cost_estimate=cost(6),
        name="projection_grads",
    )(
        at, gp, u1, n1, w_mine, *gb_parts, *z_parts, d_w2, d_w1, d_taps, gcb, condt, mu, mn, sums2, after
    )


def final_kernel(
    me_ref, p0, p1, p2, p3, x, big_g, norms, ids_row, condt, w_in, after, out, gp_t, *, piece
):
    me = me_ref[0]
    rows = gp_t.shape[0] // 4
    hidden = condt.shape[0]
    share = jnp.zeros((8, hidden), F32)
    for k, part in enumerate((p0, p1, p2, p3)):
        for i in range(rows // piece):
            at = pl.ds(pl.multiple_of((i * 4 + (me ^ k)) * piece, piece), piece)
            gp_t[at, :] = part[i * piece : (i + 1) * piece, :]
        extra = part[rows:, :hidden].astype(F32)
        share = share + extra[:8] + extra[8:]
    ids = ids_row[...]
    number = lax.broadcasted_iota(jnp.int32, (8, ids.shape[1]), 0)
    counts = jnp.sum(jnp.where(ids == number, 1.0, 0.0), axis=1, keepdims=True)
    gmu = lax.dot_general(
        share, condt[...], (((1,), (0,)), ((), ())), precision=HIGH, preferred_element_type=F32
    ) / jnp.maximum(counts, 1.0)
    gu1 = mm_nt(jnp.transpose(gp_t[...]), w_in[...])
    quarter = x.shape[0]
    own = jnp.broadcast_to(ids_row[:, tile(me, quarter)].astype(F32), (8, quarter))
    ids_own = jnp.transpose(own)[:, 0:1]
    for j in range(SEGS):
        gu1 = gu1 + jnp.where(ids_own == j, gmu[j : j + 1, :], 0.0)
    unit, scale = normed(x[...].astype(F32))
    out[...] = big_g[...] + norm_back(unit, scale, gu1 * norms[0:1, :])


def final(me, gp_parts, x, big_g, norms, ids, condt, w_in, after, piece):
    quarter, channels = x.shape
    return pl.pallas_call(
        functools.partial(final_kernel, piece=piece),
        in_specs=[SM] + [VM] * 10 + [HBM],
        out_specs=VM,
        out_shape=far((quarter, channels), F32),
        scratch_shapes=[pltpu.VMEM((2 * channels, quarter), BF16)],
        compiler_params=params(24),
        cost_estimate=cost(5),
        name="final",
    )(me, *gp_parts, x, big_g, norms, ids, condt, in_hbm(w_in), after)


def small_kernel(
    me_ref, j0, j1, j2, j3, w2, taps, ln, w1, b1, cond, wide, tap_t, cond_t, *, layout, step, width
):
    me = me_ref[0]
    parts = [part[...].astype(F32) for part in (j0, j1, j2, j3)]
    hidden = w1.shape[0]
    half = width // step
    count = 2 * width // 128
    for k, part in enumerate(parts):
        who = me ^ k
        rows = jnp.concatenate(
            [
                jnp.concatenate([part[layout["taps"] + i * count + m : layout["taps"] + i * count + m + 1, :]
                                 for m in range(count)], axis=1)
                for i in range(3)
            ]
            + [jnp.zeros((125, 2 * width), F32)],
            axis=0,
        )
        tap_t[...] = jnp.transpose(rows)
        for side in range(2):
            for i in range(half):
                at = pl.ds(pl.multiple_of((side * half * 4 + i * 4 + who) * step, step), step)
                lo = i * step
                wide[at, :hidden] = part[lo : lo + step, side * hidden : (side + 1) * hidden]
                at2 = side * width + lo
                wide[at, hidden:] = tap_t[at2 : at2 + step, :hidden]
    whole = jnp.transpose(wide[...])
    w2[...] = whole[:hidden, :]
    taps[...] = whole[hidden : hidden + 3, :]

    def common(first, last):
        a, b, c, d = [part[first:last, :] for part in parts]
        return (a + b) + (c + d)

    lanes = ln.shape[1] // 128
    sums = common(layout["ln"], layout["ln"] + 4 * lanes)
    for i in range(4):
        for m in range(lanes):
            ln[i : i + 1, m * 128 : (m + 1) * 128] = sums[i * lanes + m : i * lanes + m + 1, :]
    both = common(layout["w1"], layout["w1"] + hidden // 2)
    w1[: hidden // 2, :] = both[:, :hidden]
    w1[hidden // 2 :, :] = both[:, hidden:]
    cb = common(layout["cb"], layout["mu"])
    shares = []
    for b in range(cb.shape[0] // 4):
        lo = 8 * (b // 2)
        shares.append(cb[lo : lo + 8, (b % 2) * hidden : (b % 2 + 1) * hidden])
    shares = jnp.concatenate(shares, axis=0)
    b1[...] = jnp.sum(shares, axis=0, keepdims=True)
    for k, part in enumerate(parts):
        rows = []
        for b in range(cb.shape[0] // 4):
            lo = layout["mu"] + 8 * b
            block = part[lo : lo + 8, :]
            rows.append(
                jnp.concatenate(
                    [
                        jnp.concatenate([block[:SEGS, :], jnp.zeros((8 - SEGS, 128), F32)], axis=0),
                        jnp.concatenate(
                            [block[SEGS : 2 * SEGS, : width - 128], jnp.zeros((8 - SEGS, width - 128), F32)],
                            axis=0,
                        ),
                    ],
                    axis=1,
                )
            )
        mu = jnp.concatenate(rows, axis=0)
        cond_t[tile(me ^ k, width), :] = lax.dot_general(
            jnp.transpose(mu), shares, (((1,), (0,)), ((), ())), precision=HIGH, preferred_element_type=F32
        )
    cond[...] = jnp.transpose(cond_t[...])


def small_grads(me, parts, hidden, channels, step, bs):
    width = channels // 4
    layout = packed_layout(width, channels, bs)
    return pl.pallas_call(
        functools.partial(small_kernel, layout=layout, step=step, width=width),
        in_specs=[SM] + [VM] * 4,
        out_specs=[VM] * 6,
        out_shape=[
            far((hidden, 2 * channels), F32),
            far((3, 2 * channels), F32),
            far((4, channels), F32),
            far((hidden, hidden), F32),
            far((1, hidden), F32),
            far((hidden, channels), F32),
        ],
        scratch_shapes=[
            pltpu.VMEM((2 * channels, 2 * hidden), F32),
            pltpu.VMEM((2 * width, 128), F32),
            pltpu.VMEM((channels, hidden), F32),
        ],
        compiler_params=params(24),
        cost_estimate=cost(3),
        name="small_grads",
    )(me, *parts)


def trade_parts(parts):
    two, three, one = [swap(parts[k], "freq", k) for k in (2, 3, 1)]
    return (parts[0], one, two, three)


def tiled_device(
    tokens,
    seg_ids,
    cotangent,
    ln1_gain,
    ln1_shift,
    w_in,
    conv_taps,
    freq_w1,
    freq_b1,
    freq_w2,
    cond_w,
    w_out,
    ln2_gain,
    ln2_shift,
    w_gate,
    w_up,
    w_down,
):
    quarter, _, channels = tokens.shape
    length = seg_ids.shape[1]
    ff = w_gate.shape[1]
    fs = lax.axis_size("freq")
    bs = lax.axis_size("batch")
    me = lax.axis_index("freq")
    row = lax.axis_index("batch")
    width = channels // fs
    half = bs // 2
    step = channels // (half * fs)
    fw = ff // (bs * fs)
    cos_table, sin_table = tables(length)
    feats = features(length, freq_w1.shape[0] // 2)
    feats_aug = np.concatenate(
        [feats, np.ones((1, length), np.float32), np.zeros((7, length), np.float32)], axis=0
    )

    x_own = tokens[:, 0]
    ct_own = cotangent[:, 0]
    ids = seg_ids
    at = jnp.stack([me, row & 1, (row >> 1) & 1, (row >> 2) & 1, row]).astype(jnp.int32)
    norms = jnp.stack([ln1_gain, ln1_shift, ln2_gain, ln2_shift])
    condt = cond_w.T
    cos_c, sin_c = jnp.asarray(cos_table), jnp.asarray(sin_table)

    def gather_after(value, after):
        two = swap(value, "freq", 2)
        one = swap(value, "freq", 1)
        two = tie(two, after)
        return (value, one, two, swap(two, "freq", 1))

    def pairs(value):
        return value.reshape((value.shape[0] // 2, 2) + value.shape[1:])

    w_mine, w2x, w2t, taps, base, cos_c, sin_c = prepare(
        at, w_in, freq_w2, conv_taps, freq_w1, freq_b1, jnp.asarray(feats_aug), cos_c, sin_c, norms, step, fs
    )
    x_parts = gather_after(x_own, base)
    forward = forward_spectral(at, x_parts, ids, norms, w_mine, taps, base, w2x, condt, cos_c, sin_c)
    z_parts, (u1, n1, p, q, c, vr, vs, mu, mn, cb) = forward[:4], forward[4:]
    ct_parts = gather_after(ct_own, cb)
    z_got = trade_parts(z_parts)
    wg_mine, wu_mine = select_columns(at, cb, w_gate, w_up, fw, fs)
    h, u2, z_t = middle(at, z_got, x_own, w_out, norms, wg_mine, step)
    fed = feed_forward(
        at, u2, h, ct_own, norms, w_out, w_gate, w_up, w_down, step, channels // (bs * fs)
    )
    mixed_out, big_g, gz_parts, gb_parts, sums2 = fed[0], fed[1], fed[2:6], fed[6:10], fed[10]
    u2_parts = gather_after(u2, sums2)
    gz_got = trade_parts(gz_parts)

    keep_a, give_a, keep_b, give_b = hidden_grads(
        at, u2_parts, ct_parts, wg_mine, wu_mine, w_down.reshape(bs, fs, fw, channels), sums2
    )
    got_a = swap(give_a, "batch", 1)
    got_b = swap(give_b, "batch", 2)
    gb_got = trade_parts(gb_parts)

    back = backward_spectral(
        at, gz_got, ids, cb, taps, base, w2x, w2t, jnp.asarray(feats).astype(BF16),
        p, q, c, vr, vs, cos_c, sin_c, give_a,
    )
    gp_parts, (gp, d_taps, d_w2, d_w1, gcb) = back[:4], back[4:]
    gp_got = trade_parts(gp_parts)
    z_all = gather_after(z_t, gcb)

    keep_a, give_a, keep_b, give_b = halve(
        at, (1, 0), gp, pairs(keep_a), pairs(got_a), keep_b, got_b
    )
    got_a = swap(give_a, "batch", 2)
    got_b = swap(give_b, "batch", 1)

    keep, give, packed = projection_grads(
        at, gp, u1, n1, w_mine, gb_got, z_all, d_w2, d_w1, d_taps, gcb, condt, mu, mn, sums2, give_a, bs
    )
    got = swap(give, "batch", 1)
    keep_ff, give_ff = join(at, packed, keep_a, got_a, keep_b, got_b)
    got_ff = swap(give_ff, "batch", 4)
    grad_tokens = final(at, gp_got, x_own, big_g, norms, ids, condt, w_in, give_ff, step)

    keep, give = halve(at, (1,), grad_tokens, pairs(keep), pairs(got))
    got = swap(give, "batch", 2)
    keep, give = halve(at, (2,), grad_tokens, pairs(keep), pairs(got))
    got = swap(give, "batch", 4)
    mine = keep[0].astype(F32) + got[0].astype(F32)
    first = 2 * width // bs

    sent = packed
    for bit in range(bs.bit_length() - 1):
        sent = add(sent, swap(sent, "batch", 1 << bit), grad_tokens, BF16)
    d_w2, d_taps, ln, d_w1, d_b1, d_cond = small_grads(
        at, gather_freq(sent, me), freq_w1.shape[1], channels, step, bs
    )
    d_ff = keep_ff.astype(F32) + got_ff.astype(F32)
    return (
        mixed_out[:, None],
        grad_tokens[:, None],
        ln[0],
        ln[1],
        mine[:first].T,
        d_taps,
        d_w1,
        d_b1[0],
        d_w2,
        d_cond.T,
        mine[first:].T,
        ln[2],
        ln[3],
        d_ff[0].T,
        d_ff[1].T,
        d_ff[2],
    )


def per_device(*args):
    channels = args[0].shape[2]
    step = 2 * channels // (lax.axis_size("batch") * lax.axis_size("freq"))
    fits = lax.axis_size("batch") == 8 and lax.axis_size("freq") == 4 and step % 16 == 0
    return tiled_device(*args) if fits else plain_device(*args)


def solution(mesh):
    rows = P("freq", "batch", None)
    split = P(None, ("batch", "freq"))
    in_specs = (rows, P("batch", None), rows) + (P(),) * 14
    out_specs = (
        rows,
        rows,
        P(),
        P(),
        split,
        P(),
        P(),
        P(),
        P(),
        P(),
        split,
        P(),
        P(),
        split,
        split,
        P(("batch", "freq"), None),
    )
    return jax.shard_map(
        per_device, mesh=mesh, in_specs=in_specs, out_specs=out_specs, check_vma=False
    )
```

```python
import functools

import jax
import jax.numpy as jnp
import ml_dtypes
import numpy as np
from jax import lax
from jax.experimental import pallas as pl
from jax.experimental.pallas import tpu as pltpu
from jax.sharding import PartitionSpec as P

SEGS = 3
EPS = 1e-05
HIGH = lax.Precision.HIGHEST
F32 = jnp.float32
BF16 = jnp.bfloat16


def mm(a, b):
    return jnp.dot(a, b, preferred_element_type=F32)


def mm_nt(a, b):
    return lax.dot_general(a, b, (((1,), (1,)), ((), ())), preferred_element_type=F32)


def mm_tn(a, b):
    return lax.dot_general(a, b, (((0,), (0,)), ((), ())), preferred_element_type=F32)


def swap(value, axis, mask):
    count = lax.axis_size(axis)
    return lax.ppermute(value, axis, [(i, i ^ mask) for i in range(count)])


def pick(parts, index):
    return lax.dynamic_index_in_dim(parts, index, 0, keepdims=False)


def in_order(received, me):
    a, b, c, d = received
    low = (me & 1) == 1
    a, b = jnp.where(low, b, a), jnp.where(low, a, b)
    c, d = jnp.where(low, d, c), jnp.where(low, c, d)
    high = (me & 2) == 2
    a, c = jnp.where(high, c, a), jnp.where(high, a, c)
    b, d = jnp.where(high, d, b), jnp.where(high, b, d)
    return (a, b, c, d)


def trade(blocks, me):
    return [pick(blocks, me)] + [swap(pick(blocks, me ^ k), "freq", k) for k in (2, 3, 1)]


def trade_sorted(blocks, me):
    own, two, three, one = trade(blocks, me)
    return in_order((own, one, two, three), me)


def gather_freq(value, me):
    two = swap(value, "freq", 2)
    one = swap(value, "freq", 1)
    three = swap(two, "freq", 1)
    return (value, one, two, three)


def scatter_sum(value, order):
    bits = lax.axis_size("batch").bit_length() - 1
    me = lax.axis_index("batch")
    rest = value.shape[1:]
    value = value.reshape((2,) * bits + rest)
    left = list(range(bits - 1, -1, -1))
    for bit in order:
        dim = left.index(bit)
        mine = (me >> bit) & 1
        keep = lax.dynamic_index_in_dim(value, mine, dim, keepdims=False)
        give = lax.dynamic_index_in_dim(value, 1 - mine, dim, keepdims=False)
        got = swap(give, "batch", 1 << bit)
        total = keep.astype(F32) + got.astype(F32)
        left.remove(bit)
        value = total.astype(value.dtype) if left else total
    return value


def tables(length):
    index = np.arange(length, dtype=np.int64)
    angle = (index[:, None] * index[None, :] % (2 * length)) * (np.pi / length)
    return (
        np.cos(angle).astype(ml_dtypes.bfloat16),
        np.sin(angle).astype(ml_dtypes.bfloat16),
    )


def features(length, half):
    index = np.arange(length, dtype=np.int64)
    lags = (np.arange(half, dtype=np.int64) + 1) ** 2
    angle = (lags[:, None] * index[None, :] % (2 * length)) * (np.pi / length)
    return np.concatenate([np.cos(angle), np.sin(angle)], axis=0).astype(np.float32)


def normed(values):
    centered = values - jnp.mean(values, axis=-1, keepdims=True)
    scale = lax.rsqrt(jnp.mean(centered * centered, axis=-1, keepdims=True) + EPS)
    return centered * scale, scale


def norm_back(unit, scale, grad):
    return scale * (
        grad
        - jnp.mean(grad, axis=-1, keepdims=True)
        - unit * jnp.mean(grad * unit, axis=-1, keepdims=True)
    )


def shift_right(values):
    return jnp.pad(values, ((0, 0), (1, 0)))[:, :-1]


def shift_left(values):
    return jnp.pad(values, ((0, 0), (0, 1)))[:, 1:]


def plain_device(
    tokens,
    seg_ids,
    cotangent,
    ln1_gain,
    ln1_shift,
    w_in,
    conv_taps,
    freq_w1,
    freq_b1,
    freq_w2,
    cond_w,
    w_out,
    ln2_gain,
    ln2_shift,
    w_gate,
    w_up,
    w_down,
):
    quarter, _, channels = tokens.shape
    length = seg_ids.shape[1]
    ff = w_gate.shape[1]
    fs = lax.axis_size("freq")
    bs = lax.axis_size("batch")
    me = lax.axis_index("freq")
    width = channels // fs
    half = bs // 2
    step = channels // (half * fs)
    cos_table, sin_table = tables(length)
    feats = features(length, freq_w1.shape[0] // 2)

    x_own = tokens[:, 0]
    ct_own = cotangent[:, 0]
    ids = seg_ids
    x_parts = gather_freq(x_own, me)
    ct_parts = gather_freq(ct_own, me)

    w_in_t = (
        w_in.T.reshape(2, half, fs, step, channels)
        .transpose(2, 0, 1, 3, 4)
        .reshape(fs, 2 * width, channels)
    )
    w_in_mine = pick(w_in_t, me)
    w_out_p = (
        w_out.reshape(half, fs, step, channels).transpose(1, 0, 2, 3).reshape(channels, channels)
    )
    taps_mine = pick(
        conv_taps.reshape(3, 2, half, fs, step).transpose(3, 0, 1, 2, 4).reshape(fs, 3, 2 * width), me
    )[:, :, None]
    w2_mine = pick(
        freq_w2.reshape(-1, 2, half, fs, step).transpose(3, 0, 1, 2, 4).reshape(fs, -1, 2 * width), me
    )
    fw = ff // (bs * fs)
    wide = ff // fs

    def mine_rows(weight):
        return pick(
            weight.reshape(bs, fs, fw, channels).transpose(1, 0, 2, 3).reshape(fs, wide, channels), me
        )

    wg_mine, wu_mine, wd_mine = (mine_rows(w_gate.T), mine_rows(w_up.T), mine_rows(w_down))

    base = jnp.dot(freq_w1.T, feats, precision=HIGH) + freq_b1[:, None]

    x_row = jnp.concatenate(in_order(x_parts, me), axis=0).astype(F32)
    unit1, _ = normed(x_row)
    u1 = (unit1 * ln1_gain + ln1_shift).astype(BF16)
    n1 = unit1.astype(BF16)
    masks = (ids == jnp.arange(SEGS, dtype=jnp.int32)[:, None]).astype(F32)
    counts = jnp.sum(masks, axis=1, keepdims=True)
    mu = mm(masks.astype(BF16), u1) / counts
    mn = mm(masks.astype(BF16), n1) / counts
    cb = jnp.dot(mu, cond_w, precision=HIGH)
    p = mm_nt(w_in_mine, u1)
    same = (ids[:, 1:] == ids[:, :-1]).astype(F32)
    zero = jnp.zeros((1, 1), F32)
    prev = jnp.concatenate([zero, same], axis=1)
    nxt = jnp.concatenate([same, zero], axis=1)
    p_prev = shift_right(p) * prev
    p_next = shift_left(p) * nxt
    s = taps_mine[0] * p_prev + taps_mine[1] * p + taps_mine[2] * p_next
    q, v = s[:width], s[width:]

    pre = base[None] + cb[:, :, None]
    gate_pre = jax.nn.sigmoid(pre)
    hk = pre * gate_pre
    kk = jnp.einsum("kc,jkf->jcf", w2_mine, hk, precision=HIGH)
    kr, ki = kk[:, :width], kk[:, width:]
    vm = (v[None] * masks[:, None, :]).astype(BF16).reshape(SEGS * width, length)
    vr = mm(vm, cos_table).reshape(SEGS, width, length)
    vi = -mm(vm, sin_table).reshape(SEGS, width, length)
    weights = np.full((length,), 2.0 / (2 * length), np.float32)
    weights[0] = 1.0 / (2 * length)
    yr = ((kr * vr - ki * vi) * weights).astype(BF16).reshape(SEGS * width, length)
    yi = ((kr * vi + ki * vr) * weights).astype(BF16).reshape(SEGS * width, length)
    conv = (mm(yr, cos_table) - mm(yi, sin_table)).reshape(SEGS, width, length)
    c = jnp.sum(conv * masks[:, None, :], axis=0)
    z_mine = (q * c).astype(BF16)

    z_blocks = z_mine.reshape(width, fs, quarter).transpose(1, 0, 2)
    z_t = jnp.concatenate(trade_sorted(z_blocks, me), axis=0)

    x32 = x_own.astype(F32)
    ct32 = ct_own.astype(F32)
    h = x32 + mm_tn(z_t, w_out_p)
    unit2, scale2 = normed(h)
    u2 = (unit2 * ln2_gain + ln2_shift).astype(BF16)
    u2_parts = gather_freq(u2, me)
    g = mm(u2, w_gate)
    a = mm(u2, w_up)
    gh = mm_nt(ct_own, w_down)
    sg = jax.nn.sigmoid(g)
    silu = g * sg
    hid = (silu * a).astype(BF16)
    mixed_out = (h + mm(hid, w_down)).astype(BF16)
    gg = (gh * a * sg * (1.0 + g * (1.0 - sg))).astype(BF16)
    ga = (gh * silu).astype(BF16)
    gu2 = mm_nt(gg, w_gate) + mm_nt(ga, w_up)
    grad_ln2_gain = jnp.sum(gu2 * unit2, axis=0)
    grad_ln2_shift = jnp.sum(gu2, axis=0)
    big_g = ct32 + norm_back(unit2, scale2, gu2 * ln2_gain)
    gb = big_g.astype(BF16)
    gz_blocks = mm_nt(w_out_p, gb).astype(BF16).reshape(fs, width, quarter)
    gz = jnp.concatenate(trade_sorted(gz_blocks, me), axis=1).astype(F32)
    gb_parts = gather_freq(gb, me)

    u2_row = jnp.concatenate(u2_parts, axis=0)
    ct_row = jnp.concatenate(ct_parts, axis=0)
    g_t = mm_nt(wg_mine, u2_row)
    a_t = mm_nt(wu_mine, u2_row)
    gh_t = mm_nt(wd_mine, ct_row)
    sg_t = jax.nn.sigmoid(g_t)
    silu_t = g_t * sg_t
    hid_t = (silu_t * a_t).astype(BF16)
    gg_t = (gh_t * a_t * sg_t * (1.0 + g_t * (1.0 - sg_t))).astype(BF16)
    ga_t = (gh_t * silu_t).astype(BF16)
    d_gate = mm(gg_t, u2_row).astype(BF16)
    d_up = mm(ga_t, u2_row).astype(BF16)
    d_down = mm(hid_t, ct_row).astype(BF16)
    d_ff = jnp.stack([d_gate, d_up, d_down], axis=0).reshape(3, bs, fw, channels).transpose(1, 0, 2, 3)
    bits = bs.bit_length() - 1
    order_a = list(range(bits))
    order_b = [1, 0] + list(range(2, bits))
    cut = channels // 2
    ff_a = scatter_sum(d_ff[..., :cut], order_a)
    ff_b = scatter_sum(d_ff[..., cut:], order_b)
    d_ff = jnp.concatenate([ff_a, ff_b], axis=-1)

    gq = gz * c
    gc = gz * q
    gcm = (gc[None] * masks[:, None, :]).astype(BF16).reshape(SEGS * width, length)
    gyr = mm(gcm, cos_table).reshape(SEGS, width, length) * weights
    gyi = -mm(gcm, sin_table).reshape(SEGS, width, length) * weights
    gkr = gyr * vr + gyi * vi
    gki = gyi * vr - gyr * vi
    gvr = (kr * gyr + ki * gyi).astype(BF16).reshape(SEGS * width, length)
    gvi = (kr * gyi - ki * gyr).astype(BF16).reshape(SEGS * width, length)
    gv_all = (mm(gvr, cos_table) - mm(gvi, sin_table)).reshape(SEGS, width, length)
    gv = jnp.sum(gv_all * masks[:, None, :], axis=0)
    gs = jnp.concatenate([gq, gv], axis=0)
    d_taps = jnp.stack(
        [jnp.sum(gs * p_prev, axis=1), jnp.sum(gs * p, axis=1), jnp.sum(gs * p_next, axis=1)]
    )
    gp = (
        taps_mine[1] * gs
        + taps_mine[0] * shift_left(gs * prev)
        + taps_mine[2] * shift_right(gs * nxt)
    ).astype(BF16)

    gkk = jnp.concatenate([gkr, gki], axis=1)
    gkk_low = gkk.astype(BF16)
    hk_low = hk.astype(BF16)
    d_w2 = jnp.einsum("jkf,jcf->kc", hk_low, gkk_low, preferred_element_type=F32)
    gpre = jnp.einsum("kc,jcf->jkf", w2_mine.astype(BF16), gkk_low, preferred_element_type=F32)
    gpre = gpre * gate_pre * (1.0 + pre * (1.0 - gate_pre))
    d_w1 = jnp.einsum("ef,jkf->ek", feats, gpre, precision=HIGH)
    gcb = jnp.sum(gpre, axis=2)
    gcb_row = lax.psum(gcb, "freq")

    gp_blocks = gp.reshape(2 * width, fs, quarter).transpose(1, 0, 2)
    gp_t = jnp.concatenate(trade_sorted(gp_blocks, me), axis=0)

    u1_row = u1
    d_in = mm(gp, u1_row).astype(BF16).reshape(bs, 2 * width // bs, channels)
    d_in = scatter_sum(d_in, order_a)
    gb_row = jnp.concatenate(in_order(gb_parts, me), axis=0)
    d_out = mm(z_mine, gb_row)
    narrow = channels // bs
    d_out = scatter_sum(d_out.T.astype(BF16).reshape(bs, narrow, width), order_a)
    d_out = d_out.reshape(fs, narrow // fs, width)
    d_out = jnp.stack(trade_sorted(d_out, me), axis=0)
    d_out = (
        d_out.reshape(fs, narrow // fs, half, step).transpose(2, 0, 3, 1).reshape(channels, -1)
    )

    gmu_part = jnp.dot(gcb, cond_w.T, precision=HIGH)
    sum_gp = jnp.sum(gp.astype(F32), axis=1)
    w_mine32 = w_in_mine.astype(F32)
    d_shift1 = jnp.dot(sum_gp[None], w_mine32, precision=HIGH)[0] + jnp.sum(gmu_part, axis=0)
    d_gain1 = jnp.sum(mm(gp, n1) * w_mine32, axis=0) + jnp.sum(gmu_part * mn, axis=0)

    gmu = jnp.dot(gcb_row, cond_w.T, precision=HIGH) / counts
    own_masks = lax.dynamic_slice_in_dim(masks, me * quarter, quarter, 1)
    gu1 = mm_tn(gp_t, w_in_t.reshape(2 * channels, channels)) + lax.dot_general(
        own_masks, gmu, (((0,), (0,)), ((), ())), precision=HIGH
    )
    unit_own, scale_own = normed(x32)
    grad_tokens = big_g + norm_back(unit_own, scale_own, gu1 * ln1_gain)

    shared = [
        d_gain1,
        d_shift1,
        d_w1.reshape(-1),
        jnp.sum(gcb, axis=0),
        jnp.dot(mu.T, gcb, precision=HIGH).reshape(-1),
        grad_ln2_gain,
        grad_ln2_shift,
    ]
    owned = jnp.concatenate([d_taps, d_w2], axis=0)
    packed = jnp.concatenate(shared + [owned.reshape(-1)])
    for bit in range(bits):
        packed = packed + swap(packed, "batch", 1 << bit)
    split = packed.shape[0] - owned.size
    common, owned = packed[:split], packed[split:]
    common = common + swap(common, "freq", 1)
    common = common + swap(common, "freq", 2)
    owned = jnp.stack(in_order(gather_freq(owned, me), me), axis=0)
    owned = (
        owned.reshape(fs, -1, 2, half, step).transpose(1, 2, 3, 0, 4).reshape(-1, 2 * channels)
    )
    sizes = np.cumsum([part.size for part in shared])
    got = jnp.split(common, sizes[:-1])
    return (
        mixed_out[:, None],
        grad_tokens[:, None],
        got[0],
        got[1],
        d_in.T,
        owned[:3],
        got[2].reshape(freq_w1.shape),
        got[3],
        owned[3:],
        got[4].reshape(cond_w.shape),
        d_out,
        got[5],
        got[6],
        d_ff[0].T,
        d_ff[1].T,
        d_ff[2],
    )


VM = pl.BlockSpec(memory_space=pltpu.VMEM)
SM = pl.BlockSpec(memory_space=pltpu.SMEM)
HBM = pl.BlockSpec(memory_space=pl.ANY)
MIB = 1 << 20


def params(mib):
    return pltpu.CompilerParams(vmem_limit_bytes=mib * MIB)


def cost(micros):
    return pl.CostEstimate(
        flops=int(micros * 1000000000.0), bytes_accessed=int(micros * 3500000.0), transcendentals=0
    )


def shape(dims, dtype):
    return pltpu.VMEM(dims, dtype)


def far(dims, dtype):
    return pltpu.HBM(dims, dtype)


def in_hbm(*values):
    kept = tuple(pltpu.with_memory_space_constraint(value, pltpu.HBM) for value in values)
    return kept if len(kept) > 1 else kept[0]


def in_vmem(value):
    return pltpu.with_memory_space_constraint(value, pltpu.VMEM)


def sigmoid(value):
    return 1.0 / (1.0 + jnp.exp(-value))


def dma_all(pairs, sems, first=0):
    copies = [
        pltpu.make_async_copy(source, target, sems.at[first + i])
        for i, (source, target) in enumerate(pairs)
    ]
    for copy in copies:
        copy.start()
    return copies


def tie_kernel(*refs):
    pass


def tie(values, after):
    count = len(values)
    return pl.pallas_call(
        tie_kernel,
        in_specs=[HBM] * (count + 1),
        out_specs=[HBM] * count,
        out_shape=[jax.ShapeDtypeStruct(value.shape, value.dtype) for value in values],
        input_output_aliases={i: i for i in range(count)},
        compiler_params=params(1),
        name="tie",
    )(*values, after)


def one_hot_rows(me, rows, lanes, piece, fs):
    row = lax.broadcasted_iota(jnp.int32, (rows, lanes), 0)
    lane = lax.broadcasted_iota(jnp.int32, (rows, lanes), 1)
    block = jnp.zeros_like(row)
    for m in range(1, rows // piece):
        block = block + jnp.where(row >= m * piece, 1, 0)
    return jnp.where(lane == block * ((fs - 1) * piece) + me * piece + row, 1.0, 0.0)


def prepare_kernel(
    me_ref, w_in, freq_w2, conv_taps, freq_w1, freq_b1, feats, waves_far, norms,
    w_mine, w2x, w2t, taps, base, waves, w1_aug, sems, *, step, fs,
):
    loads = dma_all([(waves_far, waves)], sems)
    lanes = w_in.shape[1] // 4
    rows = lanes // fs
    sel = one_hot_rows(me_ref[0], rows, lanes, step, fs)
    low = sel.astype(BF16)
    hidden = freq_w2.shape[0]
    for i in range(4):
        out = slice(i * rows, (i + 1) * rows)
        group = slice(i * lanes, (i + 1) * lanes)
        w_mine[out, :] = mm_nt(low, w_in[:, group]).astype(BF16)
        both = jnp.concatenate([freq_w2[:, group], conv_taps[:, group]], axis=0)
        mine = lax.dot_general(
            sel, both, (((1,), (1,)), ((), ())), precision=HIGH, preferred_element_type=F32
        )
        taps[out, :3] = mine[:, hidden:]
        mine = mine[:, :hidden]
        high = mine.astype(BF16)
        rest = (mine - high.astype(F32)).astype(BF16)
        w2x[out, :] = jnp.concatenate([high, high, rest], axis=1)
    w2t[...] = jnp.transpose(w2x[...][:, :hidden].astype(F32)).astype(BF16)
    w1_aug[...] = jnp.zeros_like(w1_aug)
    count = freq_w1.shape[0]
    w1_aug[:count, :] = freq_w1[...]
    w1_aug[count : count + 1, :] = freq_b1[...]
    base[...] = lax.dot_general(
        w1_aug[...], feats[...], (((0,), (0,)), ((), ())), precision=HIGH, preferred_element_type=F32
    )
    for load in loads:
        load.wait()


def prepare(me, w_in, freq_w2, conv_taps, freq_w1, freq_b1, feats, waves, norms, step, fs):
    channels, both = w_in.shape
    hidden = freq_w2.shape[0]
    length = feats.shape[1]
    return pl.pallas_call(
        functools.partial(prepare_kernel, step=step, fs=fs),
        in_specs=[SM] + [VM] * 6 + [HBM] * 2,
        out_specs=[VM] * 6,
        out_shape=[
            shape((both // fs, channels), BF16),
            shape((both // fs, 3 * hidden), BF16),
            shape((hidden, both // fs), BF16),
            shape((both // fs, 8), F32),
            shape((hidden, length), F32),
            shape((2 * length, length), BF16),
        ],
        scratch_shapes=[
            pltpu.VMEM((feats.shape[0], hidden), F32),
            pltpu.SemaphoreType.DMA((1,)),
        ],
        compiler_params=params(24),
        cost_estimate=cost(3),
        name="prepare",
    )(me, *in_hbm(w_in, freq_w2, conv_taps, freq_w1), freq_b1[None], in_hbm(feats), in_hbm(waves), norms)


def select_kernel(at_ref, after, gate, up, gate_out, up_out, *, fs):
    rows = gate_out.shape[0]
    sel = one_hot_rows(at_ref[0], rows, rows * fs, rows, fs).astype(BF16)
    gate_out[...] = mm_nt(sel, gate[...]).astype(BF16)
    up_out[...] = mm_nt(sel, up[...]).astype(BF16)


def select_columns(at, after, w_gate, w_up, bs, fs):
    channels, ff = w_gate.shape
    lanes = ff // bs
    wide = pl.BlockSpec((channels, lanes), lambda i, at: (0, (i // 2) * 4 + at[2] * 2 + i % 2))
    rows = pl.BlockSpec((lanes // fs, channels), lambda i, at: (i, 0))
    return pl.pallas_call(
        functools.partial(select_kernel, fs=fs),
        grid_spec=pltpu.PrefetchScalarGridSpec(
            num_scalar_prefetch=1,
            grid=(bs // 2,),
            in_specs=[HBM, wide, wide],
            out_specs=[rows, rows],
        ),
        out_shape=[shape((ff // (2 * fs), channels), BF16)] * 2,
        compiler_params=params(20),
        cost_estimate=cost(5),
        name="select_columns",
    )(at, after, in_hbm(w_gate), in_hbm(w_up))


def row_masks(ids):
    lane = lax.broadcasted_iota(jnp.int32, ids.shape, 1)
    length = ids.shape[1]
    prev = jnp.where((ids == pltpu.roll(ids, 1, 1)) & (lane > 0), 1.0, 0.0)
    nxt = jnp.where((ids == pltpu.roll(ids, length - 1, 1)) & (lane < length - 1), 1.0, 0.0)
    return prev, nxt


def bin_weights(start, width, length):
    lane = lax.broadcasted_iota(jnp.int32, (1, width), 1) + start
    return jnp.where(lane == 0, 0.5 / length, 1.0 / length)


def tile(index, size):
    return pl.ds(pl.multiple_of(index * size, size), size)


def hidden_tile(base, cb, j, lanes):
    pre = base[:, lanes] + cb[:, j : j + 1]
    return pre, sigmoid(pre)


def kernel_tile(w2x, hk):
    high = hk.astype(BF16)
    rest = (hk - high.astype(F32)).astype(BF16)
    return mm(w2x[...], jnp.concatenate([high, rest, high], axis=0))


def forward_kernel(
    me_ref, ids_at, x0, x1, x2, x3, ids_ref, norms, w, taps, base, w2x, condt, waves,
    z0, z1, z2, z3, u1, n1, p_out, q_out, c_out, vr_out, vs_out, mu_out, mn_out, cb_out,
    p, q, vm, ycat, acc,
):
    quarter = x0.shape[0]
    width, length = q_out.shape
    tiles = length // quarter
    me = me_ref[0]
    for k, x in enumerate((x0, x1, x2, x3)):
        values = x[...].astype(F32)
        unit, _ = normed(values)
        rows = tile(me ^ k, quarter)
        n1[rows, :] = unit.astype(BF16)
        u1[rows, :] = (unit * norms[0:1, :] + norms[1:2, :]).astype(BF16)
    ids = ids_ref[...]
    number = lax.broadcasted_iota(jnp.int32, (8, length), 0)
    member = jnp.where(ids == number, 1.0, 0.0)
    counts = jnp.maximum(jnp.sum(member, axis=1, keepdims=True), 1.0)
    member_low = member.astype(BF16)
    mu = mm(member_low, u1[...]) / counts
    mu_out[...] = mu
    mn_out[...] = mm(member_low, n1[...]) / counts
    cb_out[...] = lax.dot_general(
        condt[...], mu, (((1,), (1,)), ((), ())), precision=HIGH, preferred_element_type=F32
    )
    prev, nxt = row_masks(ids)
    for t in range(tiles):
        at = slice(t * quarter, (t + 1) * quarter)
        p[:, at] = mm_nt(w[...], u1[at, :])
    chunk = width // 2
    for r in range(4):
        at = slice(r * chunk, (r + 1) * chunk)
        here = p[at, :]
        p_out[at, :] = here.astype(BF16)
        mixed = (
            taps[at, 0:1] * (pltpu.roll(here, 1, 1) * prev)
            + taps[at, 1:2] * here
            + taps[at, 2:3] * (pltpu.roll(here, length - 1, 1) * nxt)
        )
        if r < 2:
            q[at, :] = mixed
            q_out[at, :] = mixed.astype(BF16)
        else:
            for j in range(SEGS):
                lo = j * width + (r - 2) * chunk
                vm[lo : lo + chunk, :] = (mixed * member[j : j + 1, :]).astype(BF16)

    @pl.loop(0, tiles)
    def _(f):
        lanes = tile(f, quarter)
        upper = pl.ds(pl.multiple_of(f * quarter + length, quarter), quarter)
        weight = bin_weights(f * quarter, quarter, length)
        vr_all = mm(vm[...], waves[:length, lanes])
        vs_all = mm(vm[...], waves[length:, lanes])
        vr_out[:, lanes] = vr_all.astype(BF16)
        vs_out[:, lanes] = vs_all.astype(BF16)
        for j in range(SEGS):
            pre, gate = hidden_tile(base, cb_out, j, lanes)
            kk = kernel_tile(w2x, pre * gate)
            kr, ki = kk[:width] * weight, kk[width:] * weight
            at = slice(j * width, (j + 1) * width)
            vr, vs = vr_all[at], vs_all[at]
            ycat[at, lanes] = (kr * vr + ki * vs).astype(BF16)
            ycat[at, upper] = (kr * vs - ki * vr).astype(BF16)

    for k, z_out in enumerate((z0, z1, z2, z3)):
        t = me ^ k
        lanes = tile(t, quarter)
        acc[...] = jnp.zeros_like(acc)
        ids_here = ids_ref[:, lanes]
        for j in range(SEGS):

            @pl.when((ids_at[0, t * quarter] <= j) & (ids_at[0, (t + 1) * quarter - 1] >= j))
            def _():
                at = slice(j * width, (j + 1) * width)
                part = mm(ycat[at, :], waves[:, lanes])
                acc[...] += jnp.where(ids_here == j, part, 0.0)

        c = acc[...]
        c_out[:, lanes] = c.astype(BF16)
        z = (q[:, lanes] * c).astype(BF16)
        z_out[...] = z


def forward_spectral(me, x_parts, ids, norms, w, taps, base, w2x, condt, waves):
    quarter, channels = x_parts[0].shape
    length = ids.shape[1]
    width = w.shape[0] // 2
    saved = [
        (length, channels),
        (length, channels),
        (2 * width, length),
        (width, length),
        (width, length),
        (SEGS * width, length),
        (SEGS * width, length),
    ]
    small = [
        shape((8, channels), F32),
        shape((8, channels), F32),
        shape((condt.shape[0], 8), F32),
    ]
    return pl.pallas_call(
        forward_kernel,
        in_specs=[SM, SM] + [VM] * 12,
        out_specs=[VM] * (7 + len(saved)),
        out_shape=[shape((width, quarter), BF16)] * 4 + [shape(dims, BF16) for dims in saved] + small,
        scratch_shapes=[
            pltpu.VMEM((2 * width, length), F32),
            pltpu.VMEM((width, length), F32),
            pltpu.VMEM((SEGS * width, length), BF16),
            pltpu.VMEM((SEGS * width, 2 * length), BF16),
            pltpu.VMEM((width, quarter), F32),
        ],
        compiler_params=params(26),
        cost_estimate=cost(15),
        name="forward_spectral",
    )(me, ids, *x_parts, ids, norms, w, taps, base, w2x, condt, waves)


def backward_kernel(
    me_ref, ids_at, g0, g1, g2, g3, ids_ref, cb, taps, base, w2x, w2, feats,
    p, q, c, vr_in, vs_in, waves, after,
    o0, o1, o2, o3, gp_row, d_taps, d_w2, d_w1, gcb,
    gcm, gvcat, gs, acc,
):
    width, quarter = g0.shape
    length = gp_row.shape[1]
    tiles = length // quarter
    hidden = base.shape[0]
    me = me_ref[0]
    for k, g in enumerate((g0, g1, g2, g3)):
        lanes = tile(me ^ k, quarter)
        gz = g[...].astype(F32)
        gs[:width, lanes] = gz * c[:, lanes].astype(F32)
        gc = gz * q[:, lanes].astype(F32)
        ids_here = ids_ref[:, lanes]
        for j in range(SEGS):
            gcm[j * width : (j + 1) * width, lanes] = jnp.where(ids_here == j, gc, 0.0).astype(BF16)
    d_w2[...] = jnp.zeros_like(d_w2)
    d_w1[...] = jnp.zeros_like(d_w1)
    gcb[...] = jnp.zeros_like(gcb)

    @pl.loop(0, tiles)
    def _(f):
        lanes = tile(f, quarter)
        upper = pl.ds(pl.multiple_of(f * quarter + length, quarter), quarter)
        weight = bin_weights(f * quarter, quarter, length)
        gyr_all = mm(gcm[...], waves[:length, lanes]) * weight
        gys_all = mm(gcm[...], waves[length:, lanes]) * weight
        for j in range(SEGS):
            pre, gate = hidden_tile(base, cb, j, lanes)
            hk = pre * gate
            kk = kernel_tile(w2x, hk)
            kr, ki = kk[:width], kk[width:]
            at = slice(j * width, (j + 1) * width)
            gyr, gys = gyr_all[at], gys_all[at]
            vr, vs = vr_in[at, lanes].astype(F32), vs_in[at, lanes].astype(F32)
            gvcat[at, lanes] = (kr * gyr - ki * gys).astype(BF16)
            gvcat[at, upper] = (kr * gys + ki * gyr).astype(BF16)
            gkk = jnp.concatenate(
                [(gyr * vr + gys * vs).astype(BF16), (gyr * vs - gys * vr).astype(BF16)], axis=0
            )
            d_w2[...] += mm_nt(gkk, hk.astype(BF16))
            gpre = mm(w2[...], gkk) * (gate * (1.0 + pre * (1.0 - gate)))
            gcb[:, j : j + 1] += jnp.sum(gpre, axis=1, keepdims=True)
            d_w1[...] += mm_nt(feats[:, lanes], gpre.astype(BF16))

    for k in range(4):
        t = me ^ k
        lanes = tile(t, quarter)
        acc[...] = jnp.zeros_like(acc)
        ids_here = ids_ref[:, lanes]
        for j in range(SEGS):

            @pl.when((ids_at[0, t * quarter] <= j) & (ids_at[0, (t + 1) * quarter - 1] >= j))
            def _():
                at = slice(j * width, (j + 1) * width)
                part = mm(gvcat[at, :], waves[:, lanes])
                acc[...] += jnp.where(ids_here == j, part, 0.0)

        gs[width:, lanes] = acc[...]
    prev, nxt = row_masks(ids_ref[...])
    chunk = width // 2
    for r in range(4):
        at = slice(r * chunk, (r + 1) * chunk)
        here = p[at, :].astype(F32)
        grad = gs[at, :]
        d_taps[at, 0:1] = jnp.sum(grad * (pltpu.roll(here, 1, 1) * prev), axis=1, keepdims=True)
        d_taps[at, 1:2] = jnp.sum(grad * here, axis=1, keepdims=True)
        d_taps[at, 2:3] = jnp.sum(
            grad * (pltpu.roll(here, length - 1, 1) * nxt), axis=1, keepdims=True
        )
        gp_row[at, :] = (
            taps[at, 1:2] * grad
            + taps[at, 0:1] * pltpu.roll(grad * prev, length - 1, 1)
            + taps[at, 2:3] * pltpu.roll(grad * nxt, 1, 1)
        ).astype(BF16)
    share = jnp.transpose(gcb[...])[:8, :]
    high = share.astype(BF16)
    rest = (share - high.astype(F32)).astype(BF16)
    extra = jnp.concatenate([high, rest], axis=0)
    extra = jnp.concatenate([extra, jnp.zeros((16, quarter - hidden), BF16)], axis=1)
    for k, out in enumerate((o0, o1, o2, o3)):
        out[: 2 * width, :] = gp_row[:, tile(me ^ k, quarter)]
        out[2 * width :, :] = extra


def backward_spectral(
    me, gz_parts, ids, cb, taps, base, w2x, w2, feats, p, q, c, vr, vs, waves, after
):
    width, quarter = gz_parts[0].shape
    length = ids.shape[1]
    hidden = base.shape[0]
    outs = [shape((2 * width + 16, quarter), BF16)] * 4 + [
        shape((2 * width, length), BF16),
        shape((2 * width, 128), F32),
        shape((2 * width, hidden), F32),
        shape((feats.shape[0], hidden), F32),
        shape((hidden, 128), F32),
    ]
    return pl.pallas_call(
        backward_kernel,
        in_specs=[SM, SM] + [VM] * 17 + [HBM],
        out_specs=[VM] * 9,
        out_shape=outs,
        scratch_shapes=[
            pltpu.VMEM((SEGS * width, length), BF16),
            pltpu.VMEM((SEGS * width, 2 * length), BF16),
            pltpu.VMEM((2 * width, length), F32),
            pltpu.VMEM((width, quarter), F32),
        ],
        compiler_params=params(26),
        cost_estimate=cost(17),
        name="backward_spectral",
    )(
        me, ids, *gz_parts, ids, cb, taps, base, w2x, w2, feats, p, q, c, vr, vs, waves, after
    )


def middle_kernel(me_ref, z0, z1, z2, z3, x, w_out, norms, after, h_out, u2_out, z_t, *, piece):
    me = me_ref[0]
    width = z0.shape[0]
    for k, z in enumerate((z0, z1, z2, z3)):
        for i in range(width // piece):
            at = pl.ds(pl.multiple_of((i * 4 + (me ^ k)) * piece, piece), piece)
            z_t[at, :] = z[i * piece : (i + 1) * piece, :]
    h = x[...].astype(F32) + mm(jnp.transpose(z_t[...]), w_out[...])
    h_out[...] = h
    unit, _ = normed(h)
    u2_out[...] = (unit * norms[2:3, :] + norms[3:4, :]).astype(BF16)


def middle(me, z_parts, x, w_out, norms, after, piece):
    quarter, channels = x.shape
    return pl.pallas_call(
        functools.partial(middle_kernel, piece=piece),
        in_specs=[SM] + [VM] * 7 + [HBM],
        out_specs=[VM] * 3,
        out_shape=[
            shape((quarter, channels), F32),
            shape((quarter, channels), BF16),
            shape((channels, quarter), BF16),
        ],
        compiler_params=params(24),
        cost_estimate=cost(2),
        name="middle",
    )(me, *z_parts, x, in_hbm(w_out), norms, after)


def feed_kernel(
    me_ref, u2, h, ct, norms, w_out, gate, up, down,
    mixed, big_g, g0, g1, g2, g3, t_own, t_other, sums, acc_out, acc_grad, gz_t, gb_t, *, piece, thin,
):
    i = pl.program_id(0)

    @pl.when(i == 0)
    def _():
        acc_out[...] = jnp.zeros_like(acc_out)
        acc_grad[...] = jnp.zeros_like(acc_grad)

    g = mm(u2[...], gate[...])
    a = mm(u2[...], up[...])
    gh = mm_nt(ct[...], down[...])
    sg = sigmoid(g)
    silu = g * sg
    hid = (silu * a).astype(BF16)
    gg = (gh * a * (sg * (1.0 + g * (1.0 - sg)))).astype(BF16)
    ga = (gh * silu).astype(BF16)
    acc_out[...] += mm(hid, down[...])
    acc_grad[...] += mm_nt(gg, gate[...]) + mm_nt(ga, up[...])

    @pl.when(i == pl.num_programs(0) - 1)
    def _():
        me = me_ref[0]
        width = g0.shape[0]
        here = h[...]
        mixed[...] = (here + acc_out[...]).astype(BF16)
        gu2 = acc_grad[...]
        unit, scale = normed(here)
        sums[0:1, :] = jnp.sum(gu2 * unit, axis=0, keepdims=True)
        sums[1:2, :] = jnp.sum(gu2, axis=0, keepdims=True)
        total = ct[...].astype(F32) + norm_back(unit, scale, gu2 * norms[2:3, :])
        big_g[...] = total
        low = total.astype(BF16)
        gz_t[...] = mm_nt(w_out[...], low).astype(BF16)
        for k, out in enumerate((g0, g1, g2, g3)):
            for r in range(width // piece):
                at = pl.ds(pl.multiple_of((r * 4 + (me ^ k)) * piece, piece), piece)
                out[r * piece : (r + 1) * piece, :] = gz_t[at, :]
        gb_t[...] = jnp.transpose(total)
        for core, out in ((me & 1, t_own), (1 - (me & 1), t_other)):
            parts = []
            for x in range(2):
                for r in range(width // thin):
                    lo = pl.multiple_of((r * 4 + 2 * x + core) * thin, thin)
                    parts.append(gb_t[pl.ds(lo, thin), :])
            out[...] = jnp.concatenate(parts, axis=0).astype(BF16)


def feed_forward(me, u2, h, ct, norms, w_out, w_gate, w_up, w_down, piece, thin):
    quarter, channels = u2.shape
    ff = w_gate.shape[1]
    block = 512

    width = channels // 4
    outs = [
        ((quarter, channels), BF16),
        ((quarter, channels), F32),
    ] + [((width, quarter), BF16)] * 4 + [((2 * width, quarter), BF16)] * 2 + [((8, channels), F32)]
    return pl.pallas_call(
        functools.partial(feed_kernel, piece=piece, thin=thin),
        grid=(ff // block,),
        in_specs=[
            SM,
            VM,
            VM,
            VM,
            VM,
            VM,
            pl.BlockSpec((channels, block), lambda i: (0, i)),
            pl.BlockSpec((channels, block), lambda i: (0, i)),
            pl.BlockSpec((block, channels), lambda i: (i, 0)),
        ],
        out_specs=[VM] * len(outs),
        out_shape=[far(*outs[0])] + [shape(*out) for out in outs[1:]],
        scratch_shapes=[
            pltpu.VMEM((quarter, channels), F32),
            pltpu.VMEM((quarter, channels), F32),
            pltpu.VMEM((channels, quarter), BF16),
            pltpu.VMEM((channels, quarter), F32),
        ],
        compiler_params=params(28),
        cost_estimate=cost(13),
        name="feed_forward",
    )(me, u2, h, ct, norms, in_hbm(w_out), in_hbm(w_gate), in_hbm(w_up), in_hbm(w_down))


def hidden_grads_kernel(at_ref, *refs):
    u_parts, c_parts, refs = refs[:8], refs[8:16], refs[16:]
    gate, up, gt_own, gt_got, z_own, z_got, down, after, *refs = refs
    keep_a, give_a, keep_b, give_b, keep_o, give_o, rights, lefts, d_all, d_out = refs
    quarter, channels = u_parts[0].shape
    y, z = at_ref[1], at_ref[3]
    rows = gate.shape[0]
    for k in range(8):
        at = slice(k * quarter, (k + 1) * quarter)
        rights[0, at, :] = u_parts[k][...]
        rights[1, at, :] = c_parts[k][...]
    span = 2 * quarter

    @pl.loop(0, 4)
    def _(k):
        at = tile(k, span)
        g = mm_nt(gate[...], rights[0, at, :])
        a = mm_nt(up[...], rights[0, at, :])
        gh = mm_nt(down[...].reshape(rows, channels), rights[1, at, :])
        sg = sigmoid(g)
        silu = g * sg
        lefts[0, :, at] = (gh * a * (sg * (1.0 + g * (1.0 - sg)))).astype(BF16)
        lefts[1, :, at] = (gh * silu).astype(BF16)
        lefts[2, :, at] = (silu * a).astype(BF16)

    d_out[...] = mm_nt(gt_own[...], z_own[...]) + mm_nt(gt_got[...], z_got[...])
    half = keep_o.shape[0]
    x = at_ref[0] >> 1
    keep_o[...] = d_out[tile(x, half), :].astype(BF16)
    give_o[...] = d_out[tile(1 - x, half), :].astype(BF16)
    fw = rows // 4
    cut = keep_a.shape[-1]

    @pl.loop(0, 3)
    def _(m):
        grad = mm(lefts[m], rights[m >> 1]).astype(BF16)
        for i in range(4):
            d_all[i, m] = grad[i * fw : (i + 1) * fw]

    for i in range(2):
        keep_a[i] = d_all[2 * i + y, :, :, :cut]
        give_a[i] = d_all[2 * i + 1 - y, :, :, :cut]
        keep_b[i] = d_all[2 * z + i, :, :, cut:]
        give_b[i] = d_all[2 * (1 - z) + i, :, :, cut:]


def hidden_grads(at, u2_parts, ct_parts, gate, up, gt_own, gt_got, z_own, z_got, down, after):
    quarter, channels = u2_parts[0].shape
    wide = gate.shape[0]
    bs, fs, fw, _ = down.shape
    cut = 2 * channels // 3
    down = down.reshape(2, 2, 2, fs, fw, channels)
    down_spec = pl.BlockSpec((2, 1, 2, 1, fw, channels), lambda i, at: (0, at[2], 0, at[0], 0, 0))
    return pl.pallas_call(
        hidden_grads_kernel,
        grid_spec=pltpu.PrefetchScalarGridSpec(
            num_scalar_prefetch=1,
            grid=(1,),
            in_specs=[VM] * 22 + [down_spec, HBM],
            out_specs=[VM] * 6,
            scratch_shapes=[
                pltpu.VMEM((2, 8 * quarter, channels), BF16),
                pltpu.VMEM((3, wide, 8 * quarter), BF16),
                pltpu.VMEM((4, 3, fw, channels), BF16),
                pltpu.VMEM((2 * channels // fs, channels), F32),
            ],
        ),
        out_shape=[shape((2, 3, fw, cut), BF16)] * 2
        + [shape((2, 3, fw, channels - cut), BF16)] * 2
        + [shape((channels // fs, channels), BF16)] * 2,
        compiler_params=params(34),
        cost_estimate=cost(14),
        name="hidden_grads",
    )(at, *u2_parts, *ct_parts, gate, up, gt_own, gt_got, z_own, z_got, in_hbm(down), after)


def halve_kernel(at_ref, after, *refs, bits, extra):
    pairs = len(bits)
    if extra:
        ours, theirs, out = refs[2 * pairs], refs[2 * pairs + 1], refs[-1]
        out[...] = (ours[...].astype(F32) + theirs[...].astype(F32)).astype(BF16)
        refs = refs[: 2 * pairs] + refs[2 * pairs + 2 : -1]
    ins, outs = refs[: 2 * pairs], refs[2 * pairs :]
    for n in range(pairs):
        mine = at_ref[bits[n] + 1]
        keep, got = ins[2 * n], ins[2 * n + 1]
        next_keep, next_give = outs[2 * n], outs[2 * n + 1]
        for i in range(keep.shape[0]):
            for side, out in ((mine, next_keep), (1 - mine, next_give)):
                out[i] = (keep[i, side].astype(F32) + got[i, side].astype(F32)).astype(BF16)


def halve(at, bits, after, *sums):
    outs = []
    extra = len(sums) > 2 * len(bits)
    for n in range(len(bits)):
        dims = sums[2 * n].shape
        outs += [shape((dims[0],) + dims[2:], BF16)] * 2
    if extra:
        outs.append(shape(sums[-1].shape, BF16))
    return pl.pallas_call(
        functools.partial(halve_kernel, bits=bits, extra=extra),
        in_specs=[SM, HBM] + [VM] * len(sums),
        out_specs=[VM] * len(outs),
        out_shape=outs,
        compiler_params=params(24),
        cost_estimate=cost(0.3),
        name="halve",
    )(at, after, *sums)


def join_kernel(at_ref, after, keep_a, got_a, keep_b, got_b, ours, theirs, keep, give, total):
    total[...] = (ours[...].astype(F32) + theirs[...].astype(F32)).astype(BF16)
    cut = keep_a.shape[-1]
    for side, out in ((at_ref[3], keep), (1 - at_ref[3], give)):
        out[:, :cut] = (keep_a[side].astype(F32) + got_a[side].astype(F32)).astype(BF16)
        out[:, cut:] = (keep_b[side].astype(F32) + got_b[side].astype(F32)).astype(BF16)


def join(at, after, keep_a, got_a, keep_b, got_b, ours, theirs):
    _, rows, cut = keep_a.shape
    return pl.pallas_call(
        join_kernel,
        in_specs=[SM, HBM] + [VM] * 6,
        out_specs=[VM] * 3,
        out_shape=[shape((rows, cut + keep_b.shape[-1]), BF16)] * 2 + [shape(ours.shape, BF16)],
        compiler_params=params(12),
        cost_estimate=cost(0.3),
        name="join",
    )(at, after, keep_a, got_a, keep_b, got_b, ours, theirs)


def hidden_last_kernel(keep_a, got_a, keep_b, got_b, after, *outs):
    cut = keep_a.shape[-1]
    for m, out in enumerate(outs):
        out[:, :cut] = keep_a[0, m].astype(F32) + got_a[0, m].astype(F32)
        out[:, cut:] = keep_b[0, m].astype(F32) + got_b[0, m].astype(F32)


def hidden_last(keep_a, got_a, keep_b, got_b, after):
    _, count, rows, cut = keep_a.shape
    return pl.pallas_call(
        hidden_last_kernel,
        in_specs=[VM] * 4 + [HBM],
        out_specs=[VM] * count,
        out_shape=[far((rows, cut + keep_b.shape[-1]), F32)] * count,
        compiler_params=params(12),
        cost_estimate=cost(0.3),
        name="hidden_last",
    )(keep_a, got_a, keep_b, got_b, after)


def add_kernel(ours, theirs, after, out):
    out[...] = (ours[...].astype(F32) + theirs[...].astype(F32)).astype(out.dtype)


def add(ours, theirs, after, dtype):
    return pl.pallas_call(
        add_kernel,
        in_specs=[VM, VM, HBM],
        out_specs=VM,
        out_shape=shape(ours.shape, dtype),
        compiler_params=params(8),
        cost_estimate=cost(0.3),
        name="add",
    )(ours, theirs, after)


def projection_kernel(
    at_ref, gp, u1, n1, w_mine, keep_o, got_o, d_w2, d_w1, d_taps, gcb, condt, mu, mn,
    sums2, after, keep_a, give_a, keep_b, give_b, packed_out, d_in, d_out, packed, *, layout,
):
    me, y, zbit = at_ref[0], at_ref[1], at_ref[2]
    channels = u1.shape[1]
    width = keep_o.shape[0]
    d_in[...] = mm(gp[...], u1[...])
    d_out[...] = keep_o[...].astype(F32) + got_o[...].astype(F32)
    blocks = 2 * keep_a.shape[0]
    first = 2 * width // blocks
    second = width // blocks
    cut = 2 * channels // 3

    def put(out, block, lanes):
        lo = pl.multiple_of(block * first, first)
        out[:first, :] = d_in[pl.ds(lo, first), lanes].astype(BF16)
        lo = pl.multiple_of(block * second, second)
        out[first:, :] = d_out[pl.ds(lo, second), lanes].astype(BF16)

    for b in range(blocks // 2):
        put(keep_a.at[b], 2 * b + y, slice(0, cut))
        put(give_a.at[b], 2 * b + 1 - y, slice(0, cut))
    for b in range(blocks // 4):
        for i in range(2):
            put(keep_b.at[b, i], 4 * b + 2 * zbit + i, slice(cut, channels))
            put(give_b.at[b, i], 4 * b + 2 * (1 - zbit) + i, slice(cut, channels))
    packed[...] = jnp.zeros_like(packed)
    packed[:width, :] = jnp.concatenate([d_w2[:width, :], d_w2[width:, :]], axis=1)
    taps_t = jnp.transpose(d_taps[...])
    gcb_t = jnp.transpose(gcb[...])[:8, :]
    gmu = lax.dot_general(
        gcb_t, condt[...], (((1,), (0,)), ((), ())), precision=HIGH, preferred_element_type=F32
    )
    gp_n = mm(gp[...], n1[...])
    w32 = w_mine[...].astype(F32)
    gain = jnp.sum(gp_n * w32, axis=0, keepdims=True) + jnp.sum(gmu * mn[...], axis=0, keepdims=True)
    total = jnp.sum(gp[...].astype(F32), axis=1, keepdims=True)
    shift = jnp.sum(total * w32, axis=0, keepdims=True) + jnp.sum(gmu, axis=0, keepdims=True)
    for i in range(3):
        for m in range(2 * width // 128):
            at = layout["taps"] + i * (2 * width // 128) + m
            packed[at : at + 1, :] = taps_t[i : i + 1, m * 128 : (m + 1) * 128]
    for i, row in enumerate((gain, shift, sums2[0:1, :], sums2[1:2, :])):
        for m in range(channels // 128):
            at = layout["ln"] + i * (channels // 128) + m
            packed[at : at + 1, :] = row[:, m * 128 : (m + 1) * 128]
    half = d_w1.shape[0] // 2
    packed[layout["w1"] : layout["w1"] + half, :] = jnp.concatenate(
        [d_w1[:half, :], d_w1[half:, :]], axis=1
    )
    zeros = jnp.zeros_like(gcb_t)
    row = at_ref[4]
    odd = (row & 1) == 1
    both = jnp.concatenate([jnp.where(odd, zeros, gcb_t), jnp.where(odd, gcb_t, zeros)], axis=1)
    packed[pl.ds(pl.multiple_of(layout["cb"] + 8 * (row >> 1), 8), 8), :] = both
    share = jnp.zeros((8, width), F32)
    for f in range(channels // width):
        share = share + jnp.where(me == f, mu[:, f * width : (f + 1) * width], 0.0)
    rest = jnp.concatenate([share[:SEGS, 128:], jnp.zeros((SEGS, 256 - width), F32)], axis=1)
    block = jnp.concatenate([share[:SEGS, :128], rest, jnp.zeros((8 - 2 * SEGS, 128), F32)], axis=0)
    packed[pl.ds(pl.multiple_of(layout["mu"] + 8 * row, 8), 8), :] = block
    packed_out[...] = packed[...].astype(BF16)


def packed_layout(width, channels, bs):
    taps = width
    ln = taps + 3 * (2 * width // 128)
    w1 = -(-(ln + 4 * (channels // 128)) // 8) * 8
    cb = w1 + 32
    mu = cb + 4 * bs
    return {"taps": taps, "ln": ln, "w1": w1, "cb": cb, "mu": mu, "rows": -(-(mu + 8 * bs) // 16) * 16}


def projection_grads(
    at, gp, u1, n1, w_mine, keep_o, got_o, d_w2, d_w1, d_taps, gcb, condt, mu, mn, sums2, after, bs
):
    length, channels = u1.shape
    width = keep_o.shape[0]
    layout = packed_layout(width, channels, bs)
    return pl.pallas_call(
        functools.partial(projection_kernel, layout=layout),
        in_specs=[SM] + [VM] * 14 + [HBM],
        out_specs=[VM] * 5,
        out_shape=[shape((bs // 2, 3 * width // bs, 2 * channels // 3), BF16)] * 2
        + [shape((bs // 4, 2, 3 * width // bs, channels // 3), BF16)] * 2
        + [shape((layout["rows"], 128), BF16)],
        scratch_shapes=[
            pltpu.VMEM((2 * width, channels), F32),
            pltpu.VMEM((width, channels), F32),
            pltpu.VMEM((layout["rows"], 128), F32),
        ],
        compiler_params=params(24),
        cost_estimate=cost(2),
        name="projection_grads",
    )(
        at, gp, u1, n1, w_mine, keep_o, got_o, d_w2, d_w1, d_taps, gcb, condt, mu, mn, sums2, after
    )


def final_kernel(
    me_ref, p0, p1, p2, p3, x, big_g, norms, ids_row, condt, w_in, after, out, gp_t, *, piece
):
    me = me_ref[0]
    rows = gp_t.shape[0] // 4
    hidden = condt.shape[0]
    share = jnp.zeros((8, hidden), F32)
    for k, part in enumerate((p0, p1, p2, p3)):
        for i in range(rows // piece):
            at = pl.ds(pl.multiple_of((i * 4 + (me ^ k)) * piece, piece), piece)
            gp_t[at, :] = part[i * piece : (i + 1) * piece, :]
        extra = part[rows:, :hidden].astype(F32)
        share = share + extra[:8] + extra[8:]
    ids = ids_row[...]
    number = lax.broadcasted_iota(jnp.int32, (8, ids.shape[1]), 0)
    counts = jnp.sum(jnp.where(ids == number, 1.0, 0.0), axis=1, keepdims=True)
    gmu = lax.dot_general(
        share, condt[...], (((1,), (0,)), ((), ())), precision=HIGH, preferred_element_type=F32
    ) / jnp.maximum(counts, 1.0)
    gu1 = mm_nt(jnp.transpose(gp_t[...]), w_in[...])
    quarter = x.shape[0]
    own = jnp.broadcast_to(ids_row[:, tile(me, quarter)].astype(F32), (8, quarter))
    ids_own = jnp.transpose(own)[:, 0:1]
    for j in range(SEGS):
        gu1 = gu1 + jnp.where(ids_own == j, gmu[j : j + 1, :], 0.0)
    unit, scale = normed(x[...].astype(F32))
    out[...] = big_g[...] + norm_back(unit, scale, gu1 * norms[0:1, :])


def final(me, gp_parts, x, big_g, norms, ids, condt, w_in, after, piece):
    quarter, channels = x.shape
    return pl.pallas_call(
        functools.partial(final_kernel, piece=piece),
        in_specs=[SM] + [VM] * 10 + [HBM],
        out_specs=VM,
        out_shape=shape((quarter, channels), F32),
        scratch_shapes=[pltpu.VMEM((2 * channels, quarter), BF16)],
        compiler_params=params(24),
        cost_estimate=cost(1),
        name="final",
    )(me, *gp_parts, x, big_g, norms, ids, condt, in_hbm(w_in), after)


def small_kernel(
    me_ref, j0, j1, j2, j3, w2, taps, ln0, ln1, ln2, ln3, w1, b1, cond, wide, tap_t, cond_t, *, layout, step, width
):
    me = me_ref[0]
    parts = [part[...].astype(F32) for part in (j0, j1, j2, j3)]
    hidden = w1.shape[0]
    half = width // step
    count = 2 * width // 128
    for k, part in enumerate(parts):
        who = me ^ k
        rows = jnp.concatenate(
            [
                jnp.concatenate([part[layout["taps"] + i * count + m : layout["taps"] + i * count + m + 1, :]
                                 for m in range(count)], axis=1)
                for i in range(3)
            ]
            + [jnp.zeros((125, 2 * width), F32)],
            axis=0,
        )
        tap_t[...] = jnp.transpose(rows)
        for side in range(2):
            for i in range(half):
                at = pl.ds(pl.multiple_of((side * half * 4 + i * 4 + who) * step, step), step)
                lo = i * step
                wide[at, :hidden] = part[lo : lo + step, side * hidden : (side + 1) * hidden]
                at2 = side * width + lo
                wide[at, hidden:] = tap_t[at2 : at2 + step, :hidden]
    whole = jnp.transpose(wide[...])
    w2[...] = whole[:hidden, :]
    taps[...] = whole[hidden : hidden + 3, :]

    def common(first, last):
        a, b, c, d = [part[first:last, :] for part in parts]
        return (a + b) + (c + d)

    lanes = ln0.shape[0] // 128
    sums = common(layout["ln"], layout["ln"] + 4 * lanes)
    for i, out in enumerate((ln0, ln1, ln2, ln3)):
        row = jnp.concatenate([sums[i * lanes + m : i * lanes + m + 1, :] for m in range(lanes)], axis=1)
        out[...] = row.reshape(out.shape)
    both = common(layout["w1"], layout["w1"] + hidden // 2)
    w1[: hidden // 2, :] = both[:, :hidden]
    w1[hidden // 2 :, :] = both[:, hidden:]
    cb = common(layout["cb"], layout["mu"])
    shares = []
    for b in range(cb.shape[0] // 4):
        lo = 8 * (b // 2)
        shares.append(cb[lo : lo + 8, (b % 2) * hidden : (b % 2 + 1) * hidden])
    shares = jnp.concatenate(shares, axis=0)
    b1[...] = jnp.sum(shares, axis=0, keepdims=True)
    for k, part in enumerate(parts):
        rows = []
        for b in range(cb.shape[0] // 4):
            lo = layout["mu"] + 8 * b
            block = part[lo : lo + 8, :]
            rows.append(
                jnp.concatenate(
                    [
                        jnp.concatenate([block[:SEGS, :], jnp.zeros((8 - SEGS, 128), F32)], axis=0),
                        jnp.concatenate(
                            [block[SEGS : 2 * SEGS, : width - 128], jnp.zeros((8 - SEGS, width - 128), F32)],
                            axis=0,
                        ),
                    ],
                    axis=1,
                )
            )
        mu = jnp.concatenate(rows, axis=0)
        cond_t[tile(me ^ k, width), :] = lax.dot_general(
            jnp.transpose(mu), shares, (((1,), (0,)), ((), ())), precision=HIGH, preferred_element_type=F32
        )
    cond[...] = jnp.transpose(cond_t[...])


def small_grads(me, parts, hidden, channels, step, bs):
    width = channels // 4
    layout = packed_layout(width, channels, bs)
    return pl.pallas_call(
        functools.partial(small_kernel, layout=layout, step=step, width=width),
        in_specs=[SM] + [VM] * 4,
        out_specs=[VM] * 9,
        out_shape=[
            far((hidden, 2 * channels), F32),
            far((3, 2 * channels), F32),
            far((channels,), F32),
            far((channels,), F32),
            far((channels,), F32),
            far((channels,), F32),
            far((hidden, hidden), F32),
            far((1, hidden), F32),
            far((hidden, channels), F32),
        ],
        scratch_shapes=[
            pltpu.VMEM((2 * channels, 2 * hidden), F32),
            pltpu.VMEM((2 * width, 128), F32),
            pltpu.VMEM((channels, hidden), F32),
        ],
        compiler_params=params(24),
        cost_estimate=cost(3),
        name="small_grads",
    )(me, *parts)


def trade_parts(parts):
    two, three, one = [swap(parts[k], "freq", k) for k in (2, 3, 1)]
    return (parts[0], one, two, three)


def tiled_device(
    tokens,
    seg_ids,
    cotangent,
    ln1_gain,
    ln1_shift,
    w_in,
    conv_taps,
    freq_w1,
    freq_b1,
    freq_w2,
    cond_w,
    w_out,
    ln2_gain,
    ln2_shift,
    w_gate,
    w_up,
    w_down,
):
    quarter, _, channels = tokens.shape
    length = seg_ids.shape[1]
    ff = w_gate.shape[1]
    fs = lax.axis_size("freq")
    bs = lax.axis_size("batch")
    me = lax.axis_index("freq")
    row = lax.axis_index("batch")
    width = channels // fs
    half = bs // 2
    step = channels // (half * fs)
    fw = ff // (bs * fs)
    table = np.concatenate(tables(length), axis=0)
    feats = features(length, freq_w1.shape[0] // 2)
    feats_aug = np.concatenate(
        [feats, np.ones((1, length), np.float32), np.zeros((7, length), np.float32)], axis=0
    )

    x_own = tokens[:, 0]
    ct_own = cotangent[:, 0]
    ids = seg_ids
    at = jnp.stack([me, row & 1, (row >> 1) & 1, (row >> 2) & 1, row]).astype(jnp.int32)
    norms = jnp.concatenate([ln1_gain, ln1_shift, ln2_gain, ln2_shift]).reshape(4, channels)
    condt = cond_w.T

    def gather_after(value, after):
        two = swap(value, "freq", 2)
        one = swap(value, "freq", 1)
        (two,) = tie([two], after)
        return (value, one, two, swap(two, "freq", 1))

    def gather_wide(value, after):
        count = bs * fs
        parts = (
            value,
            swap(value, "freq", 2),
            swap(value, "batch", 2),
            lax.ppermute(value, ("batch", "freq"), [(i, i ^ (2 * fs + 2)) for i in range(count)]),
        )
        parts = parts[:1] + tuple(tie(parts[1:], after))
        return parts + tuple(swap(part, "freq", 1) for part in parts)

    def pairs(value):
        return value.reshape((value.shape[0] // 2, 2) + value.shape[1:])

    w_mine, w2x, w2t, taps, base, waves = prepare(
        at, w_in, freq_w2, conv_taps, freq_w1, freq_b1, jnp.asarray(feats_aug), jnp.asarray(table), norms, step, fs
    )
    x_parts = gather_after(x_own, base)
    forward = forward_spectral(at, x_parts, ids, norms, w_mine, taps, base, w2x, condt, waves)
    z_parts, (u1, n1, p, q, c, vr, vs, mu, mn, cb) = forward[:4], forward[4:]
    ct_x = swap(ct_own, "freq", 2)
    ct_z = swap(ct_own, "batch", 2)
    z_got = trade_parts(z_parts)
    wg_mine, wu_mine = select_columns(at, cb, w_gate, w_up, bs, fs)
    (ct_x,) = tie([ct_x], cb)
    ct_parts = (ct_own, ct_x, ct_z, swap(ct_x, "batch", 2))
    h, u2, z_t = middle(at, z_got, x_own, w_out, norms, wg_mine, step)
    fed = feed_forward(
        at, u2, h, ct_own, norms, w_out, w_gate, w_up, w_down, step, channels // (bs * fs)
    )
    mixed_out, big_g, gz_parts, gt_own, gt_other, sums2 = fed[0], fed[1], fed[2:6], *fed[6:]
    u2_parts = gather_wide(u2, sums2)
    ct_parts = ct_parts + tuple(swap(part, "freq", 1) for part in tie(ct_parts, sums2))
    gz_got = trade_parts(gz_parts)

    gt_got = swap(gt_other, "freq", 1)
    z_got = swap(z_t, "freq", 1)
    keep_a, give_a, keep_b, give_b, keep_o, give_o = hidden_grads(
        at, u2_parts, ct_parts, wg_mine, wu_mine, gt_own, gt_got, z_t, z_got,
        w_down.reshape(bs, fs, fw, channels), sums2,
    )
    got_a = swap(give_a, "batch", 1)
    got_b = swap(give_b, "batch", 4)
    got_o = swap(give_o, "freq", 2)

    back = backward_spectral(
        at, gz_got, ids, cb, taps, base, w2x, w2t, jnp.asarray(feats).astype(BF16),
        p, q, c, vr, vs, waves, give_a,
    )
    gp_parts, (gp, d_taps, d_w2, d_w1, gcb) = back[:4], back[4:]
    gp_got = trade_parts(gp_parts)

    keep_a, give_a, keep_b, give_b = halve(
        at, (2, 0), gp, keep_a[None], got_a[None], keep_b[None], got_b[None]
    )
    got_a = swap(give_a, "batch", 4)
    got_b = swap(give_b, "batch", 1)

    proj = projection_grads(
        at, gp, u1, n1, w_mine, keep_o, got_o, d_w2, d_w1, d_taps, gcb, condt, mu, mn, sums2, give_a, bs
    )
    p_keep_a, p_give_a, p_keep_b, p_give_b, packed = proj
    p_got_a = swap(p_give_a, "batch", 1)
    p_got_b = swap(p_give_b, "batch", 2)
    got_packed = swap(packed, "batch", 1)
    grad_tokens = final(at, gp_got, x_own, big_g, norms, ids, condt, w_in, packed, step)

    p_keep_a, p_give_a, p_keep_b, p_give_b, packed = halve(
        at, (1, 0), grad_tokens, pairs(p_keep_a), pairs(p_got_a), p_keep_b, p_got_b, packed, got_packed
    )
    p_got_a = swap(p_give_a, "batch", 2)
    p_got_b = swap(p_give_b, "batch", 1)
    got_packed = swap(packed, "batch", 2)
    d_gate, d_up, d_down = hidden_last(keep_a, got_a, keep_b, got_b, packed)
    keep, give, packed = join(
        at, d_down, p_keep_a, p_got_a, p_keep_b, p_got_b, packed, got_packed
    )
    got = swap(give, "batch", 4)
    sent = add(packed, swap(packed, "batch", 4), give, BF16)
    mine = keep.astype(F32) + got.astype(F32)
    first = 2 * width // bs

    d_w2, d_taps, *ln, d_w1, d_b1, d_cond = small_grads(
        at, gather_freq(sent, me), freq_w1.shape[1], channels, step, bs
    )
    return (
        mixed_out[:, None],
        grad_tokens[:, None],
        ln[0],
        ln[1],
        mine[:first].T,
        d_taps,
        d_w1,
        d_b1[0],
        d_w2,
        d_cond.T,
        mine[first:].T,
        ln[2],
        ln[3],
        d_gate.T,
        d_up.T,
        d_down,
    )


def per_device(*args):
    channels = args[0].shape[2]
    step = 2 * channels // (lax.axis_size("batch") * lax.axis_size("freq"))
    fits = lax.axis_size("batch") == 8 and lax.axis_size("freq") == 4 and step % 16 == 0
    return tiled_device(*args) if fits else plain_device(*args)


def solution(mesh):
    rows = P("freq", "batch", None)
    split = P(None, ("batch", "freq"))
    in_specs = (rows, P("batch", None), rows) + (P(),) * 14
    out_specs = (
        rows,
        rows,
        P(),
        P(),
        split,
        P(),
        P(),
        P(),
        P(),
        P(),
        split,
        P(),
        P(),
        split,
        split,
        P(("batch", "freq"), None),
    )
    return jax.shard_map(
        per_device, mesh=mesh, in_specs=in_specs, out_specs=out_specs, check_vma=False
    )
```

```python
import functools

import jax
import jax.numpy as jnp
import ml_dtypes
import numpy as np
from jax import lax
from jax.experimental import pallas as pl
from jax.experimental.pallas import tpu as pltpu
from jax.sharding import PartitionSpec as P

SEGS = 3
EPS = 1e-05
HIGH = lax.Precision.HIGHEST
F32 = jnp.float32
BF16 = jnp.bfloat16


def mm(a, b):
    return jnp.dot(a, b, preferred_element_type=F32)


def mm_nt(a, b):
    return lax.dot_general(a, b, (((1,), (1,)), ((), ())), preferred_element_type=F32)


def mm_tn(a, b):
    return lax.dot_general(a, b, (((0,), (0,)), ((), ())), preferred_element_type=F32)


def swap(value, axis, mask):
    count = lax.axis_size(axis)
    return lax.ppermute(value, axis, [(i, i ^ mask) for i in range(count)])


def pick(parts, index):
    return lax.dynamic_index_in_dim(parts, index, 0, keepdims=False)


def in_order(received, me):
    a, b, c, d = received
    low = (me & 1) == 1
    a, b = jnp.where(low, b, a), jnp.where(low, a, b)
    c, d = jnp.where(low, d, c), jnp.where(low, c, d)
    high = (me & 2) == 2
    a, c = jnp.where(high, c, a), jnp.where(high, a, c)
    b, d = jnp.where(high, d, b), jnp.where(high, b, d)
    return (a, b, c, d)


def trade(blocks, me):
    return [pick(blocks, me)] + [swap(pick(blocks, me ^ k), "freq", k) for k in (2, 3, 1)]


def trade_sorted(blocks, me):
    own, two, three, one = trade(blocks, me)
    return in_order((own, one, two, three), me)


def gather_freq(value, me):
    two = swap(value, "freq", 2)
    one = swap(value, "freq", 1)
    three = swap(two, "freq", 1)
    return (value, one, two, three)


def scatter_sum(value, order):
    bits = lax.axis_size("batch").bit_length() - 1
    me = lax.axis_index("batch")
    rest = value.shape[1:]
    value = value.reshape((2,) * bits + rest)
    left = list(range(bits - 1, -1, -1))
    for bit in order:
        dim = left.index(bit)
        mine = (me >> bit) & 1
        keep = lax.dynamic_index_in_dim(value, mine, dim, keepdims=False)
        give = lax.dynamic_index_in_dim(value, 1 - mine, dim, keepdims=False)
        got = swap(give, "batch", 1 << bit)
        total = keep.astype(F32) + got.astype(F32)
        left.remove(bit)
        value = total.astype(value.dtype) if left else total
    return value


def tables(length):
    index = np.arange(length, dtype=np.int64)
    angle = (index[:, None] * index[None, :] % (2 * length)) * (np.pi / length)
    return (
        np.cos(angle).astype(ml_dtypes.bfloat16),
        np.sin(angle).astype(ml_dtypes.bfloat16),
    )


def features(length, half):
    index = np.arange(length, dtype=np.int64)
    lags = (np.arange(half, dtype=np.int64) + 1) ** 2
    angle = (lags[:, None] * index[None, :] % (2 * length)) * (np.pi / length)
    return np.concatenate([np.cos(angle), np.sin(angle)], axis=0).astype(np.float32)


def normed(values):
    centered = values - jnp.mean(values, axis=-1, keepdims=True)
    scale = lax.rsqrt(jnp.mean(centered * centered, axis=-1, keepdims=True) + EPS)
    return centered * scale, scale


def norm_back(unit, scale, grad):
    return scale * (
        grad
        - jnp.mean(grad, axis=-1, keepdims=True)
        - unit * jnp.mean(grad * unit, axis=-1, keepdims=True)
    )


def shift_right(values):
    return jnp.pad(values, ((0, 0), (1, 0)))[:, :-1]


def shift_left(values):
    return jnp.pad(values, ((0, 0), (0, 1)))[:, 1:]


def plain_device(
    tokens,
    seg_ids,
    cotangent,
    ln1_gain,
    ln1_shift,
    w_in,
    conv_taps,
    freq_w1,
    freq_b1,
    freq_w2,
    cond_w,
    w_out,
    ln2_gain,
    ln2_shift,
    w_gate,
    w_up,
    w_down,
):
    quarter, _, channels = tokens.shape
    length = seg_ids.shape[1]
    ff = w_gate.shape[1]
    fs = lax.axis_size("freq")
    bs = lax.axis_size("batch")
    me = lax.axis_index("freq")
    width = channels // fs
    half = bs // 2
    step = channels // (half * fs)
    cos_table, sin_table = tables(length)
    feats = features(length, freq_w1.shape[0] // 2)

    x_own = tokens[:, 0]
    ct_own = cotangent[:, 0]
    ids = seg_ids
    x_parts = gather_freq(x_own, me)
    ct_parts = gather_freq(ct_own, me)

    w_in_t = (
        w_in.T.reshape(2, half, fs, step, channels)
        .transpose(2, 0, 1, 3, 4)
        .reshape(fs, 2 * width, channels)
    )
    w_in_mine = pick(w_in_t, me)
    w_out_p = (
        w_out.reshape(half, fs, step, channels).transpose(1, 0, 2, 3).reshape(channels, channels)
    )
    taps_mine = pick(
        conv_taps.reshape(3, 2, half, fs, step).transpose(3, 0, 1, 2, 4).reshape(fs, 3, 2 * width), me
    )[:, :, None]
    w2_mine = pick(
        freq_w2.reshape(-1, 2, half, fs, step).transpose(3, 0, 1, 2, 4).reshape(fs, -1, 2 * width), me
    )
    fw = ff // (bs * fs)
    wide = ff // fs

    def mine_rows(weight):
        return pick(
            weight.reshape(bs, fs, fw, channels).transpose(1, 0, 2, 3).reshape(fs, wide, channels), me
        )

    wg_mine, wu_mine, wd_mine = (mine_rows(w_gate.T), mine_rows(w_up.T), mine_rows(w_down))

    base = jnp.dot(freq_w1.T, feats, precision=HIGH) + freq_b1[:, None]

    x_row = jnp.concatenate(in_order(x_parts, me), axis=0).astype(F32)
    unit1, _ = normed(x_row)
    u1 = (unit1 * ln1_gain + ln1_shift).astype(BF16)
    n1 = unit1.astype(BF16)
    masks = (ids == jnp.arange(SEGS, dtype=jnp.int32)[:, None]).astype(F32)
    counts = jnp.sum(masks, axis=1, keepdims=True)
    mu = mm(masks.astype(BF16), u1) / counts
    mn = mm(masks.astype(BF16), n1) / counts
    cb = jnp.dot(mu, cond_w, precision=HIGH)
    p = mm_nt(w_in_mine, u1)
    same = (ids[:, 1:] == ids[:, :-1]).astype(F32)
    zero = jnp.zeros((1, 1), F32)
    prev = jnp.concatenate([zero, same], axis=1)
    nxt = jnp.concatenate([same, zero], axis=1)
    p_prev = shift_right(p) * prev
    p_next = shift_left(p) * nxt
    s = taps_mine[0] * p_prev + taps_mine[1] * p + taps_mine[2] * p_next
    q, v = s[:width], s[width:]

    pre = base[None] + cb[:, :, None]
    gate_pre = jax.nn.sigmoid(pre)
    hk = pre * gate_pre
    kk = jnp.einsum("kc,jkf->jcf", w2_mine, hk, precision=HIGH)
    kr, ki = kk[:, :width], kk[:, width:]
    vm = (v[None] * masks[:, None, :]).astype(BF16).reshape(SEGS * width, length)
    vr = mm(vm, cos_table).reshape(SEGS, width, length)
    vi = -mm(vm, sin_table).reshape(SEGS, width, length)
    weights = np.full((length,), 2.0 / (2 * length), np.float32)
    weights[0] = 1.0 / (2 * length)
    yr = ((kr * vr - ki * vi) * weights).astype(BF16).reshape(SEGS * width, length)
    yi = ((kr * vi + ki * vr) * weights).astype(BF16).reshape(SEGS * width, length)
    conv = (mm(yr, cos_table) - mm(yi, sin_table)).reshape(SEGS, width, length)
    c = jnp.sum(conv * masks[:, None, :], axis=0)
    z_mine = (q * c).astype(BF16)

    z_blocks = z_mine.reshape(width, fs, quarter).transpose(1, 0, 2)
    z_t = jnp.concatenate(trade_sorted(z_blocks, me), axis=0)

    x32 = x_own.astype(F32)
    ct32 = ct_own.astype(F32)
    h = x32 + mm_tn(z_t, w_out_p)
    unit2, scale2 = normed(h)
    u2 = (unit2 * ln2_gain + ln2_shift).astype(BF16)
    u2_parts = gather_freq(u2, me)
    g = mm(u2, w_gate)
    a = mm(u2, w_up)
    gh = mm_nt(ct_own, w_down)
    sg = jax.nn.sigmoid(g)
    silu = g * sg
    hid = (silu * a).astype(BF16)
    mixed_out = (h + mm(hid, w_down)).astype(BF16)
    gg = (gh * a * sg * (1.0 + g * (1.0 - sg))).astype(BF16)
    ga = (gh * silu).astype(BF16)
    gu2 = mm_nt(gg, w_gate) + mm_nt(ga, w_up)
    grad_ln2_gain = jnp.sum(gu2 * unit2, axis=0)
    grad_ln2_shift = jnp.sum(gu2, axis=0)
    big_g = ct32 + norm_back(unit2, scale2, gu2 * ln2_gain)
    gb = big_g.astype(BF16)
    gz_blocks = mm_nt(w_out_p, gb).astype(BF16).reshape(fs, width, quarter)
    gz = jnp.concatenate(trade_sorted(gz_blocks, me), axis=1).astype(F32)
    gb_parts = gather_freq(gb, me)

    u2_row = jnp.concatenate(u2_parts, axis=0)
    ct_row = jnp.concatenate(ct_parts, axis=0)
    g_t = mm_nt(wg_mine, u2_row)
    a_t = mm_nt(wu_mine, u2_row)
    gh_t = mm_nt(wd_mine, ct_row)
    sg_t = jax.nn.sigmoid(g_t)
    silu_t = g_t * sg_t
    hid_t = (silu_t * a_t).astype(BF16)
    gg_t = (gh_t * a_t * sg_t * (1.0 + g_t * (1.0 - sg_t))).astype(BF16)
    ga_t = (gh_t * silu_t).astype(BF16)
    d_gate = mm(gg_t, u2_row).astype(BF16)
    d_up = mm(ga_t, u2_row).astype(BF16)
    d_down = mm(hid_t, ct_row).astype(BF16)
    d_ff = jnp.stack([d_gate, d_up, d_down], axis=0).reshape(3, bs, fw, channels).transpose(1, 0, 2, 3)
    bits = bs.bit_length() - 1
    order_a = list(range(bits))
    order_b = [1, 0] + list(range(2, bits))
    cut = channels // 2
    ff_a = scatter_sum(d_ff[..., :cut], order_a)
    ff_b = scatter_sum(d_ff[..., cut:], order_b)
    d_ff = jnp.concatenate([ff_a, ff_b], axis=-1)

    gq = gz * c
    gc = gz * q
    gcm = (gc[None] * masks[:, None, :]).astype(BF16).reshape(SEGS * width, length)
    gyr = mm(gcm, cos_table).reshape(SEGS, width, length) * weights
    gyi = -mm(gcm, sin_table).reshape(SEGS, width, length) * weights
    gkr = gyr * vr + gyi * vi
    gki = gyi * vr - gyr * vi
    gvr = (kr * gyr + ki * gyi).astype(BF16).reshape(SEGS * width, length)
    gvi = (kr * gyi - ki * gyr).astype(BF16).reshape(SEGS * width, length)
    gv_all = (mm(gvr, cos_table) - mm(gvi, sin_table)).reshape(SEGS, width, length)
    gv = jnp.sum(gv_all * masks[:, None, :], axis=0)
    gs = jnp.concatenate([gq, gv], axis=0)
    d_taps = jnp.stack(
        [jnp.sum(gs * p_prev, axis=1), jnp.sum(gs * p, axis=1), jnp.sum(gs * p_next, axis=1)]
    )
    gp = (
        taps_mine[1] * gs
        + taps_mine[0] * shift_left(gs * prev)
        + taps_mine[2] * shift_right(gs * nxt)
    ).astype(BF16)

    gkk = jnp.concatenate([gkr, gki], axis=1)
    gkk_low = gkk.astype(BF16)
    hk_low = hk.astype(BF16)
    d_w2 = jnp.einsum("jkf,jcf->kc", hk_low, gkk_low, preferred_element_type=F32)
    gpre = jnp.einsum("kc,jcf->jkf", w2_mine.astype(BF16), gkk_low, preferred_element_type=F32)
    gpre = gpre * gate_pre * (1.0 + pre * (1.0 - gate_pre))
    d_w1 = jnp.einsum("ef,jkf->ek", feats, gpre, precision=HIGH)
    gcb = jnp.sum(gpre, axis=2)
    gcb_row = lax.psum(gcb, "freq")

    gp_blocks = gp.reshape(2 * width, fs, quarter).transpose(1, 0, 2)
    gp_t = jnp.concatenate(trade_sorted(gp_blocks, me), axis=0)

    u1_row = u1
    d_in = mm(gp, u1_row).astype(BF16).reshape(bs, 2 * width // bs, channels)
    d_in = scatter_sum(d_in, order_a)
    gb_row = jnp.concatenate(in_order(gb_parts, me), axis=0)
    d_out = mm(z_mine, gb_row)
    narrow = channels // bs
    d_out = scatter_sum(d_out.T.astype(BF16).reshape(bs, narrow, width), order_a)
    d_out = d_out.reshape(fs, narrow // fs, width)
    d_out = jnp.stack(trade_sorted(d_out, me), axis=0)
    d_out = (
        d_out.reshape(fs, narrow // fs, half, step).transpose(2, 0, 3, 1).reshape(channels, -1)
    )

    gmu_part = jnp.dot(gcb, cond_w.T, precision=HIGH)
    sum_gp = jnp.sum(gp.astype(F32), axis=1)
    w_mine32 = w_in_mine.astype(F32)
    d_shift1 = jnp.dot(sum_gp[None], w_mine32, precision=HIGH)[0] + jnp.sum(gmu_part, axis=0)
    d_gain1 = jnp.sum(mm(gp, n1) * w_mine32, axis=0) + jnp.sum(gmu_part * mn, axis=0)

    gmu = jnp.dot(gcb_row, cond_w.T, precision=HIGH) / counts
    own_masks = lax.dynamic_slice_in_dim(masks, me * quarter, quarter, 1)
    gu1 = mm_tn(gp_t, w_in_t.reshape(2 * channels, channels)) + lax.dot_general(
        own_masks, gmu, (((0,), (0,)), ((), ())), precision=HIGH
    )
    unit_own, scale_own = normed(x32)
    grad_tokens = big_g + norm_back(unit_own, scale_own, gu1 * ln1_gain)

    shared = [
        d_gain1,
        d_shift1,
        d_w1.reshape(-1),
        jnp.sum(gcb, axis=0),
        jnp.dot(mu.T, gcb, precision=HIGH).reshape(-1),
        grad_ln2_gain,
        grad_ln2_shift,
    ]
    owned = jnp.concatenate([d_taps, d_w2], axis=0)
    packed = jnp.concatenate(shared + [owned.reshape(-1)])
    for bit in range(bits):
        packed = packed + swap(packed, "batch", 1 << bit)
    split = packed.shape[0] - owned.size
    common, owned = packed[:split], packed[split:]
    common = common + swap(common, "freq", 1)
    common = common + swap(common, "freq", 2)
    owned = jnp.stack(in_order(gather_freq(owned, me), me), axis=0)
    owned = (
        owned.reshape(fs, -1, 2, half, step).transpose(1, 2, 3, 0, 4).reshape(-1, 2 * channels)
    )
    sizes = np.cumsum([part.size for part in shared])
    got = jnp.split(common, sizes[:-1])
    return (
        mixed_out[:, None],
        grad_tokens[:, None],
        got[0],
        got[1],
        d_in.T,
        owned[:3],
        got[2].reshape(freq_w1.shape),
        got[3],
        owned[3:],
        got[4].reshape(cond_w.shape),
        d_out,
        got[5],
        got[6],
        d_ff[0].T,
        d_ff[1].T,
        d_ff[2],
    )


VM = pl.BlockSpec(memory_space=pltpu.VMEM)
SM = pl.BlockSpec(memory_space=pltpu.SMEM)
HBM = pl.BlockSpec(memory_space=pl.ANY)
MIB = 1 << 20


def params(mib):
    return pltpu.CompilerParams(vmem_limit_bytes=mib * MIB)


def cost(micros):
    return pl.CostEstimate(
        flops=int(micros * 1000000000.0), bytes_accessed=int(micros * 3500000.0), transcendentals=0
    )


def shape(dims, dtype):
    return pltpu.VMEM(dims, dtype)


def far(dims, dtype):
    return pltpu.HBM(dims, dtype)


def in_hbm(*values):
    kept = tuple(pltpu.with_memory_space_constraint(value, pltpu.HBM) for value in values)
    return kept if len(kept) > 1 else kept[0]


def in_vmem(value):
    return pltpu.with_memory_space_constraint(value, pltpu.VMEM)


def sigmoid(value):
    return 1.0 / (1.0 + jnp.exp(-value))


def dma_all(pairs, sems, first=0):
    copies = [
        pltpu.make_async_copy(source, target, sems.at[first + i])
        for i, (source, target) in enumerate(pairs)
    ]
    for copy in copies:
        copy.start()
    return copies


def tie_kernel(*refs):
    pass


def tie(values, after):
    count = len(values)
    return pl.pallas_call(
        tie_kernel,
        in_specs=[HBM] * (count + 1),
        out_specs=[HBM] * count,
        out_shape=[jax.ShapeDtypeStruct(value.shape, value.dtype) for value in values],
        input_output_aliases={i: i for i in range(count)},
        compiler_params=params(1),
        name="tie",
    )(*values, after)


def one_hot_rows(me, rows, lanes, piece, fs):
    row = lax.broadcasted_iota(jnp.int32, (rows, lanes), 0)
    lane = lax.broadcasted_iota(jnp.int32, (rows, lanes), 1)
    block = jnp.zeros_like(row)
    for m in range(1, rows // piece):
        block = block + jnp.where(row >= m * piece, 1, 0)
    return jnp.where(lane == block * ((fs - 1) * piece) + me * piece + row, 1.0, 0.0)


def prepare_kernel(
    me_ref, w_in, freq_w2, conv_taps, freq_w1, freq_b1, feats, waves_far, norms,
    w_mine, w2x, w2t, taps, base, waves, w1_aug, sems, *, step, fs,
):
    loads = dma_all([(waves_far, waves)], sems)
    lanes = w_in.shape[1] // 4
    rows = lanes // fs
    sel = one_hot_rows(me_ref[0], rows, lanes, step, fs)
    low = sel.astype(BF16)
    hidden = freq_w2.shape[0]
    for i in range(4):
        out = slice(i * rows, (i + 1) * rows)
        group = slice(i * lanes, (i + 1) * lanes)
        w_mine[out, :] = mm_nt(low, w_in[:, group]).astype(BF16)
        both = jnp.concatenate([freq_w2[:, group], conv_taps[:, group]], axis=0)
        mine = lax.dot_general(
            sel, both, (((1,), (1,)), ((), ())), precision=HIGH, preferred_element_type=F32
        )
        taps[out, :3] = mine[:, hidden:]
        mine = mine[:, :hidden]
        high = mine.astype(BF16)
        rest = (mine - high.astype(F32)).astype(BF16)
        w2x[out, :] = jnp.concatenate([high, high, rest], axis=1)
    w2t[...] = jnp.transpose(w2x[...][:, :hidden].astype(F32)).astype(BF16)
    w1_aug[...] = jnp.zeros_like(w1_aug)
    count = freq_w1.shape[0]
    w1_aug[:count, :] = freq_w1[...]
    w1_aug[count : count + 1, :] = freq_b1[...]
    base[...] = lax.dot_general(
        w1_aug[...], feats[...], (((0,), (0,)), ((), ())), precision=HIGH, preferred_element_type=F32
    )
    for load in loads:
        load.wait()


def prepare(me, w_in, freq_w2, conv_taps, freq_w1, freq_b1, feats, waves, norms, step, fs):
    channels, both = w_in.shape
    hidden = freq_w2.shape[0]
    length = feats.shape[1]
    return pl.pallas_call(
        functools.partial(prepare_kernel, step=step, fs=fs),
        in_specs=[SM] + [VM] * 6 + [HBM] * 2,
        out_specs=[VM] * 6,
        out_shape=[
            shape((both // fs, channels), BF16),
            shape((both // fs, 3 * hidden), BF16),
            shape((hidden, both // fs), BF16),
            shape((both // fs, 8), F32),
            shape((hidden, length), F32),
            shape((2 * length, length), BF16),
        ],
        scratch_shapes=[
            pltpu.VMEM((feats.shape[0], hidden), F32),
            pltpu.SemaphoreType.DMA((1,)),
        ],
        compiler_params=params(24),
        cost_estimate=cost(3),
        name="prepare",
    )(me, *in_hbm(w_in, freq_w2, conv_taps, freq_w1), freq_b1[None], in_hbm(feats), in_hbm(waves), norms)


def select_kernel(at_ref, after, gate, up, gate_out, up_out, *, fs):
    rows = gate_out.shape[0]
    sel = one_hot_rows(at_ref[0], rows, rows * fs, rows, fs).astype(BF16)
    gate_out[...] = mm_nt(sel, gate[...]).astype(BF16)
    up_out[...] = mm_nt(sel, up[...]).astype(BF16)


def select_columns(at, after, w_gate, w_up, bs, fs):
    channels, ff = w_gate.shape
    lanes = ff // bs
    wide = pl.BlockSpec((channels, lanes), lambda i, at: (0, (i // 2) * 4 + at[2] * 2 + i % 2))
    rows = pl.BlockSpec((lanes // fs, channels), lambda i, at: (i, 0))
    return pl.pallas_call(
        functools.partial(select_kernel, fs=fs),
        grid_spec=pltpu.PrefetchScalarGridSpec(
            num_scalar_prefetch=1,
            grid=(bs // 2,),
            in_specs=[HBM, wide, wide],
            out_specs=[rows, rows],
        ),
        out_shape=[shape((ff // (2 * fs), channels), BF16)] * 2,
        compiler_params=params(20),
        cost_estimate=cost(5),
        name="select_columns",
    )(at, after, in_hbm(w_gate), in_hbm(w_up))


def row_masks(ids):
    lane = lax.broadcasted_iota(jnp.int32, ids.shape, 1)
    length = ids.shape[1]
    prev = jnp.where((ids == pltpu.roll(ids, 1, 1)) & (lane > 0), 1.0, 0.0)
    nxt = jnp.where((ids == pltpu.roll(ids, length - 1, 1)) & (lane < length - 1), 1.0, 0.0)
    return prev, nxt


def bin_weights(start, width, length):
    lane = lax.broadcasted_iota(jnp.int32, (1, width), 1) + start
    return jnp.where(lane == 0, 0.5 / length, 1.0 / length)


def tile(index, size):
    return pl.ds(pl.multiple_of(index * size, size), size)


def hidden_tile(base, cb, j, lanes):
    pre = base[:, lanes] + cb[:, j : j + 1]
    return pre, sigmoid(pre)


def kernel_tile(w2x, hk):
    high = hk.astype(BF16)
    rest = (hk - high.astype(F32)).astype(BF16)
    return mm(w2x[...], jnp.concatenate([high, rest, high], axis=0))


def forward_kernel(
    me_ref, ids_at, x0, x1, x2, x3, ids_ref, norms, w, taps, base, w2x, condt, waves,
    z0, z1, z2, z3, u1, n1, p_out, q_out, c_out, vr_out, vs_out, mu_out, mn_out, cb_out,
    p, q, vm, ycat, acc,
):
    quarter = x0.shape[0]
    width, length = q_out.shape
    tiles = length // quarter
    me = me_ref[0]
    for k, x in enumerate((x0, x1, x2, x3)):
        values = x[...].astype(F32)
        unit, _ = normed(values)
        rows = tile(me ^ k, quarter)
        n1[rows, :] = unit.astype(BF16)
        u1[rows, :] = (unit * norms[0:1, :] + norms[1:2, :]).astype(BF16)
    ids = ids_ref[...]
    number = lax.broadcasted_iota(jnp.int32, (8, length), 0)
    member = jnp.where(ids == number, 1.0, 0.0)
    counts = jnp.maximum(jnp.sum(member, axis=1, keepdims=True), 1.0)
    member_low = member.astype(BF16)
    mu = mm(member_low, u1[...]) / counts
    mu_out[...] = mu
    mn_out[...] = mm(member_low, n1[...]) / counts
    cb_out[...] = lax.dot_general(
        condt[...], mu, (((1,), (1,)), ((), ())), precision=HIGH, preferred_element_type=F32
    )
    prev, nxt = row_masks(ids)
    for t in range(tiles):
        at = slice(t * quarter, (t + 1) * quarter)
        p[:, at] = mm_nt(w[...], u1[at, :])
    chunk = width // 2
    for r in range(4):
        at = slice(r * chunk, (r + 1) * chunk)
        here = p[at, :]
        p_out[at, :] = here.astype(BF16)
        mixed = (
            taps[at, 0:1] * (pltpu.roll(here, 1, 1) * prev)
            + taps[at, 1:2] * here
            + taps[at, 2:3] * (pltpu.roll(here, length - 1, 1) * nxt)
        )
        if r < 2:
            q[at, :] = mixed
            q_out[at, :] = mixed.astype(BF16)
        else:
            for j in range(SEGS):
                lo = j * width + (r - 2) * chunk
                vm[lo : lo + chunk, :] = (mixed * member[j : j + 1, :]).astype(BF16)

    span = 2 * quarter

    @pl.loop(0, length // span)
    def _(f):
        lanes = tile(f, span)
        upper = pl.ds(pl.multiple_of(f * span + length, span), span)
        weight = bin_weights(f * span, span, length)
        vr_all = mm(vm[...], waves[:length, lanes])
        vs_all = mm(vm[...], waves[length:, lanes])
        vr_out[:, lanes] = vr_all.astype(BF16)
        vs_out[:, lanes] = vs_all.astype(BF16)
        for j in range(SEGS):
            pre, gate = hidden_tile(base, cb_out, j, lanes)
            kk = kernel_tile(w2x, pre * gate)
            kr, ki = kk[:width] * weight, kk[width:] * weight
            at = slice(j * width, (j + 1) * width)
            vr, vs = vr_all[at], vs_all[at]
            ycat[at, lanes] = (kr * vr + ki * vs).astype(BF16)
            ycat[at, upper] = (kr * vs - ki * vr).astype(BF16)

    for k, z_out in enumerate((z0, z1, z2, z3)):
        t = me ^ k
        lanes = tile(t, quarter)
        acc[...] = jnp.zeros_like(acc)
        ids_here = ids_ref[:, lanes]
        for j in range(SEGS):

            @pl.when((ids_at[0, t * quarter] <= j) & (ids_at[0, (t + 1) * quarter - 1] >= j))
            def _():
                at = slice(j * width, (j + 1) * width)
                part = mm(ycat[at, :], waves[:, lanes])
                acc[...] += jnp.where(ids_here == j, part, 0.0)

        c = acc[...]
        c_out[:, lanes] = c.astype(BF16)
        z = (q[:, lanes] * c).astype(BF16)
        z_out[...] = z


def forward_spectral(me, x_parts, ids, norms, w, taps, base, w2x, condt, waves):
    quarter, channels = x_parts[0].shape
    length = ids.shape[1]
    width = w.shape[0] // 2
    saved = [
        (length, channels),
        (length, channels),
        (2 * width, length),
        (width, length),
        (width, length),
        (SEGS * width, length),
        (SEGS * width, length),
    ]
    small = [
        shape((8, channels), F32),
        shape((8, channels), F32),
        shape((condt.shape[0], 8), F32),
    ]
    return pl.pallas_call(
        forward_kernel,
        in_specs=[SM, SM] + [VM] * 12,
        out_specs=[VM] * (7 + len(saved)),
        out_shape=[shape((width, quarter), BF16)] * 4 + [shape(dims, BF16) for dims in saved] + small,
        scratch_shapes=[
            pltpu.VMEM((2 * width, length), F32),
            pltpu.VMEM((width, length), F32),
            pltpu.VMEM((SEGS * width, length), BF16),
            pltpu.VMEM((SEGS * width, 2 * length), BF16),
            pltpu.VMEM((width, quarter), F32),
        ],
        compiler_params=params(26),
        cost_estimate=cost(15),
        name="forward_spectral",
    )(me, ids, *x_parts, ids, norms, w, taps, base, w2x, condt, waves)


def backward_kernel(
    me_ref, ids_at, g0, g1, g2, g3, ids_ref, cb, taps, base, w2x, w2, feats,
    p, q, c, vr_in, vs_in, waves, after,
    o0, o1, o2, o3, gp_row, d_taps, d_w2, d_w1, gcb,
    gcm, gvcat, gs, acc,
):
    width, quarter = g0.shape
    length = gp_row.shape[1]
    tiles = length // quarter
    hidden = base.shape[0]
    me = me_ref[0]
    for k, g in enumerate((g0, g1, g2, g3)):
        lanes = tile(me ^ k, quarter)
        gz = g[...].astype(F32)
        gs[:width, lanes] = gz * c[:, lanes].astype(F32)
        gc = gz * q[:, lanes].astype(F32)
        ids_here = ids_ref[:, lanes]
        for j in range(SEGS):
            gcm[j * width : (j + 1) * width, lanes] = jnp.where(ids_here == j, gc, 0.0).astype(BF16)
    d_w2[...] = jnp.zeros_like(d_w2)
    d_w1[...] = jnp.zeros_like(d_w1)
    gcb[...] = jnp.zeros_like(gcb)

    span = 2 * quarter

    @pl.loop(0, length // span)
    def _(f):
        lanes = tile(f, span)
        upper = pl.ds(pl.multiple_of(f * span + length, span), span)
        weight = bin_weights(f * span, span, length)
        gyr_all = mm(gcm[...], waves[:length, lanes]) * weight
        gys_all = mm(gcm[...], waves[length:, lanes]) * weight
        for j in range(SEGS):
            pre, gate = hidden_tile(base, cb, j, lanes)
            hk = pre * gate
            kk = kernel_tile(w2x, hk)
            kr, ki = kk[:width], kk[width:]
            at = slice(j * width, (j + 1) * width)
            gyr, gys = gyr_all[at], gys_all[at]
            vr, vs = vr_in[at, lanes].astype(F32), vs_in[at, lanes].astype(F32)
            gvcat[at, lanes] = (kr * gyr - ki * gys).astype(BF16)
            gvcat[at, upper] = (kr * gys + ki * gyr).astype(BF16)
            gkk = jnp.concatenate(
                [(gyr * vr + gys * vs).astype(BF16), (gyr * vs - gys * vr).astype(BF16)], axis=0
            )
            d_w2[...] += mm_nt(gkk, hk.astype(BF16))
            gpre = mm(w2[...], gkk) * (gate * (1.0 + pre * (1.0 - gate)))
            gcb[:, j : j + 1] += jnp.sum(gpre, axis=1, keepdims=True)
            d_w1[...] += mm_nt(feats[:, lanes], gpre.astype(BF16))

    for k in range(4):
        t = me ^ k
        lanes = tile(t, quarter)
        acc[...] = jnp.zeros_like(acc)
        ids_here = ids_ref[:, lanes]
        for j in range(SEGS):

            @pl.when((ids_at[0, t * quarter] <= j) & (ids_at[0, (t + 1) * quarter - 1] >= j))
            def _():
                at = slice(j * width, (j + 1) * width)
                part = mm(gvcat[at, :], waves[:, lanes])
                acc[...] += jnp.where(ids_here == j, part, 0.0)

        gs[width:, lanes] = acc[...]
    prev, nxt = row_masks(ids_ref[...])
    chunk = width // 2
    for r in range(4):
        at = slice(r * chunk, (r + 1) * chunk)
        here = p[at, :].astype(F32)
        grad = gs[at, :]
        d_taps[at, 0:1] = jnp.sum(grad * (pltpu.roll(here, 1, 1) * prev), axis=1, keepdims=True)
        d_taps[at, 1:2] = jnp.sum(grad * here, axis=1, keepdims=True)
        d_taps[at, 2:3] = jnp.sum(
            grad * (pltpu.roll(here, length - 1, 1) * nxt), axis=1, keepdims=True
        )
        gp_row[at, :] = (
            taps[at, 1:2] * grad
            + taps[at, 0:1] * pltpu.roll(grad * prev, length - 1, 1)
            + taps[at, 2:3] * pltpu.roll(grad * nxt, 1, 1)
        ).astype(BF16)
    share = jnp.transpose(gcb[...])[:8, :]
    high = share.astype(BF16)
    rest = (share - high.astype(F32)).astype(BF16)
    extra = jnp.concatenate([high, rest], axis=0)
    extra = jnp.concatenate([extra, jnp.zeros((16, quarter - hidden), BF16)], axis=1)
    for k, out in enumerate((o0, o1, o2, o3)):
        out[: 2 * width, :] = gp_row[:, tile(me ^ k, quarter)]
        out[2 * width :, :] = extra


def backward_spectral(
    me, gz_parts, ids, cb, taps, base, w2x, w2, feats, p, q, c, vr, vs, waves, after
):
    width, quarter = gz_parts[0].shape
    length = ids.shape[1]
    hidden = base.shape[0]
    outs = [shape((2 * width + 16, quarter), BF16)] * 4 + [
        shape((2 * width, length), BF16),
        shape((2 * width, 128), F32),
        shape((2 * width, hidden), F32),
        shape((feats.shape[0], hidden), F32),
        shape((hidden, 128), F32),
    ]
    return pl.pallas_call(
        backward_kernel,
        in_specs=[SM, SM] + [VM] * 17 + [HBM],
        out_specs=[VM] * 9,
        out_shape=outs,
        scratch_shapes=[
            pltpu.VMEM((SEGS * width, length), BF16),
            pltpu.VMEM((SEGS * width, 2 * length), BF16),
            pltpu.VMEM((2 * width, length), F32),
            pltpu.VMEM((width, quarter), F32),
        ],
        compiler_params=params(26),
        cost_estimate=cost(17),
        name="backward_spectral",
    )(
        me, ids, *gz_parts, ids, cb, taps, base, w2x, w2, feats, p, q, c, vr, vs, waves, after
    )


def middle_kernel(me_ref, z0, z1, z2, z3, x, w_out, norms, after, h_out, u2_out, z_t, *, piece):
    me = me_ref[0]
    width = z0.shape[0]
    for k, z in enumerate((z0, z1, z2, z3)):
        for i in range(width // piece):
            at = pl.ds(pl.multiple_of((i * 4 + (me ^ k)) * piece, piece), piece)
            z_t[at, :] = z[i * piece : (i + 1) * piece, :]
    h = x[...].astype(F32) + mm(jnp.transpose(z_t[...]), w_out[...])
    h_out[...] = h
    unit, _ = normed(h)
    u2_out[...] = (unit * norms[2:3, :] + norms[3:4, :]).astype(BF16)


def middle(me, z_parts, x, w_out, norms, after, piece):
    quarter, channels = x.shape
    return pl.pallas_call(
        functools.partial(middle_kernel, piece=piece),
        in_specs=[SM] + [VM] * 7 + [HBM],
        out_specs=[VM] * 3,
        out_shape=[
            shape((quarter, channels), F32),
            shape((quarter, channels), BF16),
            shape((channels, quarter), BF16),
        ],
        compiler_params=params(24),
        cost_estimate=cost(2),
        name="middle",
    )(me, *z_parts, x, in_hbm(w_out), norms, after)


def feed_kernel(
    me_ref, u2, h, ct, norms, w_out, gate, up, down,
    mixed, big_g, g0, g1, g2, g3, t_own, t_other, sums, acc_out, acc_grad, gz_t, gb_t, *, piece, thin,
):
    i = pl.program_id(0)

    @pl.when(i == 0)
    def _():
        acc_out[...] = jnp.zeros_like(acc_out)
        acc_grad[...] = jnp.zeros_like(acc_grad)

    g = mm(u2[...], gate[...])
    a = mm(u2[...], up[...])
    gh = mm_nt(ct[...], down[...])
    sg = sigmoid(g)
    silu = g * sg
    hid = (silu * a).astype(BF16)
    gg = (gh * a * (sg * (1.0 + g * (1.0 - sg)))).astype(BF16)
    ga = (gh * silu).astype(BF16)
    acc_out[...] += mm(hid, down[...])
    acc_grad[...] += mm_nt(gg, gate[...]) + mm_nt(ga, up[...])

    @pl.when(i == pl.num_programs(0) - 1)
    def _():
        me = me_ref[0]
        width = g0.shape[0]
        here = h[...]
        mixed[...] = (here + acc_out[...]).astype(BF16)
        gu2 = acc_grad[...]
        unit, scale = normed(here)
        sums[0:1, :] = jnp.sum(gu2 * unit, axis=0, keepdims=True)
        sums[1:2, :] = jnp.sum(gu2, axis=0, keepdims=True)
        total = ct[...].astype(F32) + norm_back(unit, scale, gu2 * norms[2:3, :])
        big_g[...] = total
        low = total.astype(BF16)
        gz_t[...] = mm_nt(w_out[...], low).astype(BF16)
        for k, out in enumerate((g0, g1, g2, g3)):
            for r in range(width // piece):
                at = pl.ds(pl.multiple_of((r * 4 + (me ^ k)) * piece, piece), piece)
                out[r * piece : (r + 1) * piece, :] = gz_t[at, :]
        gb_t[...] = jnp.transpose(total)
        for core, out in ((me & 1, t_own), (1 - (me & 1), t_other)):
            parts = []
            for x in range(2):
                for r in range(width // thin):
                    lo = pl.multiple_of((r * 4 + 2 * x + core) * thin, thin)
                    parts.append(gb_t[pl.ds(lo, thin), :])
            out[...] = jnp.concatenate(parts, axis=0).astype(BF16)


def feed_forward(me, u2, h, ct, norms, w_out, w_gate, w_up, w_down, piece, thin):
    quarter, channels = u2.shape
    ff = w_gate.shape[1]
    block = 512

    width = channels // 4
    outs = [
        ((quarter, channels), BF16),
        ((quarter, channels), F32),
    ] + [((width, quarter), BF16)] * 4 + [((2 * width, quarter), BF16)] * 2 + [((8, channels), F32)]
    return pl.pallas_call(
        functools.partial(feed_kernel, piece=piece, thin=thin),
        grid=(ff // block,),
        in_specs=[
            SM,
            VM,
            VM,
            VM,
            VM,
            VM,
            pl.BlockSpec((channels, block), lambda i: (0, i)),
            pl.BlockSpec((channels, block), lambda i: (0, i)),
            pl.BlockSpec((block, channels), lambda i: (i, 0)),
        ],
        out_specs=[VM] * len(outs),
        out_shape=[far(*outs[0])] + [shape(*out) for out in outs[1:]],
        scratch_shapes=[
            pltpu.VMEM((quarter, channels), F32),
            pltpu.VMEM((quarter, channels), F32),
            pltpu.VMEM((channels, quarter), BF16),
            pltpu.VMEM((channels, quarter), F32),
        ],
        compiler_params=params(28),
        cost_estimate=cost(13),
        name="feed_forward",
    )(me, u2, h, ct, norms, in_hbm(w_out), in_hbm(w_gate), in_hbm(w_up), in_hbm(w_down))


def hidden_grads_kernel(at_ref, *refs):
    u_parts, c_parts, refs = refs[:8], refs[8:16], refs[16:]
    gate, up, gt_own, gt_got, z_own, z_got, down, after, *refs = refs
    keep_a, give_a, keep_b, give_b, keep_o, give_o, rights, lefts, d_all, d_out = refs
    quarter, channels = u_parts[0].shape
    y, z = at_ref[1], at_ref[3]
    rows = gate.shape[0]
    for k in range(8):
        at = slice(k * quarter, (k + 1) * quarter)
        rights[0, at, :] = u_parts[k][...]
        rights[1, at, :] = c_parts[k][...]
    span = 2 * quarter

    @pl.loop(0, 4)
    def _(k):
        at = tile(k, span)
        g = mm_nt(gate[...], rights[0, at, :])
        a = mm_nt(up[...], rights[0, at, :])
        gh = mm_nt(down[...].reshape(rows, channels), rights[1, at, :])
        sg = sigmoid(g)
        silu = g * sg
        lefts[0, :, at] = (gh * a * (sg * (1.0 + g * (1.0 - sg)))).astype(BF16)
        lefts[1, :, at] = (gh * silu).astype(BF16)
        lefts[2, :, at] = (silu * a).astype(BF16)

    d_out[...] = mm_nt(gt_own[...], z_own[...]) + mm_nt(gt_got[...], z_got[...])
    half = keep_o.shape[0]
    x = at_ref[0] >> 1
    keep_o[...] = d_out[tile(x, half), :].astype(BF16)
    give_o[...] = d_out[tile(1 - x, half), :].astype(BF16)
    fw = rows // 4
    cut = keep_a.shape[-1]

    @pl.loop(0, 3)
    def _(m):
        grad = mm(lefts[m], rights[m >> 1]).astype(BF16)
        for i in range(4):
            d_all[i, m] = grad[i * fw : (i + 1) * fw]

    for i in range(2):
        keep_a[i] = d_all[2 * i + y, :, :, :cut]
        give_a[i] = d_all[2 * i + 1 - y, :, :, :cut]
        keep_b[i] = d_all[2 * z + i, :, :, cut:]
        give_b[i] = d_all[2 * (1 - z) + i, :, :, cut:]


def hidden_grads(at, u2_parts, ct_parts, gate, up, gt_own, gt_got, z_own, z_got, down, after):
    quarter, channels = u2_parts[0].shape
    wide = gate.shape[0]
    bs, fs, fw, _ = down.shape
    cut = 2 * channels // 3
    down = down.reshape(2, 2, 2, fs, fw, channels)
    down_spec = pl.BlockSpec((2, 1, 2, 1, fw, channels), lambda i, at: (0, at[2], 0, at[0], 0, 0))
    return pl.pallas_call(
        hidden_grads_kernel,
        grid_spec=pltpu.PrefetchScalarGridSpec(
            num_scalar_prefetch=1,
            grid=(1,),
            in_specs=[VM] * 22 + [down_spec, HBM],
            out_specs=[VM] * 6,
            scratch_shapes=[
                pltpu.VMEM((2, 8 * quarter, channels), BF16),
                pltpu.VMEM((3, wide, 8 * quarter), BF16),
                pltpu.VMEM((4, 3, fw, channels), BF16),
                pltpu.VMEM((2 * channels // fs, channels), F32),
            ],
        ),
        out_shape=[shape((2, 3, fw, cut), BF16)] * 2
        + [shape((2, 3, fw, channels - cut), BF16)] * 2
        + [shape((channels // fs, channels), BF16)] * 2,
        compiler_params=params(34),
        cost_estimate=cost(14),
        name="hidden_grads",
    )(at, *u2_parts, *ct_parts, gate, up, gt_own, gt_got, z_own, z_got, in_hbm(down), after)


def halve_kernel(at_ref, after, *refs, bits):
    pairs = len(bits)
    ins, outs = refs[: 2 * pairs], refs[2 * pairs :]
    for n in range(pairs):
        mine = at_ref[bits[n] + 1]
        keep, got = ins[2 * n], ins[2 * n + 1]
        next_keep, next_give = outs[2 * n], outs[2 * n + 1]
        for i in range(keep.shape[0]):
            for side, out in ((mine, next_keep), (1 - mine, next_give)):
                out[i] = (keep[i, side].astype(F32) + got[i, side].astype(F32)).astype(BF16)


def halve(at, bits, after, *sums):
    outs = []
    for n in range(len(bits)):
        dims = sums[2 * n].shape
        outs += [shape((dims[0],) + dims[2:], BF16)] * 2
    return pl.pallas_call(
        functools.partial(halve_kernel, bits=bits),
        in_specs=[SM, HBM] + [VM] * len(sums),
        out_specs=[VM] * len(outs),
        out_shape=outs,
        compiler_params=params(24),
        cost_estimate=cost(0.3),
        name="halve",
    )(at, after, *sums)


def load_riders(blocks, first, rows):
    parts = []
    for i in range(blocks.shape[0]):
        for m in range(blocks.shape[2] // 128):
            parts.append(blocks[i, first : first + rows, m * 128 : (m + 1) * 128].astype(F32))
    return jnp.concatenate(parts, axis=0)


def store_riders(block, packed, i, first, rows):
    columns = block.shape[1] // 128
    for m in range(columns):
        lo = (columns * i + m) * rows
        block[first : first + rows, m * 128 : (m + 1) * 128] = packed[lo : lo + rows, :]


def stage_kernel(
    at_ref, after, keep_a, got_a, keep_b, got_b, ours,
    next_keep_a, next_give_a, next_keep_b, next_give_b, total, joined, block,
):
    y, z = at_ref[1], at_ref[2]
    tall, rows = keep_a.shape[2], next_give_a.shape[1]
    flat = got_a.shape[2]
    columns = got_a.shape[3] // 128
    riders = joined.shape[0] // (4 * columns)
    start = flat - riders
    for i in range(2):
        for k in range(2):
            for m in range(columns):
                lo = (columns * (2 * i + k) + m) * riders
                piece = got_a[i, k, start:flat, m * 128 : (m + 1) * 128]
                joined[lo : lo + riders, :] = ours[lo : lo + riders, :].astype(F32) + piece.astype(F32)
    total[...] = joined[...].astype(BF16)
    for i in range(2):
        next_keep_a[i] = (keep_a[i, z].astype(F32) + got_a[i, z, :tall].astype(F32)).astype(BF16)
        block[...] = jnp.zeros_like(block)
        block[:tall, :] = keep_a[i, 1 - z].astype(F32) + got_a[i, 1 - z, :tall].astype(F32)
        store_riders(block, joined, i, rows - 2 * riders, 2 * riders)
        next_give_a[i] = block[...].astype(BF16)
        for side, out in ((y, next_keep_b), (1 - y, next_give_b)):
            out[i] = (keep_b[i, side].astype(F32) + got_b[i, side].astype(F32)).astype(BF16)


def stage(at, after, keep_a, got_a, keep_b, got_b, ours):
    _, _, tall, lanes = keep_a.shape
    narrow = keep_b.shape[-1]
    riders = ours.shape[0] // (4 * (lanes // 128))
    rows = got_a.shape[2] + riders
    return pl.pallas_call(
        stage_kernel,
        in_specs=[SM, HBM] + [VM] * 5,
        out_specs=[VM] * 5,
        out_shape=[
            shape((2, tall, lanes), BF16),
            shape((2, rows, lanes), BF16),
            shape((2, tall, narrow), BF16),
            shape((2, tall, narrow), BF16),
            shape(ours.shape, BF16),
        ],
        scratch_shapes=[pltpu.VMEM(ours.shape, F32), pltpu.VMEM((rows, lanes), F32)],
        compiler_params=params(12),
        cost_estimate=cost(0.3),
        name="stage",
    )(at, after, keep_a, got_a, keep_b, got_b, ours)


def join_kernel(at_ref, after, keep_a, got_a, keep_b, got_b, ours, keep, give, total):
    tall, cut = keep_a.shape[1:]
    riders = ours.shape[0] // (2 * (cut // 128))
    start = got_a.shape[1] - riders
    total[...] = (ours[...].astype(F32) + load_riders(got_a, start, riders)).astype(BF16)
    for side, out in ((at_ref[3], keep), (1 - at_ref[3], give)):
        out[:, :cut] = (keep_a[side].astype(F32) + got_a[side, :tall].astype(F32)).astype(BF16)
        out[:, cut:] = (keep_b[side].astype(F32) + got_b[side].astype(F32)).astype(BF16)


def join(at, after, keep_a, got_a, keep_b, got_b, ours):
    _, rows, cut = keep_a.shape
    return pl.pallas_call(
        join_kernel,
        in_specs=[SM, HBM] + [VM] * 5,
        out_specs=[VM] * 3,
        out_shape=[shape((rows, cut + keep_b.shape[-1]), BF16)] * 2 + [shape(ours.shape, BF16)],
        compiler_params=params(12),
        cost_estimate=cost(0.3),
        name="join",
    )(at, after, keep_a, got_a, keep_b, got_b, ours)


def hidden_last_kernel(keep_a, got_a, keep_b, got_b, after, *outs):
    *outs, token = outs
    token[...] = jnp.zeros_like(token)
    cut = keep_a.shape[-1]
    for m, out in enumerate(outs):
        out[:, :cut] = keep_a[0, m].astype(F32) + got_a[0, m].astype(F32)
        out[:, cut:] = keep_b[0, m].astype(F32) + got_b[0, m].astype(F32)


def hidden_last(keep_a, got_a, keep_b, got_b, after):
    _, count, rows, cut = keep_a.shape
    return pl.pallas_call(
        hidden_last_kernel,
        in_specs=[VM] * 4 + [HBM],
        out_specs=[VM] * (count + 1),
        out_shape=[far((rows, cut + keep_b.shape[-1]), F32)] * count + [shape((8, 128), F32)],
        compiler_params=params(12),
        cost_estimate=cost(0.3),
        name="hidden_last",
    )(keep_a, got_a, keep_b, got_b, after)


def add_kernel(ours, theirs, after, out):
    out[...] = (ours[...].astype(F32) + theirs[...].astype(F32)).astype(out.dtype)


def add(ours, theirs, after, dtype):
    return pl.pallas_call(
        add_kernel,
        in_specs=[VM, VM, HBM],
        out_specs=VM,
        out_shape=shape(ours.shape, dtype),
        compiler_params=params(8),
        cost_estimate=cost(0.3),
        name="add",
    )(ours, theirs, after)


def projection_kernel(
    at_ref, gp, u1, n1, w_mine, keep_o, got_o, d_w2, d_w1, d_taps, gcb, condt, mu, mn,
    sums2, after, keep_a, give_a, keep_b, give_b, packed_out, d_in, d_out, packed, sheet, *, layout,
):
    me, y, zbit = at_ref[0], at_ref[1], at_ref[2]
    channels = u1.shape[1]
    width = keep_o.shape[0]
    d_in[...] = mm(gp[...], u1[...])
    d_out[...] = keep_o[...].astype(F32) + got_o[...].astype(F32)
    blocks = 2 * keep_a.shape[0]
    first = 2 * width // blocks
    second = width // blocks
    cut = channels // 2

    def put(out, block, lanes):
        lo = pl.multiple_of(block * first, first)
        out[:first, :] = d_in[pl.ds(lo, first), lanes].astype(BF16)
        lo = pl.multiple_of(block * second, second)
        out[first:, :] = d_out[pl.ds(lo, second), lanes].astype(BF16)

    for b in range(blocks // 2):
        put(keep_a.at[b], 2 * b + y, slice(0, cut))
    for b in range(blocks // 4):
        for i in range(2):
            put(keep_b.at[b, i], 4 * b + 2 * zbit + i, slice(cut, channels))
            put(give_b.at[b, i], 4 * b + 2 * (1 - zbit) + i, slice(cut, channels))
    packed[...] = jnp.zeros_like(packed)
    packed[:width, :] = jnp.concatenate([d_w2[:width, :], d_w2[width:, :]], axis=1)
    taps_t = jnp.transpose(d_taps[...])
    gcb_t = jnp.transpose(gcb[...])[:8, :]
    gmu = lax.dot_general(
        gcb_t, condt[...], (((1,), (0,)), ((), ())), precision=HIGH, preferred_element_type=F32
    )
    gp_n = mm(gp[...], n1[...])
    w32 = w_mine[...].astype(F32)
    gain = jnp.sum(gp_n * w32, axis=0, keepdims=True) + jnp.sum(gmu * mn[...], axis=0, keepdims=True)
    total = jnp.sum(gp[...].astype(F32), axis=1, keepdims=True)
    shift = jnp.sum(total * w32, axis=0, keepdims=True) + jnp.sum(gmu, axis=0, keepdims=True)
    for i in range(3):
        for m in range(2 * width // 128):
            at = layout["taps"] + i * (2 * width // 128) + m
            packed[at : at + 1, :] = taps_t[i : i + 1, m * 128 : (m + 1) * 128]
    for i, row in enumerate((gain, shift, sums2[0:1, :], sums2[1:2, :])):
        for m in range(channels // 128):
            at = layout["ln"] + i * (channels // 128) + m
            packed[at : at + 1, :] = row[:, m * 128 : (m + 1) * 128]
    half = d_w1.shape[0] // 2
    packed[layout["w1"] : layout["w1"] + half, :] = jnp.concatenate(
        [d_w1[:half, :], d_w1[half:, :]], axis=1
    )
    zeros = jnp.zeros_like(gcb_t)
    row = at_ref[4]
    odd = (row & 1) == 1
    both = jnp.concatenate([jnp.where(odd, zeros, gcb_t), jnp.where(odd, gcb_t, zeros)], axis=1)
    packed[pl.ds(pl.multiple_of(layout["cb"] + 8 * (row >> 1), 8), 8), :] = both
    share = jnp.zeros((8, width), F32)
    for f in range(channels // width):
        share = share + jnp.where(me == f, mu[:, f * width : (f + 1) * width], 0.0)
    rest = jnp.concatenate([share[:SEGS, 128:], jnp.zeros((SEGS, 256 - width), F32)], axis=1)
    block = jnp.concatenate([share[:SEGS, :128], rest, jnp.zeros((8 - 2 * SEGS, 128), F32)], axis=0)
    packed[pl.ds(pl.multiple_of(layout["mu"] + 8 * row, 8), 8), :] = block
    packed_out[...] = packed[...].astype(BF16)
    riders = packed.shape[0] // (4 * (cut // 128))
    for b in range(blocks // 2):
        sheet[...] = jnp.zeros_like(sheet)
        lo = pl.multiple_of((2 * b + 1 - y) * first, first)
        sheet[:first, :] = d_in[pl.ds(lo, first), :cut]
        lo = pl.multiple_of((2 * b + 1 - y) * second, second)
        sheet[first : first + second, :] = d_out[pl.ds(lo, second), :cut]
        store_riders(sheet, packed, b, sheet.shape[0] - riders, riders)
        give_a[b] = sheet[...].astype(BF16)


def packed_layout(width, channels, bs):
    taps = width
    ln = taps + 3 * (2 * width // 128)
    w1 = -(-(ln + 4 * (channels // 128)) // 8) * 8
    cb = w1 + 32
    mu = cb + 4 * bs
    return {"taps": taps, "ln": ln, "w1": w1, "cb": cb, "mu": mu, "rows": -(-(mu + 8 * bs) // 128) * 128}


def projection_grads(
    at, gp, u1, n1, w_mine, keep_o, got_o, d_w2, d_w1, d_taps, gcb, condt, mu, mn, sums2, after, bs
):
    length, channels = u1.shape
    width = keep_o.shape[0]
    layout = packed_layout(width, channels, bs)
    tall = 3 * width // bs
    flat = -(-tall // 16) * 16 + layout["rows"] // (4 * (channels // 256))
    return pl.pallas_call(
        functools.partial(projection_kernel, layout=layout),
        in_specs=[SM] + [VM] * 14 + [HBM],
        out_specs=[VM] * 5,
        out_shape=[
            shape((bs // 2, tall, channels // 2), BF16),
            shape((bs // 2, flat, channels // 2), BF16),
        ]
        + [shape((bs // 4, 2, 3 * width // bs, channels // 2), BF16)] * 2
        + [shape((layout["rows"], 128), BF16)],
        scratch_shapes=[
            pltpu.VMEM((2 * width, channels), F32),
            pltpu.VMEM((width, channels), F32),
            pltpu.VMEM((layout["rows"], 128), F32),
            pltpu.VMEM((flat, channels // 2), F32),
        ],
        compiler_params=params(24),
        cost_estimate=cost(2),
        name="projection_grads",
    )(
        at, gp, u1, n1, w_mine, keep_o, got_o, d_w2, d_w1, d_taps, gcb, condt, mu, mn, sums2, after
    )


def final_kernel(
    me_ref, p0, p1, p2, p3, x, big_g, norms, ids_row, condt, w_in, after, out, gp_t, *, piece
):
    me = me_ref[0]
    rows = gp_t.shape[0] // 4
    hidden = condt.shape[0]
    share = jnp.zeros((8, hidden), F32)
    for k, part in enumerate((p0, p1, p2, p3)):
        for i in range(rows // piece):
            at = pl.ds(pl.multiple_of((i * 4 + (me ^ k)) * piece, piece), piece)
            gp_t[at, :] = part[i * piece : (i + 1) * piece, :]
        extra = part[rows:, :hidden].astype(F32)
        share = share + extra[:8] + extra[8:]
    ids = ids_row[...]
    number = lax.broadcasted_iota(jnp.int32, (8, ids.shape[1]), 0)
    counts = jnp.sum(jnp.where(ids == number, 1.0, 0.0), axis=1, keepdims=True)
    gmu = lax.dot_general(
        share, condt[...], (((1,), (0,)), ((), ())), precision=HIGH, preferred_element_type=F32
    ) / jnp.maximum(counts, 1.0)
    gu1 = mm_nt(jnp.transpose(gp_t[...]), w_in[...])
    quarter = x.shape[0]
    own = jnp.broadcast_to(ids_row[:, tile(me, quarter)].astype(F32), (8, quarter))
    ids_own = jnp.transpose(own)[:, 0:1]
    for j in range(SEGS):
        gu1 = gu1 + jnp.where(ids_own == j, gmu[j : j + 1, :], 0.0)
    unit, scale = normed(x[...].astype(F32))
    out[...] = big_g[...] + norm_back(unit, scale, gu1 * norms[0:1, :])


def final(me, gp_parts, x, big_g, norms, ids, condt, w_in, after, piece):
    quarter, channels = x.shape
    return pl.pallas_call(
        functools.partial(final_kernel, piece=piece),
        in_specs=[SM] + [VM] * 10 + [HBM],
        out_specs=VM,
        out_shape=shape((quarter, channels), F32),
        scratch_shapes=[pltpu.VMEM((2 * channels, quarter), BF16)],
        compiler_params=params(24),
        cost_estimate=cost(0.3),
        name="final",
    )(me, *gp_parts, x, big_g, norms, ids, condt, in_hbm(w_in), after)


def small_kernel(
    me_ref, j0, j1, j2, j3, w2, taps, ln0, ln1, ln2, ln3, w1, b1, cond, wide, tap_t, cond_t, *, layout, step, width
):
    me = me_ref[0]
    parts = [part[...].astype(F32) for part in (j0, j1, j2, j3)]
    hidden = w1.shape[0]
    half = width // step
    count = 2 * width // 128
    for k, part in enumerate(parts):
        who = me ^ k
        rows = jnp.concatenate(
            [
                jnp.concatenate([part[layout["taps"] + i * count + m : layout["taps"] + i * count + m + 1, :]
                                 for m in range(count)], axis=1)
                for i in range(3)
            ]
            + [jnp.zeros((125, 2 * width), F32)],
            axis=0,
        )
        tap_t[...] = jnp.transpose(rows)
        for side in range(2):
            for i in range(half):
                at = pl.ds(pl.multiple_of((side * half * 4 + i * 4 + who) * step, step), step)
                lo = i * step
                wide[at, :hidden] = part[lo : lo + step, side * hidden : (side + 1) * hidden]
                at2 = side * width + lo
                wide[at, hidden:] = tap_t[at2 : at2 + step, :hidden]
    whole = jnp.transpose(wide[...])
    w2[...] = whole[:hidden, :]
    taps[...] = whole[hidden : hidden + 3, :]

    def common(first, last):
        a, b, c, d = [part[first:last, :] for part in parts]
        return (a + b) + (c + d)

    lanes = ln0.shape[0] // 128
    sums = common(layout["ln"], layout["ln"] + 4 * lanes)
    for i, out in enumerate((ln0, ln1, ln2, ln3)):
        row = jnp.concatenate([sums[i * lanes + m : i * lanes + m + 1, :] for m in range(lanes)], axis=1)
        out[...] = row.reshape(out.shape)
    both = common(layout["w1"], layout["w1"] + hidden // 2)
    w1[: hidden // 2, :] = both[:, :hidden]
    w1[hidden // 2 :, :] = both[:, hidden:]
    cb = common(layout["cb"], layout["mu"])
    shares = []
    for b in range(cb.shape[0] // 4):
        lo = 8 * (b // 2)
        shares.append(cb[lo : lo + 8, (b % 2) * hidden : (b % 2 + 1) * hidden])
    shares = jnp.concatenate(shares, axis=0)
    b1[...] = jnp.sum(shares, axis=0, keepdims=True)
    for k, part in enumerate(parts):
        rows = []
        for b in range(cb.shape[0] // 4):
            lo = layout["mu"] + 8 * b
            block = part[lo : lo + 8, :]
            rows.append(
                jnp.concatenate(
                    [
                        jnp.concatenate([block[:SEGS, :], jnp.zeros((8 - SEGS, 128), F32)], axis=0),
                        jnp.concatenate(
                            [block[SEGS : 2 * SEGS, : width - 128], jnp.zeros((8 - SEGS, width - 128), F32)],
                            axis=0,
                        ),
                    ],
                    axis=1,
                )
            )
        mu = jnp.concatenate(rows, axis=0)
        cond_t[tile(me ^ k, width), :] = lax.dot_general(
            jnp.transpose(mu), shares, (((1,), (0,)), ((), ())), precision=HIGH, preferred_element_type=F32
        )
    cond[...] = jnp.transpose(cond_t[...])


def small_grads(me, parts, hidden, channels, step, bs):
    width = channels // 4
    layout = packed_layout(width, channels, bs)
    return pl.pallas_call(
        functools.partial(small_kernel, layout=layout, step=step, width=width),
        in_specs=[SM] + [VM] * 4,
        out_specs=[VM] * 9,
        out_shape=[
            far((hidden, 2 * channels), F32),
            far((3, 2 * channels), F32),
            far((channels,), F32),
            far((channels,), F32),
            far((channels,), F32),
            far((channels,), F32),
            far((hidden, hidden), F32),
            far((1, hidden), F32),
            far((hidden, channels), F32),
        ],
        scratch_shapes=[
            pltpu.VMEM((2 * channels, 2 * hidden), F32),
            pltpu.VMEM((2 * width, 128), F32),
            pltpu.VMEM((channels, hidden), F32),
        ],
        compiler_params=params(24),
        cost_estimate=cost(3),
        name="small_grads",
    )(me, *parts)


def trade_parts(parts):
    two, three, one = [swap(parts[k], "freq", k) for k in (2, 3, 1)]
    return (parts[0], one, two, three)


def tiled_device(
    tokens,
    seg_ids,
    cotangent,
    ln1_gain,
    ln1_shift,
    w_in,
    conv_taps,
    freq_w1,
    freq_b1,
    freq_w2,
    cond_w,
    w_out,
    ln2_gain,
    ln2_shift,
    w_gate,
    w_up,
    w_down,
):
    quarter, _, channels = tokens.shape
    length = seg_ids.shape[1]
    ff = w_gate.shape[1]
    fs = lax.axis_size("freq")
    bs = lax.axis_size("batch")
    me = lax.axis_index("freq")
    row = lax.axis_index("batch")
    width = channels // fs
    half = bs // 2
    step = channels // (half * fs)
    fw = ff // (bs * fs)
    table = np.concatenate(tables(length), axis=0)
    feats = features(length, freq_w1.shape[0] // 2)
    feats_aug = np.concatenate(
        [feats, np.ones((1, length), np.float32), np.zeros((7, length), np.float32)], axis=0
    )

    x_own = tokens[:, 0]
    ct_own = cotangent[:, 0]
    ids = seg_ids
    at = jnp.stack([me, row & 1, (row >> 1) & 1, (row >> 2) & 1, row]).astype(jnp.int32)
    norms = jnp.concatenate([ln1_gain, ln1_shift, ln2_gain, ln2_shift]).reshape(4, channels)
    condt = cond_w.T

    def gather_after(value, after):
        two = swap(value, "freq", 2)
        one = swap(value, "freq", 1)
        (two,) = tie([two], after)
        return (value, one, two, swap(two, "freq", 1))

    def gather_wide(value, after):
        count = bs * fs
        parts = (
            value,
            swap(value, "freq", 2),
            swap(value, "batch", 2),
            lax.ppermute(value, ("batch", "freq"), [(i, i ^ (2 * fs + 2)) for i in range(count)]),
        )
        parts = parts[:1] + tuple(tie(parts[1:], after))
        return parts + tuple(swap(part, "freq", 1) for part in parts)

    def pairs(value):
        return value.reshape((value.shape[0] // 2, 2) + value.shape[1:])

    w_mine, w2x, w2t, taps, base, waves = prepare(
        at, w_in, freq_w2, conv_taps, freq_w1, freq_b1, jnp.asarray(feats_aug), jnp.asarray(table), norms, step, fs
    )
    x_parts = gather_after(x_own, base)
    forward = forward_spectral(at, x_parts, ids, norms, w_mine, taps, base, w2x, condt, waves)
    z_parts, (u1, n1, p, q, c, vr, vs, mu, mn, cb) = forward[:4], forward[4:]
    ct_x = swap(ct_own, "freq", 2)
    ct_z = swap(ct_own, "batch", 2)
    z_got = trade_parts(z_parts)
    wg_mine, wu_mine = select_columns(at, cb, w_gate, w_up, bs, fs)
    (ct_x,) = tie([ct_x], cb)
    ct_parts = (ct_own, ct_x, ct_z, swap(ct_x, "batch", 2))
    h, u2, z_t = middle(at, z_got, x_own, w_out, norms, wg_mine, step)
    fed = feed_forward(
        at, u2, h, ct_own, norms, w_out, w_gate, w_up, w_down, step, channels // (bs * fs)
    )
    mixed_out, big_g, gz_parts, gt_own, gt_other, sums2 = fed[0], fed[1], fed[2:6], *fed[6:]
    u2_parts = gather_wide(u2, sums2)
    ct_parts = ct_parts + tuple(swap(part, "freq", 1) for part in tie(ct_parts, sums2))
    gz_got = trade_parts(gz_parts)

    gt_got = swap(gt_other, "freq", 1)
    z_got = swap(z_t, "freq", 1)
    keep_a, give_a, keep_b, give_b, keep_o, give_o = hidden_grads(
        at, u2_parts, ct_parts, wg_mine, wu_mine, gt_own, gt_got, z_t, z_got,
        w_down.reshape(bs, fs, fw, channels), sums2,
    )
    got_a = swap(give_a, "batch", 1)
    got_b = swap(give_b, "batch", 4)
    got_o = swap(give_o, "freq", 2)

    back = backward_spectral(
        at, gz_got, ids, cb, taps, base, w2x, w2t, jnp.asarray(feats).astype(BF16),
        p, q, c, vr, vs, waves, give_a,
    )
    gp_parts, (gp, d_taps, d_w2, d_w1, gcb) = back[:4], back[4:]
    gp_got = trade_parts(gp_parts)

    keep_a, give_a, keep_b, give_b = halve(
        at, (2, 0), gp, keep_a[None], got_a[None], keep_b[None], got_b[None]
    )
    got_a = swap(give_a, "batch", 4)
    got_b = swap(give_b, "batch", 1)

    proj = projection_grads(
        at, gp, u1, n1, w_mine, keep_o, got_o, d_w2, d_w1, d_taps, gcb, condt, mu, mn, sums2, give_a, bs
    )
    p_keep_a, p_give_a, p_keep_b, p_give_b, packed = proj
    p_got_a = swap(p_give_a, "batch", 1)
    p_got_b = swap(p_give_b, "batch", 2)
    p_keep_a, p_give_a, p_keep_b, p_give_b, packed = stage(
        at, p_give_a, pairs(p_keep_a), pairs(p_got_a), p_keep_b, p_got_b, packed
    )
    p_got_a = swap(p_give_a, "batch", 2)
    p_got_b = swap(p_give_b, "batch", 1)
    d_gate, d_up, d_down, token = hidden_last(keep_a, got_a, keep_b, got_b, packed)
    keep, give, packed = join(at, token, p_keep_a, p_got_a, p_keep_b, p_got_b, packed)
    grad_tokens = final(at, gp_got, x_own, big_g, norms, ids, condt, w_in, packed, step)
    got = swap(give, "batch", 4)
    sent = add(packed, swap(packed, "batch", 4), give, BF16)
    mine = keep.astype(F32) + got.astype(F32)
    first = 2 * width // bs

    d_w2, d_taps, *ln, d_w1, d_b1, d_cond = small_grads(
        at, gather_freq(sent, me), freq_w1.shape[1], channels, step, bs
    )
    return (
        mixed_out[:, None],
        grad_tokens[:, None],
        ln[0],
        ln[1],
        mine[:first].T,
        d_taps,
        d_w1,
        d_b1[0],
        d_w2,
        d_cond.T,
        mine[first:].T,
        ln[2],
        ln[3],
        d_gate.T,
        d_up.T,
        d_down,
    )


def per_device(*args):
    channels = args[0].shape[2]
    step = 2 * channels // (lax.axis_size("batch") * lax.axis_size("freq"))
    fits = lax.axis_size("batch") == 8 and lax.axis_size("freq") == 4 and step % 16 == 0
    return tiled_device(*args) if fits else plain_device(*args)


def solution(mesh):
    rows = P("freq", "batch", None)
    split = P(None, ("batch", "freq"))
    in_specs = (rows, P("batch", None), rows) + (P(),) * 14
    out_specs = (
        rows,
        rows,
        P(),
        P(),
        split,
        P(),
        P(),
        P(),
        P(),
        P(),
        split,
        P(),
        P(),
        split,
        split,
        P(("batch", "freq"), None),
    )
    return jax.shard_map(
        per_device, mesh=mesh, in_specs=in_specs, out_specs=out_specs, check_vma=False
    )
```

```python
import functools

import jax
import jax.numpy as jnp
import ml_dtypes
import numpy as np
from jax import lax
from jax.experimental import pallas as pl
from jax.experimental.pallas import tpu as pltpu
from jax.sharding import PartitionSpec as P

SEGS = 3
EPS = 1e-05
HIGH = lax.Precision.HIGHEST
F32 = jnp.float32
BF16 = jnp.bfloat16


def mm(a, b):
    return jnp.dot(a, b, preferred_element_type=F32)


def mm_nt(a, b):
    return lax.dot_general(a, b, (((1,), (1,)), ((), ())), preferred_element_type=F32)


def mm_tn(a, b):
    return lax.dot_general(a, b, (((0,), (0,)), ((), ())), preferred_element_type=F32)


def swap(value, axis, mask):
    count = lax.axis_size(axis)
    return lax.ppermute(value, axis, [(i, i ^ mask) for i in range(count)])


def pick(parts, index):
    return lax.dynamic_index_in_dim(parts, index, 0, keepdims=False)


def in_order(received, me):
    a, b, c, d = received
    low = (me & 1) == 1
    a, b = jnp.where(low, b, a), jnp.where(low, a, b)
    c, d = jnp.where(low, d, c), jnp.where(low, c, d)
    high = (me & 2) == 2
    a, c = jnp.where(high, c, a), jnp.where(high, a, c)
    b, d = jnp.where(high, d, b), jnp.where(high, b, d)
    return (a, b, c, d)


def trade(blocks, me):
    return [pick(blocks, me)] + [swap(pick(blocks, me ^ k), "freq", k) for k in (2, 3, 1)]


def trade_sorted(blocks, me):
    own, two, three, one = trade(blocks, me)
    return in_order((own, one, two, three), me)


def gather_freq(value, me):
    two = swap(value, "freq", 2)
    one = swap(value, "freq", 1)
    three = swap(two, "freq", 1)
    return (value, one, two, three)


def scatter_sum(value, order):
    bits = lax.axis_size("batch").bit_length() - 1
    me = lax.axis_index("batch")
    rest = value.shape[1:]
    value = value.reshape((2,) * bits + rest)
    left = list(range(bits - 1, -1, -1))
    for bit in order:
        dim = left.index(bit)
        mine = (me >> bit) & 1
        keep = lax.dynamic_index_in_dim(value, mine, dim, keepdims=False)
        give = lax.dynamic_index_in_dim(value, 1 - mine, dim, keepdims=False)
        got = swap(give, "batch", 1 << bit)
        total = keep.astype(F32) + got.astype(F32)
        left.remove(bit)
        value = total.astype(value.dtype) if left else total
    return value


def tables(length):
    index = np.arange(length, dtype=np.int64)
    angle = (index[:, None] * index[None, :] % (2 * length)) * (np.pi / length)
    return (
        np.cos(angle).astype(ml_dtypes.bfloat16),
        np.sin(angle).astype(ml_dtypes.bfloat16),
    )


def features(length, half):
    index = np.arange(length, dtype=np.int64)
    lags = (np.arange(half, dtype=np.int64) + 1) ** 2
    angle = (lags[:, None] * index[None, :] % (2 * length)) * (np.pi / length)
    return np.concatenate([np.cos(angle), np.sin(angle)], axis=0).astype(np.float32)


def normed(values):
    centered = values - jnp.mean(values, axis=-1, keepdims=True)
    scale = lax.rsqrt(jnp.mean(centered * centered, axis=-1, keepdims=True) + EPS)
    return centered * scale, scale


def norm_back(unit, scale, grad):
    return scale * (
        grad
        - jnp.mean(grad, axis=-1, keepdims=True)
        - unit * jnp.mean(grad * unit, axis=-1, keepdims=True)
    )


def shift_right(values):
    return jnp.pad(values, ((0, 0), (1, 0)))[:, :-1]


def shift_left(values):
    return jnp.pad(values, ((0, 0), (0, 1)))[:, 1:]


def plain_device(
    tokens,
    seg_ids,
    cotangent,
    ln1_gain,
    ln1_shift,
    w_in,
    conv_taps,
    freq_w1,
    freq_b1,
    freq_w2,
    cond_w,
    w_out,
    ln2_gain,
    ln2_shift,
    w_gate,
    w_up,
    w_down,
):
    quarter, _, channels = tokens.shape
    length = seg_ids.shape[1]
    ff = w_gate.shape[1]
    fs = lax.axis_size("freq")
    bs = lax.axis_size("batch")
    me = lax.axis_index("freq")
    width = channels // fs
    half = bs // 2
    step = channels // (half * fs)
    cos_table, sin_table = tables(length)
    feats = features(length, freq_w1.shape[0] // 2)

    x_own = tokens[:, 0]
    ct_own = cotangent[:, 0]
    ids = seg_ids
    x_parts = gather_freq(x_own, me)
    ct_parts = gather_freq(ct_own, me)

    w_in_t = (
        w_in.T.reshape(2, half, fs, step, channels)
        .transpose(2, 0, 1, 3, 4)
        .reshape(fs, 2 * width, channels)
    )
    w_in_mine = pick(w_in_t, me)
    w_out_p = (
        w_out.reshape(half, fs, step, channels).transpose(1, 0, 2, 3).reshape(channels, channels)
    )
    taps_mine = pick(
        conv_taps.reshape(3, 2, half, fs, step).transpose(3, 0, 1, 2, 4).reshape(fs, 3, 2 * width), me
    )[:, :, None]
    w2_mine = pick(
        freq_w2.reshape(-1, 2, half, fs, step).transpose(3, 0, 1, 2, 4).reshape(fs, -1, 2 * width), me
    )
    fw = ff // (bs * fs)
    wide = ff // fs

    def mine_rows(weight):
        return pick(
            weight.reshape(bs, fs, fw, channels).transpose(1, 0, 2, 3).reshape(fs, wide, channels), me
        )

    wg_mine, wu_mine, wd_mine = (mine_rows(w_gate.T), mine_rows(w_up.T), mine_rows(w_down))

    base = jnp.dot(freq_w1.T, feats, precision=HIGH) + freq_b1[:, None]

    x_row = jnp.concatenate(in_order(x_parts, me), axis=0).astype(F32)
    unit1, _ = normed(x_row)
    u1 = (unit1 * ln1_gain + ln1_shift).astype(BF16)
    n1 = unit1.astype(BF16)
    masks = (ids == jnp.arange(SEGS, dtype=jnp.int32)[:, None]).astype(F32)
    counts = jnp.sum(masks, axis=1, keepdims=True)
    mu = mm(masks.astype(BF16), u1) / counts
    mn = mm(masks.astype(BF16), n1) / counts
    cb = jnp.dot(mu, cond_w, precision=HIGH)
    p = mm_nt(w_in_mine, u1)
    same = (ids[:, 1:] == ids[:, :-1]).astype(F32)
    zero = jnp.zeros((1, 1), F32)
    prev = jnp.concatenate([zero, same], axis=1)
    nxt = jnp.concatenate([same, zero], axis=1)
    p_prev = shift_right(p) * prev
    p_next = shift_left(p) * nxt
    s = taps_mine[0] * p_prev + taps_mine[1] * p + taps_mine[2] * p_next
    q, v = s[:width], s[width:]

    pre = base[None] + cb[:, :, None]
    gate_pre = jax.nn.sigmoid(pre)
    hk = pre * gate_pre
    kk = jnp.einsum("kc,jkf->jcf", w2_mine, hk, precision=HIGH)
    kr, ki = kk[:, :width], kk[:, width:]
    vm = (v[None] * masks[:, None, :]).astype(BF16).reshape(SEGS * width, length)
    vr = mm(vm, cos_table).reshape(SEGS, width, length)
    vi = -mm(vm, sin_table).reshape(SEGS, width, length)
    weights = np.full((length,), 2.0 / (2 * length), np.float32)
    weights[0] = 1.0 / (2 * length)
    yr = ((kr * vr - ki * vi) * weights).astype(BF16).reshape(SEGS * width, length)
    yi = ((kr * vi + ki * vr) * weights).astype(BF16).reshape(SEGS * width, length)
    conv = (mm(yr, cos_table) - mm(yi, sin_table)).reshape(SEGS, width, length)
    c = jnp.sum(conv * masks[:, None, :], axis=0)
    z_mine = (q * c).astype(BF16)

    z_blocks = z_mine.reshape(width, fs, quarter).transpose(1, 0, 2)
    z_t = jnp.concatenate(trade_sorted(z_blocks, me), axis=0)

    x32 = x_own.astype(F32)
    ct32 = ct_own.astype(F32)
    h = x32 + mm_tn(z_t, w_out_p)
    unit2, scale2 = normed(h)
    u2 = (unit2 * ln2_gain + ln2_shift).astype(BF16)
    u2_parts = gather_freq(u2, me)
    g = mm(u2, w_gate)
    a = mm(u2, w_up)
    gh = mm_nt(ct_own, w_down)
    sg = jax.nn.sigmoid(g)
    silu = g * sg
    hid = (silu * a).astype(BF16)
    mixed_out = (h + mm(hid, w_down)).astype(BF16)
    gg = (gh * a * sg * (1.0 + g * (1.0 - sg))).astype(BF16)
    ga = (gh * silu).astype(BF16)
    gu2 = mm_nt(gg, w_gate) + mm_nt(ga, w_up)
    grad_ln2_gain = jnp.sum(gu2 * unit2, axis=0)
    grad_ln2_shift = jnp.sum(gu2, axis=0)
    big_g = ct32 + norm_back(unit2, scale2, gu2 * ln2_gain)
    gb = big_g.astype(BF16)
    gz_blocks = mm_nt(w_out_p, gb).astype(BF16).reshape(fs, width, quarter)
    gz = jnp.concatenate(trade_sorted(gz_blocks, me), axis=1).astype(F32)
    gb_parts = gather_freq(gb, me)

    u2_row = jnp.concatenate(u2_parts, axis=0)
    ct_row = jnp.concatenate(ct_parts, axis=0)
    g_t = mm_nt(wg_mine, u2_row)
    a_t = mm_nt(wu_mine, u2_row)
    gh_t = mm_nt(wd_mine, ct_row)
    sg_t = jax.nn.sigmoid(g_t)
    silu_t = g_t * sg_t
    hid_t = (silu_t * a_t).astype(BF16)
    gg_t = (gh_t * a_t * sg_t * (1.0 + g_t * (1.0 - sg_t))).astype(BF16)
    ga_t = (gh_t * silu_t).astype(BF16)
    d_gate = mm(gg_t, u2_row).astype(BF16)
    d_up = mm(ga_t, u2_row).astype(BF16)
    d_down = mm(hid_t, ct_row).astype(BF16)
    d_ff = jnp.stack([d_gate, d_up, d_down], axis=0).reshape(3, bs, fw, channels).transpose(1, 0, 2, 3)
    bits = bs.bit_length() - 1
    order_a = list(range(bits))
    order_b = [1, 0] + list(range(2, bits))
    cut = channels // 2
    ff_a = scatter_sum(d_ff[..., :cut], order_a)
    ff_b = scatter_sum(d_ff[..., cut:], order_b)
    d_ff = jnp.concatenate([ff_a, ff_b], axis=-1)

    gq = gz * c
    gc = gz * q
    gcm = (gc[None] * masks[:, None, :]).astype(BF16).reshape(SEGS * width, length)
    gyr = mm(gcm, cos_table).reshape(SEGS, width, length) * weights
    gyi = -mm(gcm, sin_table).reshape(SEGS, width, length) * weights
    gkr = gyr * vr + gyi * vi
    gki = gyi * vr - gyr * vi
    gvr = (kr * gyr + ki * gyi).astype(BF16).reshape(SEGS * width, length)
    gvi = (kr * gyi - ki * gyr).astype(BF16).reshape(SEGS * width, length)
    gv_all = (mm(gvr, cos_table) - mm(gvi, sin_table)).reshape(SEGS, width, length)
    gv = jnp.sum(gv_all * masks[:, None, :], axis=0)
    gs = jnp.concatenate([gq, gv], axis=0)
    d_taps = jnp.stack(
        [jnp.sum(gs * p_prev, axis=1), jnp.sum(gs * p, axis=1), jnp.sum(gs * p_next, axis=1)]
    )
    gp = (
        taps_mine[1] * gs
        + taps_mine[0] * shift_left(gs * prev)
        + taps_mine[2] * shift_right(gs * nxt)
    ).astype(BF16)

    gkk = jnp.concatenate([gkr, gki], axis=1)
    gkk_low = gkk.astype(BF16)
    hk_low = hk.astype(BF16)
    d_w2 = jnp.einsum("jkf,jcf->kc", hk_low, gkk_low, preferred_element_type=F32)
    gpre = jnp.einsum("kc,jcf->jkf", w2_mine.astype(BF16), gkk_low, preferred_element_type=F32)
    gpre = gpre * gate_pre * (1.0 + pre * (1.0 - gate_pre))
    d_w1 = jnp.einsum("ef,jkf->ek", feats, gpre, precision=HIGH)
    gcb = jnp.sum(gpre, axis=2)
    gcb_row = lax.psum(gcb, "freq")

    gp_blocks = gp.reshape(2 * width, fs, quarter).transpose(1, 0, 2)
    gp_t = jnp.concatenate(trade_sorted(gp_blocks, me), axis=0)

    u1_row = u1
    d_in = mm(gp, u1_row).astype(BF16).reshape(bs, 2 * width // bs, channels)
    d_in = scatter_sum(d_in, order_a)
    gb_row = jnp.concatenate(in_order(gb_parts, me), axis=0)
    d_out = mm(z_mine, gb_row)
    narrow = channels // bs
    d_out = scatter_sum(d_out.T.astype(BF16).reshape(bs, narrow, width), order_a)
    d_out = d_out.reshape(fs, narrow // fs, width)
    d_out = jnp.stack(trade_sorted(d_out, me), axis=0)
    d_out = (
        d_out.reshape(fs, narrow // fs, half, step).transpose(2, 0, 3, 1).reshape(channels, -1)
    )

    gmu_part = jnp.dot(gcb, cond_w.T, precision=HIGH)
    sum_gp = jnp.sum(gp.astype(F32), axis=1)
    w_mine32 = w_in_mine.astype(F32)
    d_shift1 = jnp.dot(sum_gp[None], w_mine32, precision=HIGH)[0] + jnp.sum(gmu_part, axis=0)
    d_gain1 = jnp.sum(mm(gp, n1) * w_mine32, axis=0) + jnp.sum(gmu_part * mn, axis=0)

    gmu = jnp.dot(gcb_row, cond_w.T, precision=HIGH) / counts
    own_masks = lax.dynamic_slice_in_dim(masks, me * quarter, quarter, 1)
    gu1 = mm_tn(gp_t, w_in_t.reshape(2 * channels, channels)) + lax.dot_general(
        own_masks, gmu, (((0,), (0,)), ((), ())), precision=HIGH
    )
    unit_own, scale_own = normed(x32)
    grad_tokens = big_g + norm_back(unit_own, scale_own, gu1 * ln1_gain)

    shared = [
        d_gain1,
        d_shift1,
        d_w1.reshape(-1),
        jnp.sum(gcb, axis=0),
        jnp.dot(mu.T, gcb, precision=HIGH).reshape(-1),
        grad_ln2_gain,
        grad_ln2_shift,
    ]
    owned = jnp.concatenate([d_taps, d_w2], axis=0)
    packed = jnp.concatenate(shared + [owned.reshape(-1)])
    for bit in range(bits):
        packed = packed + swap(packed, "batch", 1 << bit)
    split = packed.shape[0] - owned.size
    common, owned = packed[:split], packed[split:]
    common = common + swap(common, "freq", 1)
    common = common + swap(common, "freq", 2)
    owned = jnp.stack(in_order(gather_freq(owned, me), me), axis=0)
    owned = (
        owned.reshape(fs, -1, 2, half, step).transpose(1, 2, 3, 0, 4).reshape(-1, 2 * channels)
    )
    sizes = np.cumsum([part.size for part in shared])
    got = jnp.split(common, sizes[:-1])
    return (
        mixed_out[:, None],
        grad_tokens[:, None],
        got[0],
        got[1],
        d_in.T,
        owned[:3],
        got[2].reshape(freq_w1.shape),
        got[3],
        owned[3:],
        got[4].reshape(cond_w.shape),
        d_out,
        got[5],
        got[6],
        d_ff[0].T,
        d_ff[1].T,
        d_ff[2],
    )


VM = pl.BlockSpec(memory_space=pltpu.VMEM)
SM = pl.BlockSpec(memory_space=pltpu.SMEM)
HBM = pl.BlockSpec(memory_space=pl.ANY)
MIB = 1 << 20


def params(mib):
    return pltpu.CompilerParams(vmem_limit_bytes=mib * MIB)


def cost(micros):
    return pl.CostEstimate(
        flops=int(micros * 1000000000.0), bytes_accessed=int(micros * 3500000.0), transcendentals=0
    )


def shape(dims, dtype):
    return pltpu.VMEM(dims, dtype)


def far(dims, dtype):
    return pltpu.HBM(dims, dtype)


def in_hbm(*values):
    kept = tuple(pltpu.with_memory_space_constraint(value, pltpu.HBM) for value in values)
    return kept if len(kept) > 1 else kept[0]


def in_vmem(value):
    return pltpu.with_memory_space_constraint(value, pltpu.VMEM)


def sigmoid(value):
    return 1.0 / (1.0 + jnp.exp(-value))


def dma_all(pairs, sems, first=0):
    copies = [
        pltpu.make_async_copy(source, target, sems.at[first + i])
        for i, (source, target) in enumerate(pairs)
    ]
    for copy in copies:
        copy.start()
    return copies


def tie_kernel(*refs):
    pass


def tie(values, *after):
    count = len(values)
    return pl.pallas_call(
        tie_kernel,
        in_specs=[HBM] * (count + len(after)),
        out_specs=[HBM] * count,
        out_shape=[jax.ShapeDtypeStruct(value.shape, value.dtype) for value in values],
        input_output_aliases={i: i for i in range(count)},
        compiler_params=params(1),
        name="tie",
    )(*values, *after)


def one_hot_rows(me, rows, lanes, piece, fs):
    row = lax.broadcasted_iota(jnp.int32, (rows, lanes), 0)
    lane = lax.broadcasted_iota(jnp.int32, (rows, lanes), 1)
    block = jnp.zeros_like(row)
    for m in range(1, rows // piece):
        block = block + jnp.where(row >= m * piece, 1, 0)
    return jnp.where(lane == block * ((fs - 1) * piece) + me * piece + row, 1.0, 0.0)


def prepare_kernel(
    me_ref, w_in, freq_w2, conv_taps, freq_w1, freq_b1, feats, waves_far, w_far, x_far, cond_far, norms,
    w_mine, w2x, w2t, taps, base, waves, w_near, x_near, cond_near, w1_aug, sems, *, step, fs,
):
    loads = dma_all(
        [(waves_far, waves), (w_far, w_near), (x_far, x_near), (cond_far, cond_near)], sems
    )
    lanes = w_in.shape[1] // 4
    rows = lanes // fs
    sel = one_hot_rows(me_ref[0], rows, lanes, step, fs)
    low = sel.astype(BF16)
    hidden = freq_w2.shape[0]
    for i in range(4):
        out = slice(i * rows, (i + 1) * rows)
        group = slice(i * lanes, (i + 1) * lanes)
        w_mine[out, :] = mm_nt(low, w_in[:, group]).astype(BF16)
        both = jnp.concatenate([freq_w2[:, group], conv_taps[:, group]], axis=0)
        mine = lax.dot_general(
            sel, both, (((1,), (1,)), ((), ())), precision=HIGH, preferred_element_type=F32
        )
        taps[out, :3] = mine[:, hidden:]
        mine = mine[:, :hidden]
        high = mine.astype(BF16)
        rest = (mine - high.astype(F32)).astype(BF16)
        w2x[out, :] = jnp.concatenate([high, high, rest], axis=1)
    w2t[...] = jnp.transpose(w2x[...][:, :hidden].astype(F32)).astype(BF16)
    w1_aug[...] = jnp.zeros_like(w1_aug)
    count = freq_w1.shape[0]
    w1_aug[:count, :] = freq_w1[...]
    w1_aug[count : count + 1, :] = freq_b1[...]
    base[...] = lax.dot_general(
        w1_aug[...], feats[...], (((0,), (0,)), ((), ())), precision=HIGH, preferred_element_type=F32
    )
    for load in loads:
        load.wait()


def prepare(me, w_in, freq_w2, conv_taps, freq_w1, freq_b1, feats, waves, w_out, x, condt, norms, step, fs):
    channels, both = w_in.shape
    hidden = freq_w2.shape[0]
    length = feats.shape[1]
    return pl.pallas_call(
        functools.partial(prepare_kernel, step=step, fs=fs),
        in_specs=[SM] + [VM] * 6 + [HBM] * 5,
        out_specs=[VM] * 9,
        out_shape=[
            shape((both // fs, channels), BF16),
            shape((both // fs, 3 * hidden), BF16),
            shape((hidden, both // fs), BF16),
            shape((both // fs, 8), F32),
            shape((hidden, length), F32),
            shape((2 * length, length), BF16),
            shape(w_out.shape, BF16),
            shape(x.shape, BF16),
            shape(condt.shape, F32),
        ],
        scratch_shapes=[
            pltpu.VMEM((feats.shape[0], hidden), F32),
            pltpu.SemaphoreType.DMA((4,)),
        ],
        compiler_params=params(24),
        cost_estimate=cost(3),
        name="prepare",
    )(me, *in_hbm(w_in, freq_w2, conv_taps, freq_w1), freq_b1[None], in_hbm(feats), in_hbm(waves), *in_hbm(w_out, x, condt), norms)


def select_kernel(at_ref, after, gate, up, down, gate_out, up_out, down_out, *, fs):
    down_out[...] = down[0, 0]
    rows = gate_out.shape[0]
    sel = one_hot_rows(at_ref[0], rows, rows * fs, rows, fs).astype(BF16)
    gate_out[...] = mm_nt(sel, gate[...]).astype(BF16)
    up_out[...] = mm_nt(sel, up[...]).astype(BF16)


def select_columns(at, after, w_gate, w_up, w_down, bs, fs):
    channels, ff = w_gate.shape
    lanes = ff // bs
    wide = pl.BlockSpec((channels, lanes), lambda i, at: (0, (i // 2) * 4 + at[2] * 2 + i % 2))
    rows = pl.BlockSpec((lanes // fs, channels), lambda i, at: (i, 0))
    down = pl.BlockSpec(
        (1, 1, lanes // fs, channels),
        lambda i, at: ((i // 2) * 4 + at[2] * 2 + i % 2, at[0], 0, 0),
    )
    return pl.pallas_call(
        functools.partial(select_kernel, fs=fs),
        grid_spec=pltpu.PrefetchScalarGridSpec(
            num_scalar_prefetch=1,
            grid=(bs // 2,),
            in_specs=[HBM, wide, wide, down],
            out_specs=[rows, rows, rows],
        ),
        out_shape=[shape((ff // (2 * fs), channels), BF16)] * 3,
        compiler_params=params(20),
        cost_estimate=cost(5),
        name="select_columns",
    )(at, after, in_hbm(w_gate), in_hbm(w_up), in_hbm(w_down.reshape(bs, fs, lanes // fs, channels)))


def row_masks(ids):
    lane = lax.broadcasted_iota(jnp.int32, ids.shape, 1)
    length = ids.shape[1]
    prev = jnp.where((ids == pltpu.roll(ids, 1, 1)) & (lane > 0), 1.0, 0.0)
    nxt = jnp.where((ids == pltpu.roll(ids, length - 1, 1)) & (lane < length - 1), 1.0, 0.0)
    return prev, nxt


def bin_weights(start, width, length):
    lane = lax.broadcasted_iota(jnp.int32, (1, width), 1) + start
    return jnp.where(lane == 0, 0.5 / length, 1.0 / length)


def tile(index, size):
    return pl.ds(pl.multiple_of(index * size, size), size)


def hidden_tile(base, cb, j, lanes):
    pre = base[:, lanes] + cb[:, j : j + 1]
    return pre, sigmoid(pre)


def kernel_tile(w2x, hk):
    high = hk.astype(BF16)
    rest = (hk - high.astype(F32)).astype(BF16)
    return mm(w2x[...], jnp.concatenate([high, rest, high], axis=0))


def forward_kernel(
    me_ref, ids_at, x0, x1, x2, x3, ids_ref, norms, w, taps, base, w2x, condt, waves,
    z0, z1, z2, z3, u1, n1, p_out, q_out, c_out, vr_out, vs_out, mu_out, mn_out, cb_out,
    p, q, vm, ycat, acc,
):
    quarter = x0.shape[0]
    width, length = q_out.shape
    tiles = length // quarter
    me = me_ref[0]
    for k, x in enumerate((x0, x1, x2, x3)):
        values = x[...].astype(F32)
        unit, _ = normed(values)
        rows = tile(me ^ k, quarter)
        n1[rows, :] = unit.astype(BF16)
        u1[rows, :] = (unit * norms[0:1, :] + norms[1:2, :]).astype(BF16)
    ids = ids_ref[...]
    number = lax.broadcasted_iota(jnp.int32, (8, length), 0)
    member = jnp.where(ids == number, 1.0, 0.0)
    counts = jnp.maximum(jnp.sum(member, axis=1, keepdims=True), 1.0)
    member_low = member.astype(BF16)
    mu = mm(member_low, u1[...]) / counts
    mu_out[...] = mu
    mn_out[...] = mm(member_low, n1[...]) / counts
    cb_out[...] = lax.dot_general(
        condt[...], mu, (((1,), (1,)), ((), ())), precision=HIGH, preferred_element_type=F32
    )
    prev, nxt = row_masks(ids)
    for t in range(tiles):
        at = slice(t * quarter, (t + 1) * quarter)
        p[:, at] = mm_nt(w[...], u1[at, :])
    chunk = width // 2
    for r in range(4):
        at = slice(r * chunk, (r + 1) * chunk)
        here = p[at, :]
        p_out[at, :] = here.astype(BF16)
        mixed = (
            taps[at, 0:1] * (pltpu.roll(here, 1, 1) * prev)
            + taps[at, 1:2] * here
            + taps[at, 2:3] * (pltpu.roll(here, length - 1, 1) * nxt)
        )
        if r < 2:
            q[at, :] = mixed
            q_out[at, :] = mixed.astype(BF16)
        else:
            for j in range(SEGS):
                lo = j * width + (r - 2) * chunk
                vm[lo : lo + chunk, :] = (mixed * member[j : j + 1, :]).astype(BF16)

    span = 2 * quarter

    @pl.loop(0, length // span)
    def _(f):
        lanes = tile(f, span)
        upper = pl.ds(pl.multiple_of(f * span + length, span), span)
        weight = bin_weights(f * span, span, length)
        vr_all = mm(vm[...], waves[:length, lanes])
        vs_all = mm(vm[...], waves[length:, lanes])
        vr_out[:, lanes] = vr_all.astype(BF16)
        vs_out[:, lanes] = vs_all.astype(BF16)
        for j in range(SEGS):
            pre, gate = hidden_tile(base, cb_out, j, lanes)
            kk = kernel_tile(w2x, pre * gate)
            kr, ki = kk[:width] * weight, kk[width:] * weight
            at = slice(j * width, (j + 1) * width)
            vr, vs = vr_all[at], vs_all[at]
            ycat[at, lanes] = (kr * vr + ki * vs).astype(BF16)
            ycat[at, upper] = (kr * vs - ki * vr).astype(BF16)

    for k, z_out in enumerate((z0, z1, z2, z3)):
        t = me ^ k
        lanes = tile(t, quarter)
        acc[...] = jnp.zeros_like(acc)
        ids_here = ids_ref[:, lanes]
        for j in range(SEGS):

            @pl.when((ids_at[0, t * quarter] <= j) & (ids_at[0, (t + 1) * quarter - 1] >= j))
            def _():
                at = slice(j * width, (j + 1) * width)
                part = mm(ycat[at, :], waves[:, lanes])
                acc[...] += jnp.where(ids_here == j, part, 0.0)

        c = acc[...]
        c_out[:, lanes] = c.astype(BF16)
        z = (q[:, lanes] * c).astype(BF16)
        z_out[...] = z


def forward_spectral(me, x_parts, ids, norms, w, taps, base, w2x, condt, waves):
    quarter, channels = x_parts[0].shape
    length = ids.shape[1]
    width = w.shape[0] // 2
    saved = [
        (length, channels),
        (length, channels),
        (2 * width, length),
        (width, length),
        (width, length),
        (SEGS * width, length),
        (SEGS * width, length),
    ]
    small = [
        shape((8, channels), F32),
        shape((8, channels), F32),
        shape((condt.shape[0], 8), F32),
    ]
    return pl.pallas_call(
        forward_kernel,
        in_specs=[SM, SM] + [VM] * 12,
        out_specs=[VM] * (7 + len(saved)),
        out_shape=[shape((width, quarter), BF16)] * 4 + [shape(dims, BF16) for dims in saved] + small,
        scratch_shapes=[
            pltpu.VMEM((2 * width, length), F32),
            pltpu.VMEM((width, length), F32),
            pltpu.VMEM((SEGS * width, length), BF16),
            pltpu.VMEM((SEGS * width, 2 * length), BF16),
            pltpu.VMEM((width, quarter), F32),
        ],
        compiler_params=params(26),
        cost_estimate=cost(15),
        name="forward_spectral",
    )(me, ids, *x_parts, ids, norms, w, taps, base, w2x, condt, waves)


def backward_kernel(
    me_ref, ids_at, g0, g1, g2, g3, ids_ref, cb, taps, base, w2x, w2, feats,
    p, q, c, vr_in, vs_in, waves, after,
    o0, o1, o2, o3, gp_row, d_taps, d_w2, d_w1, gcb,
    gcm, gvcat, gs, acc,
):
    width, quarter = g0.shape
    length = gp_row.shape[1]
    tiles = length // quarter
    hidden = base.shape[0]
    me = me_ref[0]
    for k, g in enumerate((g0, g1, g2, g3)):
        lanes = tile(me ^ k, quarter)
        gz = g[...].astype(F32)
        gs[:width, lanes] = gz * c[:, lanes].astype(F32)
        gc = gz * q[:, lanes].astype(F32)
        ids_here = ids_ref[:, lanes]
        for j in range(SEGS):
            gcm[j * width : (j + 1) * width, lanes] = jnp.where(ids_here == j, gc, 0.0).astype(BF16)
    d_w2[...] = jnp.zeros_like(d_w2)
    d_w1[...] = jnp.zeros_like(d_w1)
    gcb[...] = jnp.zeros_like(gcb)

    span = 2 * quarter

    @pl.loop(0, length // span)
    def _(f):
        lanes = tile(f, span)
        upper = pl.ds(pl.multiple_of(f * span + length, span), span)
        weight = bin_weights(f * span, span, length)
        gyr_all = mm(gcm[...], waves[:length, lanes]) * weight
        gys_all = mm(gcm[...], waves[length:, lanes]) * weight
        for j in range(SEGS):
            pre, gate = hidden_tile(base, cb, j, lanes)
            hk = pre * gate
            kk = kernel_tile(w2x, hk)
            kr, ki = kk[:width], kk[width:]
            at = slice(j * width, (j + 1) * width)
            gyr, gys = gyr_all[at], gys_all[at]
            vr, vs = vr_in[at, lanes].astype(F32), vs_in[at, lanes].astype(F32)
            gvcat[at, lanes] = (kr * gyr - ki * gys).astype(BF16)
            gvcat[at, upper] = (kr * gys + ki * gyr).astype(BF16)
            gkk = jnp.concatenate(
                [(gyr * vr + gys * vs).astype(BF16), (gyr * vs - gys * vr).astype(BF16)], axis=0
            )
            d_w2[...] += mm_nt(gkk, hk.astype(BF16))
            gpre = mm(w2[...], gkk) * (gate * (1.0 + pre * (1.0 - gate)))
            gcb[:, j : j + 1] += jnp.sum(gpre, axis=1, keepdims=True)
            d_w1[...] += mm_nt(feats[:, lanes], gpre.astype(BF16))

    for k in range(4):
        t = me ^ k
        lanes = tile(t, quarter)
        acc[...] = jnp.zeros_like(acc)
        ids_here = ids_ref[:, lanes]
        for j in range(SEGS):

            @pl.when((ids_at[0, t * quarter] <= j) & (ids_at[0, (t + 1) * quarter - 1] >= j))
            def _():
                at = slice(j * width, (j + 1) * width)
                part = mm(gvcat[at, :], waves[:, lanes])
                acc[...] += jnp.where(ids_here == j, part, 0.0)

        gs[width:, lanes] = acc[...]
    prev, nxt = row_masks(ids_ref[...])
    chunk = width // 2
    for r in range(4):
        at = slice(r * chunk, (r + 1) * chunk)
        here = p[at, :].astype(F32)
        grad = gs[at, :]
        d_taps[at, 0:1] = jnp.sum(grad * (pltpu.roll(here, 1, 1) * prev), axis=1, keepdims=True)
        d_taps[at, 1:2] = jnp.sum(grad * here, axis=1, keepdims=True)
        d_taps[at, 2:3] = jnp.sum(
            grad * (pltpu.roll(here, length - 1, 1) * nxt), axis=1, keepdims=True
        )
        gp_row[at, :] = (
            taps[at, 1:2] * grad
            + taps[at, 0:1] * pltpu.roll(grad * prev, length - 1, 1)
            + taps[at, 2:3] * pltpu.roll(grad * nxt, 1, 1)
        ).astype(BF16)
    share = jnp.transpose(gcb[...])[:8, :]
    high = share.astype(BF16)
    rest = (share - high.astype(F32)).astype(BF16)
    extra = jnp.concatenate([high, rest], axis=0)
    extra = jnp.concatenate([extra, jnp.zeros((16, quarter - hidden), BF16)], axis=1)
    for k, out in enumerate((o0, o1, o2, o3)):
        out[: 2 * width, :] = gp_row[:, tile(me ^ k, quarter)]
        out[2 * width :, :] = extra


def backward_spectral(
    me, gz_parts, ids, cb, taps, base, w2x, w2, feats, p, q, c, vr, vs, waves, after
):
    width, quarter = gz_parts[0].shape
    length = ids.shape[1]
    hidden = base.shape[0]
    outs = [shape((2 * width + 16, quarter), BF16)] * 4 + [
        shape((2 * width, length), BF16),
        shape((2 * width, 128), F32),
        shape((2 * width, hidden), F32),
        shape((feats.shape[0], hidden), F32),
        shape((hidden, 128), F32),
    ]
    return pl.pallas_call(
        backward_kernel,
        in_specs=[SM, SM] + [VM] * 17 + [HBM],
        out_specs=[VM] * 9,
        out_shape=outs,
        scratch_shapes=[
            pltpu.VMEM((SEGS * width, length), BF16),
            pltpu.VMEM((SEGS * width, 2 * length), BF16),
            pltpu.VMEM((2 * width, length), F32),
            pltpu.VMEM((width, quarter), F32),
        ],
        compiler_params=params(26),
        cost_estimate=cost(17),
        name="backward_spectral",
    )(
        me, ids, *gz_parts, ids, cb, taps, base, w2x, w2, feats, p, q, c, vr, vs, waves, after
    )


def middle_kernel(me_ref, z0, z1, z2, z3, x, w_out, norms, after, h_out, u2_out, z_t, *, piece):
    me = me_ref[0]
    width = z0.shape[0]
    for k, z in enumerate((z0, z1, z2, z3)):
        for i in range(width // piece):
            at = pl.ds(pl.multiple_of((i * 4 + (me ^ k)) * piece, piece), piece)
            z_t[at, :] = z[i * piece : (i + 1) * piece, :]
    h = x[...].astype(F32) + mm(jnp.transpose(z_t[...]), w_out[...])
    h_out[...] = h
    unit, _ = normed(h)
    u2_out[...] = (unit * norms[2:3, :] + norms[3:4, :]).astype(BF16)


def middle(me, z_parts, x, w_out, norms, after, piece):
    quarter, channels = x.shape
    return pl.pallas_call(
        functools.partial(middle_kernel, piece=piece),
        in_specs=[SM] + [VM] * 7 + [HBM],
        out_specs=[VM] * 3,
        out_shape=[
            shape((quarter, channels), F32),
            shape((quarter, channels), BF16),
            shape((channels, quarter), BF16),
        ],
        compiler_params=params(24),
        cost_estimate=cost(2),
        name="middle",
    )(me, *z_parts, x, w_out, norms, after)


def feed_kernel(
    me_ref, u2, h, ct, norms, w_out, gate, up, down,
    mixed, big_g, g0, g1, g2, g3, t_own, t_other, sums, acc_out, acc_grad, gz_t, gb_t, *, piece, thin,
):
    i = pl.program_id(0)

    @pl.when(i == 0)
    def _():
        acc_out[...] = jnp.zeros_like(acc_out)
        acc_grad[...] = jnp.zeros_like(acc_grad)

    g = mm(u2[...], gate[...])
    a = mm(u2[...], up[...])
    gh = mm_nt(ct[...], down[...])
    sg = sigmoid(g)
    silu = g * sg
    hid = (silu * a).astype(BF16)
    gg = (gh * a * (sg * (1.0 + g * (1.0 - sg)))).astype(BF16)
    ga = (gh * silu).astype(BF16)
    acc_out[...] += mm(hid, down[...])
    acc_grad[...] += mm_nt(gg, gate[...]) + mm_nt(ga, up[...])

    @pl.when(i == pl.num_programs(0) - 1)
    def _():
        me = me_ref[0]
        width = g0.shape[0]
        here = h[...]
        mixed[...] = (here + acc_out[...]).astype(BF16)
        gu2 = acc_grad[...]
        unit, scale = normed(here)
        sums[0:1, :] = jnp.sum(gu2 * unit, axis=0, keepdims=True)
        sums[1:2, :] = jnp.sum(gu2, axis=0, keepdims=True)
        total = ct[...].astype(F32) + norm_back(unit, scale, gu2 * norms[2:3, :])
        big_g[...] = total
        low = total.astype(BF16)
        gz_t[...] = mm_nt(w_out[...], low).astype(BF16)
        for k, out in enumerate((g0, g1, g2, g3)):
            for r in range(width // piece):
                at = pl.ds(pl.multiple_of((r * 4 + (me ^ k)) * piece, piece), piece)
                out[r * piece : (r + 1) * piece, :] = gz_t[at, :]
        gb_t[...] = jnp.transpose(total)
        for core, out in ((me & 1, t_own), (1 - (me & 1), t_other)):
            parts = []
            for x in range(2):
                for r in range(width // thin):
                    lo = pl.multiple_of((r * 4 + 2 * x + core) * thin, thin)
                    parts.append(gb_t[pl.ds(lo, thin), :])
            out[...] = jnp.concatenate(parts, axis=0).astype(BF16)


def feed_forward(me, u2, h, ct, norms, w_out, w_gate, w_up, w_down, piece, thin):
    quarter, channels = u2.shape
    ff = w_gate.shape[1]
    block = 512

    width = channels // 4
    outs = [
        ((quarter, channels), BF16),
        ((quarter, channels), F32),
    ] + [((width, quarter), BF16)] * 4 + [((2 * width, quarter), BF16)] * 2 + [((8, channels), F32)]
    return pl.pallas_call(
        functools.partial(feed_kernel, piece=piece, thin=thin),
        grid=(ff // block,),
        in_specs=[
            SM,
            VM,
            VM,
            VM,
            VM,
            VM,
            pl.BlockSpec((channels, block), lambda i: (0, i)),
            pl.BlockSpec((channels, block), lambda i: (0, i)),
            pl.BlockSpec((block, channels), lambda i: (i, 0)),
        ],
        out_specs=[VM] * len(outs),
        out_shape=[far(*outs[0])] + [shape(*out) for out in outs[1:]],
        scratch_shapes=[
            pltpu.VMEM((quarter, channels), F32),
            pltpu.VMEM((quarter, channels), F32),
            pltpu.VMEM((channels, quarter), BF16),
            pltpu.VMEM((channels, quarter), F32),
        ],
        compiler_params=params(28),
        cost_estimate=cost(13),
        name="feed_forward",
    )(me, u2, h, ct, norms, w_out, in_hbm(w_gate), in_hbm(w_up), in_hbm(w_down))


def hidden_grads_kernel(at_ref, *refs):
    u_parts, c_parts, refs = refs[:8], refs[8:16], refs[16:]
    gate, up, gt_own, gt_got, z_own, z_got, down, after, *refs = refs
    keep_a, give_a, keep_b, give_b, keep_o, give_o, rights, lefts, d_all, d_out = refs
    quarter, channels = u_parts[0].shape
    y, z = at_ref[1], at_ref[3]
    rows = gate.shape[0]
    for k in range(8):
        at = slice(k * quarter, (k + 1) * quarter)
        rights[0, at, :] = u_parts[k][...]
        rights[1, at, :] = c_parts[k][...]
    span = 2 * quarter

    @pl.loop(0, 4)
    def _(k):
        at = tile(k, span)
        g = mm_nt(gate[...], rights[0, at, :])
        a = mm_nt(up[...], rights[0, at, :])
        gh = mm_nt(down[...], rights[1, at, :])
        sg = sigmoid(g)
        silu = g * sg
        lefts[0, :, at] = (gh * a * (sg * (1.0 + g * (1.0 - sg)))).astype(BF16)
        lefts[1, :, at] = (gh * silu).astype(BF16)
        lefts[2, :, at] = (silu * a).astype(BF16)

    d_out[...] = mm_nt(gt_own[...], z_own[...]) + mm_nt(gt_got[...], z_got[...])
    half = keep_o.shape[0]
    x = at_ref[0] >> 1
    keep_o[...] = d_out[tile(x, half), :].astype(BF16)
    give_o[...] = d_out[tile(1 - x, half), :].astype(BF16)
    fw = rows // 4
    cut = keep_a.shape[-1]

    @pl.loop(0, 3)
    def _(m):
        grad = mm(lefts[m], rights[m >> 1]).astype(BF16)
        for i in range(4):
            d_all[i, m] = grad[i * fw : (i + 1) * fw]

    for i in range(2):
        keep_a[i] = d_all[2 * i + y, :, :, :cut]
        give_a[i] = d_all[2 * i + 1 - y, :, :, :cut]
        keep_b[i] = d_all[2 * z + i, :, :, cut:]
        give_b[i] = d_all[2 * (1 - z) + i, :, :, cut:]


def hidden_grads(at, u2_parts, ct_parts, gate, up, gt_own, gt_got, z_own, z_got, down, after):
    quarter, channels = u2_parts[0].shape
    wide = gate.shape[0]
    fw = wide // 4
    fs = 4
    cut = 2 * channels // 3
    return pl.pallas_call(
        hidden_grads_kernel,
        grid_spec=pltpu.PrefetchScalarGridSpec(
            num_scalar_prefetch=1,
            grid=(1,),
            in_specs=[VM] * 23 + [HBM],
            out_specs=[VM] * 6,
            scratch_shapes=[
                pltpu.VMEM((2, 8 * quarter, channels), BF16),
                pltpu.VMEM((3, wide, 8 * quarter), BF16),
                pltpu.VMEM((4, 3, fw, channels), BF16),
                pltpu.VMEM((2 * channels // fs, channels), F32),
            ],
        ),
        out_shape=[shape((2, 3, fw, cut), BF16)] * 2
        + [shape((2, 3, fw, channels - cut), BF16)] * 2
        + [shape((channels // fs, channels), BF16)] * 2,
        compiler_params=params(34),
        cost_estimate=cost(14),
        name="hidden_grads",
    )(at, *u2_parts, *ct_parts, gate, up, gt_own, gt_got, z_own, z_got, down, after)


def halve_kernel(at_ref, after, *refs, bits):
    pairs = len(bits)
    ins, outs = refs[: 2 * pairs], refs[2 * pairs :]
    for n in range(pairs):
        mine = at_ref[bits[n] + 1]
        keep, got = ins[2 * n], ins[2 * n + 1]
        next_keep, next_give = outs[2 * n], outs[2 * n + 1]
        for i in range(keep.shape[0]):
            for side, out in ((mine, next_keep), (1 - mine, next_give)):
                out[i] = (keep[i, side].astype(F32) + got[i, side].astype(F32)).astype(BF16)


def halve(at, bits, after, *sums):
    outs = []
    for n in range(len(bits)):
        dims = sums[2 * n].shape
        outs += [shape((dims[0],) + dims[2:], BF16)] * 2
    return pl.pallas_call(
        functools.partial(halve_kernel, bits=bits),
        in_specs=[SM, HBM] + [VM] * len(sums),
        out_specs=[VM] * len(outs),
        out_shape=outs,
        compiler_params=params(24),
        cost_estimate=cost(0.3),
        name="halve",
    )(at, after, *sums)


def load_riders(blocks, first, rows):
    parts = []
    for i in range(blocks.shape[0]):
        for m in range(blocks.shape[2] // 128):
            parts.append(blocks[i, first : first + rows, m * 128 : (m + 1) * 128].astype(F32))
    return jnp.concatenate(parts, axis=0)


def store_riders(block, packed, i, first, rows):
    columns = block.shape[1] // 128
    for m in range(columns):
        lo = (columns * i + m) * rows
        block[first : first + rows, m * 128 : (m + 1) * 128] = packed[lo : lo + rows, :]


def stage_kernel(
    at_ref, after, keep_a, got_a, keep_b, got_b, ours,
    next_keep_a, next_give_a, next_keep_b, next_give_b, total, joined, block,
):
    y, z = at_ref[1], at_ref[2]
    tall, rows = keep_a.shape[2], next_give_a.shape[1]
    flat = got_a.shape[2]
    columns = got_a.shape[3] // 128
    riders = joined.shape[0] // (4 * columns)
    start = flat - riders
    for i in range(2):
        for k in range(2):
            for m in range(columns):
                lo = (columns * (2 * i + k) + m) * riders
                piece = got_a[i, k, start:flat, m * 128 : (m + 1) * 128]
                joined[lo : lo + riders, :] = ours[lo : lo + riders, :].astype(F32) + piece.astype(F32)
    total[...] = joined[...].astype(BF16)
    for i in range(2):
        next_keep_a[i] = (keep_a[i, z].astype(F32) + got_a[i, z, :tall].astype(F32)).astype(BF16)
        block[...] = jnp.zeros_like(block)
        block[:tall, :] = keep_a[i, 1 - z].astype(F32) + got_a[i, 1 - z, :tall].astype(F32)
        store_riders(block, joined, i, rows - 2 * riders, 2 * riders)
        next_give_a[i] = block[...].astype(BF16)
        for side, out in ((y, next_keep_b), (1 - y, next_give_b)):
            out[i] = (keep_b[i, side].astype(F32) + got_b[i, side].astype(F32)).astype(BF16)


def stage(at, after, keep_a, got_a, keep_b, got_b, ours):
    _, _, tall, lanes = keep_a.shape
    narrow = keep_b.shape[-1]
    riders = ours.shape[0] // (4 * (lanes // 128))
    rows = got_a.shape[2] + riders
    return pl.pallas_call(
        stage_kernel,
        in_specs=[SM, HBM] + [VM] * 5,
        out_specs=[VM] * 5,
        out_shape=[
            shape((2, tall, lanes), BF16),
            shape((2, rows, lanes), BF16),
            shape((2, tall, narrow), BF16),
            shape((2, tall, narrow), BF16),
            shape(ours.shape, BF16),
        ],
        scratch_shapes=[pltpu.VMEM(ours.shape, F32), pltpu.VMEM((rows, lanes), F32)],
        compiler_params=params(12),
        cost_estimate=cost(0.3),
        name="stage",
    )(at, after, keep_a, got_a, keep_b, got_b, ours)


def join_kernel(at_ref, after, keep_a, got_a, keep_b, got_b, ours, keep, give, total):
    tall, cut = keep_a.shape[1:]
    riders = ours.shape[0] // (2 * (cut // 128))
    start = got_a.shape[1] - riders
    total[...] = (ours[...].astype(F32) + load_riders(got_a, start, riders)).astype(BF16)
    for side, out in ((at_ref[3], keep), (1 - at_ref[3], give)):
        out[:, :cut] = (keep_a[side].astype(F32) + got_a[side, :tall].astype(F32)).astype(BF16)
        out[:, cut:] = (keep_b[side].astype(F32) + got_b[side].astype(F32)).astype(BF16)


def join(at, after, keep_a, got_a, keep_b, got_b, ours):
    _, rows, cut = keep_a.shape
    return pl.pallas_call(
        join_kernel,
        in_specs=[SM, HBM] + [VM] * 5,
        out_specs=[VM] * 3,
        out_shape=[shape((rows, cut + keep_b.shape[-1]), BF16)] * 2 + [shape(ours.shape, BF16)],
        compiler_params=params(12),
        cost_estimate=cost(0.3),
        name="join",
    )(at, after, keep_a, got_a, keep_b, got_b, ours)


def hidden_last_kernel(keep_a, got_a, keep_b, got_b, after, *outs):
    *outs, token = outs
    token[...] = jnp.zeros_like(token)
    cut = keep_a.shape[-1]
    for m, out in enumerate(outs):
        out[:, :cut] = keep_a[0, m].astype(F32) + got_a[0, m].astype(F32)
        out[:, cut:] = keep_b[0, m].astype(F32) + got_b[0, m].astype(F32)


def hidden_last(keep_a, got_a, keep_b, got_b, after):
    _, count, rows, cut = keep_a.shape
    return pl.pallas_call(
        hidden_last_kernel,
        in_specs=[VM] * 4 + [HBM],
        out_specs=[VM] * (count + 1),
        out_shape=[far((rows, cut + keep_b.shape[-1]), F32)] * count + [shape((8, 128), F32)],
        compiler_params=params(12),
        cost_estimate=cost(0.3),
        name="hidden_last",
    )(keep_a, got_a, keep_b, got_b, after)


def add_kernel(ours, theirs, after, out):
    out[...] = (ours[...].astype(F32) + theirs[...].astype(F32)).astype(out.dtype)


def add(ours, theirs, after, dtype):
    return pl.pallas_call(
        add_kernel,
        in_specs=[VM, VM, HBM],
        out_specs=VM,
        out_shape=shape(ours.shape, dtype),
        compiler_params=params(8),
        cost_estimate=cost(0.3),
        name="add",
    )(ours, theirs, after)


def projection_kernel(
    at_ref, gp, u1, n1, w_mine, keep_o, got_o, d_w2, d_w1, d_taps, gcb, condt, mu, mn,
    sums2, after, keep_a, give_a, keep_b, give_b, packed_out, d_in, d_out, packed, sheet, *, layout,
):
    me, y, zbit = at_ref[0], at_ref[1], at_ref[2]
    channels = u1.shape[1]
    width = keep_o.shape[0]
    d_in[...] = mm(gp[...], u1[...])
    d_out[...] = keep_o[...].astype(F32) + got_o[...].astype(F32)
    blocks = 2 * keep_a.shape[0]
    first = 2 * width // blocks
    second = width // blocks
    cut = channels // 2

    def put(out, block, lanes):
        lo = pl.multiple_of(block * first, first)
        out[:first, :] = d_in[pl.ds(lo, first), lanes].astype(BF16)
        lo = pl.multiple_of(block * second, second)
        out[first:, :] = d_out[pl.ds(lo, second), lanes].astype(BF16)

    for b in range(blocks // 2):
        put(keep_a.at[b], 2 * b + y, slice(0, cut))
    for b in range(blocks // 4):
        for i in range(2):
            put(keep_b.at[b, i], 4 * b + 2 * zbit + i, slice(cut, channels))
            put(give_b.at[b, i], 4 * b + 2 * (1 - zbit) + i, slice(cut, channels))
    packed[...] = jnp.zeros_like(packed)
    packed[:width, :] = jnp.concatenate([d_w2[:width, :], d_w2[width:, :]], axis=1)
    taps_t = jnp.transpose(d_taps[...])
    gcb_t = jnp.transpose(gcb[...])[:8, :]
    gmu = lax.dot_general(
        gcb_t, condt[...], (((1,), (0,)), ((), ())), precision=HIGH, preferred_element_type=F32
    )
    gp_n = mm(gp[...], n1[...])
    w32 = w_mine[...].astype(F32)
    gain = jnp.sum(gp_n * w32, axis=0, keepdims=True) + jnp.sum(gmu * mn[...], axis=0, keepdims=True)
    total = jnp.sum(gp[...].astype(F32), axis=1, keepdims=True)
    shift = jnp.sum(total * w32, axis=0, keepdims=True) + jnp.sum(gmu, axis=0, keepdims=True)
    for i in range(3):
        for m in range(2 * width // 128):
            at = layout["taps"] + i * (2 * width // 128) + m
            packed[at : at + 1, :] = taps_t[i : i + 1, m * 128 : (m + 1) * 128]
    for i, row in enumerate((gain, shift, sums2[0:1, :], sums2[1:2, :])):
        for m in range(channels // 128):
            at = layout["ln"] + i * (channels // 128) + m
            packed[at : at + 1, :] = row[:, m * 128 : (m + 1) * 128]
    half = d_w1.shape[0] // 2
    packed[layout["w1"] : layout["w1"] + half, :] = jnp.concatenate(
        [d_w1[:half, :], d_w1[half:, :]], axis=1
    )
    zeros = jnp.zeros_like(gcb_t)
    row = at_ref[4]
    odd = (row & 1) == 1
    both = jnp.concatenate([jnp.where(odd, zeros, gcb_t), jnp.where(odd, gcb_t, zeros)], axis=1)
    packed[pl.ds(pl.multiple_of(layout["cb"] + 8 * (row >> 1), 8), 8), :] = both
    share = jnp.zeros((8, width), F32)
    for f in range(channels // width):
        share = share + jnp.where(me == f, mu[:, f * width : (f + 1) * width], 0.0)
    rest = jnp.concatenate([share[:SEGS, 128:], jnp.zeros((SEGS, 256 - width), F32)], axis=1)
    block = jnp.concatenate([share[:SEGS, :128], rest, jnp.zeros((8 - 2 * SEGS, 128), F32)], axis=0)
    packed[pl.ds(pl.multiple_of(layout["mu"] + 8 * row, 8), 8), :] = block
    packed_out[...] = packed[...].astype(BF16)
    riders = packed.shape[0] // (4 * (cut // 128))
    for b in range(blocks // 2):
        sheet[...] = jnp.zeros_like(sheet)
        lo = pl.multiple_of((2 * b + 1 - y) * first, first)
        sheet[:first, :] = d_in[pl.ds(lo, first), :cut]
        lo = pl.multiple_of((2 * b + 1 - y) * second, second)
        sheet[first : first + second, :] = d_out[pl.ds(lo, second), :cut]
        store_riders(sheet, packed, b, sheet.shape[0] - riders, riders)
        give_a[b] = sheet[...].astype(BF16)


def packed_layout(width, channels, bs):
    taps = width
    ln = taps + 3 * (2 * width // 128)
    w1 = -(-(ln + 4 * (channels // 128)) // 8) * 8
    cb = w1 + 32
    mu = cb + 4 * bs
    return {"taps": taps, "ln": ln, "w1": w1, "cb": cb, "mu": mu, "rows": -(-(mu + 8 * bs) // 128) * 128}


def projection_grads(
    at, gp, u1, n1, w_mine, keep_o, got_o, d_w2, d_w1, d_taps, gcb, condt, mu, mn, sums2, after, bs
):
    length, channels = u1.shape
    width = keep_o.shape[0]
    layout = packed_layout(width, channels, bs)
    tall = 3 * width // bs
    flat = -(-tall // 16) * 16 + layout["rows"] // (4 * (channels // 256))
    return pl.pallas_call(
        functools.partial(projection_kernel, layout=layout),
        in_specs=[SM] + [VM] * 14 + [HBM],
        out_specs=[VM] * 5,
        out_shape=[
            shape((bs // 2, tall, channels // 2), BF16),
            shape((bs // 2, flat, channels // 2), BF16),
        ]
        + [shape((bs // 4, 2, 3 * width // bs, channels // 2), BF16)] * 2
        + [shape((layout["rows"], 128), BF16)],
        scratch_shapes=[
            pltpu.VMEM((2 * width, channels), F32),
            pltpu.VMEM((width, channels), F32),
            pltpu.VMEM((layout["rows"], 128), F32),
            pltpu.VMEM((flat, channels // 2), F32),
        ],
        compiler_params=params(24),
        cost_estimate=cost(2),
        name="projection_grads",
    )(
        at, gp, u1, n1, w_mine, keep_o, got_o, d_w2, d_w1, d_taps, gcb, condt, mu, mn, sums2, after
    )


def final_kernel(
    me_ref, p0, p1, p2, p3, x, big_g, norms, ids_row, condt, w_in, after, out, gp_t, *, piece
):
    me = me_ref[0]
    rows = gp_t.shape[0] // 4
    hidden = condt.shape[0]
    share = jnp.zeros((8, hidden), F32)
    for k, part in enumerate((p0, p1, p2, p3)):
        for i in range(rows // piece):
            at = pl.ds(pl.multiple_of((i * 4 + (me ^ k)) * piece, piece), piece)
            gp_t[at, :] = part[i * piece : (i + 1) * piece, :]
        extra = part[rows:, :hidden].astype(F32)
        share = share + extra[:8] + extra[8:]
    ids = ids_row[...]
    number = lax.broadcasted_iota(jnp.int32, (8, ids.shape[1]), 0)
    counts = jnp.sum(jnp.where(ids == number, 1.0, 0.0), axis=1, keepdims=True)
    gmu = lax.dot_general(
        share, condt[...], (((1,), (0,)), ((), ())), precision=HIGH, preferred_element_type=F32
    ) / jnp.maximum(counts, 1.0)
    gu1 = mm_nt(jnp.transpose(gp_t[...]), w_in[...])
    quarter = x.shape[0]
    own = jnp.broadcast_to(ids_row[:, tile(me, quarter)].astype(F32), (8, quarter))
    ids_own = jnp.transpose(own)[:, 0:1]
    for j in range(SEGS):
        gu1 = gu1 + jnp.where(ids_own == j, gmu[j : j + 1, :], 0.0)
    unit, scale = normed(x[...].astype(F32))
    out[...] = big_g[...] + norm_back(unit, scale, gu1 * norms[0:1, :])


def final(me, gp_parts, x, big_g, norms, ids, condt, w_in, after, piece):
    quarter, channels = x.shape
    return pl.pallas_call(
        functools.partial(final_kernel, piece=piece),
        in_specs=[SM] + [VM] * 10 + [HBM],
        out_specs=VM,
        out_shape=shape((quarter, channels), F32),
        scratch_shapes=[pltpu.VMEM((2 * channels, quarter), BF16)],
        compiler_params=params(24),
        cost_estimate=cost(0.3),
        name="final",
    )(me, *gp_parts, x, big_g, norms, ids, condt, in_hbm(w_in), after)


def small_kernel(
    me_ref, j0, j1, j2, j3, w2, taps, ln0, ln1, ln2, ln3, w1, b1, cond, wide, tap_t, cond_t, *, layout, step, width
):
    me = me_ref[0]
    parts = [part[...].astype(F32) for part in (j0, j1, j2, j3)]
    hidden = w1.shape[0]
    half = width // step
    count = 2 * width // 128
    for k, part in enumerate(parts):
        who = me ^ k
        rows = jnp.concatenate(
            [
                jnp.concatenate([part[layout["taps"] + i * count + m : layout["taps"] + i * count + m + 1, :]
                                 for m in range(count)], axis=1)
                for i in range(3)
            ]
            + [jnp.zeros((125, 2 * width), F32)],
            axis=0,
        )
        tap_t[...] = jnp.transpose(rows)
        for side in range(2):
            for i in range(half):
                at = pl.ds(pl.multiple_of((side * half * 4 + i * 4 + who) * step, step), step)
                lo = i * step
                wide[at, :hidden] = part[lo : lo + step, side * hidden : (side + 1) * hidden]
                at2 = side * width + lo
                wide[at, hidden:] = tap_t[at2 : at2 + step, :hidden]
    whole = jnp.transpose(wide[...])
    w2[...] = whole[:hidden, :]
    taps[...] = whole[hidden : hidden + 3, :]

    def common(first, last):
        a, b, c, d = [part[first:last, :] for part in parts]
        return (a + b) + (c + d)

    lanes = ln0.shape[0] // 128
    sums = common(layout["ln"], layout["ln"] + 4 * lanes)
    for i, out in enumerate((ln0, ln1, ln2, ln3)):
        row = jnp.concatenate([sums[i * lanes + m : i * lanes + m + 1, :] for m in range(lanes)], axis=1)
        out[...] = row.reshape(out.shape)
    both = common(layout["w1"], layout["w1"] + hidden // 2)
    w1[: hidden // 2, :] = both[:, :hidden]
    w1[hidden // 2 :, :] = both[:, hidden:]
    cb = common(layout["cb"], layout["mu"])
    shares = []
    for b in range(cb.shape[0] // 4):
        lo = 8 * (b // 2)
        shares.append(cb[lo : lo + 8, (b % 2) * hidden : (b % 2 + 1) * hidden])
    shares = jnp.concatenate(shares, axis=0)
    b1[...] = jnp.sum(shares, axis=0, keepdims=True)
    for k, part in enumerate(parts):
        rows = []
        for b in range(cb.shape[0] // 4):
            lo = layout["mu"] + 8 * b
            block = part[lo : lo + 8, :]
            rows.append(
                jnp.concatenate(
                    [
                        jnp.concatenate([block[:SEGS, :], jnp.zeros((8 - SEGS, 128), F32)], axis=0),
                        jnp.concatenate(
                            [block[SEGS : 2 * SEGS, : width - 128], jnp.zeros((8 - SEGS, width - 128), F32)],
                            axis=0,
                        ),
                    ],
                    axis=1,
                )
            )
        mu = jnp.concatenate(rows, axis=0)
        cond_t[tile(me ^ k, width), :] = lax.dot_general(
            jnp.transpose(mu), shares, (((1,), (0,)), ((), ())), precision=HIGH, preferred_element_type=F32
        )
    cond[...] = jnp.transpose(cond_t[...])


def small_grads(me, parts, hidden, channels, step, bs):
    width = channels // 4
    layout = packed_layout(width, channels, bs)
    return pl.pallas_call(
        functools.partial(small_kernel, layout=layout, step=step, width=width),
        in_specs=[SM] + [VM] * 4,
        out_specs=[VM] * 9,
        out_shape=[
            far((hidden, 2 * channels), F32),
            far((3, 2 * channels), F32),
            far((channels,), F32),
            far((channels,), F32),
            far((channels,), F32),
            far((channels,), F32),
            far((hidden, hidden), F32),
            far((1, hidden), F32),
            far((hidden, channels), F32),
        ],
        scratch_shapes=[
            pltpu.VMEM((2 * channels, 2 * hidden), F32),
            pltpu.VMEM((2 * width, 128), F32),
            pltpu.VMEM((channels, hidden), F32),
        ],
        compiler_params=params(24),
        cost_estimate=cost(3),
        name="small_grads",
    )(me, *parts)


def trade_parts(parts):
    two, three, one = [swap(parts[k], "freq", k) for k in (2, 3, 1)]
    return (parts[0], one, two, three)


def tiled_device(
    tokens,
    seg_ids,
    cotangent,
    ln1_gain,
    ln1_shift,
    w_in,
    conv_taps,
    freq_w1,
    freq_b1,
    freq_w2,
    cond_w,
    w_out,
    ln2_gain,
    ln2_shift,
    w_gate,
    w_up,
    w_down,
):
    quarter, _, channels = tokens.shape
    length = seg_ids.shape[1]
    ff = w_gate.shape[1]
    fs = lax.axis_size("freq")
    bs = lax.axis_size("batch")
    me = lax.axis_index("freq")
    row = lax.axis_index("batch")
    width = channels // fs
    half = bs // 2
    step = channels // (half * fs)
    fw = ff // (bs * fs)
    table = np.concatenate(tables(length), axis=0)
    feats = features(length, freq_w1.shape[0] // 2)
    feats_aug = np.concatenate(
        [feats, np.ones((1, length), np.float32), np.zeros((7, length), np.float32)], axis=0
    )

    x_own = tokens[:, 0]
    ct_own = cotangent[:, 0]
    ids = seg_ids
    at = jnp.stack([me, row & 1, (row >> 1) & 1, (row >> 2) & 1, row]).astype(jnp.int32)
    norms = jnp.concatenate([ln1_gain, ln1_shift, ln2_gain, ln2_shift]).reshape(4, channels)
    condt = cond_w.T

    def gather_after(value, after):
        two = swap(value, "freq", 2)
        one = swap(value, "freq", 1)
        (two,) = tie([two], after)
        return (value, one, two, swap(two, "freq", 1))

    def gather_wide(value, *after):
        count = bs * fs
        parts = (
            value,
            swap(value, "freq", 2),
            swap(value, "batch", 2),
            lax.ppermute(value, ("batch", "freq"), [(i, i ^ (2 * fs + 2)) for i in range(count)]),
        )
        parts = parts[:1] + tuple(tie(parts[1:], *after))
        return parts + tuple(swap(part, "freq", 1) for part in parts)

    def pairs(value):
        return value.reshape((value.shape[0] // 2, 2) + value.shape[1:])

    w_mine, w2x, w2t, taps, base, waves, w_near, x_near, condt = prepare(
        at, w_in, freq_w2, conv_taps, freq_w1, freq_b1, jnp.asarray(feats_aug), jnp.asarray(table), w_out,
        x_own, condt, norms, step, fs
    )
    x_parts = gather_after(x_own, base)
    x_parts = (x_near,) + x_parts[1:]
    forward = forward_spectral(at, x_parts, ids, norms, w_mine, taps, base, w2x, condt, waves)
    z_parts, (u1, n1, p, q, c, vr, vs, mu, mn, cb) = forward[:4], forward[4:]
    ct_x = swap(ct_own, "freq", 2)
    ct_z = swap(ct_own, "batch", 2)
    z_got = trade_parts(z_parts)
    wg_mine, wu_mine, wd_mine = select_columns(at, cb, w_gate, w_up, w_down, bs, fs)
    (ct_x,) = tie([ct_x], cb)
    ct_parts = (ct_own, ct_x, ct_z, swap(ct_x, "batch", 2))
    h, u2, z_t = middle(at, z_got, x_near, w_near, norms, wg_mine, step)
    fed = feed_forward(
        at, u2, h, ct_own, norms, w_near, w_gate, w_up, w_down, step, channels // (bs * fs)
    )
    mixed_out, big_g, gz_parts, gt_own, gt_other, sums2 = fed[0], fed[1], fed[2:6], *fed[6:]
    gt_got = swap(gt_other, "freq", 1)
    ct_parts = ct_parts + tuple(swap(part, "freq", 1) for part in tie(ct_parts, sums2))
    u2_parts = gather_wide(u2, sums2, ct_parts[4])
    gz_got = trade_parts(gz_parts)

    z_got = swap(z_t, "freq", 1)
    keep_a, give_a, keep_b, give_b, keep_o, give_o = hidden_grads(
        at, u2_parts, ct_parts, wg_mine, wu_mine, gt_own, gt_got, z_t, z_got,
        wd_mine, sums2,
    )
    got_a = swap(give_a, "batch", 1)
    got_b = swap(give_b, "batch", 4)
    got_o = swap(give_o, "freq", 2)

    back = backward_spectral(
        at, gz_got, ids, cb, taps, base, w2x, w2t, jnp.asarray(feats).astype(BF16),
        p, q, c, vr, vs, waves, give_a,
    )
    gp_parts, (gp, d_taps, d_w2, d_w1, gcb) = back[:4], back[4:]
    gp_got = trade_parts(gp_parts)

    keep_a, give_a, keep_b, give_b = halve(
        at, (2, 0), gp, keep_a[None], got_a[None], keep_b[None], got_b[None]
    )
    got_a = swap(give_a, "batch", 4)
    got_b = swap(give_b, "batch", 1)

    proj = projection_grads(
        at, gp, u1, n1, w_mine, keep_o, got_o, d_w2, d_w1, d_taps, gcb, condt, mu, mn, sums2, give_a, bs
    )
    p_keep_a, p_give_a, p_keep_b, p_give_b, packed = proj
    p_got_a = swap(p_give_a, "batch", 1)
    p_got_b = swap(p_give_b, "batch", 2)
    p_keep_a, p_give_a, p_keep_b, p_give_b, packed = stage(
        at, p_give_a, pairs(p_keep_a), pairs(p_got_a), p_keep_b, p_got_b, packed
    )
    p_got_a = swap(p_give_a, "batch", 2)
    p_got_b = swap(p_give_b, "batch", 1)
    d_gate, d_up, d_down, token = hidden_last(keep_a, got_a, keep_b, got_b, packed)
    keep, give, packed = join(at, token, p_keep_a, p_got_a, p_keep_b, p_got_b, packed)
    grad_tokens = final(at, gp_got, x_own, big_g, norms, ids, condt, w_in, packed, step)
    got = swap(give, "batch", 4)
    sent = add(packed, swap(packed, "batch", 4), give, BF16)
    (grad_tokens,) = tie([grad_tokens], sent)
    mine = keep.astype(F32) + got.astype(F32)
    first = 2 * width // bs

    d_w2, d_taps, *ln, d_w1, d_b1, d_cond = small_grads(
        at, gather_freq(sent, me), freq_w1.shape[1], channels, step, bs
    )
    return (
        mixed_out[:, None],
        grad_tokens[:, None],
        ln[0],
        ln[1],
        mine[:first].T,
        d_taps,
        d_w1,
        d_b1[0],
        d_w2,
        d_cond.T,
        mine[first:].T,
        ln[2],
        ln[3],
        d_gate.T,
        d_up.T,
        d_down,
    )


def per_device(*args):
    channels = args[0].shape[2]
    step = 2 * channels // (lax.axis_size("batch") * lax.axis_size("freq"))
    fits = lax.axis_size("batch") == 8 and lax.axis_size("freq") == 4 and step % 16 == 0
    return tiled_device(*args) if fits else plain_device(*args)


def solution(mesh):
    rows = P("freq", "batch", None)
    split = P(None, ("batch", "freq"))
    in_specs = (rows, P("batch", None), rows) + (P(),) * 14
    out_specs = (
        rows,
        rows,
        P(),
        P(),
        split,
        P(),
        P(),
        P(),
        P(),
        P(),
        split,
        P(),
        P(),
        split,
        split,
        P(("batch", "freq"), None),
    )
    return jax.shard_map(
        per_device, mesh=mesh, in_specs=in_specs, out_specs=out_specs, check_vma=False
    )
```

```python
import functools

import jax
import jax.numpy as jnp
import ml_dtypes
import numpy as np
from jax import lax
from jax.experimental import pallas as pl
from jax.experimental.pallas import tpu as pltpu
from jax.sharding import PartitionSpec as P

SEGS = 3
EPS = 1e-05
HIGH = lax.Precision.HIGHEST
F32 = jnp.float32
BF16 = jnp.bfloat16


def mm(a, b):
    return jnp.dot(a, b, preferred_element_type=F32)


def mm_nt(a, b):
    return lax.dot_general(a, b, (((1,), (1,)), ((), ())), preferred_element_type=F32)


def mm_tn(a, b):
    return lax.dot_general(a, b, (((0,), (0,)), ((), ())), preferred_element_type=F32)


def swap(value, axis, mask):
    count = lax.axis_size(axis)
    return lax.ppermute(value, axis, [(i, i ^ mask) for i in range(count)])


def pick(parts, index):
    return lax.dynamic_index_in_dim(parts, index, 0, keepdims=False)


def in_order(received, me):
    a, b, c, d = received
    low = (me & 1) == 1
    a, b = jnp.where(low, b, a), jnp.where(low, a, b)
    c, d = jnp.where(low, d, c), jnp.where(low, c, d)
    high = (me & 2) == 2
    a, c = jnp.where(high, c, a), jnp.where(high, a, c)
    b, d = jnp.where(high, d, b), jnp.where(high, b, d)
    return (a, b, c, d)


def trade(blocks, me):
    return [pick(blocks, me)] + [swap(pick(blocks, me ^ k), "freq", k) for k in (2, 3, 1)]


def trade_sorted(blocks, me):
    own, two, three, one = trade(blocks, me)
    return in_order((own, one, two, three), me)


def gather_freq(value, me):
    two = swap(value, "freq", 2)
    one = swap(value, "freq", 1)
    three = swap(two, "freq", 1)
    return (value, one, two, three)


def scatter_sum(value, order):
    bits = lax.axis_size("batch").bit_length() - 1
    me = lax.axis_index("batch")
    rest = value.shape[1:]
    value = value.reshape((2,) * bits + rest)
    left = list(range(bits - 1, -1, -1))
    for bit in order:
        dim = left.index(bit)
        mine = (me >> bit) & 1
        keep = lax.dynamic_index_in_dim(value, mine, dim, keepdims=False)
        give = lax.dynamic_index_in_dim(value, 1 - mine, dim, keepdims=False)
        got = swap(give, "batch", 1 << bit)
        total = keep.astype(F32) + got.astype(F32)
        left.remove(bit)
        value = total.astype(value.dtype) if left else total
    return value


def tables(length):
    index = np.arange(length, dtype=np.int64)
    angle = (index[:, None] * index[None, :] % (2 * length)) * (np.pi / length)
    return (
        np.cos(angle).astype(ml_dtypes.bfloat16),
        np.sin(angle).astype(ml_dtypes.bfloat16),
    )


def features(length, half):
    index = np.arange(length, dtype=np.int64)
    lags = (np.arange(half, dtype=np.int64) + 1) ** 2
    angle = (lags[:, None] * index[None, :] % (2 * length)) * (np.pi / length)
    return np.concatenate([np.cos(angle), np.sin(angle)], axis=0).astype(np.float32)


def normed(values):
    centered = values - jnp.mean(values, axis=-1, keepdims=True)
    scale = lax.rsqrt(jnp.mean(centered * centered, axis=-1, keepdims=True) + EPS)
    return centered * scale, scale


def norm_back(unit, scale, grad):
    return scale * (
        grad
        - jnp.mean(grad, axis=-1, keepdims=True)
        - unit * jnp.mean(grad * unit, axis=-1, keepdims=True)
    )


def shift_right(values):
    return jnp.pad(values, ((0, 0), (1, 0)))[:, :-1]


def shift_left(values):
    return jnp.pad(values, ((0, 0), (0, 1)))[:, 1:]


def plain_device(
    tokens,
    seg_ids,
    cotangent,
    ln1_gain,
    ln1_shift,
    w_in,
    conv_taps,
    freq_w1,
    freq_b1,
    freq_w2,
    cond_w,
    w_out,
    ln2_gain,
    ln2_shift,
    w_gate,
    w_up,
    w_down,
):
    quarter, _, channels = tokens.shape
    length = seg_ids.shape[1]
    ff = w_gate.shape[1]
    fs = lax.axis_size("freq")
    bs = lax.axis_size("batch")
    me = lax.axis_index("freq")
    width = channels // fs
    half = bs // 2
    step = channels // (half * fs)
    cos_table, sin_table = tables(length)
    feats = features(length, freq_w1.shape[0] // 2)

    x_own = tokens[:, 0]
    ct_own = cotangent[:, 0]
    ids = seg_ids
    x_parts = gather_freq(x_own, me)
    ct_parts = gather_freq(ct_own, me)

    w_in_t = (
        w_in.T.reshape(2, half, fs, step, channels)
        .transpose(2, 0, 1, 3, 4)
        .reshape(fs, 2 * width, channels)
    )
    w_in_mine = pick(w_in_t, me)
    w_out_p = (
        w_out.reshape(half, fs, step, channels).transpose(1, 0, 2, 3).reshape(channels, channels)
    )
    taps_mine = pick(
        conv_taps.reshape(3, 2, half, fs, step).transpose(3, 0, 1, 2, 4).reshape(fs, 3, 2 * width), me
    )[:, :, None]
    w2_mine = pick(
        freq_w2.reshape(-1, 2, half, fs, step).transpose(3, 0, 1, 2, 4).reshape(fs, -1, 2 * width), me
    )
    fw = ff // (bs * fs)
    wide = ff // fs

    def mine_rows(weight):
        return pick(
            weight.reshape(bs, fs, fw, channels).transpose(1, 0, 2, 3).reshape(fs, wide, channels), me
        )

    wg_mine, wu_mine, wd_mine = (mine_rows(w_gate.T), mine_rows(w_up.T), mine_rows(w_down))

    base = jnp.dot(freq_w1.T, feats, precision=HIGH) + freq_b1[:, None]

    x_row = jnp.concatenate(in_order(x_parts, me), axis=0).astype(F32)
    unit1, _ = normed(x_row)
    u1 = (unit1 * ln1_gain + ln1_shift).astype(BF16)
    n1 = unit1.astype(BF16)
    masks = (ids == jnp.arange(SEGS, dtype=jnp.int32)[:, None]).astype(F32)
    counts = jnp.sum(masks, axis=1, keepdims=True)
    mu = mm(masks.astype(BF16), u1) / counts
    mn = mm(masks.astype(BF16), n1) / counts
    cb = jnp.dot(mu, cond_w, precision=HIGH)
    p = mm_nt(w_in_mine, u1)
    same = (ids[:, 1:] == ids[:, :-1]).astype(F32)
    zero = jnp.zeros((1, 1), F32)
    prev = jnp.concatenate([zero, same], axis=1)
    nxt = jnp.concatenate([same, zero], axis=1)
    p_prev = shift_right(p) * prev
    p_next = shift_left(p) * nxt
    s = taps_mine[0] * p_prev + taps_mine[1] * p + taps_mine[2] * p_next
    q, v = s[:width], s[width:]

    pre = base[None] + cb[:, :, None]
    gate_pre = jax.nn.sigmoid(pre)
    hk = pre * gate_pre
    kk = jnp.einsum("kc,jkf->jcf", w2_mine, hk, precision=HIGH)
    kr, ki = kk[:, :width], kk[:, width:]
    vm = (v[None] * masks[:, None, :]).astype(BF16).reshape(SEGS * width, length)
    vr = mm(vm, cos_table).reshape(SEGS, width, length)
    vi = -mm(vm, sin_table).reshape(SEGS, width, length)
    weights = np.full((length,), 2.0 / (2 * length), np.float32)
    weights[0] = 1.0 / (2 * length)
    yr = ((kr * vr - ki * vi) * weights).astype(BF16).reshape(SEGS * width, length)
    yi = ((kr * vi + ki * vr) * weights).astype(BF16).reshape(SEGS * width, length)
    conv = (mm(yr, cos_table) - mm(yi, sin_table)).reshape(SEGS, width, length)
    c = jnp.sum(conv * masks[:, None, :], axis=0)
    z_mine = (q * c).astype(BF16)

    z_blocks = z_mine.reshape(width, fs, quarter).transpose(1, 0, 2)
    z_t = jnp.concatenate(trade_sorted(z_blocks, me), axis=0)

    x32 = x_own.astype(F32)
    ct32 = ct_own.astype(F32)
    h = x32 + mm_tn(z_t, w_out_p)
    unit2, scale2 = normed(h)
    u2 = (unit2 * ln2_gain + ln2_shift).astype(BF16)
    u2_parts = gather_freq(u2, me)
    g = mm(u2, w_gate)
    a = mm(u2, w_up)
    gh = mm_nt(ct_own, w_down)
    sg = jax.nn.sigmoid(g)
    silu = g * sg
    hid = (silu * a).astype(BF16)
    mixed_out = (h + mm(hid, w_down)).astype(BF16)
    gg = (gh * a * sg * (1.0 + g * (1.0 - sg))).astype(BF16)
    ga = (gh * silu).astype(BF16)
    gu2 = mm_nt(gg, w_gate) + mm_nt(ga, w_up)
    grad_ln2_gain = jnp.sum(gu2 * unit2, axis=0)
    grad_ln2_shift = jnp.sum(gu2, axis=0)
    big_g = ct32 + norm_back(unit2, scale2, gu2 * ln2_gain)
    gb = big_g.astype(BF16)
    gz_blocks = mm_nt(w_out_p, gb).astype(BF16).reshape(fs, width, quarter)
    gz = jnp.concatenate(trade_sorted(gz_blocks, me), axis=1).astype(F32)
    gb_parts = gather_freq(gb, me)

    u2_row = jnp.concatenate(u2_parts, axis=0)
    ct_row = jnp.concatenate(ct_parts, axis=0)
    g_t = mm_nt(wg_mine, u2_row)
    a_t = mm_nt(wu_mine, u2_row)
    gh_t = mm_nt(wd_mine, ct_row)
    sg_t = jax.nn.sigmoid(g_t)
    silu_t = g_t * sg_t
    hid_t = (silu_t * a_t).astype(BF16)
    gg_t = (gh_t * a_t * sg_t * (1.0 + g_t * (1.0 - sg_t))).astype(BF16)
    ga_t = (gh_t * silu_t).astype(BF16)
    d_gate = mm(gg_t, u2_row).astype(BF16)
    d_up = mm(ga_t, u2_row).astype(BF16)
    d_down = mm(hid_t, ct_row).astype(BF16)
    d_ff = jnp.stack([d_gate, d_up, d_down], axis=0).reshape(3, bs, fw, channels).transpose(1, 0, 2, 3)
    bits = bs.bit_length() - 1
    order_a = list(range(bits))
    order_b = [1, 0] + list(range(2, bits))
    cut = channels // 2
    ff_a = scatter_sum(d_ff[..., :cut], order_a)
    ff_b = scatter_sum(d_ff[..., cut:], order_b)
    d_ff = jnp.concatenate([ff_a, ff_b], axis=-1)

    gq = gz * c
    gc = gz * q
    gcm = (gc[None] * masks[:, None, :]).astype(BF16).reshape(SEGS * width, length)
    gyr = mm(gcm, cos_table).reshape(SEGS, width, length) * weights
    gyi = -mm(gcm, sin_table).reshape(SEGS, width, length) * weights
    gkr = gyr * vr + gyi * vi
    gki = gyi * vr - gyr * vi
    gvr = (kr * gyr + ki * gyi).astype(BF16).reshape(SEGS * width, length)
    gvi = (kr * gyi - ki * gyr).astype(BF16).reshape(SEGS * width, length)
    gv_all = (mm(gvr, cos_table) - mm(gvi, sin_table)).reshape(SEGS, width, length)
    gv = jnp.sum(gv_all * masks[:, None, :], axis=0)
    gs = jnp.concatenate([gq, gv], axis=0)
    d_taps = jnp.stack(
        [jnp.sum(gs * p_prev, axis=1), jnp.sum(gs * p, axis=1), jnp.sum(gs * p_next, axis=1)]
    )
    gp = (
        taps_mine[1] * gs
        + taps_mine[0] * shift_left(gs * prev)
        + taps_mine[2] * shift_right(gs * nxt)
    ).astype(BF16)

    gkk = jnp.concatenate([gkr, gki], axis=1)
    gkk_low = gkk.astype(BF16)
    hk_low = hk.astype(BF16)
    d_w2 = jnp.einsum("jkf,jcf->kc", hk_low, gkk_low, preferred_element_type=F32)
    gpre = jnp.einsum("kc,jcf->jkf", w2_mine.astype(BF16), gkk_low, preferred_element_type=F32)
    gpre = gpre * gate_pre * (1.0 + pre * (1.0 - gate_pre))
    d_w1 = jnp.einsum("ef,jkf->ek", feats, gpre, precision=HIGH)
    gcb = jnp.sum(gpre, axis=2)
    gcb_row = lax.psum(gcb, "freq")

    gp_blocks = gp.reshape(2 * width, fs, quarter).transpose(1, 0, 2)
    gp_t = jnp.concatenate(trade_sorted(gp_blocks, me), axis=0)

    u1_row = u1
    d_in = mm(gp, u1_row).astype(BF16).reshape(bs, 2 * width // bs, channels)
    d_in = scatter_sum(d_in, order_a)
    gb_row = jnp.concatenate(in_order(gb_parts, me), axis=0)
    d_out = mm(z_mine, gb_row)
    narrow = channels // bs
    d_out = scatter_sum(d_out.T.astype(BF16).reshape(bs, narrow, width), order_a)
    d_out = d_out.reshape(fs, narrow // fs, width)
    d_out = jnp.stack(trade_sorted(d_out, me), axis=0)
    d_out = (
        d_out.reshape(fs, narrow // fs, half, step).transpose(2, 0, 3, 1).reshape(channels, -1)
    )

    gmu_part = jnp.dot(gcb, cond_w.T, precision=HIGH)
    sum_gp = jnp.sum(gp.astype(F32), axis=1)
    w_mine32 = w_in_mine.astype(F32)
    d_shift1 = jnp.dot(sum_gp[None], w_mine32, precision=HIGH)[0] + jnp.sum(gmu_part, axis=0)
    d_gain1 = jnp.sum(mm(gp, n1) * w_mine32, axis=0) + jnp.sum(gmu_part * mn, axis=0)

    gmu = jnp.dot(gcb_row, cond_w.T, precision=HIGH) / counts
    own_masks = lax.dynamic_slice_in_dim(masks, me * quarter, quarter, 1)
    gu1 = mm_tn(gp_t, w_in_t.reshape(2 * channels, channels)) + lax.dot_general(
        own_masks, gmu, (((0,), (0,)), ((), ())), precision=HIGH
    )
    unit_own, scale_own = normed(x32)
    grad_tokens = big_g + norm_back(unit_own, scale_own, gu1 * ln1_gain)

    shared = [
        d_gain1,
        d_shift1,
        d_w1.reshape(-1),
        jnp.sum(gcb, axis=0),
        jnp.dot(mu.T, gcb, precision=HIGH).reshape(-1),
        grad_ln2_gain,
        grad_ln2_shift,
    ]
    owned = jnp.concatenate([d_taps, d_w2], axis=0)
    packed = jnp.concatenate(shared + [owned.reshape(-1)])
    for bit in range(bits):
        packed = packed + swap(packed, "batch", 1 << bit)
    split = packed.shape[0] - owned.size
    common, owned = packed[:split], packed[split:]
    common = common + swap(common, "freq", 1)
    common = common + swap(common, "freq", 2)
    owned = jnp.stack(in_order(gather_freq(owned, me), me), axis=0)
    owned = (
        owned.reshape(fs, -1, 2, half, step).transpose(1, 2, 3, 0, 4).reshape(-1, 2 * channels)
    )
    sizes = np.cumsum([part.size for part in shared])
    got = jnp.split(common, sizes[:-1])
    return (
        mixed_out[:, None],
        grad_tokens[:, None],
        got[0],
        got[1],
        d_in.T,
        owned[:3],
        got[2].reshape(freq_w1.shape),
        got[3],
        owned[3:],
        got[4].reshape(cond_w.shape),
        d_out,
        got[5],
        got[6],
        d_ff[0].T,
        d_ff[1].T,
        d_ff[2],
    )


VM = pl.BlockSpec(memory_space=pltpu.VMEM)
SM = pl.BlockSpec(memory_space=pltpu.SMEM)
HBM = pl.BlockSpec(memory_space=pl.ANY)
MIB = 1 << 20


def params(mib):
    return pltpu.CompilerParams(vmem_limit_bytes=mib * MIB)


def cost(micros):
    return pl.CostEstimate(
        flops=int(micros * 1000000000.0), bytes_accessed=int(micros * 3500000.0), transcendentals=0
    )


def shape(dims, dtype):
    return pltpu.VMEM(dims, dtype)


def far(dims, dtype):
    return pltpu.HBM(dims, dtype)


def in_hbm(*values):
    kept = tuple(pltpu.with_memory_space_constraint(value, pltpu.HBM) for value in values)
    return kept if len(kept) > 1 else kept[0]


def in_vmem(value):
    return pltpu.with_memory_space_constraint(value, pltpu.VMEM)


def sigmoid(value):
    return 1.0 / (1.0 + jnp.exp(-value))


def dma_all(pairs, sems, first=0):
    copies = [
        pltpu.make_async_copy(source, target, sems.at[first + i])
        for i, (source, target) in enumerate(pairs)
    ]
    for copy in copies:
        copy.start()
    return copies


def tie_kernel(*refs):
    pass


def tie(values, *after):
    count = len(values)
    return pl.pallas_call(
        tie_kernel,
        in_specs=[HBM] * (count + len(after)),
        out_specs=[HBM] * count,
        out_shape=[jax.ShapeDtypeStruct(value.shape, value.dtype) for value in values],
        input_output_aliases={i: i for i in range(count)},
        compiler_params=params(1),
        name="tie",
    )(*values, *after)


def one_hot_rows(me, rows, lanes, piece, fs):
    row = lax.broadcasted_iota(jnp.int32, (rows, lanes), 0)
    lane = lax.broadcasted_iota(jnp.int32, (rows, lanes), 1)
    block = jnp.zeros_like(row)
    for m in range(1, rows // piece):
        block = block + jnp.where(row >= m * piece, 1, 0)
    return jnp.where(lane == block * ((fs - 1) * piece) + me * piece + row, 1.0, 0.0)


def prepare_kernel(
    me_ref, w_in, freq_w2, conv_taps, freq_w1, freq_b1, feats, waves_far, w_far, x_far, cond_far, norms,
    w_mine, w2x, w2t, taps, base, waves, w_near, x_near, cond_near, w1_aug, sems, *, step, fs,
):
    loads = dma_all(
        [(waves_far, waves), (w_far, w_near), (x_far, x_near), (cond_far, cond_near)], sems
    )
    lanes = w_in.shape[1] // 4
    rows = lanes // fs
    sel = one_hot_rows(me_ref[0], rows, lanes, step, fs)
    low = sel.astype(BF16)
    hidden = freq_w2.shape[0]
    for i in range(4):
        out = slice(i * rows, (i + 1) * rows)
        group = slice(i * lanes, (i + 1) * lanes)
        w_mine[out, :] = mm_nt(low, w_in[:, group]).astype(BF16)
        both = jnp.concatenate([freq_w2[:, group], conv_taps[:, group]], axis=0)
        mine = lax.dot_general(
            sel, both, (((1,), (1,)), ((), ())), precision=HIGH, preferred_element_type=F32
        )
        taps[out, :3] = mine[:, hidden:]
        mine = mine[:, :hidden]
        high = mine.astype(BF16)
        rest = (mine - high.astype(F32)).astype(BF16)
        w2x[out, :] = jnp.concatenate([high, high, rest], axis=1)
    w2t[...] = jnp.transpose(w2x[...][:, :hidden].astype(F32)).astype(BF16)
    w1_aug[...] = jnp.zeros_like(w1_aug)
    count = freq_w1.shape[0]
    w1_aug[:count, :] = freq_w1[...]
    w1_aug[count : count + 1, :] = freq_b1[...]
    base[...] = lax.dot_general(
        w1_aug[...], feats[...], (((0,), (0,)), ((), ())), precision=HIGH, preferred_element_type=F32
    )
    for load in loads:
        load.wait()


def prepare(me, w_in, freq_w2, conv_taps, freq_w1, freq_b1, feats, waves, w_out, x, condt, norms, step, fs):
    channels, both = w_in.shape
    hidden = freq_w2.shape[0]
    length = feats.shape[1]
    return pl.pallas_call(
        functools.partial(prepare_kernel, step=step, fs=fs),
        in_specs=[SM] + [VM] * 6 + [HBM] * 5,
        out_specs=[VM] * 9,
        out_shape=[
            shape((both // fs, channels), BF16),
            shape((both // fs, 3 * hidden), BF16),
            shape((hidden, both // fs), BF16),
            shape((both // fs, 8), F32),
            shape((hidden, length), F32),
            shape((2 * length, length), BF16),
            shape(w_out.shape, BF16),
            shape(x.shape, BF16),
            shape(condt.shape, F32),
        ],
        scratch_shapes=[
            pltpu.VMEM((feats.shape[0], hidden), F32),
            pltpu.SemaphoreType.DMA((4,)),
        ],
        compiler_params=params(24),
        cost_estimate=cost(3),
        name="prepare",
    )(me, *in_hbm(w_in, freq_w2, conv_taps, freq_w1), freq_b1[None], in_hbm(feats), in_hbm(waves), *in_hbm(w_out, x, condt), norms)


def select_kernel(at_ref, after, gate, up, down, gate_out, up_out, down_out, *, fs):
    down_out[...] = down[0, 0]
    rows = gate_out.shape[0]
    sel = one_hot_rows(at_ref[0], rows, rows * fs, rows, fs).astype(BF16)
    gate_out[...] = mm_nt(sel, gate[...]).astype(BF16)
    up_out[...] = mm_nt(sel, up[...]).astype(BF16)


def select_columns(at, after, w_gate, w_up, w_down, bs, fs):
    channels, ff = w_gate.shape
    lanes = ff // bs
    wide = pl.BlockSpec((channels, lanes), lambda i, at: (0, (i // 2) * 4 + at[2] * 2 + i % 2))
    rows = pl.BlockSpec((lanes // fs, channels), lambda i, at: (i, 0))
    down = pl.BlockSpec(
        (1, 1, lanes // fs, channels),
        lambda i, at: ((i // 2) * 4 + at[2] * 2 + i % 2, at[0], 0, 0),
    )
    return pl.pallas_call(
        functools.partial(select_kernel, fs=fs),
        grid_spec=pltpu.PrefetchScalarGridSpec(
            num_scalar_prefetch=1,
            grid=(bs // 2,),
            in_specs=[HBM, wide, wide, down],
            out_specs=[rows, rows, rows],
        ),
        out_shape=[shape((ff // (2 * fs), channels), BF16)] * 3,
        compiler_params=params(20),
        cost_estimate=cost(5),
        name="select_columns",
    )(at, after, in_hbm(w_gate), in_hbm(w_up), in_hbm(w_down.reshape(bs, fs, lanes // fs, channels)))


def row_masks(ids):
    lane = lax.broadcasted_iota(jnp.int32, ids.shape, 1)
    length = ids.shape[1]
    prev = jnp.where((ids == pltpu.roll(ids, 1, 1)) & (lane > 0), 1.0, 0.0)
    nxt = jnp.where((ids == pltpu.roll(ids, length - 1, 1)) & (lane < length - 1), 1.0, 0.0)
    return prev, nxt


def bin_weights(start, width, length):
    lane = lax.broadcasted_iota(jnp.int32, (1, width), 1) + start
    return jnp.where(lane == 0, 0.5 / length, 1.0 / length)


def tile(index, size):
    return pl.ds(pl.multiple_of(index * size, size), size)


def hidden_tile(base, cb, j, lanes):
    pre = base[:, lanes] + cb[:, j : j + 1]
    return pre, sigmoid(pre)


def kernel_tile(w2x, hk):
    high = hk.astype(BF16)
    rest = (hk - high.astype(F32)).astype(BF16)
    return mm(w2x[...], jnp.concatenate([high, rest, high], axis=0))


def forward_kernel(
    me_ref, ids_at, x0, x1, x2, x3, ids_ref, norms, w, taps, base, w2x, condt, waves,
    z0, z1, z2, z3, u1, n1, p_out, q_out, c_out, vr_out, vs_out, mu_out, mn_out, cb_out,
    p, q, vm, ycat, acc,
):
    quarter = x0.shape[0]
    width, length = q_out.shape
    tiles = length // quarter
    me = me_ref[0]
    for k, x in enumerate((x0, x1, x2, x3)):
        values = x[...].astype(F32)
        unit, _ = normed(values)
        rows = tile(me ^ k, quarter)
        n1[rows, :] = unit.astype(BF16)
        u1[rows, :] = (unit * norms[0:1, :] + norms[1:2, :]).astype(BF16)
    ids = ids_ref[...]
    number = lax.broadcasted_iota(jnp.int32, (8, length), 0)
    member = jnp.where(ids == number, 1.0, 0.0)
    counts = jnp.maximum(jnp.sum(member, axis=1, keepdims=True), 1.0)
    member_low = member.astype(BF16)
    mu = mm(member_low, u1[...]) / counts
    mu_out[...] = mu
    mn_out[...] = mm(member_low, n1[...]) / counts
    cb_out[...] = lax.dot_general(
        condt[...], mu, (((1,), (1,)), ((), ())), precision=HIGH, preferred_element_type=F32
    )
    prev, nxt = row_masks(ids)
    for t in range(tiles):
        at = slice(t * quarter, (t + 1) * quarter)
        p[:, at] = mm_nt(w[...], u1[at, :])
    chunk = width // 2
    for r in range(4):
        at = slice(r * chunk, (r + 1) * chunk)
        here = p[at, :]
        p_out[at, :] = here.astype(BF16)
        mixed = (
            taps[at, 0:1] * (pltpu.roll(here, 1, 1) * prev)
            + taps[at, 1:2] * here
            + taps[at, 2:3] * (pltpu.roll(here, length - 1, 1) * nxt)
        )
        if r < 2:
            q[at, :] = mixed
            q_out[at, :] = mixed.astype(BF16)
        else:
            for j in range(SEGS):
                lo = j * width + (r - 2) * chunk
                vm[lo : lo + chunk, :] = (mixed * member[j : j + 1, :]).astype(BF16)

    span = 2 * quarter

    @pl.loop(0, length // span)
    def _(f):
        lanes = tile(f, span)
        upper = pl.ds(pl.multiple_of(f * span + length, span), span)
        weight = bin_weights(f * span, span, length)
        vr_all = mm(vm[...], waves[:length, lanes])
        vs_all = mm(vm[...], waves[length:, lanes])
        vr_out[:, lanes] = vr_all.astype(BF16)
        vs_out[:, lanes] = vs_all.astype(BF16)
        for j in range(SEGS):
            pre, gate = hidden_tile(base, cb_out, j, lanes)
            kk = kernel_tile(w2x, pre * gate)
            kr, ki = kk[:width] * weight, kk[width:] * weight
            at = slice(j * width, (j + 1) * width)
            vr, vs = vr_all[at], vs_all[at]
            ycat[at, lanes] = (kr * vr + ki * vs).astype(BF16)
            ycat[at, upper] = (kr * vs - ki * vr).astype(BF16)

    for k, z_out in enumerate((z0, z1, z2, z3)):
        t = me ^ k
        lanes = tile(t, quarter)
        acc[...] = jnp.zeros_like(acc)
        ids_here = ids_ref[:, lanes]
        for j in range(SEGS):

            @pl.when((ids_at[0, t * quarter] <= j) & (ids_at[0, (t + 1) * quarter - 1] >= j))
            def _():
                at = slice(j * width, (j + 1) * width)
                part = mm(ycat[at, :], waves[:, lanes])
                acc[...] += jnp.where(ids_here == j, part, 0.0)

        c = acc[...]
        c_out[:, lanes] = c.astype(BF16)
        z = (q[:, lanes] * c).astype(BF16)
        z_out[...] = z


def forward_spectral(me, x_parts, ids, norms, w, taps, base, w2x, condt, waves):
    quarter, channels = x_parts[0].shape
    length = ids.shape[1]
    width = w.shape[0] // 2
    saved = [
        (length, channels),
        (length, channels),
        (2 * width, length),
        (width, length),
        (width, length),
        (SEGS * width, length),
        (SEGS * width, length),
    ]
    small = [
        shape((8, channels), F32),
        shape((8, channels), F32),
        shape((condt.shape[0], 8), F32),
    ]
    return pl.pallas_call(
        forward_kernel,
        in_specs=[SM, SM] + [VM] * 12,
        out_specs=[VM] * (7 + len(saved)),
        out_shape=[shape((width, quarter), BF16)] * 4 + [shape(dims, BF16) for dims in saved] + small,
        scratch_shapes=[
            pltpu.VMEM((2 * width, length), F32),
            pltpu.VMEM((width, length), F32),
            pltpu.VMEM((SEGS * width, length), BF16),
            pltpu.VMEM((SEGS * width, 2 * length), BF16),
            pltpu.VMEM((width, quarter), F32),
        ],
        compiler_params=params(26),
        cost_estimate=cost(15),
        name="forward_spectral",
    )(me, ids, *x_parts, ids, norms, w, taps, base, w2x, condt, waves)


def backward_kernel(
    me_ref, ids_at, g0, g1, g2, g3, ids_ref, cb, taps, base, w2x, w2, feats,
    p, q, c, vr_in, vs_in, waves, after,
    o0, o1, o2, o3, gp_row, d_taps, d_w2, d_w1, gcb,
    gcm, gvcat, gs, acc,
):
    width, quarter = g0.shape
    length = gp_row.shape[1]
    tiles = length // quarter
    hidden = base.shape[0]
    me = me_ref[0]
    for k, g in enumerate((g0, g1, g2, g3)):
        lanes = tile(me ^ k, quarter)
        gz = g[...].astype(F32)
        gs[:width, lanes] = gz * c[:, lanes].astype(F32)
        gc = gz * q[:, lanes].astype(F32)
        ids_here = ids_ref[:, lanes]
        for j in range(SEGS):
            gcm[j * width : (j + 1) * width, lanes] = jnp.where(ids_here == j, gc, 0.0).astype(BF16)
    d_w2[...] = jnp.zeros_like(d_w2)
    d_w1[...] = jnp.zeros_like(d_w1)
    gcb[...] = jnp.zeros_like(gcb)

    span = 2 * quarter

    @pl.loop(0, length // span)
    def _(f):
        lanes = tile(f, span)
        upper = pl.ds(pl.multiple_of(f * span + length, span), span)
        weight = bin_weights(f * span, span, length)
        gyr_all = mm(gcm[...], waves[:length, lanes]) * weight
        gys_all = mm(gcm[...], waves[length:, lanes]) * weight
        for j in range(SEGS):
            pre, gate = hidden_tile(base, cb, j, lanes)
            hk = pre * gate
            kk = kernel_tile(w2x, hk)
            kr, ki = kk[:width], kk[width:]
            at = slice(j * width, (j + 1) * width)
            gyr, gys = gyr_all[at], gys_all[at]
            vr, vs = vr_in[at, lanes].astype(F32), vs_in[at, lanes].astype(F32)
            gvcat[at, lanes] = (kr * gyr - ki * gys).astype(BF16)
            gvcat[at, upper] = (kr * gys + ki * gyr).astype(BF16)
            gkk = jnp.concatenate(
                [(gyr * vr + gys * vs).astype(BF16), (gyr * vs - gys * vr).astype(BF16)], axis=0
            )
            d_w2[...] += mm_nt(gkk, hk.astype(BF16))
            gpre = mm(w2[...], gkk) * (gate * (1.0 + pre * (1.0 - gate)))
            gcb[:, j : j + 1] += jnp.sum(gpre, axis=1, keepdims=True)
            d_w1[...] += mm_nt(feats[:, lanes], gpre.astype(BF16))

    for k in range(4):
        t = me ^ k
        lanes = tile(t, quarter)
        acc[...] = jnp.zeros_like(acc)
        ids_here = ids_ref[:, lanes]
        for j in range(SEGS):

            @pl.when((ids_at[0, t * quarter] <= j) & (ids_at[0, (t + 1) * quarter - 1] >= j))
            def _():
                at = slice(j * width, (j + 1) * width)
                part = mm(gvcat[at, :], waves[:, lanes])
                acc[...] += jnp.where(ids_here == j, part, 0.0)

        gs[width:, lanes] = acc[...]
    prev, nxt = row_masks(ids_ref[...])
    chunk = width // 2
    for r in range(4):
        at = slice(r * chunk, (r + 1) * chunk)
        here = p[at, :].astype(F32)
        grad = gs[at, :]
        d_taps[at, 0:1] = jnp.sum(grad * (pltpu.roll(here, 1, 1) * prev), axis=1, keepdims=True)
        d_taps[at, 1:2] = jnp.sum(grad * here, axis=1, keepdims=True)
        d_taps[at, 2:3] = jnp.sum(
            grad * (pltpu.roll(here, length - 1, 1) * nxt), axis=1, keepdims=True
        )
        gp_row[at, :] = (
            taps[at, 1:2] * grad
            + taps[at, 0:1] * pltpu.roll(grad * prev, length - 1, 1)
            + taps[at, 2:3] * pltpu.roll(grad * nxt, 1, 1)
        ).astype(BF16)
    share = jnp.transpose(gcb[...])[:8, :]
    high = share.astype(BF16)
    rest = (share - high.astype(F32)).astype(BF16)
    extra = jnp.concatenate([high, rest], axis=0)
    extra = jnp.concatenate([extra, jnp.zeros((16, quarter - hidden), BF16)], axis=1)
    for k, out in enumerate((o0, o1, o2, o3)):
        out[: 2 * width, :] = gp_row[:, tile(me ^ k, quarter)]
        out[2 * width :, :] = extra


def backward_spectral(
    me, gz_parts, ids, cb, taps, base, w2x, w2, feats, p, q, c, vr, vs, waves, after
):
    width, quarter = gz_parts[0].shape
    length = ids.shape[1]
    hidden = base.shape[0]
    outs = [shape((2 * width + 16, quarter), BF16)] * 4 + [
        shape((2 * width, length), BF16),
        shape((2 * width, 128), F32),
        shape((2 * width, hidden), F32),
        shape((feats.shape[0], hidden), F32),
        shape((hidden, 128), F32),
    ]
    return pl.pallas_call(
        backward_kernel,
        in_specs=[SM, SM] + [VM] * 17 + [HBM],
        out_specs=[VM] * 9,
        out_shape=outs,
        scratch_shapes=[
            pltpu.VMEM((SEGS * width, length), BF16),
            pltpu.VMEM((SEGS * width, 2 * length), BF16),
            pltpu.VMEM((2 * width, length), F32),
            pltpu.VMEM((width, quarter), F32),
        ],
        compiler_params=params(26),
        cost_estimate=cost(17),
        name="backward_spectral",
    )(
        me, ids, *gz_parts, ids, cb, taps, base, w2x, w2, feats, p, q, c, vr, vs, waves, after
    )


def middle_kernel(me_ref, z0, z1, z2, z3, x, w_out, norms, after, h_out, u2_out, z_t, *, piece):
    me = me_ref[0]
    width = z0.shape[0]
    for k, z in enumerate((z0, z1, z2, z3)):
        for i in range(width // piece):
            at = pl.ds(pl.multiple_of((i * 4 + (me ^ k)) * piece, piece), piece)
            z_t[at, :] = z[i * piece : (i + 1) * piece, :]
    h = x[...].astype(F32) + mm(jnp.transpose(z_t[...]), w_out[...])
    h_out[...] = h
    unit, _ = normed(h)
    u2_out[...] = (unit * norms[2:3, :] + norms[3:4, :]).astype(BF16)


def middle(me, z_parts, x, w_out, norms, after, piece):
    quarter, channels = x.shape
    return pl.pallas_call(
        functools.partial(middle_kernel, piece=piece),
        in_specs=[SM] + [VM] * 7 + [HBM],
        out_specs=[VM] * 3,
        out_shape=[
            shape((quarter, channels), F32),
            shape((quarter, channels), BF16),
            shape((channels, quarter), BF16),
        ],
        compiler_params=params(24),
        cost_estimate=cost(2),
        name="middle",
    )(me, *z_parts, x, w_out, norms, after)


def feed_kernel(
    me_ref, u2, h, ct, norms, w_out, gate, up, down,
    mixed, big_g, g0, g1, g2, g3, t_own, t_other, sums, acc_out, acc_grad, gz_t, gb_t, *, piece, thin,
):
    i = pl.program_id(0)

    @pl.when(i == 0)
    def _():
        acc_out[...] = jnp.zeros_like(acc_out)
        acc_grad[...] = jnp.zeros_like(acc_grad)

    g = mm(u2[...], gate[...])
    a = mm(u2[...], up[...])
    gh = mm_nt(ct[...], down[...])
    sg = sigmoid(g)
    silu = g * sg
    hid = (silu * a).astype(BF16)
    gg = (gh * a * (sg * (1.0 + g * (1.0 - sg)))).astype(BF16)
    ga = (gh * silu).astype(BF16)
    acc_out[...] += mm(hid, down[...])
    acc_grad[...] += mm_nt(gg, gate[...]) + mm_nt(ga, up[...])

    @pl.when(i == pl.num_programs(0) - 1)
    def _():
        me = me_ref[0]
        width = g0.shape[0]
        here = h[...]
        mixed[...] = (here + acc_out[...]).astype(BF16)
        gu2 = acc_grad[...]
        unit, scale = normed(here)
        sums[0:1, :] = jnp.sum(gu2 * unit, axis=0, keepdims=True)
        sums[1:2, :] = jnp.sum(gu2, axis=0, keepdims=True)
        total = ct[...].astype(F32) + norm_back(unit, scale, gu2 * norms[2:3, :])
        big_g[...] = total
        low = total.astype(BF16)
        gz_t[...] = mm_nt(w_out[...], low).astype(BF16)
        for k, out in enumerate((g0, g1, g2, g3)):
            for r in range(width // piece):
                at = pl.ds(pl.multiple_of((r * 4 + (me ^ k)) * piece, piece), piece)
                out[r * piece : (r + 1) * piece, :] = gz_t[at, :]
        gb_t[...] = jnp.transpose(total)
        for core, out in ((me & 1, t_own), (1 - (me & 1), t_other)):
            parts = []
            for x in range(2):
                for r in range(width // thin):
                    lo = pl.multiple_of((r * 4 + 2 * x + core) * thin, thin)
                    parts.append(gb_t[pl.ds(lo, thin), :])
            out[...] = jnp.concatenate(parts, axis=0).astype(BF16)


def feed_forward(me, u2, h, ct, norms, w_out, w_gate, w_up, w_down, piece, thin):
    quarter, channels = u2.shape
    ff = w_gate.shape[1]
    block = 512

    width = channels // 4
    outs = [
        ((quarter, channels), BF16),
        ((quarter, channels), F32),
    ] + [((width, quarter), BF16)] * 4 + [((2 * width, quarter), BF16)] * 2 + [((8, channels), F32)]
    return pl.pallas_call(
        functools.partial(feed_kernel, piece=piece, thin=thin),
        grid=(ff // block,),
        in_specs=[
            SM,
            VM,
            VM,
            VM,
            VM,
            VM,
            pl.BlockSpec((channels, block), lambda i: (0, i)),
            pl.BlockSpec((channels, block), lambda i: (0, i)),
            pl.BlockSpec((block, channels), lambda i: (i, 0)),
        ],
        out_specs=[VM] * len(outs),
        out_shape=[far(*outs[0])] + [shape(*out) for out in outs[1:]],
        scratch_shapes=[
            pltpu.VMEM((quarter, channels), F32),
            pltpu.VMEM((quarter, channels), F32),
            pltpu.VMEM((channels, quarter), BF16),
            pltpu.VMEM((channels, quarter), F32),
        ],
        compiler_params=params(28),
        cost_estimate=cost(13),
        name="feed_forward",
    )(me, u2, h, ct, norms, w_out, in_hbm(w_gate), in_hbm(w_up), in_hbm(w_down))


def hidden_grads_kernel(at_ref, *refs):
    u_parts, c_parts, refs = refs[:8], refs[8:16], refs[16:]
    gate, up, gt_own, gt_got, z_own, z_got, down, after, *refs = refs
    keep_a, give_a, keep_b, give_b, keep_o, give_o, rights, lefts, d_all, d_out = refs
    quarter, channels = u_parts[0].shape
    y, z = at_ref[1], at_ref[3]
    rows = gate.shape[0]
    for k in range(8):
        at = slice(k * quarter, (k + 1) * quarter)
        rights[0, at, :] = u_parts[k][...]
        rights[1, at, :] = c_parts[k][...]
    span = 2 * quarter

    @pl.loop(0, 4)
    def _(k):
        at = tile(k, span)
        g = mm_nt(gate[...], rights[0, at, :])
        a = mm_nt(up[...], rights[0, at, :])
        gh = mm_nt(down[...], rights[1, at, :])
        sg = sigmoid(g)
        silu = g * sg
        lefts[0, :, at] = (gh * a * (sg * (1.0 + g * (1.0 - sg)))).astype(BF16)
        lefts[1, :, at] = (gh * silu).astype(BF16)
        lefts[2, :, at] = (silu * a).astype(BF16)

    d_out[...] = mm_nt(gt_own[...], z_own[...]) + mm_nt(gt_got[...], z_got[...])
    half = keep_o.shape[0]
    x = at_ref[0] >> 1
    keep_o[...] = d_out[tile(x, half), :].astype(BF16)
    give_o[...] = d_out[tile(1 - x, half), :].astype(BF16)
    fw = rows // 4
    cut = keep_a.shape[-1]

    @pl.loop(0, 3)
    def _(m):
        grad = mm(lefts[m], rights[m >> 1]).astype(BF16)
        for i in range(4):
            d_all[i, m] = grad[i * fw : (i + 1) * fw]

    for i in range(2):
        keep_a[i] = d_all[2 * i + y, :, :, :cut]
        give_a[i] = d_all[2 * i + 1 - y, :, :, :cut]
        keep_b[i] = d_all[2 * z + i, :, :, cut:]
        give_b[i] = d_all[2 * (1 - z) + i, :, :, cut:]


def hidden_grads(at, u2_parts, ct_parts, gate, up, gt_own, gt_got, z_own, z_got, down, after):
    quarter, channels = u2_parts[0].shape
    wide = gate.shape[0]
    fw = wide // 4
    fs = 4
    cut = 2 * channels // 3
    return pl.pallas_call(
        hidden_grads_kernel,
        grid_spec=pltpu.PrefetchScalarGridSpec(
            num_scalar_prefetch=1,
            grid=(1,),
            in_specs=[VM] * 23 + [HBM],
            out_specs=[VM] * 6,
            scratch_shapes=[
                pltpu.VMEM((2, 8 * quarter, channels), BF16),
                pltpu.VMEM((3, wide, 8 * quarter), BF16),
                pltpu.VMEM((4, 3, fw, channels), BF16),
                pltpu.VMEM((2 * channels // fs, channels), F32),
            ],
        ),
        out_shape=[shape((2, 3, fw, cut), BF16)] * 2
        + [shape((2, 3, fw, channels - cut), BF16)] * 2
        + [shape((channels // fs, channels), BF16)] * 2,
        compiler_params=params(34),
        cost_estimate=cost(14),
        name="hidden_grads",
    )(at, *u2_parts, *ct_parts, gate, up, gt_own, gt_got, z_own, z_got, down, after)


def halve_kernel(at_ref, after, *refs, bits):
    pairs = len(bits)
    ins, outs = refs[: 2 * pairs], refs[2 * pairs :]
    for n in range(pairs):
        mine = at_ref[bits[n] + 1]
        keep, got = ins[2 * n], ins[2 * n + 1]
        next_keep, next_give = outs[2 * n], outs[2 * n + 1]
        for i in range(keep.shape[0]):
            for side, out in ((mine, next_keep), (1 - mine, next_give)):
                out[i] = (keep[i, side].astype(F32) + got[i, side].astype(F32)).astype(BF16)


def halve(at, bits, after, *sums):
    outs = []
    for n in range(len(bits)):
        dims = sums[2 * n].shape
        outs += [shape((dims[0],) + dims[2:], BF16)] * 2
    return pl.pallas_call(
        functools.partial(halve_kernel, bits=bits),
        in_specs=[SM, HBM] + [VM] * len(sums),
        out_specs=[VM] * len(outs),
        out_shape=outs,
        compiler_params=params(24),
        cost_estimate=cost(0.3),
        name="halve",
    )(at, after, *sums)


def load_riders(blocks, first, rows):
    parts = []
    for i in range(blocks.shape[0]):
        for m in range(blocks.shape[2] // 128):
            parts.append(blocks[i, first : first + rows, m * 128 : (m + 1) * 128].astype(F32))
    return jnp.concatenate(parts, axis=0)


def store_riders(block, packed, i, first, rows):
    columns = block.shape[1] // 128
    for m in range(columns):
        lo = (columns * i + m) * rows
        block[first : first + rows, m * 128 : (m + 1) * 128] = packed[lo : lo + rows, :]


def stage_kernel(
    at_ref, after, keep_a, got_a, keep_b, got_b, ours,
    next_keep_a, next_give_a, next_keep_b, next_give_b, total, joined, block,
):
    y, z = at_ref[1], at_ref[2]
    tall, rows = keep_a.shape[2], next_give_a.shape[1]
    flat = got_a.shape[2]
    columns = got_a.shape[3] // 128
    riders = joined.shape[0] // (4 * columns)
    start = flat - riders
    for i in range(2):
        for k in range(2):
            for m in range(columns):
                lo = (columns * (2 * i + k) + m) * riders
                piece = got_a[i, k, start:flat, m * 128 : (m + 1) * 128]
                joined[lo : lo + riders, :] = ours[lo : lo + riders, :].astype(F32) + piece.astype(F32)
    total[...] = joined[...].astype(BF16)
    for i in range(2):
        next_keep_a[i] = (keep_a[i, z].astype(F32) + got_a[i, z, :tall].astype(F32)).astype(BF16)
        block[...] = jnp.zeros_like(block)
        block[:tall, :] = keep_a[i, 1 - z].astype(F32) + got_a[i, 1 - z, :tall].astype(F32)
        store_riders(block, joined, i, rows - 2 * riders, 2 * riders)
        next_give_a[i] = block[...].astype(BF16)
        for side, out in ((y, next_keep_b), (1 - y, next_give_b)):
            out[i] = (keep_b[i, side].astype(F32) + got_b[i, side].astype(F32)).astype(BF16)


def stage(at, after, keep_a, got_a, keep_b, got_b, ours):
    _, _, tall, lanes = keep_a.shape
    narrow = keep_b.shape[-1]
    riders = ours.shape[0] // (4 * (lanes // 128))
    rows = got_a.shape[2] + riders
    return pl.pallas_call(
        stage_kernel,
        in_specs=[SM, HBM] + [VM] * 5,
        out_specs=[VM] * 5,
        out_shape=[
            shape((2, tall, lanes), BF16),
            shape((2, rows, lanes), BF16),
            shape((2, tall, narrow), BF16),
            shape((2, tall, narrow), BF16),
            shape(ours.shape, BF16),
        ],
        scratch_shapes=[pltpu.VMEM(ours.shape, F32), pltpu.VMEM((rows, lanes), F32)],
        compiler_params=params(12),
        cost_estimate=cost(0.3),
        name="stage",
    )(at, after, keep_a, got_a, keep_b, got_b, ours)


def join_kernel(at_ref, after, keep_a, got_a, keep_b, got_b, ours, keep, give, total):
    tall, cut = keep_a.shape[1:]
    riders = ours.shape[0] // (2 * (cut // 128))
    start = got_a.shape[1] - riders
    total[...] = (ours[...].astype(F32) + load_riders(got_a, start, riders)).astype(BF16)
    for side, out in ((at_ref[3], keep), (1 - at_ref[3], give)):
        out[:, :cut] = (keep_a[side].astype(F32) + got_a[side, :tall].astype(F32)).astype(BF16)
        out[:, cut:] = (keep_b[side].astype(F32) + got_b[side].astype(F32)).astype(BF16)


def join(at, after, keep_a, got_a, keep_b, got_b, ours):
    _, rows, cut = keep_a.shape
    return pl.pallas_call(
        join_kernel,
        in_specs=[SM, HBM] + [VM] * 5,
        out_specs=[VM] * 3,
        out_shape=[shape((rows, cut + keep_b.shape[-1]), BF16)] * 2 + [shape(ours.shape, BF16)],
        compiler_params=params(12),
        cost_estimate=cost(0.3),
        name="join",
    )(at, after, keep_a, got_a, keep_b, got_b, ours)


def hidden_last_kernel(keep_a, got_a, keep_b, got_b, after, *outs):
    *outs, token = outs
    token[...] = jnp.zeros_like(token)
    cut = keep_a.shape[-1]
    for m, out in enumerate(outs):
        out[:, :cut] = keep_a[0, m].astype(F32) + got_a[0, m].astype(F32)
        out[:, cut:] = keep_b[0, m].astype(F32) + got_b[0, m].astype(F32)


def hidden_last(keep_a, got_a, keep_b, got_b, after):
    _, count, rows, cut = keep_a.shape
    return pl.pallas_call(
        hidden_last_kernel,
        in_specs=[VM] * 4 + [HBM],
        out_specs=[VM] * (count + 1),
        out_shape=[far((rows, cut + keep_b.shape[-1]), F32)] * count + [shape((8, 128), F32)],
        compiler_params=params(12),
        cost_estimate=cost(0.3),
        name="hidden_last",
    )(keep_a, got_a, keep_b, got_b, after)


def add_kernel(ours, theirs, after, out):
    out[...] = (ours[...].astype(F32) + theirs[...].astype(F32)).astype(out.dtype)


def add(ours, theirs, after, dtype):
    return pl.pallas_call(
        add_kernel,
        in_specs=[VM, VM, HBM],
        out_specs=VM,
        out_shape=shape(ours.shape, dtype),
        compiler_params=params(8),
        cost_estimate=cost(0.3),
        name="add",
    )(ours, theirs, after)


def projection_kernel(
    at_ref, gp, u1, n1, w_mine, keep_o, got_o, d_w2, d_w1, d_taps, gcb, condt, mu, mn,
    sums2, after, keep_a, give_a, keep_b, give_b, packed_out, d_in, d_out, packed, sheet, *, layout,
):
    me, y, zbit = at_ref[0], at_ref[1], at_ref[2]
    channels = u1.shape[1]
    width = keep_o.shape[0]
    d_in[...] = mm(gp[...], u1[...])
    d_out[...] = keep_o[...].astype(F32) + got_o[...].astype(F32)
    blocks = 2 * keep_a.shape[0]
    first = 2 * width // blocks
    second = width // blocks
    cut = channels // 2

    def put(out, block, lanes):
        lo = pl.multiple_of(block * first, first)
        out[:first, :] = d_in[pl.ds(lo, first), lanes].astype(BF16)
        lo = pl.multiple_of(block * second, second)
        out[first:, :] = d_out[pl.ds(lo, second), lanes].astype(BF16)

    for b in range(blocks // 2):
        put(keep_a.at[b], 2 * b + y, slice(0, cut))
    for b in range(blocks // 4):
        for i in range(2):
            put(keep_b.at[b, i], 4 * b + 2 * zbit + i, slice(cut, channels))
            put(give_b.at[b, i], 4 * b + 2 * (1 - zbit) + i, slice(cut, channels))
    packed[...] = jnp.zeros_like(packed)
    packed[:width, :] = jnp.concatenate([d_w2[:width, :], d_w2[width:, :]], axis=1)
    taps_t = jnp.transpose(d_taps[...])
    gcb_t = jnp.transpose(gcb[...])[:8, :]
    gmu = lax.dot_general(
        gcb_t, condt[...], (((1,), (0,)), ((), ())), precision=HIGH, preferred_element_type=F32
    )
    gp_n = mm(gp[...], n1[...])
    w32 = w_mine[...].astype(F32)
    gain = jnp.sum(gp_n * w32, axis=0, keepdims=True) + jnp.sum(gmu * mn[...], axis=0, keepdims=True)
    total = jnp.sum(gp[...].astype(F32), axis=1, keepdims=True)
    shift = jnp.sum(total * w32, axis=0, keepdims=True) + jnp.sum(gmu, axis=0, keepdims=True)
    for i in range(3):
        for m in range(2 * width // 128):
            at = layout["taps"] + i * (2 * width // 128) + m
            packed[at : at + 1, :] = taps_t[i : i + 1, m * 128 : (m + 1) * 128]
    for i, row in enumerate((gain, shift, sums2[0:1, :], sums2[1:2, :])):
        for m in range(channels // 128):
            at = layout["ln"] + i * (channels // 128) + m
            packed[at : at + 1, :] = row[:, m * 128 : (m + 1) * 128]
    half = d_w1.shape[0] // 2
    packed[layout["w1"] : layout["w1"] + half, :] = jnp.concatenate(
        [d_w1[:half, :], d_w1[half:, :]], axis=1
    )
    zeros = jnp.zeros_like(gcb_t)
    row = at_ref[4]
    odd = (row & 1) == 1
    both = jnp.concatenate([jnp.where(odd, zeros, gcb_t), jnp.where(odd, gcb_t, zeros)], axis=1)
    packed[pl.ds(pl.multiple_of(layout["cb"] + 8 * (row >> 1), 8), 8), :] = both
    share = jnp.zeros((8, width), F32)
    for f in range(channels // width):
        share = share + jnp.where(me == f, mu[:, f * width : (f + 1) * width], 0.0)
    rest = jnp.concatenate([share[:SEGS, 128:], jnp.zeros((SEGS, 256 - width), F32)], axis=1)
    block = jnp.concatenate([share[:SEGS, :128], rest, jnp.zeros((8 - 2 * SEGS, 128), F32)], axis=0)
    packed[pl.ds(pl.multiple_of(layout["mu"] + 8 * row, 8), 8), :] = block
    packed_out[...] = packed[...].astype(BF16)
    riders = packed.shape[0] // (4 * (cut // 128))
    for b in range(blocks // 2):
        sheet[...] = jnp.zeros_like(sheet)
        lo = pl.multiple_of((2 * b + 1 - y) * first, first)
        sheet[:first, :] = d_in[pl.ds(lo, first), :cut]
        lo = pl.multiple_of((2 * b + 1 - y) * second, second)
        sheet[first : first + second, :] = d_out[pl.ds(lo, second), :cut]
        store_riders(sheet, packed, b, sheet.shape[0] - riders, riders)
        give_a[b] = sheet[...].astype(BF16)


def packed_layout(width, channels, bs):
    taps = width
    ln = taps + 3 * (2 * width // 128)
    w1 = -(-(ln + 4 * (channels // 128)) // 8) * 8
    cb = w1 + 32
    mu = cb + 4 * bs
    return {"taps": taps, "ln": ln, "w1": w1, "cb": cb, "mu": mu, "rows": -(-(mu + 8 * bs) // 128) * 128}


def projection_grads(
    at, gp, u1, n1, w_mine, keep_o, got_o, d_w2, d_w1, d_taps, gcb, condt, mu, mn, sums2, after, bs
):
    length, channels = u1.shape
    width = keep_o.shape[0]
    layout = packed_layout(width, channels, bs)
    tall = 3 * width // bs
    flat = -(-tall // 16) * 16 + layout["rows"] // (4 * (channels // 256))
    return pl.pallas_call(
        functools.partial(projection_kernel, layout=layout),
        in_specs=[SM] + [VM] * 14 + [HBM],
        out_specs=[VM] * 5,
        out_shape=[
            shape((bs // 2, tall, channels // 2), BF16),
            shape((bs // 2, flat, channels // 2), BF16),
        ]
        + [shape((bs // 4, 2, 3 * width // bs, channels // 2), BF16)] * 2
        + [shape((layout["rows"], 128), BF16)],
        scratch_shapes=[
            pltpu.VMEM((2 * width, channels), F32),
            pltpu.VMEM((width, channels), F32),
            pltpu.VMEM((layout["rows"], 128), F32),
            pltpu.VMEM((flat, channels // 2), F32),
        ],
        compiler_params=params(24),
        cost_estimate=cost(2),
        name="projection_grads",
    )(
        at, gp, u1, n1, w_mine, keep_o, got_o, d_w2, d_w1, d_taps, gcb, condt, mu, mn, sums2, after
    )


def final_kernel(
    me_ref, p0, p1, p2, p3, x, big_g, norms, ids_row, condt, w_in, after, out, gp_t, *, piece
):
    me = me_ref[0]
    rows = gp_t.shape[0] // 4
    hidden = condt.shape[0]
    share = jnp.zeros((8, hidden), F32)
    for k, part in enumerate((p0, p1, p2, p3)):
        for i in range(rows // piece):
            at = pl.ds(pl.multiple_of((i * 4 + (me ^ k)) * piece, piece), piece)
            gp_t[at, :] = part[i * piece : (i + 1) * piece, :]
        extra = part[rows:, :hidden].astype(F32)
        share = share + extra[:8] + extra[8:]
    ids = ids_row[...]
    number = lax.broadcasted_iota(jnp.int32, (8, ids.shape[1]), 0)
    counts = jnp.sum(jnp.where(ids == number, 1.0, 0.0), axis=1, keepdims=True)
    gmu = lax.dot_general(
        share, condt[...], (((1,), (0,)), ((), ())), precision=HIGH, preferred_element_type=F32
    ) / jnp.maximum(counts, 1.0)
    gu1 = mm_nt(jnp.transpose(gp_t[...]), w_in[...])
    quarter = x.shape[0]
    own = jnp.broadcast_to(ids_row[:, tile(me, quarter)].astype(F32), (8, quarter))
    ids_own = jnp.transpose(own)[:, 0:1]
    for j in range(SEGS):
        gu1 = gu1 + jnp.where(ids_own == j, gmu[j : j + 1, :], 0.0)
    unit, scale = normed(x[...].astype(F32))
    out[...] = big_g[...] + norm_back(unit, scale, gu1 * norms[0:1, :])


def final(me, gp_parts, x, big_g, norms, ids, condt, w_in, after, piece):
    quarter, channels = x.shape
    return pl.pallas_call(
        functools.partial(final_kernel, piece=piece),
        in_specs=[SM] + [VM] * 10 + [HBM],
        out_specs=VM,
        out_shape=shape((quarter, channels), F32),
        scratch_shapes=[pltpu.VMEM((2 * channels, quarter), BF16)],
        compiler_params=params(24),
        cost_estimate=cost(0.3),
        name="final",
    )(me, *gp_parts, x, big_g, norms, ids, condt, in_hbm(w_in), after)


def small_kernel(
    me_ref, j0, j1, j2, j3, w2, taps, ln0, ln1, ln2, ln3, w1, b1, cond, wide, tap_t, cond_t, *, layout, step, width
):
    me = me_ref[0]
    parts = [part[...].astype(F32) for part in (j0, j1, j2, j3)]
    hidden = w1.shape[0]
    half = width // step
    count = 2 * width // 128
    for k, part in enumerate(parts):
        who = me ^ k
        rows = jnp.concatenate(
            [
                jnp.concatenate([part[layout["taps"] + i * count + m : layout["taps"] + i * count + m + 1, :]
                                 for m in range(count)], axis=1)
                for i in range(3)
            ]
            + [jnp.zeros((125, 2 * width), F32)],
            axis=0,
        )
        tap_t[...] = jnp.transpose(rows)
        for side in range(2):
            for i in range(half):
                at = pl.ds(pl.multiple_of((side * half * 4 + i * 4 + who) * step, step), step)
                lo = i * step
                wide[at, :hidden] = part[lo : lo + step, side * hidden : (side + 1) * hidden]
                at2 = side * width + lo
                wide[at, hidden:] = tap_t[at2 : at2 + step, :hidden]
    whole = jnp.transpose(wide[...])
    w2[...] = whole[:hidden, :]
    taps[...] = whole[hidden : hidden + 3, :]

    def common(first, last):
        a, b, c, d = [part[first:last, :] for part in parts]
        return (a + b) + (c + d)

    lanes = ln0.shape[0] // 128
    sums = common(layout["ln"], layout["ln"] + 4 * lanes)
    for i, out in enumerate((ln0, ln1, ln2, ln3)):
        row = jnp.concatenate([sums[i * lanes + m : i * lanes + m + 1, :] for m in range(lanes)], axis=1)
        out[...] = row.reshape(out.shape)
    both = common(layout["w1"], layout["w1"] + hidden // 2)
    w1[: hidden // 2, :] = both[:, :hidden]
    w1[hidden // 2 :, :] = both[:, hidden:]
    cb = common(layout["cb"], layout["mu"])
    shares = []
    for b in range(cb.shape[0] // 4):
        lo = 8 * (b // 2)
        shares.append(cb[lo : lo + 8, (b % 2) * hidden : (b % 2 + 1) * hidden])
    shares = jnp.concatenate(shares, axis=0)
    b1[...] = jnp.sum(shares, axis=0, keepdims=True)
    for k, part in enumerate(parts):
        rows = []
        for b in range(cb.shape[0] // 4):
            lo = layout["mu"] + 8 * b
            block = part[lo : lo + 8, :]
            rows.append(
                jnp.concatenate(
                    [
                        jnp.concatenate([block[:SEGS, :], jnp.zeros((8 - SEGS, 128), F32)], axis=0),
                        jnp.concatenate(
                            [block[SEGS : 2 * SEGS, : width - 128], jnp.zeros((8 - SEGS, width - 128), F32)],
                            axis=0,
                        ),
                    ],
                    axis=1,
                )
            )
        mu = jnp.concatenate(rows, axis=0)
        cond_t[tile(me ^ k, width), :] = lax.dot_general(
            jnp.transpose(mu), shares, (((1,), (0,)), ((), ())), precision=HIGH, preferred_element_type=F32
        )
    cond[...] = jnp.transpose(cond_t[...])


def small_grads(me, parts, hidden, channels, step, bs):
    width = channels // 4
    layout = packed_layout(width, channels, bs)
    return pl.pallas_call(
        functools.partial(small_kernel, layout=layout, step=step, width=width),
        in_specs=[SM] + [VM] * 4,
        out_specs=[VM] * 9,
        out_shape=[
            far((hidden, 2 * channels), F32),
            far((3, 2 * channels), F32),
            far((channels,), F32),
            far((channels,), F32),
            far((channels,), F32),
            far((channels,), F32),
            far((hidden, hidden), F32),
            far((1, hidden), F32),
            far((hidden, channels), F32),
        ],
        scratch_shapes=[
            pltpu.VMEM((2 * channels, 2 * hidden), F32),
            pltpu.VMEM((2 * width, 128), F32),
            pltpu.VMEM((channels, hidden), F32),
        ],
        compiler_params=params(24),
        cost_estimate=cost(3),
        name="small_grads",
    )(me, *parts)


def trade_parts(parts):
    two, three, one = [swap(parts[k], "freq", k) for k in (2, 3, 1)]
    return (parts[0], one, two, three)


def tiled_device(
    tokens,
    seg_ids,
    cotangent,
    ln1_gain,
    ln1_shift,
    w_in,
    conv_taps,
    freq_w1,
    freq_b1,
    freq_w2,
    cond_w,
    w_out,
    ln2_gain,
    ln2_shift,
    w_gate,
    w_up,
    w_down,
):
    quarter, _, channels = tokens.shape
    length = seg_ids.shape[1]
    ff = w_gate.shape[1]
    fs = lax.axis_size("freq")
    bs = lax.axis_size("batch")
    me = lax.axis_index("freq")
    row = lax.axis_index("batch")
    width = channels // fs
    half = bs // 2
    step = channels // (half * fs)
    fw = ff // (bs * fs)
    table = np.concatenate(tables(length), axis=0)
    feats = features(length, freq_w1.shape[0] // 2)
    feats_aug = np.concatenate(
        [feats, np.ones((1, length), np.float32), np.zeros((7, length), np.float32)], axis=0
    )

    x_own = tokens[:, 0]
    ct_own = cotangent[:, 0]
    ids = seg_ids
    at = jnp.stack([me, row & 1, (row >> 1) & 1, (row >> 2) & 1, row]).astype(jnp.int32)
    norms = jnp.concatenate([ln1_gain, ln1_shift, ln2_gain, ln2_shift]).reshape(4, channels)
    condt = cond_w.T

    def gather_after(value, after):
        two = swap(value, "freq", 2)
        one = swap(value, "freq", 1)
        (two,) = tie([two], after)
        return (value, one, two, swap(two, "freq", 1))

    def gather_wide(value, *after):
        count = bs * fs
        parts = (
            value,
            swap(value, "freq", 2),
            swap(value, "batch", 2),
            lax.ppermute(value, ("batch", "freq"), [(i, i ^ (2 * fs + 2)) for i in range(count)]),
        )
        parts = parts[:1] + tuple(tie(parts[1:], *after))
        return parts + tuple(swap(part, "freq", 1) for part in parts)

    def pairs(value):
        return value.reshape((value.shape[0] // 2, 2) + value.shape[1:])

    w_mine, w2x, w2t, taps, base, waves, w_near, x_near, condt = prepare(
        at, w_in, freq_w2, conv_taps, freq_w1, freq_b1, jnp.asarray(feats_aug), jnp.asarray(table), w_out,
        x_own, condt, norms, step, fs
    )
    x_parts = gather_after(x_own, base)
    x_parts = (x_near,) + x_parts[1:]
    forward = forward_spectral(at, x_parts, ids, norms, w_mine, taps, base, w2x, condt, waves)
    z_parts, (u1, n1, p, q, c, vr, vs, mu, mn, cb) = forward[:4], forward[4:]
    ct_x = swap(ct_own, "freq", 2)
    ct_z = swap(ct_own, "batch", 2)
    z_got = trade_parts(z_parts)
    wg_mine, wu_mine, wd_mine = select_columns(at, cb, w_gate, w_up, w_down, bs, fs)
    (ct_x,) = tie([ct_x], cb)
    ct_parts = (ct_own, ct_x, ct_z, swap(ct_x, "batch", 2))
    h, u2, z_t = middle(at, z_got, x_near, w_near, norms, wg_mine, step)
    fed = feed_forward(
        at, u2, h, ct_own, norms, w_near, w_gate, w_up, w_down, step, channels // (bs * fs)
    )
    mixed_out, big_g, gz_parts, gt_own, gt_other, sums2 = fed[0], fed[1], fed[2:6], *fed[6:]
    gt_got = swap(gt_other, "freq", 1)
    ct_parts = ct_parts + tuple(swap(part, "freq", 1) for part in tie(ct_parts, sums2))
    u2_parts = gather_wide(u2, sums2, ct_parts[4])
    gz_got = trade_parts(gz_parts)

    z_got = swap(z_t, "freq", 1)
    keep_a, give_a, keep_b, give_b, keep_o, give_o = hidden_grads(
        at, u2_parts, ct_parts, wg_mine, wu_mine, gt_own, gt_got, z_t, z_got,
        wd_mine, sums2,
    )
    got_a = swap(give_a, "batch", 1)
    got_b = swap(give_b, "batch", 4)
    got_o = swap(give_o, "freq", 2)

    back = backward_spectral(
        at, gz_got, ids, cb, taps, base, w2x, w2t, jnp.asarray(feats).astype(BF16),
        p, q, c, vr, vs, waves, give_a,
    )
    gp_parts, (gp, d_taps, d_w2, d_w1, gcb) = back[:4], back[4:]
    gp_got = trade_parts(gp_parts)

    proj = projection_grads(
        at, gp, u1, n1, w_mine, keep_o, got_o, d_w2, d_w1, d_taps, gcb, condt, mu, mn, sums2, gcb, bs
    )
    p_keep_a, p_give_a, p_keep_b, p_give_b, packed = proj
    p_got_a = swap(p_give_a, "batch", 1)
    p_got_b = swap(p_give_b, "batch", 2)
    keep_a, give_a, keep_b, give_b = halve(
        at, (2, 0), p_give_a, keep_a[None], got_a[None], keep_b[None], got_b[None]
    )
    got_a = swap(give_a, "batch", 4)
    got_b = swap(give_b, "batch", 1)

    p_keep_a, p_give_a, p_keep_b, p_give_b, packed = stage(
        at, p_give_a, pairs(p_keep_a), pairs(p_got_a), p_keep_b, p_got_b, packed
    )
    p_got_a = swap(p_give_a, "batch", 2)
    p_got_b = swap(p_give_b, "batch", 1)
    d_gate, d_up, d_down, token = hidden_last(keep_a, got_a, keep_b, got_b, packed)
    keep, give, packed = join(at, token, p_keep_a, p_got_a, p_keep_b, p_got_b, packed)
    grad_tokens = final(at, gp_got, x_own, big_g, norms, ids, condt, w_in, packed, step)
    got = swap(give, "batch", 4)
    sent = add(packed, swap(packed, "batch", 4), give, BF16)
    (grad_tokens,) = tie([grad_tokens], sent)
    mine = keep.astype(F32) + got.astype(F32)
    first = 2 * width // bs

    d_w2, d_taps, *ln, d_w1, d_b1, d_cond = small_grads(
        at, gather_freq(sent, me), freq_w1.shape[1], channels, step, bs
    )
    return (
        mixed_out[:, None],
        grad_tokens[:, None],
        ln[0],
        ln[1],
        mine[:first].T,
        d_taps,
        d_w1,
        d_b1[0],
        d_w2,
        d_cond.T,
        mine[first:].T,
        ln[2],
        ln[3],
        d_gate.T,
        d_up.T,
        d_down,
    )


def per_device(*args):
    channels = args[0].shape[2]
    step = 2 * channels // (lax.axis_size("batch") * lax.axis_size("freq"))
    fits = lax.axis_size("batch") == 8 and lax.axis_size("freq") == 4 and step % 16 == 0
    return tiled_device(*args) if fits else plain_device(*args)


def solution(mesh):
    rows = P("freq", "batch", None)
    split = P(None, ("batch", "freq"))
    in_specs = (rows, P("batch", None), rows) + (P(),) * 14
    out_specs = (
        rows,
        rows,
        P(),
        P(),
        split,
        P(),
        P(),
        P(),
        P(),
        P(),
        split,
        P(),
        P(),
        split,
        split,
        P(("batch", "freq"), None),
    )
    return jax.shard_map(
        per_device, mesh=mesh, in_specs=in_specs, out_specs=out_specs, check_vma=False
    )
```

```python
import functools

import jax
import jax.numpy as jnp
import ml_dtypes
import numpy as np
from jax import lax
from jax.experimental import pallas as pl
from jax.experimental.pallas import tpu as pltpu
from jax.sharding import PartitionSpec as P

SEGS = 3
EPS = 1e-05
HIGH = lax.Precision.HIGHEST
F32 = jnp.float32
BF16 = jnp.bfloat16


def mm(a, b):
    return jnp.dot(a, b, preferred_element_type=F32)


def mm_nt(a, b):
    return lax.dot_general(a, b, (((1,), (1,)), ((), ())), preferred_element_type=F32)


def mm_tn(a, b):
    return lax.dot_general(a, b, (((0,), (0,)), ((), ())), preferred_element_type=F32)


def swap(value, axis, mask):
    count = lax.axis_size(axis)
    return lax.ppermute(value, axis, [(i, i ^ mask) for i in range(count)])


def pick(parts, index):
    return lax.dynamic_index_in_dim(parts, index, 0, keepdims=False)


def in_order(received, me):
    a, b, c, d = received
    low = (me & 1) == 1
    a, b = jnp.where(low, b, a), jnp.where(low, a, b)
    c, d = jnp.where(low, d, c), jnp.where(low, c, d)
    high = (me & 2) == 2
    a, c = jnp.where(high, c, a), jnp.where(high, a, c)
    b, d = jnp.where(high, d, b), jnp.where(high, b, d)
    return (a, b, c, d)


def trade(blocks, me):
    return [pick(blocks, me)] + [swap(pick(blocks, me ^ k), "freq", k) for k in (2, 3, 1)]


def trade_sorted(blocks, me):
    own, two, three, one = trade(blocks, me)
    return in_order((own, one, two, three), me)


def gather_freq(value, me):
    two = swap(value, "freq", 2)
    one = swap(value, "freq", 1)
    three = swap(two, "freq", 1)
    return (value, one, two, three)


def scatter_sum(value, order):
    bits = lax.axis_size("batch").bit_length() - 1
    me = lax.axis_index("batch")
    rest = value.shape[1:]
    value = value.reshape((2,) * bits + rest)
    left = list(range(bits - 1, -1, -1))
    for bit in order:
        dim = left.index(bit)
        mine = (me >> bit) & 1
        keep = lax.dynamic_index_in_dim(value, mine, dim, keepdims=False)
        give = lax.dynamic_index_in_dim(value, 1 - mine, dim, keepdims=False)
        got = swap(give, "batch", 1 << bit)
        total = keep.astype(F32) + got.astype(F32)
        left.remove(bit)
        value = total.astype(value.dtype) if left else total
    return value


def tables(length):
    index = np.arange(length, dtype=np.int64)
    angle = (index[:, None] * index[None, :] % (2 * length)) * (np.pi / length)
    return (
        np.cos(angle).astype(ml_dtypes.bfloat16),
        np.sin(angle).astype(ml_dtypes.bfloat16),
    )


def features(length, half):
    index = np.arange(length, dtype=np.int64)
    lags = (np.arange(half, dtype=np.int64) + 1) ** 2
    angle = (lags[:, None] * index[None, :] % (2 * length)) * (np.pi / length)
    return np.concatenate([np.cos(angle), np.sin(angle)], axis=0).astype(np.float32)


def normed(values):
    centered = values - jnp.mean(values, axis=-1, keepdims=True)
    scale = lax.rsqrt(jnp.mean(centered * centered, axis=-1, keepdims=True) + EPS)
    return centered * scale, scale


def norm_back(unit, scale, grad):
    return scale * (
        grad
        - jnp.mean(grad, axis=-1, keepdims=True)
        - unit * jnp.mean(grad * unit, axis=-1, keepdims=True)
    )


def shift_right(values):
    return jnp.pad(values, ((0, 0), (1, 0)))[:, :-1]


def shift_left(values):
    return jnp.pad(values, ((0, 0), (0, 1)))[:, 1:]


def plain_device(
    tokens,
    seg_ids,
    cotangent,
    ln1_gain,
    ln1_shift,
    w_in,
    conv_taps,
    freq_w1,
    freq_b1,
    freq_w2,
    cond_w,
    w_out,
    ln2_gain,
    ln2_shift,
    w_gate,
    w_up,
    w_down,
):
    quarter, _, channels = tokens.shape
    length = seg_ids.shape[1]
    ff = w_gate.shape[1]
    fs = lax.axis_size("freq")
    bs = lax.axis_size("batch")
    me = lax.axis_index("freq")
    width = channels // fs
    half = bs // 2
    step = channels // (half * fs)
    cos_table, sin_table = tables(length)
    feats = features(length, freq_w1.shape[0] // 2)

    x_own = tokens[:, 0]
    ct_own = cotangent[:, 0]
    ids = seg_ids
    x_parts = gather_freq(x_own, me)
    ct_parts = gather_freq(ct_own, me)

    w_in_t = (
        w_in.T.reshape(2, half, fs, step, channels)
        .transpose(2, 0, 1, 3, 4)
        .reshape(fs, 2 * width, channels)
    )
    w_in_mine = pick(w_in_t, me)
    w_out_p = (
        w_out.reshape(half, fs, step, channels).transpose(1, 0, 2, 3).reshape(channels, channels)
    )
    taps_mine = pick(
        conv_taps.reshape(3, 2, half, fs, step).transpose(3, 0, 1, 2, 4).reshape(fs, 3, 2 * width), me
    )[:, :, None]
    w2_mine = pick(
        freq_w2.reshape(-1, 2, half, fs, step).transpose(3, 0, 1, 2, 4).reshape(fs, -1, 2 * width), me
    )
    fw = ff // (bs * fs)
    wide = ff // fs

    def mine_rows(weight):
        return pick(
            weight.reshape(bs, fs, fw, channels).transpose(1, 0, 2, 3).reshape(fs, wide, channels), me
        )

    wg_mine, wu_mine, wd_mine = (mine_rows(w_gate.T), mine_rows(w_up.T), mine_rows(w_down))

    base = jnp.dot(freq_w1.T, feats, precision=HIGH) + freq_b1[:, None]

    x_row = jnp.concatenate(in_order(x_parts, me), axis=0).astype(F32)
    unit1, _ = normed(x_row)
    u1 = (unit1 * ln1_gain + ln1_shift).astype(BF16)
    n1 = unit1.astype(BF16)
    masks = (ids == jnp.arange(SEGS, dtype=jnp.int32)[:, None]).astype(F32)
    counts = jnp.sum(masks, axis=1, keepdims=True)
    mu = mm(masks.astype(BF16), u1) / counts
    mn = mm(masks.astype(BF16), n1) / counts
    cb = jnp.dot(mu, cond_w, precision=HIGH)
    p = mm_nt(w_in_mine, u1)
    same = (ids[:, 1:] == ids[:, :-1]).astype(F32)
    zero = jnp.zeros((1, 1), F32)
    prev = jnp.concatenate([zero, same], axis=1)
    nxt = jnp.concatenate([same, zero], axis=1)
    p_prev = shift_right(p) * prev
    p_next = shift_left(p) * nxt
    s = taps_mine[0] * p_prev + taps_mine[1] * p + taps_mine[2] * p_next
    q, v = s[:width], s[width:]

    pre = base[None] + cb[:, :, None]
    gate_pre = jax.nn.sigmoid(pre)
    hk = pre * gate_pre
    kk = jnp.einsum("kc,jkf->jcf", w2_mine, hk, precision=HIGH)
    kr, ki = kk[:, :width], kk[:, width:]
    vm = (v[None] * masks[:, None, :]).astype(BF16).reshape(SEGS * width, length)
    vr = mm(vm, cos_table).reshape(SEGS, width, length)
    vi = -mm(vm, sin_table).reshape(SEGS, width, length)
    weights = np.full((length,), 2.0 / (2 * length), np.float32)
    weights[0] = 1.0 / (2 * length)
    yr = ((kr * vr - ki * vi) * weights).astype(BF16).reshape(SEGS * width, length)
    yi = ((kr * vi + ki * vr) * weights).astype(BF16).reshape(SEGS * width, length)
    conv = (mm(yr, cos_table) - mm(yi, sin_table)).reshape(SEGS, width, length)
    c = jnp.sum(conv * masks[:, None, :], axis=0)
    z_mine = (q * c).astype(BF16)

    z_blocks = z_mine.reshape(width, fs, quarter).transpose(1, 0, 2)
    z_t = jnp.concatenate(trade_sorted(z_blocks, me), axis=0)

    x32 = x_own.astype(F32)
    ct32 = ct_own.astype(F32)
    h = x32 + mm_tn(z_t, w_out_p)
    unit2, scale2 = normed(h)
    u2 = (unit2 * ln2_gain + ln2_shift).astype(BF16)
    u2_parts = gather_freq(u2, me)
    g = mm(u2, w_gate)
    a = mm(u2, w_up)
    gh = mm_nt(ct_own, w_down)
    sg = jax.nn.sigmoid(g)
    silu = g * sg
    hid = (silu * a).astype(BF16)
    mixed_out = (h + mm(hid, w_down)).astype(BF16)
    gg = (gh * a * sg * (1.0 + g * (1.0 - sg))).astype(BF16)
    ga = (gh * silu).astype(BF16)
    gu2 = mm_nt(gg, w_gate) + mm_nt(ga, w_up)
    grad_ln2_gain = jnp.sum(gu2 * unit2, axis=0)
    grad_ln2_shift = jnp.sum(gu2, axis=0)
    big_g = ct32 + norm_back(unit2, scale2, gu2 * ln2_gain)
    gb = big_g.astype(BF16)
    gz_blocks = mm_nt(w_out_p, gb).astype(BF16).reshape(fs, width, quarter)
    gz = jnp.concatenate(trade_sorted(gz_blocks, me), axis=1).astype(F32)
    gb_parts = gather_freq(gb, me)

    u2_row = jnp.concatenate(u2_parts, axis=0)
    ct_row = jnp.concatenate(ct_parts, axis=0)
    g_t = mm_nt(wg_mine, u2_row)
    a_t = mm_nt(wu_mine, u2_row)
    gh_t = mm_nt(wd_mine, ct_row)
    sg_t = jax.nn.sigmoid(g_t)
    silu_t = g_t * sg_t
    hid_t = (silu_t * a_t).astype(BF16)
    gg_t = (gh_t * a_t * sg_t * (1.0 + g_t * (1.0 - sg_t))).astype(BF16)
    ga_t = (gh_t * silu_t).astype(BF16)
    d_gate = mm(gg_t, u2_row).astype(BF16)
    d_up = mm(ga_t, u2_row).astype(BF16)
    d_down = mm(hid_t, ct_row).astype(BF16)
    d_ff = jnp.stack([d_gate, d_up, d_down], axis=0).reshape(3, bs, fw, channels).transpose(1, 0, 2, 3)
    bits = bs.bit_length() - 1
    order_a = list(range(bits))
    order_b = [1, 0] + list(range(2, bits))
    cut = channels // 2
    ff_a = scatter_sum(d_ff[..., :cut], order_a)
    ff_b = scatter_sum(d_ff[..., cut:], order_b)
    d_ff = jnp.concatenate([ff_a, ff_b], axis=-1)

    gq = gz * c
    gc = gz * q
    gcm = (gc[None] * masks[:, None, :]).astype(BF16).reshape(SEGS * width, length)
    gyr = mm(gcm, cos_table).reshape(SEGS, width, length) * weights
    gyi = -mm(gcm, sin_table).reshape(SEGS, width, length) * weights
    gkr = gyr * vr + gyi * vi
    gki = gyi * vr - gyr * vi
    gvr = (kr * gyr + ki * gyi).astype(BF16).reshape(SEGS * width, length)
    gvi = (kr * gyi - ki * gyr).astype(BF16).reshape(SEGS * width, length)
    gv_all = (mm(gvr, cos_table) - mm(gvi, sin_table)).reshape(SEGS, width, length)
    gv = jnp.sum(gv_all * masks[:, None, :], axis=0)
    gs = jnp.concatenate([gq, gv], axis=0)
    d_taps = jnp.stack(
        [jnp.sum(gs * p_prev, axis=1), jnp.sum(gs * p, axis=1), jnp.sum(gs * p_next, axis=1)]
    )
    gp = (
        taps_mine[1] * gs
        + taps_mine[0] * shift_left(gs * prev)
        + taps_mine[2] * shift_right(gs * nxt)
    ).astype(BF16)

    gkk = jnp.concatenate([gkr, gki], axis=1)
    gkk_low = gkk.astype(BF16)
    hk_low = hk.astype(BF16)
    d_w2 = jnp.einsum("jkf,jcf->kc", hk_low, gkk_low, preferred_element_type=F32)
    gpre = jnp.einsum("kc,jcf->jkf", w2_mine.astype(BF16), gkk_low, preferred_element_type=F32)
    gpre = gpre * gate_pre * (1.0 + pre * (1.0 - gate_pre))
    d_w1 = jnp.einsum("ef,jkf->ek", feats, gpre, precision=HIGH)
    gcb = jnp.sum(gpre, axis=2)
    gcb_row = lax.psum(gcb, "freq")

    gp_blocks = gp.reshape(2 * width, fs, quarter).transpose(1, 0, 2)
    gp_t = jnp.concatenate(trade_sorted(gp_blocks, me), axis=0)

    u1_row = u1
    d_in = mm(gp, u1_row).astype(BF16).reshape(bs, 2 * width // bs, channels)
    d_in = scatter_sum(d_in, order_a)
    gb_row = jnp.concatenate(in_order(gb_parts, me), axis=0)
    d_out = mm(z_mine, gb_row)
    narrow = channels // bs
    d_out = scatter_sum(d_out.T.astype(BF16).reshape(bs, narrow, width), order_a)
    d_out = d_out.reshape(fs, narrow // fs, width)
    d_out = jnp.stack(trade_sorted(d_out, me), axis=0)
    d_out = (
        d_out.reshape(fs, narrow // fs, half, step).transpose(2, 0, 3, 1).reshape(channels, -1)
    )

    gmu_part = jnp.dot(gcb, cond_w.T, precision=HIGH)
    sum_gp = jnp.sum(gp.astype(F32), axis=1)
    w_mine32 = w_in_mine.astype(F32)
    d_shift1 = jnp.dot(sum_gp[None], w_mine32, precision=HIGH)[0] + jnp.sum(gmu_part, axis=0)
    d_gain1 = jnp.sum(mm(gp, n1) * w_mine32, axis=0) + jnp.sum(gmu_part * mn, axis=0)

    gmu = jnp.dot(gcb_row, cond_w.T, precision=HIGH) / counts
    own_masks = lax.dynamic_slice_in_dim(masks, me * quarter, quarter, 1)
    gu1 = mm_tn(gp_t, w_in_t.reshape(2 * channels, channels)) + lax.dot_general(
        own_masks, gmu, (((0,), (0,)), ((), ())), precision=HIGH
    )
    unit_own, scale_own = normed(x32)
    grad_tokens = big_g + norm_back(unit_own, scale_own, gu1 * ln1_gain)

    shared = [
        d_gain1,
        d_shift1,
        d_w1.reshape(-1),
        jnp.sum(gcb, axis=0),
        jnp.dot(mu.T, gcb, precision=HIGH).reshape(-1),
        grad_ln2_gain,
        grad_ln2_shift,
    ]
    owned = jnp.concatenate([d_taps, d_w2], axis=0)
    packed = jnp.concatenate(shared + [owned.reshape(-1)])
    for bit in range(bits):
        packed = packed + swap(packed, "batch", 1 << bit)
    split = packed.shape[0] - owned.size
    common, owned = packed[:split], packed[split:]
    common = common + swap(common, "freq", 1)
    common = common + swap(common, "freq", 2)
    owned = jnp.stack(in_order(gather_freq(owned, me), me), axis=0)
    owned = (
        owned.reshape(fs, -1, 2, half, step).transpose(1, 2, 3, 0, 4).reshape(-1, 2 * channels)
    )
    sizes = np.cumsum([part.size for part in shared])
    got = jnp.split(common, sizes[:-1])
    return (
        mixed_out[:, None],
        grad_tokens[:, None],
        got[0],
        got[1],
        d_in.T,
        owned[:3],
        got[2].reshape(freq_w1.shape),
        got[3],
        owned[3:],
        got[4].reshape(cond_w.shape),
        d_out,
        got[5],
        got[6],
        d_ff[0].T,
        d_ff[1].T,
        d_ff[2],
    )


VM = pl.BlockSpec(memory_space=pltpu.VMEM)
SM = pl.BlockSpec(memory_space=pltpu.SMEM)
HBM = pl.BlockSpec(memory_space=pl.ANY)
MIB = 1 << 20


def params(mib):
    return pltpu.CompilerParams(vmem_limit_bytes=mib * MIB)


def cost(micros):
    return pl.CostEstimate(
        flops=int(micros * 1000000000.0), bytes_accessed=int(micros * 3500000.0), transcendentals=0
    )


def shape(dims, dtype):
    return pltpu.VMEM(dims, dtype)


def far(dims, dtype):
    return pltpu.HBM(dims, dtype)


def in_hbm(*values):
    kept = tuple(pltpu.with_memory_space_constraint(value, pltpu.HBM) for value in values)
    return kept if len(kept) > 1 else kept[0]


def in_vmem(value):
    return pltpu.with_memory_space_constraint(value, pltpu.VMEM)


def sigmoid(value):
    return 1.0 / (1.0 + jnp.exp(-value))


def dma_all(pairs, sems, first=0):
    copies = [
        pltpu.make_async_copy(source, target, sems.at[first + i])
        for i, (source, target) in enumerate(pairs)
    ]
    for copy in copies:
        copy.start()
    return copies


def tie_kernel(*refs):
    pass


def tie(values, *after):
    count = len(values)
    return pl.pallas_call(
        tie_kernel,
        in_specs=[HBM] * (count + len(after)),
        out_specs=[HBM] * count,
        out_shape=[jax.ShapeDtypeStruct(value.shape, value.dtype) for value in values],
        input_output_aliases={i: i for i in range(count)},
        compiler_params=params(1),
        name="tie",
    )(*values, *after)


def one_hot_rows(me, rows, lanes, piece, fs):
    row = lax.broadcasted_iota(jnp.int32, (rows, lanes), 0)
    lane = lax.broadcasted_iota(jnp.int32, (rows, lanes), 1)
    block = jnp.zeros_like(row)
    for m in range(1, rows // piece):
        block = block + jnp.where(row >= m * piece, 1, 0)
    return jnp.where(lane == block * ((fs - 1) * piece) + me * piece + row, 1.0, 0.0)


def prepare_kernel(
    me_ref, w_in, freq_w2, conv_taps, freq_w1, freq_b1, feats, waves_far, w_far, x_far, cond_far, norms,
    w_mine, w2x, w2t, taps, base, waves, w_near, x_near, cond_near, w1_aug, sems, *, step, fs,
):
    loads = dma_all(
        [(waves_far, waves), (w_far, w_near), (x_far, x_near), (cond_far, cond_near)], sems
    )
    lanes = w_in.shape[1] // 4
    rows = lanes // fs
    sel = one_hot_rows(me_ref[0], rows, lanes, step, fs)
    low = sel.astype(BF16)
    hidden = freq_w2.shape[0]
    for i in range(4):
        out = slice(i * rows, (i + 1) * rows)
        group = slice(i * lanes, (i + 1) * lanes)
        w_mine[out, :] = mm_nt(low, w_in[:, group]).astype(BF16)
        both = jnp.concatenate([freq_w2[:, group], conv_taps[:, group]], axis=0)
        mine = lax.dot_general(
            sel, both, (((1,), (1,)), ((), ())), precision=HIGH, preferred_element_type=F32
        )
        taps[out, :3] = mine[:, hidden:]
        mine = mine[:, :hidden]
        high = mine.astype(BF16)
        rest = (mine - high.astype(F32)).astype(BF16)
        w2x[out, :] = jnp.concatenate([high, high, rest], axis=1)
    w2t[...] = jnp.transpose(w2x[...][:, :hidden].astype(F32)).astype(BF16)
    w1_aug[...] = jnp.zeros_like(w1_aug)
    count = freq_w1.shape[0]
    w1_aug[:count, :] = freq_w1[...]
    w1_aug[count : count + 1, :] = freq_b1[...]
    base[...] = lax.dot_general(
        w1_aug[...], feats[...], (((0,), (0,)), ((), ())), precision=HIGH, preferred_element_type=F32
    )
    for load in loads:
        load.wait()


def prepare(me, w_in, freq_w2, conv_taps, freq_w1, freq_b1, feats, waves, w_out, x, condt, norms, step, fs):
    channels, both = w_in.shape
    hidden = freq_w2.shape[0]
    length = feats.shape[1]
    return pl.pallas_call(
        functools.partial(prepare_kernel, step=step, fs=fs),
        in_specs=[SM] + [VM] * 6 + [HBM] * 5,
        out_specs=[VM] * 9,
        out_shape=[
            shape((both // fs, channels), BF16),
            shape((both // fs, 3 * hidden), BF16),
            shape((hidden, both // fs), BF16),
            shape((both // fs, 8), F32),
            shape((hidden, length), F32),
            shape((2 * length, length), BF16),
            shape(w_out.shape, BF16),
            shape(x.shape, BF16),
            shape(condt.shape, F32),
        ],
        scratch_shapes=[
            pltpu.VMEM((feats.shape[0], hidden), F32),
            pltpu.SemaphoreType.DMA((4,)),
        ],
        compiler_params=params(24),
        cost_estimate=cost(3),
        name="prepare",
    )(me, *in_hbm(w_in, freq_w2, conv_taps, freq_w1), freq_b1[None], in_hbm(feats), in_hbm(waves), *in_hbm(w_out, x, condt), norms)


def select_kernel(at_ref, after, gate, up, down, gate_out, up_out, down_out, *, fs):
    down_out[...] = down[0, 0]
    rows = gate_out.shape[0]
    sel = one_hot_rows(at_ref[0], rows, rows * fs, rows, fs).astype(BF16)
    gate_out[...] = mm_nt(sel, gate[...]).astype(BF16)
    up_out[...] = mm_nt(sel, up[...]).astype(BF16)


def select_columns(at, after, w_gate, w_up, w_down, bs, fs):
    channels, ff = w_gate.shape
    lanes = ff // bs
    wide = pl.BlockSpec((channels, lanes), lambda i, at: (0, (i // 2) * 4 + at[2] * 2 + i % 2))
    rows = pl.BlockSpec((lanes // fs, channels), lambda i, at: (i, 0))
    down = pl.BlockSpec(
        (1, 1, lanes // fs, channels),
        lambda i, at: ((i // 2) * 4 + at[2] * 2 + i % 2, at[0], 0, 0),
    )
    return pl.pallas_call(
        functools.partial(select_kernel, fs=fs),
        grid_spec=pltpu.PrefetchScalarGridSpec(
            num_scalar_prefetch=1,
            grid=(bs // 2,),
            in_specs=[HBM, wide, wide, down],
            out_specs=[rows, rows, rows],
        ),
        out_shape=[shape((ff // (2 * fs), channels), BF16)] * 3,
        compiler_params=params(20),
        cost_estimate=cost(5),
        name="select_columns",
    )(at, after, in_hbm(w_gate), in_hbm(w_up), in_hbm(w_down.reshape(bs, fs, lanes // fs, channels)))


def row_masks(ids):
    lane = lax.broadcasted_iota(jnp.int32, ids.shape, 1)
    length = ids.shape[1]
    prev = jnp.where((ids == pltpu.roll(ids, 1, 1)) & (lane > 0), 1.0, 0.0)
    nxt = jnp.where((ids == pltpu.roll(ids, length - 1, 1)) & (lane < length - 1), 1.0, 0.0)
    return prev, nxt


def bin_weights(start, width, length):
    lane = lax.broadcasted_iota(jnp.int32, (1, width), 1) + start
    return jnp.where(lane == 0, 0.5 / length, 1.0 / length)


def tile(index, size):
    return pl.ds(pl.multiple_of(index * size, size), size)


def hidden_tile(base, cb, j, lanes):
    pre = base[:, lanes] + cb[:, j : j + 1]
    return pre, sigmoid(pre)


def kernel_tile(w2x, hk):
    high = hk.astype(BF16)
    rest = (hk - high.astype(F32)).astype(BF16)
    return mm(w2x[...], jnp.concatenate([high, rest, high], axis=0))


def forward_kernel(
    me_ref, ids_at, x0, x1, x2, x3, ids_ref, norms, w, taps, base, w2x, condt, waves,
    z0, z1, z2, z3, u1, n1, p_out, q_out, c_out, vr_out, vs_out, mu_out, mn_out, cb_out,
    p, q, vm, ycat, acc,
):
    quarter = x0.shape[0]
    width, length = q_out.shape
    tiles = length // quarter
    me = me_ref[0]
    for k, x in enumerate((x0, x1, x2, x3)):
        values = x[...].astype(F32)
        unit, _ = normed(values)
        rows = tile(me ^ k, quarter)
        n1[rows, :] = unit.astype(BF16)
        u1[rows, :] = (unit * norms[0:1, :] + norms[1:2, :]).astype(BF16)
    ids = ids_ref[...]
    number = lax.broadcasted_iota(jnp.int32, (8, length), 0)
    member = jnp.where(ids == number, 1.0, 0.0)
    counts = jnp.maximum(jnp.sum(member, axis=1, keepdims=True), 1.0)
    member_low = member.astype(BF16)
    mu = mm(member_low, u1[...]) / counts
    mu_out[...] = mu
    mn_out[...] = mm(member_low, n1[...]) / counts
    cb_out[...] = lax.dot_general(
        condt[...], mu, (((1,), (1,)), ((), ())), precision=HIGH, preferred_element_type=F32
    )
    prev, nxt = row_masks(ids)
    for t in range(tiles):
        at = slice(t * quarter, (t + 1) * quarter)
        p[:, at] = mm_nt(w[...], u1[at, :])
    chunk = width // 2
    for r in range(4):
        at = slice(r * chunk, (r + 1) * chunk)
        here = p[at, :]
        p_out[at, :] = here.astype(BF16)
        mixed = (
            taps[at, 0:1] * (pltpu.roll(here, 1, 1) * prev)
            + taps[at, 1:2] * here
            + taps[at, 2:3] * (pltpu.roll(here, length - 1, 1) * nxt)
        )
        if r < 2:
            q[at, :] = mixed
            q_out[at, :] = mixed.astype(BF16)
        else:
            for j in range(SEGS):
                lo = j * width + (r - 2) * chunk
                vm[lo : lo + chunk, :] = (mixed * member[j : j + 1, :]).astype(BF16)

    span = 4 * quarter

    @pl.loop(0, length // span)
    def _(f):
        lanes = tile(f, span)
        upper = pl.ds(pl.multiple_of(f * span + length, span), span)
        weight = bin_weights(f * span, span, length)
        vr_all = mm(vm[...], waves[:length, lanes])
        vs_all = mm(vm[...], waves[length:, lanes])
        vr_out[:, lanes] = vr_all.astype(BF16)
        vs_out[:, lanes] = vs_all.astype(BF16)
        for j in range(SEGS):
            pre, gate = hidden_tile(base, cb_out, j, lanes)
            kk = kernel_tile(w2x, pre * gate)
            kr, ki = kk[:width] * weight, kk[width:] * weight
            at = slice(j * width, (j + 1) * width)
            vr, vs = vr_all[at], vs_all[at]
            ycat[at, lanes] = (kr * vr + ki * vs).astype(BF16)
            ycat[at, upper] = (kr * vs - ki * vr).astype(BF16)

    for k, z_out in enumerate((z0, z1, z2, z3)):
        t = me ^ k
        lanes = tile(t, quarter)
        acc[...] = jnp.zeros_like(acc)
        ids_here = ids_ref[:, lanes]
        for j in range(SEGS):

            @pl.when((ids_at[0, t * quarter] <= j) & (ids_at[0, (t + 1) * quarter - 1] >= j))
            def _():
                at = slice(j * width, (j + 1) * width)
                part = mm(ycat[at, :], waves[:, lanes])
                acc[...] += jnp.where(ids_here == j, part, 0.0)

        c = acc[...]
        c_out[:, lanes] = c.astype(BF16)
        z = (q[:, lanes] * c).astype(BF16)
        z_out[...] = z


def forward_spectral(me, x_parts, ids, norms, w, taps, base, w2x, condt, waves):
    quarter, channels = x_parts[0].shape
    length = ids.shape[1]
    width = w.shape[0] // 2
    saved = [
        (length, channels),
        (length, channels),
        (2 * width, length),
        (width, length),
        (width, length),
        (SEGS * width, length),
        (SEGS * width, length),
    ]
    small = [
        shape((8, channels), F32),
        shape((8, channels), F32),
        shape((condt.shape[0], 8), F32),
    ]
    return pl.pallas_call(
        forward_kernel,
        in_specs=[SM, SM] + [VM] * 12,
        out_specs=[VM] * (7 + len(saved)),
        out_shape=[shape((width, quarter), BF16)] * 4 + [shape(dims, BF16) for dims in saved] + small,
        scratch_shapes=[
            pltpu.VMEM((2 * width, length), F32),
            pltpu.VMEM((width, length), F32),
            pltpu.VMEM((SEGS * width, length), BF16),
            pltpu.VMEM((SEGS * width, 2 * length), BF16),
            pltpu.VMEM((width, quarter), F32),
        ],
        compiler_params=params(26),
        cost_estimate=cost(15),
        name="forward_spectral",
    )(me, ids, *x_parts, ids, norms, w, taps, base, w2x, condt, waves)


def backward_kernel(
    me_ref, ids_at, g0, g1, g2, g3, ids_ref, cb, taps, base, w2x, w2, feats,
    p, q, c, vr_in, vs_in, waves, after,
    o0, o1, o2, o3, gp_row, d_taps, d_w2, d_w1, gcb,
    gcm, gvcat, gs, acc,
):
    width, quarter = g0.shape
    length = gp_row.shape[1]
    tiles = length // quarter
    hidden = base.shape[0]
    me = me_ref[0]
    for k, g in enumerate((g0, g1, g2, g3)):
        lanes = tile(me ^ k, quarter)
        gz = g[...].astype(F32)
        gs[:width, lanes] = gz * c[:, lanes].astype(F32)
        gc = gz * q[:, lanes].astype(F32)
        ids_here = ids_ref[:, lanes]
        for j in range(SEGS):
            gcm[j * width : (j + 1) * width, lanes] = jnp.where(ids_here == j, gc, 0.0).astype(BF16)
    d_w2[...] = jnp.zeros_like(d_w2)
    d_w1[...] = jnp.zeros_like(d_w1)
    gcb[...] = jnp.zeros_like(gcb)

    span = 2 * quarter

    @pl.loop(0, length // span)
    def _(f):
        lanes = tile(f, span)
        upper = pl.ds(pl.multiple_of(f * span + length, span), span)
        weight = bin_weights(f * span, span, length)
        gyr_all = mm(gcm[...], waves[:length, lanes]) * weight
        gys_all = mm(gcm[...], waves[length:, lanes]) * weight
        for j in range(SEGS):
            pre, gate = hidden_tile(base, cb, j, lanes)
            hk = pre * gate
            kk = kernel_tile(w2x, hk)
            kr, ki = kk[:width], kk[width:]
            at = slice(j * width, (j + 1) * width)
            gyr, gys = gyr_all[at], gys_all[at]
            vr, vs = vr_in[at, lanes].astype(F32), vs_in[at, lanes].astype(F32)
            gvcat[at, lanes] = (kr * gyr - ki * gys).astype(BF16)
            gvcat[at, upper] = (kr * gys + ki * gyr).astype(BF16)
            gkk = jnp.concatenate(
                [(gyr * vr + gys * vs).astype(BF16), (gyr * vs - gys * vr).astype(BF16)], axis=0
            )
            d_w2[...] += mm_nt(gkk, hk.astype(BF16))
            gpre = mm(w2[...], gkk) * (gate * (1.0 + pre * (1.0 - gate)))
            gcb[:, j : j + 1] += jnp.sum(gpre, axis=1, keepdims=True)
            d_w1[...] += mm_nt(feats[:, lanes], gpre.astype(BF16))

    for k in range(4):
        t = me ^ k
        lanes = tile(t, quarter)
        acc[...] = jnp.zeros_like(acc)
        ids_here = ids_ref[:, lanes]
        for j in range(SEGS):

            @pl.when((ids_at[0, t * quarter] <= j) & (ids_at[0, (t + 1) * quarter - 1] >= j))
            def _():
                at = slice(j * width, (j + 1) * width)
                part = mm(gvcat[at, :], waves[:, lanes])
                acc[...] += jnp.where(ids_here == j, part, 0.0)

        gs[width:, lanes] = acc[...]
    prev, nxt = row_masks(ids_ref[...])
    chunk = width // 2
    for r in range(4):
        at = slice(r * chunk, (r + 1) * chunk)
        here = p[at, :].astype(F32)
        grad = gs[at, :]
        d_taps[at, 0:1] = jnp.sum(grad * (pltpu.roll(here, 1, 1) * prev), axis=1, keepdims=True)
        d_taps[at, 1:2] = jnp.sum(grad * here, axis=1, keepdims=True)
        d_taps[at, 2:3] = jnp.sum(
            grad * (pltpu.roll(here, length - 1, 1) * nxt), axis=1, keepdims=True
        )
        gp_row[at, :] = (
            taps[at, 1:2] * grad
            + taps[at, 0:1] * pltpu.roll(grad * prev, length - 1, 1)
            + taps[at, 2:3] * pltpu.roll(grad * nxt, 1, 1)
        ).astype(BF16)
    share = jnp.transpose(gcb[...])[:8, :]
    high = share.astype(BF16)
    rest = (share - high.astype(F32)).astype(BF16)
    extra = jnp.concatenate([high, rest], axis=0)
    extra = jnp.concatenate([extra, jnp.zeros((16, quarter - hidden), BF16)], axis=1)
    for k, out in enumerate((o0, o1, o2, o3)):
        out[: 2 * width, :] = gp_row[:, tile(me ^ k, quarter)]
        out[2 * width :, :] = extra


def backward_spectral(
    me, gz_parts, ids, cb, taps, base, w2x, w2, feats, p, q, c, vr, vs, waves, after
):
    width, quarter = gz_parts[0].shape
    length = ids.shape[1]
    hidden = base.shape[0]
    outs = [shape((2 * width + 16, quarter), BF16)] * 4 + [
        shape((2 * width, length), BF16),
        shape((2 * width, 128), F32),
        shape((2 * width, hidden), F32),
        shape((feats.shape[0], hidden), F32),
        shape((hidden, 128), F32),
    ]
    return pl.pallas_call(
        backward_kernel,
        in_specs=[SM, SM] + [VM] * 17 + [HBM],
        out_specs=[VM] * 9,
        out_shape=outs,
        scratch_shapes=[
            pltpu.VMEM((SEGS * width, length), BF16),
            pltpu.VMEM((SEGS * width, 2 * length), BF16),
            pltpu.VMEM((2 * width, length), F32),
            pltpu.VMEM((width, quarter), F32),
        ],
        compiler_params=params(26),
        cost_estimate=cost(17),
        name="backward_spectral",
    )(
        me, ids, *gz_parts, ids, cb, taps, base, w2x, w2, feats, p, q, c, vr, vs, waves, after
    )


def middle_kernel(me_ref, z0, z1, z2, z3, x, w_out, norms, after, h_out, u2_out, z_t, *, piece):
    me = me_ref[0]
    width = z0.shape[0]
    for k, z in enumerate((z0, z1, z2, z3)):
        for i in range(width // piece):
            at = pl.ds(pl.multiple_of((i * 4 + (me ^ k)) * piece, piece), piece)
            z_t[at, :] = z[i * piece : (i + 1) * piece, :]
    h = x[...].astype(F32) + mm(jnp.transpose(z_t[...]), w_out[...])
    h_out[...] = h
    unit, _ = normed(h)
    u2_out[...] = (unit * norms[2:3, :] + norms[3:4, :]).astype(BF16)


def middle(me, z_parts, x, w_out, norms, after, piece):
    quarter, channels = x.shape
    return pl.pallas_call(
        functools.partial(middle_kernel, piece=piece),
        in_specs=[SM] + [VM] * 7 + [HBM],
        out_specs=[VM] * 3,
        out_shape=[
            shape((quarter, channels), F32),
            shape((quarter, channels), BF16),
            shape((channels, quarter), BF16),
        ],
        compiler_params=params(24),
        cost_estimate=cost(2),
        name="middle",
    )(me, *z_parts, x, w_out, norms, after)


def feed_kernel(
    me_ref, u2, h, ct, norms, w_out, gate, up, down,
    mixed, big_g, g0, g1, g2, g3, t_own, t_other, sums, acc_out, acc_grad, gz_t, gb_t, *, piece, thin,
):
    i = pl.program_id(0)

    @pl.when(i == 0)
    def _():
        acc_out[...] = jnp.zeros_like(acc_out)
        acc_grad[...] = jnp.zeros_like(acc_grad)

    g = mm(u2[...], gate[...])
    a = mm(u2[...], up[...])
    gh = mm_nt(ct[...], down[...])
    sg = sigmoid(g)
    silu = g * sg
    hid = (silu * a).astype(BF16)
    gg = (gh * a * (sg * (1.0 + g * (1.0 - sg)))).astype(BF16)
    ga = (gh * silu).astype(BF16)
    acc_out[...] += mm(hid, down[...])
    acc_grad[...] += mm_nt(gg, gate[...]) + mm_nt(ga, up[...])

    @pl.when(i == pl.num_programs(0) - 1)
    def _():
        me = me_ref[0]
        width = g0.shape[0]
        here = h[...]
        mixed[...] = (here + acc_out[...]).astype(BF16)
        gu2 = acc_grad[...]
        unit, scale = normed(here)
        sums[0:1, :] = jnp.sum(gu2 * unit, axis=0, keepdims=True)
        sums[1:2, :] = jnp.sum(gu2, axis=0, keepdims=True)
        total = ct[...].astype(F32) + norm_back(unit, scale, gu2 * norms[2:3, :])
        big_g[...] = total
        low = total.astype(BF16)
        gz_t[...] = mm_nt(w_out[...], low).astype(BF16)
        for k, out in enumerate((g0, g1, g2, g3)):
            for r in range(width // piece):
                at = pl.ds(pl.multiple_of((r * 4 + (me ^ k)) * piece, piece), piece)
                out[r * piece : (r + 1) * piece, :] = gz_t[at, :]
        gb_t[...] = jnp.transpose(total)
        for core, out in ((me & 1, t_own), (1 - (me & 1), t_other)):
            parts = []
            for x in range(2):
                for r in range(width // thin):
                    lo = pl.multiple_of((r * 4 + 2 * x + core) * thin, thin)
                    parts.append(gb_t[pl.ds(lo, thin), :])
            out[...] = jnp.concatenate(parts, axis=0).astype(BF16)


def feed_forward(me, u2, h, ct, norms, w_out, w_gate, w_up, w_down, piece, thin):
    quarter, channels = u2.shape
    ff = w_gate.shape[1]
    block = 512

    width = channels // 4
    outs = [
        ((quarter, channels), BF16),
        ((quarter, channels), F32),
    ] + [((width, quarter), BF16)] * 4 + [((2 * width, quarter), BF16)] * 2 + [((8, channels), F32)]
    return pl.pallas_call(
        functools.partial(feed_kernel, piece=piece, thin=thin),
        grid=(ff // block,),
        in_specs=[
            SM,
            VM,
            VM,
            VM,
            VM,
            VM,
            pl.BlockSpec((channels, block), lambda i: (0, i)),
            pl.BlockSpec((channels, block), lambda i: (0, i)),
            pl.BlockSpec((block, channels), lambda i: (i, 0)),
        ],
        out_specs=[VM] * len(outs),
        out_shape=[far(*outs[0])] + [shape(*out) for out in outs[1:]],
        scratch_shapes=[
            pltpu.VMEM((quarter, channels), F32),
            pltpu.VMEM((quarter, channels), F32),
            pltpu.VMEM((channels, quarter), BF16),
            pltpu.VMEM((channels, quarter), F32),
        ],
        compiler_params=params(28),
        cost_estimate=cost(13),
        name="feed_forward",
    )(me, u2, h, ct, norms, w_out, in_hbm(w_gate), in_hbm(w_up), in_hbm(w_down))


def hidden_grads_kernel(at_ref, *refs):
    u_parts, c_parts, refs = refs[:8], refs[8:16], refs[16:]
    gate, up, gt_own, gt_got, z_own, z_got, down, after, *refs = refs
    keep_a, give_a, keep_b, give_b, keep_o, give_o, rights, lefts, d_all, d_out = refs
    quarter, channels = u_parts[0].shape
    y, z = at_ref[1], at_ref[3]
    rows = gate.shape[0]
    for k in range(8):
        at = slice(k * quarter, (k + 1) * quarter)
        rights[0, at, :] = u_parts[k][...]
        rights[1, at, :] = c_parts[k][...]
    span = 2 * quarter

    @pl.loop(0, 4)
    def _(k):
        at = tile(k, span)
        g = mm_nt(gate[...], rights[0, at, :])
        a = mm_nt(up[...], rights[0, at, :])
        gh = mm_nt(down[...], rights[1, at, :])
        sg = sigmoid(g)
        silu = g * sg
        lefts[0, :, at] = (gh * a * (sg * (1.0 + g * (1.0 - sg)))).astype(BF16)
        lefts[1, :, at] = (gh * silu).astype(BF16)
        lefts[2, :, at] = (silu * a).astype(BF16)

    d_out[...] = mm_nt(gt_own[...], z_own[...]) + mm_nt(gt_got[...], z_got[...])
    half = keep_o.shape[0]
    x = at_ref[0] >> 1
    keep_o[...] = d_out[tile(x, half), :].astype(BF16)
    give_o[...] = d_out[tile(1 - x, half), :].astype(BF16)
    fw = rows // 4
    cut = keep_a.shape[-1]

    @pl.loop(0, 3)
    def _(m):
        grad = mm(lefts[m], rights[m >> 1]).astype(BF16)
        for i in range(4):
            d_all[i, m] = grad[i * fw : (i + 1) * fw]

    for i in range(2):
        keep_a[i] = d_all[2 * i + y, :, :, :cut]
        give_a[i] = d_all[2 * i + 1 - y, :, :, :cut]
        keep_b[i] = d_all[2 * z + i, :, :, cut:]
        give_b[i] = d_all[2 * (1 - z) + i, :, :, cut:]


def hidden_grads(at, u2_parts, ct_parts, gate, up, gt_own, gt_got, z_own, z_got, down, after):
    quarter, channels = u2_parts[0].shape
    wide = gate.shape[0]
    fw = wide // 4
    fs = 4
    cut = 2 * channels // 3
    return pl.pallas_call(
        hidden_grads_kernel,
        grid_spec=pltpu.PrefetchScalarGridSpec(
            num_scalar_prefetch=1,
            grid=(1,),
            in_specs=[VM] * 23 + [HBM],
            out_specs=[VM] * 6,
            scratch_shapes=[
                pltpu.VMEM((2, 8 * quarter, channels), BF16),
                pltpu.VMEM((3, wide, 8 * quarter), BF16),
                pltpu.VMEM((4, 3, fw, channels), BF16),
                pltpu.VMEM((2 * channels // fs, channels), F32),
            ],
        ),
        out_shape=[shape((2, 3, fw, cut), BF16)] * 2
        + [shape((2, 3, fw, channels - cut), BF16)] * 2
        + [shape((channels // fs, channels), BF16)] * 2,
        compiler_params=params(34),
        cost_estimate=cost(14),
        name="hidden_grads",
    )(at, *u2_parts, *ct_parts, gate, up, gt_own, gt_got, z_own, z_got, down, after)


def halve_kernel(at_ref, after, *refs, bits):
    pairs = len(bits)
    ins, outs = refs[: 2 * pairs], refs[2 * pairs :]
    for n in range(pairs):
        mine = at_ref[bits[n] + 1]
        keep, got = ins[2 * n], ins[2 * n + 1]
        next_keep, next_give = outs[2 * n], outs[2 * n + 1]
        for i in range(keep.shape[0]):
            for side, out in ((mine, next_keep), (1 - mine, next_give)):
                out[i] = (keep[i, side].astype(F32) + got[i, side].astype(F32)).astype(BF16)


def halve(at, bits, after, *sums):
    outs = []
    for n in range(len(bits)):
        dims = sums[2 * n].shape
        outs += [shape((dims[0],) + dims[2:], BF16)] * 2
    return pl.pallas_call(
        functools.partial(halve_kernel, bits=bits),
        in_specs=[SM, HBM] + [VM] * len(sums),
        out_specs=[VM] * len(outs),
        out_shape=outs,
        compiler_params=params(24),
        cost_estimate=cost(0.3),
        name="halve",
    )(at, after, *sums)


def load_riders(blocks, first, rows):
    parts = []
    for i in range(blocks.shape[0]):
        for m in range(blocks.shape[2] // 128):
            parts.append(blocks[i, first : first + rows, m * 128 : (m + 1) * 128].astype(F32))
    return jnp.concatenate(parts, axis=0)


def store_riders(block, packed, i, first, rows):
    columns = block.shape[1] // 128
    for m in range(columns):
        lo = (columns * i + m) * rows
        block[first : first + rows, m * 128 : (m + 1) * 128] = packed[lo : lo + rows, :]


def stage_kernel(
    at_ref, after, keep_a, got_a, keep_b, got_b, ours,
    next_keep_a, next_give_a, next_keep_b, next_give_b, total, joined, block,
):
    y, z = at_ref[1], at_ref[2]
    tall, rows = keep_a.shape[2], next_give_a.shape[1]
    flat = got_a.shape[2]
    columns = got_a.shape[3] // 128
    riders = joined.shape[0] // (4 * columns)
    start = flat - riders
    for i in range(2):
        for k in range(2):
            for m in range(columns):
                lo = (columns * (2 * i + k) + m) * riders
                piece = got_a[i, k, start:flat, m * 128 : (m + 1) * 128]
                joined[lo : lo + riders, :] = ours[lo : lo + riders, :].astype(F32) + piece.astype(F32)
    total[...] = joined[...].astype(BF16)
    for i in range(2):
        next_keep_a[i] = (keep_a[i, z].astype(F32) + got_a[i, z, :tall].astype(F32)).astype(BF16)
        block[...] = jnp.zeros_like(block)
        block[:tall, :] = keep_a[i, 1 - z].astype(F32) + got_a[i, 1 - z, :tall].astype(F32)
        store_riders(block, joined, i, rows - 2 * riders, 2 * riders)
        next_give_a[i] = block[...].astype(BF16)
        for side, out in ((y, next_keep_b), (1 - y, next_give_b)):
            out[i] = (keep_b[i, side].astype(F32) + got_b[i, side].astype(F32)).astype(BF16)


def stage(at, after, keep_a, got_a, keep_b, got_b, ours):
    _, _, tall, lanes = keep_a.shape
    narrow = keep_b.shape[-1]
    riders = ours.shape[0] // (4 * (lanes // 128))
    rows = got_a.shape[2] + riders
    return pl.pallas_call(
        stage_kernel,
        in_specs=[SM, HBM] + [VM] * 5,
        out_specs=[VM] * 5,
        out_shape=[
            shape((2, tall, lanes), BF16),
            shape((2, rows, lanes), BF16),
            shape((2, tall, narrow), BF16),
            shape((2, tall, narrow), BF16),
            shape(ours.shape, BF16),
        ],
        scratch_shapes=[pltpu.VMEM(ours.shape, F32), pltpu.VMEM((rows, lanes), F32)],
        compiler_params=params(12),
        cost_estimate=cost(0.3),
        name="stage",
    )(at, after, keep_a, got_a, keep_b, got_b, ours)


def join_kernel(at_ref, after, keep_a, got_a, keep_b, got_b, ours, keep, give, total):
    tall, cut = keep_a.shape[1:]
    riders = ours.shape[0] // (2 * (cut // 128))
    start = got_a.shape[1] - riders
    total[...] = (ours[...].astype(F32) + load_riders(got_a, start, riders)).astype(BF16)
    for side, out in ((at_ref[3], keep), (1 - at_ref[3], give)):
        out[:, :cut] = (keep_a[side].astype(F32) + got_a[side, :tall].astype(F32)).astype(BF16)
        out[:, cut:] = (keep_b[side].astype(F32) + got_b[side].astype(F32)).astype(BF16)


def join(at, after, keep_a, got_a, keep_b, got_b, ours):
    _, rows, cut = keep_a.shape
    return pl.pallas_call(
        join_kernel,
        in_specs=[SM, HBM] + [VM] * 5,
        out_specs=[VM] * 3,
        out_shape=[shape((rows, cut + keep_b.shape[-1]), BF16)] * 2 + [shape(ours.shape, BF16)],
        compiler_params=params(12),
        cost_estimate=cost(0.3),
        name="join",
    )(at, after, keep_a, got_a, keep_b, got_b, ours)


def hidden_last_kernel(keep_a, got_a, keep_b, got_b, after, *outs):
    *outs, token = outs
    token[...] = jnp.zeros_like(token)
    cut = keep_a.shape[-1]
    for m, out in enumerate(outs):
        out[:, :cut] = keep_a[0, m].astype(F32) + got_a[0, m].astype(F32)
        out[:, cut:] = keep_b[0, m].astype(F32) + got_b[0, m].astype(F32)


def hidden_last(keep_a, got_a, keep_b, got_b, after):
    _, count, rows, cut = keep_a.shape
    return pl.pallas_call(
        hidden_last_kernel,
        in_specs=[VM] * 4 + [HBM],
        out_specs=[VM] * (count + 1),
        out_shape=[far((rows, cut + keep_b.shape[-1]), F32)] * count + [shape((8, 128), F32)],
        compiler_params=params(12),
        cost_estimate=cost(0.3),
        name="hidden_last",
    )(keep_a, got_a, keep_b, got_b, after)


def add_kernel(ours, theirs, after, out):
    out[...] = (ours[...].astype(F32) + theirs[...].astype(F32)).astype(out.dtype)


def add(ours, theirs, after, dtype):
    return pl.pallas_call(
        add_kernel,
        in_specs=[VM, VM, HBM],
        out_specs=VM,
        out_shape=shape(ours.shape, dtype),
        compiler_params=params(8),
        cost_estimate=cost(0.3),
        name="add",
    )(ours, theirs, after)


def projection_kernel(
    at_ref, gp, u1, n1, w_mine, keep_o, got_o, d_w2, d_w1, d_taps, gcb, condt, mu, mn,
    sums2, after, keep_a, give_a, keep_b, give_b, packed_out, d_in, d_out, packed, sheet, *, layout,
):
    me, y, zbit = at_ref[0], at_ref[1], at_ref[2]
    channels = u1.shape[1]
    width = keep_o.shape[0]
    d_in[...] = mm(gp[...], u1[...])
    d_out[...] = keep_o[...].astype(F32) + got_o[...].astype(F32)
    blocks = 2 * keep_a.shape[0]
    first = 2 * width // blocks
    second = width // blocks
    cut = channels // 2

    def put(out, block, lanes):
        lo = pl.multiple_of(block * first, first)
        out[:first, :] = d_in[pl.ds(lo, first), lanes].astype(BF16)
        lo = pl.multiple_of(block * second, second)
        out[first:, :] = d_out[pl.ds(lo, second), lanes].astype(BF16)

    for b in range(blocks // 2):
        put(keep_a.at[b], 2 * b + y, slice(0, cut))
    for b in range(blocks // 4):
        for i in range(2):
            put(keep_b.at[b, i], 4 * b + 2 * zbit + i, slice(cut, channels))
            put(give_b.at[b, i], 4 * b + 2 * (1 - zbit) + i, slice(cut, channels))
    packed[...] = jnp.zeros_like(packed)
    packed[:width, :] = jnp.concatenate([d_w2[:width, :], d_w2[width:, :]], axis=1)
    taps_t = jnp.transpose(d_taps[...])
    gcb_t = jnp.transpose(gcb[...])[:8, :]
    gmu = lax.dot_general(
        gcb_t, condt[...], (((1,), (0,)), ((), ())), precision=HIGH, preferred_element_type=F32
    )
    gp_n = mm(gp[...], n1[...])
    w32 = w_mine[...].astype(F32)
    gain = jnp.sum(gp_n * w32, axis=0, keepdims=True) + jnp.sum(gmu * mn[...], axis=0, keepdims=True)
    total = jnp.sum(gp[...].astype(F32), axis=1, keepdims=True)
    shift = jnp.sum(total * w32, axis=0, keepdims=True) + jnp.sum(gmu, axis=0, keepdims=True)
    for i in range(3):
        for m in range(2 * width // 128):
            at = layout["taps"] + i * (2 * width // 128) + m
            packed[at : at + 1, :] = taps_t[i : i + 1, m * 128 : (m + 1) * 128]
    for i, row in enumerate((gain, shift, sums2[0:1, :], sums2[1:2, :])):
        for m in range(channels // 128):
            at = layout["ln"] + i * (channels // 128) + m
            packed[at : at + 1, :] = row[:, m * 128 : (m + 1) * 128]
    half = d_w1.shape[0] // 2
    packed[layout["w1"] : layout["w1"] + half, :] = jnp.concatenate(
        [d_w1[:half, :], d_w1[half:, :]], axis=1
    )
    zeros = jnp.zeros_like(gcb_t)
    row = at_ref[4]
    odd = (row & 1) == 1
    both = jnp.concatenate([jnp.where(odd, zeros, gcb_t), jnp.where(odd, gcb_t, zeros)], axis=1)
    packed[pl.ds(pl.multiple_of(layout["cb"] + 8 * (row >> 1), 8), 8), :] = both
    share = jnp.zeros((8, width), F32)
    for f in range(channels // width):
        share = share + jnp.where(me == f, mu[:, f * width : (f + 1) * width], 0.0)
    rest = jnp.concatenate([share[:SEGS, 128:], jnp.zeros((SEGS, 256 - width), F32)], axis=1)
    block = jnp.concatenate([share[:SEGS, :128], rest, jnp.zeros((8 - 2 * SEGS, 128), F32)], axis=0)
    packed[pl.ds(pl.multiple_of(layout["mu"] + 8 * row, 8), 8), :] = block
    packed_out[...] = packed[...].astype(BF16)
    riders = packed.shape[0] // (4 * (cut // 128))
    for b in range(blocks // 2):
        sheet[...] = jnp.zeros_like(sheet)
        lo = pl.multiple_of((2 * b + 1 - y) * first, first)
        sheet[:first, :] = d_in[pl.ds(lo, first), :cut]
        lo = pl.multiple_of((2 * b + 1 - y) * second, second)
        sheet[first : first + second, :] = d_out[pl.ds(lo, second), :cut]
        store_riders(sheet, packed, b, sheet.shape[0] - riders, riders)
        give_a[b] = sheet[...].astype(BF16)


def packed_layout(width, channels, bs):
    taps = width
    ln = taps + 3 * (2 * width // 128)
    w1 = -(-(ln + 4 * (channels // 128)) // 8) * 8
    cb = w1 + 32
    mu = cb + 4 * bs
    return {"taps": taps, "ln": ln, "w1": w1, "cb": cb, "mu": mu, "rows": -(-(mu + 8 * bs) // 128) * 128}


def projection_grads(
    at, gp, u1, n1, w_mine, keep_o, got_o, d_w2, d_w1, d_taps, gcb, condt, mu, mn, sums2, after, bs
):
    length, channels = u1.shape
    width = keep_o.shape[0]
    layout = packed_layout(width, channels, bs)
    tall = 3 * width // bs
    flat = -(-tall // 16) * 16 + layout["rows"] // (4 * (channels // 256))
    return pl.pallas_call(
        functools.partial(projection_kernel, layout=layout),
        in_specs=[SM] + [VM] * 14 + [HBM],
        out_specs=[VM] * 5,
        out_shape=[
            shape((bs // 2, tall, channels // 2), BF16),
            shape((bs // 2, flat, channels // 2), BF16),
        ]
        + [shape((bs // 4, 2, 3 * width // bs, channels // 2), BF16)] * 2
        + [shape((layout["rows"], 128), BF16)],
        scratch_shapes=[
            pltpu.VMEM((2 * width, channels), F32),
            pltpu.VMEM((width, channels), F32),
            pltpu.VMEM((layout["rows"], 128), F32),
            pltpu.VMEM((flat, channels // 2), F32),
        ],
        compiler_params=params(24),
        cost_estimate=cost(2),
        name="projection_grads",
    )(
        at, gp, u1, n1, w_mine, keep_o, got_o, d_w2, d_w1, d_taps, gcb, condt, mu, mn, sums2, after
    )


def final_kernel(
    me_ref, p0, p1, p2, p3, x, big_g, norms, ids_row, condt, w_in, after, out, gp_t, *, piece
):
    me = me_ref[0]
    rows = gp_t.shape[0] // 4
    hidden = condt.shape[0]
    share = jnp.zeros((8, hidden), F32)
    for k, part in enumerate((p0, p1, p2, p3)):
        for i in range(rows // piece):
            at = pl.ds(pl.multiple_of((i * 4 + (me ^ k)) * piece, piece), piece)
            gp_t[at, :] = part[i * piece : (i + 1) * piece, :]
        extra = part[rows:, :hidden].astype(F32)
        share = share + extra[:8] + extra[8:]
    ids = ids_row[...]
    number = lax.broadcasted_iota(jnp.int32, (8, ids.shape[1]), 0)
    counts = jnp.sum(jnp.where(ids == number, 1.0, 0.0), axis=1, keepdims=True)
    gmu = lax.dot_general(
        share, condt[...], (((1,), (0,)), ((), ())), precision=HIGH, preferred_element_type=F32
    ) / jnp.maximum(counts, 1.0)
    gu1 = mm_nt(jnp.transpose(gp_t[...]), w_in[...])
    quarter = x.shape[0]
    own = jnp.broadcast_to(ids_row[:, tile(me, quarter)].astype(F32), (8, quarter))
    ids_own = jnp.transpose(own)[:, 0:1]
    for j in range(SEGS):
        gu1 = gu1 + jnp.where(ids_own == j, gmu[j : j + 1, :], 0.0)
    unit, scale = normed(x[...].astype(F32))
    out[...] = big_g[...] + norm_back(unit, scale, gu1 * norms[0:1, :])


def final(me, gp_parts, x, big_g, norms, ids, condt, w_in, after, piece):
    quarter, channels = x.shape
    return pl.pallas_call(
        functools.partial(final_kernel, piece=piece),
        in_specs=[SM] + [VM] * 10 + [HBM],
        out_specs=VM,
        out_shape=shape((quarter, channels), F32),
        scratch_shapes=[pltpu.VMEM((2 * channels, quarter), BF16)],
        compiler_params=params(24),
        cost_estimate=cost(0.3),
        name="final",
    )(me, *gp_parts, x, big_g, norms, ids, condt, in_hbm(w_in), after)


def small_kernel(
    me_ref, j0, j1, j2, j3, w2, taps, ln0, ln1, ln2, ln3, w1, b1, cond, wide, tap_t, cond_t, *, layout, step, width
):
    me = me_ref[0]
    parts = [part[...].astype(F32) for part in (j0, j1, j2, j3)]
    hidden = w1.shape[0]
    half = width // step
    count = 2 * width // 128
    for k, part in enumerate(parts):
        who = me ^ k
        rows = jnp.concatenate(
            [
                jnp.concatenate([part[layout["taps"] + i * count + m : layout["taps"] + i * count + m + 1, :]
                                 for m in range(count)], axis=1)
                for i in range(3)
            ]
            + [jnp.zeros((125, 2 * width), F32)],
            axis=0,
        )
        tap_t[...] = jnp.transpose(rows)
        for side in range(2):
            for i in range(half):
                at = pl.ds(pl.multiple_of((side * half * 4 + i * 4 + who) * step, step), step)
                lo = i * step
                wide[at, :hidden] = part[lo : lo + step, side * hidden : (side + 1) * hidden]
                at2 = side * width + lo
                wide[at, hidden:] = tap_t[at2 : at2 + step, :hidden]
    whole = jnp.transpose(wide[...])
    w2[...] = whole[:hidden, :]
    taps[...] = whole[hidden : hidden + 3, :]

    def common(first, last):
        a, b, c, d = [part[first:last, :] for part in parts]
        return (a + b) + (c + d)

    lanes = ln0.shape[0] // 128
    sums = common(layout["ln"], layout["ln"] + 4 * lanes)
    for i, out in enumerate((ln0, ln1, ln2, ln3)):
        row = jnp.concatenate([sums[i * lanes + m : i * lanes + m + 1, :] for m in range(lanes)], axis=1)
        out[...] = row.reshape(out.shape)
    both = common(layout["w1"], layout["w1"] + hidden // 2)
    w1[: hidden // 2, :] = both[:, :hidden]
    w1[hidden // 2 :, :] = both[:, hidden:]
    cb = common(layout["cb"], layout["mu"])
    shares = []
    for b in range(cb.shape[0] // 4):
        lo = 8 * (b // 2)
        shares.append(cb[lo : lo + 8, (b % 2) * hidden : (b % 2 + 1) * hidden])
    shares = jnp.concatenate(shares, axis=0)
    b1[...] = jnp.sum(shares, axis=0, keepdims=True)
    for k, part in enumerate(parts):
        rows = []
        for b in range(cb.shape[0] // 4):
            lo = layout["mu"] + 8 * b
            block = part[lo : lo + 8, :]
            rows.append(
                jnp.concatenate(
                    [
                        jnp.concatenate([block[:SEGS, :], jnp.zeros((8 - SEGS, 128), F32)], axis=0),
                        jnp.concatenate(
                            [block[SEGS : 2 * SEGS, : width - 128], jnp.zeros((8 - SEGS, width - 128), F32)],
                            axis=0,
                        ),
                    ],
                    axis=1,
                )
            )
        mu = jnp.concatenate(rows, axis=0)
        cond_t[tile(me ^ k, width), :] = lax.dot_general(
            jnp.transpose(mu), shares, (((1,), (0,)), ((), ())), precision=HIGH, preferred_element_type=F32
        )
    cond[...] = jnp.transpose(cond_t[...])


def small_grads(me, parts, hidden, channels, step, bs):
    width = channels // 4
    layout = packed_layout(width, channels, bs)
    return pl.pallas_call(
        functools.partial(small_kernel, layout=layout, step=step, width=width),
        in_specs=[SM] + [VM] * 4,
        out_specs=[VM] * 9,
        out_shape=[
            far((hidden, 2 * channels), F32),
            far((3, 2 * channels), F32),
            far((channels,), F32),
            far((channels,), F32),
            far((channels,), F32),
            far((channels,), F32),
            far((hidden, hidden), F32),
            far((1, hidden), F32),
            far((hidden, channels), F32),
        ],
        scratch_shapes=[
            pltpu.VMEM((2 * channels, 2 * hidden), F32),
            pltpu.VMEM((2 * width, 128), F32),
            pltpu.VMEM((channels, hidden), F32),
        ],
        compiler_params=params(24),
        cost_estimate=cost(3),
        name="small_grads",
    )(me, *parts)


def trade_parts(parts):
    two, three, one = [swap(parts[k], "freq", k) for k in (2, 3, 1)]
    return (parts[0], one, two, three)


def tiled_device(
    tokens,
    seg_ids,
    cotangent,
    ln1_gain,
    ln1_shift,
    w_in,
    conv_taps,
    freq_w1,
    freq_b1,
    freq_w2,
    cond_w,
    w_out,
    ln2_gain,
    ln2_shift,
    w_gate,
    w_up,
    w_down,
):
    quarter, _, channels = tokens.shape
    length = seg_ids.shape[1]
    ff = w_gate.shape[1]
    fs = lax.axis_size("freq")
    bs = lax.axis_size("batch")
    me = lax.axis_index("freq")
    row = lax.axis_index("batch")
    width = channels // fs
    half = bs // 2
    step = channels // (half * fs)
    fw = ff // (bs * fs)
    table = np.concatenate(tables(length), axis=0)
    feats = features(length, freq_w1.shape[0] // 2)
    feats_aug = np.concatenate(
        [feats, np.ones((1, length), np.float32), np.zeros((7, length), np.float32)], axis=0
    )

    x_own = tokens[:, 0]
    ct_own = cotangent[:, 0]
    ids = seg_ids
    at = jnp.stack([me, row & 1, (row >> 1) & 1, (row >> 2) & 1, row]).astype(jnp.int32)
    norms = jnp.concatenate([ln1_gain, ln1_shift, ln2_gain, ln2_shift]).reshape(4, channels)
    condt = cond_w.T

    def gather_after(value, after):
        two = swap(value, "freq", 2)
        one = swap(value, "freq", 1)
        (two,) = tie([two], after)
        return (value, one, two, swap(two, "freq", 1))

    def gather_wide(value, *after):
        count = bs * fs
        parts = (
            value,
            swap(value, "freq", 2),
            swap(value, "batch", 2),
            lax.ppermute(value, ("batch", "freq"), [(i, i ^ (2 * fs + 2)) for i in range(count)]),
        )
        parts = parts[:1] + tuple(tie(parts[1:], *after))
        return parts + tuple(swap(part, "freq", 1) for part in parts)

    def pairs(value):
        return value.reshape((value.shape[0] // 2, 2) + value.shape[1:])

    w_mine, w2x, w2t, taps, base, waves, w_near, x_near, condt = prepare(
        at, w_in, freq_w2, conv_taps, freq_w1, freq_b1, jnp.asarray(feats_aug), jnp.asarray(table), w_out,
        x_own, condt, norms, step, fs
    )
    x_parts = gather_after(x_own, base)
    x_parts = (x_near,) + x_parts[1:]
    forward = forward_spectral(at, x_parts, ids, norms, w_mine, taps, base, w2x, condt, waves)
    z_parts, (u1, n1, p, q, c, vr, vs, mu, mn, cb) = forward[:4], forward[4:]
    ct_x = swap(ct_own, "freq", 2)
    ct_z = swap(ct_own, "batch", 2)
    z_got = trade_parts(z_parts)
    wg_mine, wu_mine, wd_mine = select_columns(at, cb, w_gate, w_up, w_down, bs, fs)
    (ct_x,) = tie([ct_x], cb)
    ct_parts = (ct_own, ct_x, ct_z, swap(ct_x, "batch", 2))
    h, u2, z_t = middle(at, z_got, x_near, w_near, norms, wg_mine, step)
    fed = feed_forward(
        at, u2, h, ct_own, norms, w_near, w_gate, w_up, w_down, step, channels // (bs * fs)
    )
    mixed_out, big_g, gz_parts, gt_own, gt_other, sums2 = fed[0], fed[1], fed[2:6], *fed[6:]
    gt_got = swap(gt_other, "freq", 1)
    ct_parts = ct_parts + tuple(swap(part, "freq", 1) for part in tie(ct_parts, sums2))
    u2_parts = gather_wide(u2, sums2, ct_parts[4])
    gz_got = trade_parts(gz_parts)

    z_got = swap(z_t, "freq", 1)
    keep_a, give_a, keep_b, give_b, keep_o, give_o = hidden_grads(
        at, u2_parts, ct_parts, wg_mine, wu_mine, gt_own, gt_got, z_t, z_got,
        wd_mine, sums2,
    )
    got_a = swap(give_a, "batch", 1)
    got_b = swap(give_b, "batch", 4)
    got_o = swap(give_o, "freq", 2)

    back = backward_spectral(
        at, gz_got, ids, cb, taps, base, w2x, w2t, jnp.asarray(feats).astype(BF16),
        p, q, c, vr, vs, waves, give_a,
    )
    gp_parts, (gp, d_taps, d_w2, d_w1, gcb) = back[:4], back[4:]
    gp_got = trade_parts(gp_parts)

    proj = projection_grads(
        at, gp, u1, n1, w_mine, keep_o, got_o, d_w2, d_w1, d_taps, gcb, condt, mu, mn, sums2, gcb, bs
    )
    p_keep_a, p_give_a, p_keep_b, p_give_b, packed = proj
    p_got_a = swap(p_give_a, "batch", 1)
    p_got_b = swap(p_give_b, "batch", 2)
    keep_a, give_a, keep_b, give_b = halve(
        at, (2, 0), p_give_a, keep_a[None], got_a[None], keep_b[None], got_b[None]
    )
    got_a = swap(give_a, "batch", 4)
    got_b = swap(give_b, "batch", 1)

    p_keep_a, p_give_a, p_keep_b, p_give_b, packed = stage(
        at, p_give_a, pairs(p_keep_a), pairs(p_got_a), p_keep_b, p_got_b, packed
    )
    p_got_a = swap(p_give_a, "batch", 2)
    p_got_b = swap(p_give_b, "batch", 1)
    d_gate, d_up, d_down, token = hidden_last(keep_a, got_a, keep_b, got_b, packed)
    keep, give, packed = join(at, token, p_keep_a, p_got_a, p_keep_b, p_got_b, packed)
    grad_tokens = final(at, gp_got, x_own, big_g, norms, ids, condt, w_in, packed, step)
    got = swap(give, "batch", 4)
    sent = add(packed, swap(packed, "batch", 4), give, BF16)
    (grad_tokens,) = tie([grad_tokens], sent)
    mine = keep.astype(F32) + got.astype(F32)
    first = 2 * width // bs

    d_w2, d_taps, *ln, d_w1, d_b1, d_cond = small_grads(
        at, gather_freq(sent, me), freq_w1.shape[1], channels, step, bs
    )
    return (
        mixed_out[:, None],
        grad_tokens[:, None],
        ln[0],
        ln[1],
        mine[:first].T,
        d_taps,
        d_w1,
        d_b1[0],
        d_w2,
        d_cond.T,
        mine[first:].T,
        ln[2],
        ln[3],
        d_gate.T,
        d_up.T,
        d_down,
    )


def per_device(*args):
    channels = args[0].shape[2]
    step = 2 * channels // (lax.axis_size("batch") * lax.axis_size("freq"))
    fits = lax.axis_size("batch") == 8 and lax.axis_size("freq") == 4 and step % 16 == 0
    return tiled_device(*args) if fits else plain_device(*args)


def solution(mesh):
    rows = P("freq", "batch", None)
    split = P(None, ("batch", "freq"))
    in_specs = (rows, P("batch", None), rows) + (P(),) * 14
    out_specs = (
        rows,
        rows,
        P(),
        P(),
        split,
        P(),
        P(),
        P(),
        P(),
        P(),
        split,
        P(),
        P(),
        split,
        split,
        P(("batch", "freq"), None),
    )
    return jax.shard_map(
        per_device, mesh=mesh, in_specs=in_specs, out_specs=out_specs, check_vma=False
    )
```
